32 devices in a mesh: fsdp: 8 (over z, y), ctx: 2 (over x), tp: 2 (over core).
Axes of the slice: x: 2, y: 2, z: 4, core: 2. Of those that a mesh axis runs over, the one named last changes fastest.
Arguments:
- tokens: bfloat16 [12288, 1536], P(('fsdp', 'ctx')), may hold values from -6 to 6
- out_cotangent: bfloat16 [12288, 1536], P(('fsdp', 'ctx')), may hold values from -6 to 6
- lengths: int32 [8, 4], P('fsdp'), may hold values from 1 to 1152, 1536 in all within a row
- adapter_of_doc: int32 [8, 4], P('fsdp'), may hold values from 0 to 7
- routes: int32 [12288, 8], P(('fsdp', 'ctx')), may hold values from 0 to 15, all different within a row; in each aligned block of 768 rows (0 to 767, 768 to 1535, ...) at most 576 rows name the same one
- attn_gain: float32 [1536], replicated, may hold values from 0.5 to 1.5
- ffn_gain: float32 [1536], replicated, may hold values from 0.5 to 1.5
- w_query: bfloat16 [1536, 1536], P('fsdp', 'tp'), may hold values from -0.15625 to 0.15625
- key_matrix: bfloat16 [1536, 512], P('fsdp', 'tp'), may hold values from -0.15625 to 0.15625
- value_matrix: bfloat16 [1536, 512], P('fsdp', 'tp'), may hold values from -0.15625 to 0.15625
- w_out: bfloat16 [1536, 1536], P('tp', 'fsdp'), may hold values from -0.625 to 0.625
- w_router: bfloat16 [1536, 16], P('fsdp'), may hold values from -0.078125 to 0.078125
- w_gate: bfloat16 [16, 1536, 512], P('fsdp', None, 'tp'), may hold values from -0.15625 to 0.15625
- w_up: bfloat16 [16, 1536, 512], P('fsdp', None, 'tp'), may hold values from -0.15625 to 0.15625
- w_down: bfloat16 [16, 512, 1536], P('fsdp', 'tp'), may hold values from -0.75 to 0.75
- a_query: bfloat16 [1536, 128], P('fsdp'), may hold values from -0.15625 to 0.15625
- b_query: bfloat16 [128, 1536], P('fsdp'), may hold values from -1.5 to 1.5
- a_key: bfloat16 [1536, 128], P('fsdp'), may hold values from -0.15625 to 0.15625
- key_second_factor: bfloat16 [128, 512], P('fsdp'), may hold values from -1.5 to 1.5
- a_value: bfloat16 [1536, 128], P('fsdp'), may hold values from -0.15625 to 0.15625
- value_second_factor: bfloat16 [128, 512], P('fsdp'), may hold values from -1.5 to 1.5
- a_out: bfloat16 [1536, 128], P('fsdp'), may hold values from -0.15625 to 0.15625
- b_out: bfloat16 [128, 1536], P('fsdp'), may hold values from -6 to 6
- a_router: bfloat16 [1536, 128], P('fsdp'), may hold values from -0.15625 to 0.15625
- b_router: bfloat16 [128, 16], P('fsdp'), may hold values from -0.75 to 0.75
- a_gate: bfloat16 [1536, 128], P('fsdp'), may hold values from -0.15625 to 0.15625
- b_gate: bfloat16 [128, 512], P('fsdp'), may hold values from -1.5 to 1.5
- a_up: bfloat16 [1536, 128], P('fsdp'), may hold values from -0.15625 to 0.15625
- b_up: bfloat16 [128, 512], P('fsdp'), may hold values from -1.5 to 1.5
- a_down: bfloat16 [512, 128], P('fsdp'), may hold values from -0.25 to 0.25
- b_down: bfloat16 [128, 1536], P('fsdp'), may hold values from -4 to 4
Outputs:
- output: bfloat16 [12288, 1536], P(('fsdp', 'ctx'))
- grad_tokens: bfloat16 [12288, 1536], P(('fsdp', 'ctx'))
- grad_a_query: float32 [1536, 128], P('fsdp')
- grad_b_query: float32 [128, 1536], P('fsdp')
- grad_a_key: float32 [1536, 128], P('fsdp')
- grad_b_key: float32 [128, 512], P('fsdp')
- grad_a_value: float32 [1536, 128], P('fsdp')
- grad_b_value: float32 [128, 512], P('fsdp')
- grad_a_out: float32 [1536, 128], P('fsdp')
- grad_b_out: float32 [128, 1536], P('fsdp')
- grad_a_router: float32 [1536, 128], P('fsdp')
- grad_b_router: float32 [128, 16], P('fsdp')
- grad_a_gate: float32 [1536, 128], P('fsdp')
- grad_b_gate: float32 [128, 512], P('fsdp')
- grad_a_up: float32 [1536, 128], P('fsdp')
- grad_b_up: float32 [128, 512], P('fsdp')
- grad_a_down: float32 [512, 128], P('fsdp')
- grad_b_down: float32 [128, 1536], P('fsdp')
The draws below stay inside these ranges and needn't reach their ends.
Inputs may be any that keep to these rules, and one draw needn't show every extreme that they name: `lengths`: each row sums to 1536; every row has one document of exactly 1152 tokens. `routes`: each row names 8 different experts. Within the 768 rows of one device no expert is named more than 576 times, and some expert reaches 576 in some device's rows.
All inputs are finite; a program needn't handle non-finite values.
Results may differ from the reference program's by a relative error of at most 0.024.
Values may be sent and summed in bfloat16 or wider, within the bound.
A program may use at most 512 MiB of HBM per device.

```python
import math
import jax
import jax.numpy as jnp
import numpy as np
from jax import lax

MODEL_WIDTH = 1536
QUERY_HEADS = 24
KEY_VALUE_HEADS = 8
HEAD_SIZE = 64
FFE = 512
TOPK = 8
ADAPTER_RANK = 16
ADAPTER_COUNT = 8
NDOC = 4
TOK_DEV = 768
GROUP = 1536
LONGEST = 1152
TOKEN_COUNT = 12288
EXPERTS = 16
CAP = 576
N_FSDP = 8
N_CTX = 2
N_TP = 2


def plant(entries, stream_key, low, top_value):
    shape = entries.shape
    spot = [jax.random.randint(jax.random.fold_in(stream_key, axis), (), 0, shape[axis]) for axis in range(len(shape))]
    entries = entries.at[tuple(spot)].set(low)
    longest = shape.index(max(shape))
    spot[longest] = (spot[longest] + 1) % shape[longest]
    return entries.at[tuple(spot)].set(top_value)


def shard_levels(own_key, extent, split, low, high):
    loudness, own = 1.0, jax.random.fold_in(own_key, 6)
    for dim, parts in split:
        heights = jnp.exp(jax.random.uniform(jax.random.fold_in(own, dim), (parts,), jnp.float32, low / len(split), high / len(split)))
        loudness = loudness * jnp.repeat(heights, extent[dim] // parts).reshape([-1 if axis == dim else 1 for axis in range(len(extent))])
    return loudness


def split_up(count, total, reach, slope):
    loads = [(1 << 20) // math.isqrt(grade ** slope) + 1 for grade in range(2, count + 1)]
    surplus, counts = total - reach - (count - 1), [1] * (count - 1)
    while surplus > 0:
        movable = [i for i in range(count - 1) if counts[i] < reach]
        pool, left = sum([loads[i] for i in movable]), surplus
        for i in movable:
            more = min(reach - counts[i], max(1, left * loads[i] // pool), surplus)
            counts[i] = counts[i] + more
            surplus = surplus - more
    return np.array([reach] + counts)


def ragged_sizes(rng, number_of, total, limit, skew):
    if number_of == 2:
        one = jax.random.randint(rng, (), max(1, total - limit), min(limit, total - 1) + 1)
        return jnp.stack([one, total - one])
    sizes = jnp.asarray(split_up(number_of, total, limit, skew), jnp.int32)
    pairs = (number_of - 1) // 2
    giver, receiver = sizes[1:1 + 2 * pairs:2], sizes[2:2 + 2 * pairs:2]
    slack = jnp.minimum(giver - 1, limit - receiver)
    shifted = jax.random.randint(jax.random.fold_in(rng, 1), (pairs,), 0, 1 << 20) % (slack + 1)
    sizes = sizes.at[1:1 + 2 * pairs:2].set(giver - shifted).at[2:2 + 2 * pairs:2].set(receiver + shifted)
    return sizes[jax.random.permutation(jax.random.fold_in(rng, 2), number_of)]


def assign_block(key, own, number, rows, count, top, reach, slope):
    ranking = jax.random.permutation(key, count)
    packed, ordinary = shares(count, rows * top, reach, slope, True), shares(count, rows * top, reach, slope, False)
    places = jnp.arange(count)

    def named(tallies, offset_by):
        used = int((tallies > 0).sum())
        fixed = max(1, used // 4)
        shifted = fixed + (places - fixed + offset_by * (used - fixed)) % max(1, count - fixed)
        return jnp.zeros((count,), jnp.int32).at[ranking[jnp.where(places < fixed, places, shifted)]].set(jnp.asarray(tallies, jnp.int32))

    tallies = jnp.where(number % 4 == 0, named(packed, number // 4), named(ordinary, number - number // 4 - 1))
    mixed = jax.random.permutation(jax.random.fold_in(own, 3), count)
    giver, sink = mixed[0:count // 2 * 2:2], mixed[1:count // 2 * 2:2]
    room = jnp.minimum(tallies[giver] - 1, reach - tallies[sink]) // 2
    room = jnp.where((giver == ranking[0]) | (sink == ranking[0]) | (tallies[sink] == 0), 0, jnp.maximum(room, 0))
    shifted = jax.random.randint(jax.random.fold_in(own, 4), (count // 2,), 0, 1 << 20) % (room + 1)
    tallies = tallies.at[giver].add(-shifted).at[sink].add(shifted)
    members = jnp.searchsorted(jnp.cumsum(tallies), jnp.arange(rows * top), side="right").astype(jnp.int32)
    table = members.reshape(top, rows).T
    table = table[jax.random.permutation(jax.random.fold_in(own, 1), rows)]
    offset_by = jax.random.randint(jax.random.fold_in(own, 2), (rows, 1), 0, top)
    return jnp.take_along_axis(table, (jnp.arange(top)[None, :] + offset_by) % top, axis=1)


def shares(count, total, most, skew, full):
    loads = [(1 << 20) // math.isqrt(standing ** skew) + 1 for standing in range(1, count + 1)]
    largest = most if full else min(most, max(-(-total // count), total * loads[0] // sum(loads)))
    least = 1 if total - largest >= count - 1 else 0
    counts, surplus = [largest] + [least] * (count - 1), total - largest - least * (count - 1)
    while surplus > 0:
        free = [i for i in range(1, count) if counts[i] < largest] or [i for i in range(1, count) if counts[i] < most]
        pool, left = sum([loads[i] for i in free]), surplus
        for i in free:
            addition = min(most - counts[i], max(1, left * loads[i] // pool), surplus)
            counts[i] = counts[i] + addition
            surplus = surplus - addition
    return np.array(counts)


def centred(key, dims, deviation, most, split=(), kind=jnp.bfloat16):
    array = deviation * jax.random.normal(key, dims, jnp.float32)
    if split:
        array = array * shard_levels(key, dims, split, -0.22, 0.18)
    return jnp.clip(array, -most, most).astype(kind)


def setup_inputs(seed: int = 0) -> dict:
    key_list = jax.random.split(jax.random.key(seed), 32)
    tokens = centred(key_list[0], (TOKEN_COUNT, MODEL_WIDTH), 1.0, 6.0, ((0, 16),))
    out_cotangent = centred(key_list[1], (TOKEN_COUNT, MODEL_WIDTH), 1.0, 6.0, ((0, 16),))
    lengths = jax.vmap(lambda own: ragged_sizes(own, NDOC, GROUP, LONGEST, 2))(jax.random.split(key_list[2], N_FSDP)).reshape((N_FSDP, NDOC)).astype(jnp.int32)
    adapter_of_doc = plant(jax.random.randint(key_list[3], (N_FSDP, NDOC), 0, ADAPTER_COUNT), jax.random.fold_in(key_list[3], 1), 0, ADAPTER_COUNT - 1).astype(jnp.int32)
    routes_keys = jax.random.split(jax.random.fold_in(key_list[4], 1), TOKEN_COUNT // TOK_DEV)
    routes_turns = jax.random.permutation(jax.random.fold_in(key_list[4], 3), TOKEN_COUNT // TOK_DEV)
    routes = jax.vmap(lambda own, number: assign_block(jax.random.fold_in(key_list[4], 2), own, number, TOK_DEV, EXPERTS, TOPK, CAP, 2))(routes_keys, routes_turns).reshape((TOKEN_COUNT, TOPK))
    attn_gain = jnp.clip(1.0 + 0.1 * jax.random.normal(key_list[5], (MODEL_WIDTH,), jnp.float32), 0.5, 1.5)
    ffn_gain = jnp.clip(1.0 + 0.1 * jax.random.normal(key_list[6], (MODEL_WIDTH,), jnp.float32), 0.5, 1.5)
    w_query = centred(key_list[7], (MODEL_WIDTH, QUERY_HEADS * HEAD_SIZE), MODEL_WIDTH ** -0.5, 0.15625, ((0, 8), (1, 2)))
    key_matrix = centred(key_list[8], (MODEL_WIDTH, KEY_VALUE_HEADS * HEAD_SIZE), MODEL_WIDTH ** -0.5, 0.15625, ((0, 8), (1, 2)))
    value_matrix = centred(key_list[9], (MODEL_WIDTH, KEY_VALUE_HEADS * HEAD_SIZE), MODEL_WIDTH ** -0.5, 0.15625, ((0, 8), (1, 2)))
    w_out = centred(key_list[10], (QUERY_HEADS * HEAD_SIZE, MODEL_WIDTH), (max(QUERY_HEADS * HEAD_SIZE // 16, 1)) ** -0.5, 0.625, ((0, 2), (1, 8)))
    w_router = centred(key_list[11], (MODEL_WIDTH, EXPERTS), (4 * MODEL_WIDTH) ** -0.5, 0.078125, ((0, 8),))
    w_gate = centred(key_list[12], (EXPERTS, MODEL_WIDTH, FFE), MODEL_WIDTH ** -0.5, 0.15625, ((0, 8), (2, 2)))
    w_up = centred(key_list[13], (EXPERTS, MODEL_WIDTH, FFE), MODEL_WIDTH ** -0.5, 0.15625, ((0, 8), (2, 2)))
    w_down = centred(key_list[14], (EXPERTS, FFE, MODEL_WIDTH), (max(FFE // 8, 1)) ** -0.5, 0.75, ((0, 8), (1, 2)))
    a_query = centred(key_list[15], (MODEL_WIDTH, ADAPTER_COUNT * ADAPTER_RANK), MODEL_WIDTH ** -0.5, 0.15625, ((0, 8),))
    b_query = centred(key_list[16], (ADAPTER_COUNT * ADAPTER_RANK, QUERY_HEADS * HEAD_SIZE), ADAPTER_RANK ** -0.5, 1.5, ((0, 8),))
    a_key = centred(key_list[17], (MODEL_WIDTH, ADAPTER_COUNT * ADAPTER_RANK), MODEL_WIDTH ** -0.5, 0.15625, ((0, 8),))
    key_second_factor = centred(key_list[18], (ADAPTER_COUNT * ADAPTER_RANK, KEY_VALUE_HEADS * HEAD_SIZE), ADAPTER_RANK ** -0.5, 1.5, ((0, 8),))
    a_value = centred(key_list[19], (MODEL_WIDTH, ADAPTER_COUNT * ADAPTER_RANK), MODEL_WIDTH ** -0.5, 0.15625, ((0, 8),))
    value_second_factor = centred(key_list[20], (ADAPTER_COUNT * ADAPTER_RANK, KEY_VALUE_HEADS * HEAD_SIZE), ADAPTER_RANK ** -0.5, 1.5, ((0, 8),))
    a_out = centred(key_list[21], (QUERY_HEADS * HEAD_SIZE, ADAPTER_COUNT * ADAPTER_RANK), (QUERY_HEADS * HEAD_SIZE) ** -0.5, 0.15625, ((0, 8),))
    b_out = centred(key_list[22], (ADAPTER_COUNT * ADAPTER_RANK, MODEL_WIDTH), (max(ADAPTER_RANK // 16, 1)) ** -0.5, 6.0, ((0, 8),))
    a_router = centred(key_list[23], (MODEL_WIDTH, ADAPTER_COUNT * ADAPTER_RANK), MODEL_WIDTH ** -0.5, 0.15625, ((0, 8),))
    b_router = centred(key_list[24], (ADAPTER_COUNT * ADAPTER_RANK, EXPERTS), (4 * ADAPTER_RANK) ** -0.5, 0.75, ((0, 8),))
    a_gate = centred(key_list[25], (MODEL_WIDTH, ADAPTER_COUNT * ADAPTER_RANK), MODEL_WIDTH ** -0.5, 0.15625, ((0, 8),))
    b_gate = centred(key_list[26], (ADAPTER_COUNT * ADAPTER_RANK, FFE), ADAPTER_RANK ** -0.5, 1.5, ((0, 8),))
    a_up = centred(key_list[27], (MODEL_WIDTH, ADAPTER_COUNT * ADAPTER_RANK), MODEL_WIDTH ** -0.5, 0.15625, ((0, 8),))
    b_up = centred(key_list[28], (ADAPTER_COUNT * ADAPTER_RANK, FFE), ADAPTER_RANK ** -0.5, 1.5, ((0, 8),))
    a_down = centred(key_list[29], (FFE, ADAPTER_COUNT * ADAPTER_RANK), FFE ** -0.5, 0.25, ((0, 8),))
    b_down = centred(key_list[30], (ADAPTER_COUNT * ADAPTER_RANK, MODEL_WIDTH), (max(ADAPTER_RANK // 8, 1)) ** -0.5, 4.0, ((0, 8),))
    return {"tokens": tokens, "out_cotangent": out_cotangent, "lengths": lengths, "adapter_of_doc": adapter_of_doc, "routes": routes, "attn_gain": attn_gain, "ffn_gain": ffn_gain, "w_query": w_query, "key_matrix": key_matrix, "value_matrix": value_matrix, "w_out": w_out, "w_router": w_router, "w_gate": w_gate, "w_up": w_up, "w_down": w_down, "a_query": a_query, "b_query": b_query, "a_key": a_key, "key_second_factor": key_second_factor, "a_value": a_value, "value_second_factor": value_second_factor, "a_out": a_out, "b_out": b_out, "a_router": a_router, "b_router": b_router, "a_gate": a_gate, "b_gate": b_gate, "a_up": a_up, "b_up": b_up, "a_down": a_down, "b_down": b_down}


@jax.custom_vjp
def lowrank_middle(v):
    return lax.optimization_barrier(v.astype(jnp.bfloat16)).astype(jnp.float32)

@jax.custom_vjp
def low_back(v):
    return v

def low_keep(v):
    return (lowrank_middle(v), None)

def low_pass(kept, grad):
    return (grad,)

def back_keep(v):
    return (v, None)

def back_low(kept, grad):
    return (lowrank_middle(grad),)
lowrank_middle.defvjp(low_keep, low_pass)
low_back.defvjp(back_keep, back_low)
norm_eps = 1e-05

def matmul(left, right):
    return jnp.dot(left, right, precision=lax.Precision.HIGHEST)

def rms_norm(values, gain):
    return values * lax.rsqrt(lax.optimization_barrier(jnp.mean(values * values, axis=-1, keepdims=True)) + norm_eps) * gain

def rotary_apply(values, cosine_table, sine_table):
    half = values.shape[-1] // 2
    first = values[..., :half]
    second = values[..., half:]
    return jnp.concatenate([first * cosine_table - second * sine_table, first * sine_table + second * cosine_table], axis=-1)

def doc_layout(lengths, adapter_of_doc, query_group):
    ends = jnp.cumsum(lengths, axis=1).astype(jnp.int32)
    starts = (ends - lengths).astype(jnp.int32)
    place = jnp.arange(query_group, dtype=jnp.int32)
    document_index = lax.optimization_barrier(jnp.sum((place[None, :, None] >= ends[:, None, :]).astype(jnp.int32), axis=2)).astype(jnp.int32)
    picked = (document_index[:, :, None] == jnp.arange(lengths.shape[1], dtype=jnp.int32)[None, None, :]).astype(jnp.int32)
    begin = lax.optimization_barrier(jnp.sum(picked * starts[:, None, :], axis=2)).astype(jnp.int32)
    chosen = lax.optimization_barrier(jnp.sum(picked * adapter_of_doc[:, None, :], axis=2)).astype(jnp.int32)
    return (document_index, (place[None, :] - begin).astype(jnp.int32), chosen)

def reference(tokens, out_cotangent, lengths, adapter_of_doc, routes, attn_gain, ffn_gain, w_query, key_matrix, value_matrix, w_out, w_router, w_gate, w_up, w_down, a_query, b_query, a_key, key_second_factor, a_value, value_second_factor, a_out, b_out, a_router, b_router, a_gate, b_gate, a_up, b_up, a_down, b_down):
    query_group = TOK_DEV * N_CTX
    document_index, position, chosen = doc_layout(lengths, adapter_of_doc, query_group)
    chosen_flat = chosen.reshape(-1)
    rank_cols = ADAPTER_COUNT * ADAPTER_RANK
    adapter_mask = (chosen_flat[:, None] == (jnp.arange(rank_cols, dtype=jnp.int32) // ADAPTER_RANK)[None, :]).astype(jnp.float32)
    half = HEAD_SIZE // 2
    freq = 10000.0 ** (-jnp.arange(half, dtype=jnp.float32) / half)
    angles = position.reshape(-1).astype(jnp.float32)[:, None] * freq[None, :]
    cosine_table = jnp.cos(angles)[:, None, :]
    sine_table = jnp.sin(angles)[:, None, :]
    scale = 1.0 / math.sqrt(HEAD_SIZE)
    query_w = w_query.astype(jnp.float32)
    key_w = key_matrix.astype(jnp.float32)
    value_w = value_matrix.astype(jnp.float32)
    out_w = w_out.astype(jnp.float32)
    router_w = w_router.astype(jnp.float32)
    gate_all = w_gate.astype(jnp.float32)
    up_all = w_up.astype(jnp.float32)
    down_all = w_down.astype(jnp.float32)
    blocks = N_FSDP * N_CTX
    flat = routes.reshape(blocks, TOK_DEV * TOPK)
    hot = (flat[:, :, None] == jnp.arange(EXPERTS, dtype=jnp.int32)[None, None, :]).astype(jnp.int32)
    slot = lax.optimization_barrier(jnp.sum((jnp.cumsum(hot, axis=1).astype(jnp.int32) - hot) * hot, axis=2)).astype(jnp.int32)
    block_ids = jnp.arange(blocks, dtype=jnp.int32)[:, None]
    route_ids = (jnp.arange(TOK_DEV * TOPK, dtype=jnp.int32)[None, :] + block_ids * (TOK_DEV * TOPK)).astype(jnp.int32)
    owner = jnp.full((blocks, EXPERTS * CAP), -1, dtype=jnp.int32).at[block_ids, flat * CAP + slot].set(route_ids)
    owner = owner.reshape(blocks, EXPERTS, CAP).transpose(1, 0, 2).reshape(EXPERTS, blocks * CAP)
    width = FFE // N_TP

    def attend_heads(block):
        query_rows, keys, values, docs = block
        place = jnp.arange(query_group, dtype=jnp.int32)
        allowed = (docs[:, None] == docs[None, :]) & (place[None, :] <= place[:, None])
        reshaped_input = query_rows.reshape(query_group, KEY_VALUE_HEADS, QUERY_HEADS // KEY_VALUE_HEADS, HEAD_SIZE)
        scores = jnp.einsum('qgrd,kgd->grqk', reshaped_input, keys, precision=lax.Precision.HIGHEST)
        scores = low_back(scores * scale)
        scores = jnp.where(allowed[None, None], scores, -1e+30)
        weights = jax.nn.softmax(scores, axis=-1)
        mixed_heads = jnp.einsum('grqk,kgd->qgrd', lowrank_middle(weights), values, precision=lax.Precision.HIGHEST)
        return mixed_heads.reshape(query_group, QUERY_HEADS * HEAD_SIZE)

    def forward(inputs, adapters):
        aq, bq, ak, bk, av, bv, ao, bo, ar, br, ag, bg, au, bu, ad, bd = adapters

        def lowrank(normed, first, second):
            return matmul(matmul(normed, first) * adapter_mask, second)
        normed = lowrank_middle(rms_norm(inputs, attn_gain))
        query_state = low_back(matmul(normed, query_w) + lowrank(normed, aq, bq))
        key = low_back(matmul(normed, key_w) + lowrank(normed, ak, bk))
        value_state = lowrank_middle(low_back(matmul(normed, value_w) + lowrank(normed, av, bv)))
        query_state = lowrank_middle(rotary_apply(query_state.reshape(TOKEN_COUNT, QUERY_HEADS, HEAD_SIZE), cosine_table, sine_table))
        key = lowrank_middle(rotary_apply(key.reshape(TOKEN_COUNT, KEY_VALUE_HEADS, HEAD_SIZE), cosine_table, sine_table))
        mixed_heads = lax.map(jax.checkpoint(attend_heads), (query_state.reshape(N_FSDP, query_group, QUERY_HEADS, HEAD_SIZE), key.reshape(N_FSDP, query_group, KEY_VALUE_HEADS, HEAD_SIZE), value_state.reshape(N_FSDP, query_group, KEY_VALUE_HEADS, HEAD_SIZE), document_index))
        mixed_heads = lowrank_middle(low_back(mixed_heads.reshape(TOKEN_COUNT, QUERY_HEADS * HEAD_SIZE)))
        attended = low_back(matmul(mixed_heads, out_w) + lowrank(mixed_heads, ao, bo))
        hidden = inputs + attended
        normed_two = lowrank_middle(rms_norm(hidden, ffn_gain))
        logits = low_back(matmul(normed_two, router_w) + lowrank(normed_two, ar, br))
        gates = jax.nn.softmax(jnp.take_along_axis(logits, routes, axis=1), axis=-1)
        low_in = lowrank_middle(jnp.concatenate([matmul(normed_two, ag) * adapter_mask, matmul(normed_two, au) * adapter_mask], axis=1))
        gate_flat = gates.reshape(-1)

        def expert_step(total, item):
            gate_w, up_w, down_w, owned = item
            live = (owned >= 0).astype(jnp.float32)[:, None]
            safe = jnp.maximum(owned, 0)
            token = safe // TOPK
            rows_in = normed_two[token] * live
            lows_in = low_in[token] * live
            masks = adapter_mask[token] * live
            weight = gate_flat[safe][:, None] * live
            summed = jnp.zeros((owned.shape[0], MODEL_WIDTH), jnp.float32)
            for part in range(N_TP):
                lo_col = part * width
                hi_col = lo_col + width
                rows_part = low_back(rows_in)
                low_part = low_back(lows_in)
                gate_val = low_back(matmul(rows_part, gate_w[:, lo_col:hi_col]) + matmul(low_part[:, :rank_cols], bg[:, lo_col:hi_col]))
                up_val = low_back(matmul(rows_part, up_w[:, lo_col:hi_col]) + matmul(low_part[:, rank_cols:], bu[:, lo_col:hi_col]))
                act = lowrank_middle(jax.nn.silu(gate_val) * up_val)
                down_low = lowrank_middle(matmul(act, ad[lo_col:hi_col]) * masks)
                summed = summed + lowrank_middle(low_back(matmul(act, down_w[lo_col:hi_col]) + matmul(down_low, bd)))
            return (total.at[token].add(weight * summed), None)
        moe, unused = lax.scan(jax.checkpoint(expert_step), jnp.zeros((TOKEN_COUNT, MODEL_WIDTH), jnp.float32), (gate_all, up_all, down_all, owner))
        return hidden + moe
    adapters = tuple((item.astype(jnp.float32) for item in (a_query, b_query, a_key, key_second_factor, a_value, value_second_factor, a_out, b_out, a_router, b_router, a_gate, b_gate, a_up, b_up, a_down, b_down)))
    result, pullback = jax.vjp(forward, tokens.astype(jnp.float32), adapters)
    grad_in, grads = pullback(out_cotangent.astype(jnp.float32))
    return (result.astype(jnp.bfloat16), grad_in.astype(jnp.bfloat16), grads[0], grads[1], grads[2], grads[3], grads[4], grads[5], grads[6], grads[7], grads[8], grads[9], grads[10], grads[11], grads[12], grads[13], grads[14], grads[15])
```

```python
import math

import jax
import jax.numpy as jnp
from jax import lax
from jax.sharding import PartitionSpec as P

HEAD_SIZE = 64
ADAPTER_RANK = 16
LANES = 128
norm_eps = 1e-05
BF = jnp.bfloat16
F32 = jnp.float32


def dot(left, right, dims=((1,), (0,))):
    return lax.dot_general(left, right, (dims, ((), ())), preferred_element_type=F32)


def dot_t(left, right):
    return dot(left, right, ((1,), (1,)))


def t_dot(left, right):
    return dot(left, right, ((0,), (0,)))


def rms_norm(values, gain):
    return values * lax.rsqrt(jnp.mean(values * values, axis=-1, keepdims=True) + norm_eps) * gain


def norm_back(values, gain, grad):
    unused, pull = jax.vjp(lambda inner: rms_norm(inner, gain), values)
    return pull(grad)[0]


def rotary_apply(values, cosine_table, sine_table):
    half = values.shape[-1] // 2
    first = values[..., :half]
    second = values[..., half:]
    return jnp.concatenate(
        [first * cosine_table - second * sine_table, first * sine_table + second * cosine_table],
        axis=-1,
    )


def levels(n):
    outer = 4 if n % 4 == 0 else n
    return outer, n // outer


def spread(block):
    n = lax.axis_size("fsdp")
    outer, inner = levels(n)
    me = lax.axis_index("fsdp")
    held = [block]
    for unused in range(outer - 1):
        held.append(lax.ppermute(held[-1], "fsdp", [(i, (i + inner) % n) for i in range(n)]))
    rows = [held]
    turn = [(i, i // inner * inner + (i % inner + 1) % inner) for i in range(n)]
    for unused in range(inner - 1):
        rows.append([lax.ppermute(h, "fsdp", turn) for h in rows[-1]])
    found = []
    for dj, row in enumerate(rows):
        for do, part in enumerate(row):
            owner = (me // inner - do + outer) % outer * inner + (me % inner - dj + inner) % inner
            found.append((owner, part))
    return found


def gathered(block):
    n = lax.axis_size("fsdp")
    whole = jnp.zeros((n,) + block.shape, block.dtype)
    for owner, part in spread(block):
        whole = lax.dynamic_update_index_in_dim(whole, part, owner, 0)
    return whole


def tiles(matrix):
    rows, cols = matrix.shape
    if cols % LANES:
        matrix = jnp.pad(matrix, ((0, 0), (0, LANES - cols % LANES)))
    return [matrix[:, i : i + LANES] for i in range(0, matrix.shape[1], LANES)]


def on_device(
    tokens, out_cotangent, lengths, adapter_of_doc, routes, attn_gain, ffn_gain,
    w_query, key_matrix, value_matrix, w_out, w_router, w_gate, w_up, w_down,
    a_query, b_query, a_key, key_second_factor, a_value, value_second_factor,
    a_out, b_out, a_router, b_router, a_gate, b_gate, a_up, b_up, a_down, b_down,
):
    rows, width = tokens.shape
    n = lax.axis_size("fsdp")
    n_tp = lax.axis_size("tp")
    tp_at = lax.axis_index("tp")
    ctx_at = lax.axis_index("ctx")
    group = rows * lax.axis_size("ctx")
    q_width = w_query.shape[1]
    kv_width = key_matrix.shape[1]
    ff_width = w_gate.shape[2]
    local_experts = w_gate.shape[0]
    experts = w_router.shape[1]
    ranks = a_query.shape[1]
    share = w_query.shape[0]
    low_rows = b_query.shape[0]

    def tp_cols(matrix, size):
        return lax.dynamic_slice_in_dim(matrix, tp_at * size, size, 1)

    def packed_low(parts, height):
        stack = jnp.concatenate(sum([tiles(p) for p in parts], []), axis=0)
        blocks = -(-stack.shape[0] // height)
        stack = jnp.pad(stack, ((0, blocks * height - stack.shape[0]), (0, 0)))
        return [stack[i * height : (i + 1) * height] for i in range(blocks)]

    first_low = [tp_cols(b_query, q_width), tp_cols(key_second_factor, kv_width), tp_cols(value_second_factor, kv_width)]
    second_low = [tp_cols(b_gate, ff_width), tp_cols(b_up, ff_width), b_out, b_down, b_router]
    base_one = [w_query, key_matrix, value_matrix, a_query, a_key, a_value]
    pack_one = jnp.concatenate(base_one + packed_low(first_low, share), axis=1)
    router_pad = jnp.pad(w_router, ((0, 0), (0, LANES - experts)))
    base_two = [w_out.T, a_router, a_gate, a_up, router_pad, a_out]
    pack_two = jnp.concatenate(base_two + packed_low(second_low + [a_down], share), axis=1)
    expert_block = jnp.concatenate([w_gate, w_up, jnp.swapaxes(w_down, 1, 2)], axis=2)

    one = gathered(pack_one)
    two = gathered(pack_two)
    expert_parts = spread(expert_block)

    def unpack_low(whole, col, parts):
        flat = whole[:, :, col:]
        flat = flat.reshape(n, share, -1, LANES).transpose(0, 2, 1, 3).reshape(n, -1, LANES)
        found = []
        at = 0
        for height, cols in parts:
            count = -(-cols // LANES)
            piece = flat[:, at : at + count * height].reshape(n, count, height, LANES)
            found.append(piece.transpose(0, 2, 1, 3).reshape(n * height, count * LANES))
            at += count * height
        return found

    w_one = one.reshape(n * share, -1)
    cols_one = q_width + 2 * kv_width + 3 * ranks
    query_b, key_b, value_b = unpack_low(one, cols_one, [(low_rows, q_width), (low_rows, kv_width), (low_rows, kv_width)])
    w_two = two.reshape(n * share, -1)
    cols_two = q_width + 5 * ranks
    gate_b, up_b, out_b, down_b, router_b, down_a = unpack_low(
        two,
        cols_two,
        [(low_rows, ff_width), (low_rows, ff_width), (low_rows, width), (low_rows, width), (low_rows, experts), (a_down.shape[0], ranks)],
    )
    out_wt = w_two[:, :q_width]
    router_a = w_two[:, q_width : q_width + ranks]
    gate_a = w_two[:, q_width + ranks : q_width + 2 * ranks]
    up_a = w_two[:, q_width + 2 * ranks : q_width + 3 * ranks]
    router_w = w_two[:, q_width + 3 * ranks : q_width + 4 * ranks]
    out_a = lax.dynamic_slice_in_dim(w_two[:, q_width + 4 * ranks : q_width + 5 * ranks], tp_at * q_width, q_width, 0)
    down_at = lax.dynamic_slice_in_dim(down_a, tp_at * ff_width, ff_width, 0)

    ends = jnp.cumsum(lengths[0])
    starts = ends - lengths[0]
    place = jnp.arange(group, dtype=jnp.int32)
    doc = jnp.sum((place[:, None] >= ends[None, :]).astype(jnp.int32), axis=1)
    picked = (doc[:, None] == jnp.arange(lengths.shape[1], dtype=jnp.int32)[None, :]).astype(jnp.int32)
    begin = jnp.sum(picked * starts[None, :], axis=1)
    chosen = jnp.sum(picked * adapter_of_doc[0][None, :], axis=1)
    start = ctx_at * rows
    query_index = start + jnp.arange(rows, dtype=jnp.int32)
    begin_local = lax.dynamic_slice_in_dim(begin, start, rows)
    chosen_local = lax.dynamic_slice_in_dim(chosen, start, rows)
    key_index = start - rows + jnp.arange(2 * rows, dtype=jnp.int32)
    allowed = (
        (key_index[None, :] <= query_index[:, None])
        & (key_index[None, :] >= begin_local[:, None])
        & (key_index[None, :] >= 0)
    )
    mask = (chosen_local[:, None] == (jnp.arange(ranks, dtype=jnp.int32) // ADAPTER_RANK)[None, :]).astype(F32)
    half = HEAD_SIZE // 2
    freq = 10000.0 ** (-jnp.arange(half, dtype=F32) / half)
    angles = (query_index - begin_local).astype(F32)[:, None] * freq[None, :]
    cosine_table = jnp.cos(angles)[:, None, :]
    sine_table = jnp.sin(angles)[:, None, :]
    scale = 1.0 / math.sqrt(HEAD_SIZE)
    heads_kv = kv_width // HEAD_SIZE
    per_group = q_width // kv_width

    xfull = tokens.astype(F32)
    normed = rms_norm(xfull, attn_gain).astype(BF)
    raw = dot(normed, w_one[:, :cols_one])
    qkv = q_width + 2 * kv_width
    query_u = (raw[:, qkv : qkv + ranks] * mask).astype(BF)
    key_u = (raw[:, qkv + ranks : qkv + 2 * ranks] * mask).astype(BF)
    value_u = (raw[:, qkv + 2 * ranks : qkv + 3 * ranks] * mask).astype(BF)
    query_pre = raw[:, :q_width] + dot(query_u, query_b)
    key_pre = raw[:, q_width : q_width + kv_width] + dot(key_u, key_b)
    value_state = (raw[:, q_width + kv_width : qkv] + dot(value_u, value_b)).astype(BF)
    query_state = (
        rotary_apply(query_pre.reshape(rows, -1, HEAD_SIZE), cosine_table, sine_table).reshape(rows, q_width).astype(BF)
    )
    key = rotary_apply(key_pre.reshape(rows, -1, HEAD_SIZE), cosine_table, sine_table).reshape(rows, kv_width).astype(BF)
    far = lax.ppermute(jnp.concatenate([key, value_state], axis=1), "ctx", [(i, i + 1) for i in range(lax.axis_size("ctx") - 1)])
    keys_h = jnp.concatenate([far[:, :kv_width], key], axis=0).reshape(2 * rows, heads_kv, HEAD_SIZE)
    values_h = jnp.concatenate([far[:, kv_width:], value_state], axis=0).reshape(2 * rows, heads_kv, HEAD_SIZE)
    query_h = query_state.reshape(rows, heads_kv, per_group, HEAD_SIZE)

    def score_block():
        s = jnp.einsum("qgrd,kgd->grqk", query_h, keys_h, preferred_element_type=F32) * scale
        return jnp.where(allowed[None, None], s, -1e30)

    scores = score_block()
    top = jnp.max(scores, axis=-1, keepdims=True)
    expd = jnp.exp(scores - top)
    total = jnp.sum(expd, axis=-1, keepdims=True)
    probs = expd / total
    log_total = top + jnp.log(total)
    mixed_heads = (
        jnp.einsum("grqk,kgd->qgrd", probs.astype(BF), values_h, preferred_element_type=F32).reshape(rows, q_width).astype(BF)
    )
    out_u = dot(mixed_heads, out_a) * mask
    attn_part = dot_t(mixed_heads, out_wt) + dot(out_u.astype(BF), out_b)
    hidden = xfull + lax.psum(attn_part, "tp")
    normed_two = rms_norm(hidden, ffn_gain).astype(BF)
    lows = dot(normed_two, w_two[:, q_width : q_width + 4 * ranks])
    router_u = (lows[:, :ranks] * mask).astype(BF)
    zin_gate = (lows[:, ranks : 2 * ranks] * mask).astype(BF)
    zin_up = (lows[:, 2 * ranks : 3 * ranks] * mask).astype(BF)
    logits = lows[:, 3 * ranks : 3 * ranks + experts] + dot(router_u, router_b)[:, :experts]
    selected = jnp.any(routes[:, :, None] == jnp.arange(experts, dtype=jnp.int32)[None, None, :], axis=1)
    gates = jax.nn.softmax(jnp.where(selected, logits, -jnp.inf), axis=-1)

    cot = out_cotangent
    dout = cot.astype(F32)
    gate_low = dot(zin_gate, gate_b)
    up_low = dot(zin_up, up_b)
    down_back = dot_t(cot, down_b) * mask
    act_low = dot_t(down_back.astype(BF), down_at)
    moe = jnp.zeros((rows, width), F32)
    dn2 = jnp.zeros((rows, width), F32)
    act_sum = jnp.zeros((rows, ff_width), F32)
    dg_sum = jnp.zeros((rows, ff_width), F32)
    du_sum = jnp.zeros((rows, ff_width), F32)
    dgate = jnp.zeros((rows, experts), F32)
    for owner, part in expert_parts:
        for j in range(local_experts):
            e = owner * local_experts + j
            w_gu = part[j][:, : 2 * ff_width]
            w_d = part[j][:, 2 * ff_width :]
            g = lax.dynamic_slice_in_dim(gates, e, 1, 1)
            pre = dot(normed_two, w_gu)
            gv = pre[:, :ff_width] + gate_low
            uv = pre[:, ff_width:] + up_low
            sig = jax.nn.sigmoid(gv)
            silu = gv * sig
            act = silu * uv
            back = dot(cot, w_d) + act_low
            col = jnp.sum(act * back, axis=1, keepdims=True)
            dgate = dgate + jnp.where(jnp.arange(experts)[None, :] == e, col, 0.0)
            act_g = (act * g).astype(BF)
            back = back * g
            dg = (back * uv * sig * (1.0 + gv * (1.0 - sig))).astype(BF)
            du = (back * silu).astype(BF)
            moe = moe + dot_t(act_g, w_d)
            dn2 = dn2 + dot_t(jnp.concatenate([dg, du], axis=1), w_gu)
            act_sum = act_sum + act_g.astype(F32)
            dg_sum = dg_sum + dg.astype(F32)
            du_sum = du_sum + du.astype(F32)
    down_low = (dot(act_sum.astype(BF), down_at) * mask).astype(BF)
    moe = moe + dot(down_low, down_b)
    output = (hidden + lax.psum(moe.astype(BF), "tp").astype(F32)).astype(BF)
    grad_bd = t_dot(down_low, cot)
    grad_ad = t_dot(act_sum.astype(BF), down_back.astype(BF))
    dg_sum = dg_sum.astype(BF)
    du_sum = du_sum.astype(BF)
    grad_bg = t_dot(zin_gate, dg_sum)
    grad_bu = t_dot(zin_up, du_sum)
    gate_du = (dot_t(dg_sum, gate_b) * mask).astype(BF)
    up_du = (dot_t(du_sum, up_b) * mask).astype(BF)
    dn2 = dn2 + dot_t(gate_du, gate_a) + dot_t(up_du, up_a)
    grad_ag = t_dot(normed_two, gate_du)
    grad_au = t_dot(normed_two, up_du)
    dn2, dgate = lax.psum((dn2, dgate), "tp")
    dlogits = (gates * (dgate - jnp.sum(gates * dgate, axis=-1, keepdims=True))).astype(BF)
    dlogits = jnp.pad(dlogits, ((0, 0), (0, LANES - experts)))
    router_du = (dot_t(dlogits, router_b) * mask).astype(BF)
    dn2 = dn2 + dot_t(dlogits, router_w) + dot_t(router_du, router_a)
    grad_br = t_dot(router_u, dlogits)[:, :experts]
    grad_ar = t_dot(normed_two, router_du)
    dhidden = dout + norm_back(hidden, ffn_gain, dn2)
    dattn = dhidden.astype(BF)
    out_du = (dot_t(dattn, out_b) * mask).astype(BF)
    dmixed = (dot(dattn, out_wt) + dot_t(out_du, out_a)).astype(BF)
    grad_bo = t_dot(out_u.astype(BF), dattn)
    grad_ao = t_dot(mixed_heads, out_du)
    probs_again = jnp.exp(score_block() - log_total)
    dmixed_h = dmixed.reshape(rows, heads_kv, per_group, HEAD_SIZE)
    dvalues = jnp.einsum("grqk,qgrd->kgd", probs_again.astype(BF), dmixed_h, preferred_element_type=F32).reshape(2 * rows, kv_width)
    dprobs = jnp.einsum("qgrd,kgd->grqk", dmixed_h, values_h, preferred_element_type=F32)
    dscores = (probs_again * (dprobs - jnp.sum(probs_again * dprobs, axis=-1, keepdims=True))).astype(BF)
    dquery = jnp.einsum("grqk,kgd->qgrd", dscores, keys_h, preferred_element_type=F32) * scale
    dkeys = (jnp.einsum("grqk,qgrd->kgd", dscores, query_h, preferred_element_type=F32) * scale).reshape(2 * rows, kv_width)
    far_back = lax.ppermute(
        jnp.concatenate([dkeys[:rows], dvalues[:rows]], axis=1).astype(BF),
        "ctx",
        [(i + 1, i) for i in range(lax.axis_size("ctx") - 1)],
    ).astype(F32)
    dkey = dkeys[rows:] + far_back[:, :kv_width]
    dvalue = (dvalues[rows:] + far_back[:, kv_width:]).astype(BF)
    dquery_pre = rotary_apply(dquery.reshape(rows, -1, HEAD_SIZE), cosine_table, -sine_table).reshape(rows, q_width).astype(BF)
    dkey_pre = rotary_apply(dkey.reshape(rows, -1, HEAD_SIZE), cosine_table, -sine_table).reshape(rows, kv_width).astype(BF)
    query_du = (dot_t(dquery_pre, query_b) * mask).astype(BF)
    key_du = (dot_t(dkey_pre, key_b) * mask).astype(BF)
    value_du = (dot_t(dvalue, value_b) * mask).astype(BF)
    everything = jnp.concatenate([dquery_pre, dkey_pre, dvalue, query_du, key_du, value_du], axis=1)
    dn1 = dot_t(everything, w_one[:, :cols_one])
    grad_a3 = t_dot(normed, everything[:, qkv:])
    grad_bq = t_dot(query_u, dquery_pre)
    grad_bk = t_dot(key_u, dkey_pre)
    grad_bv = t_dot(value_u, dvalue)
    dn1 = lax.psum(dn1.astype(BF), "tp").astype(F32)
    grad_tokens = (dhidden + norm_back(xfull, attn_gain, dn1)).astype(BF)

    def place_cols(piece, full_cols):
        blank = jnp.zeros((piece.shape[0], full_cols), F32)
        return lax.dynamic_update_slice_in_dim(blank, piece, tp_at * piece.shape[1], 1)

    def place_rows(piece, full_rows):
        blank = jnp.zeros((full_rows, piece.shape[1]), F32)
        return lax.dynamic_update_slice_in_dim(blank, piece, tp_at * piece.shape[0], 0)

    only_first = (tp_at == 0).astype(F32)
    grads = (
        grad_a3[:, :ranks],
        place_cols(grad_bq, q_width * n_tp),
        grad_a3[:, ranks : 2 * ranks],
        place_cols(grad_bk, kv_width * n_tp),
        grad_a3[:, 2 * ranks :],
        place_cols(grad_bv, kv_width * n_tp),
        place_rows(grad_ao, q_width * n_tp),
        grad_bo,
        grad_ar * only_first,
        grad_br * only_first,
        grad_ag,
        place_cols(grad_bg, ff_width * n_tp),
        grad_au,
        place_cols(grad_bu, ff_width * n_tp),
        place_rows(grad_ad, ff_width * n_tp),
        grad_bd,
    )
    flat = []
    for g in grads:
        height, cols = g.shape[0] // n, g.shape[1]
        count = -(-cols // LANES)
        g = jnp.pad(g.astype(BF), ((0, 0), (0, count * LANES - cols)))
        flat.append(g.reshape(n, height, count, LANES).transpose(0, 2, 1, 3).reshape(n, count * height, LANES))
    flat = jnp.concatenate(flat, axis=1)
    mine = lax.psum_scatter(flat, "fsdp", scatter_dimension=0, tiled=False)
    mine = lax.psum(mine, ("ctx", "tp")).astype(F32)
    final = []
    at = 0
    for g in grads:
        height, cols = g.shape[0] // n, g.shape[1]
        count = -(-cols // LANES)
        piece = mine[at : at + count * height].reshape(count, height, LANES).transpose(1, 0, 2).reshape(height, count * LANES)
        final.append(piece[:, :cols])
        at += count * height
    return (output, grad_tokens, *final)


def solution(mesh):
    both = P(("fsdp", "ctx"), None)
    split = P("fsdp", None)
    placed = (
        both, both, split, split, both, P(), P(),
        P("fsdp", "tp"), P("fsdp", "tp"), P("fsdp", "tp"), P("tp", "fsdp"), split,
        P("fsdp", None, "tp"), P("fsdp", None, "tp"), P("fsdp", "tp", None),
    ) + (split,) * 16
    return jax.shard_map(
        on_device, mesh=mesh, in_specs=placed, out_specs=(both, both) + (split,) * 16, check_vma=False
    )
```

```python
import functools

import jax
import jax.numpy as jnp
from jax import lax
from jax.experimental import pallas as pl
from jax.experimental.pallas import tpu as pltpu
from jax.sharding import PartitionSpec as P

HEAD_SIZE = 64
ADAPTER_RANK = 16
LANES = 128
norm_eps = 1e-05
BF = jnp.bfloat16
F32 = jnp.float32


MESH = pl.DeviceIdType.MESH


def dot(left, right, dims=((1,), (0,)), precision=None):
    return lax.dot_general(left, right, (dims, ((), ())), preferred_element_type=F32, precision=precision)


def dot_t(left, right):
    return dot(left, right, ((1,), (1,)))


def t_dot(left, right):
    return dot(left, right, ((0,), (0,)))


def rms_norm(values, gain):
    return values * lax.rsqrt(jnp.mean(values * values, axis=-1, keepdims=True) + norm_eps) * gain


def norm_back(values, gain, grad):
    unused, pull = jax.vjp(lambda inner: rms_norm(inner, gain), values)
    return pull(grad)[0]


def rotary_apply(values, cosine_table, sine_table):
    half = values.shape[-1] // 2
    first = values[..., :half]
    second = values[..., half:]
    return jnp.concatenate(
        [first * cosine_table - second * sine_table, first * sine_table + second * cosine_table],
        axis=-1,
    )


def levels(n):
    outer = 4 if n % 4 == 0 else n
    return outer, n // outer


def spread(block):
    n = lax.axis_size("fsdp")
    outer, inner = levels(n)
    me = lax.axis_index("fsdp")
    held = [block]
    for unused in range(outer - 1):
        held.append(lax.ppermute(held[-1], "fsdp", [(i, (i + inner) % n) for i in range(n)]))
    rows = [held]
    turn = [(i, i // inner * inner + (i % inner + 1) % inner) for i in range(n)]
    for unused in range(inner - 1):
        rows.append([lax.ppermute(h, "fsdp", turn) for h in rows[-1]])
    found = []
    for dj, row in enumerate(rows):
        for do, part in enumerate(row):
            owner = (me // inner - do + outer) % outer * inner + (me % inner - dj + inner) % inner
            found.append((owner, part))
    return found


def gathered(block):
    n = lax.axis_size("fsdp")
    whole = jnp.zeros((n,) + block.shape, block.dtype)
    for owner, part in spread(block):
        whole = lax.dynamic_update_index_in_dim(whole, part, owner, 0)
    return whole


def fill_bias(bias, start_ref, begin_ref, rows):
    step = rows // 3
    for at in range(0, 2 * rows, step):
        key = start_ref[0] - rows + at + lax.broadcasted_iota(jnp.int32, (step, rows), 0)
        query = start_ref[0] + lax.broadcasted_iota(jnp.int32, (step, rows), 1)
        ok = (key <= query) & (key >= begin_ref[...]) & (key >= 0)
        bias[pl.ds(at, step), :] = jnp.where(ok, 0.0, -1e30)


def split_heads(ref, out, count, rows, at=0):
    for h in range(count):
        out[h, pl.ds(at, rows), :] = ref[:, h * HEAD_SIZE : (h + 1) * HEAD_SIZE]


def attend_kernel(group, q_blocks, start_ref, begin_ref, q_ref, ko_ref, vo_ref, kf_ref, vf_ref, o_ref, lse_ref, bias, ks, vts, qs, ots):
    rows = q_ref.shape[0]
    width = rows // q_blocks
    heads = 2 * group
    @pl.when(pl.program_id(0) == 0)
    def _():
        fill_bias(bias, start_ref, begin_ref, rows)
    split_heads(kf_ref, ks, 2, rows, 0)
    split_heads(ko_ref, ks, 2, rows, rows)
    split_heads(q_ref, qs, heads, rows, 0)
    vts[:, pl.ds(0, rows)] = vf_ref[...].astype(F32).T.astype(BF)
    vts[:, pl.ds(rows, rows)] = vo_ref[...].astype(F32).T.astype(BF)
    for b in range(q_blocks):
        keys = rows + (b + 1) * width
        def one(h, _):
            g = h // group
            s = dot_t(ks[g, pl.ds(0, keys), :], qs[h, pl.ds(b * width, width), :]) + bias[pl.ds(0, keys), pl.ds(b * width, width)]
            top = jnp.max(s, axis=0, keepdims=True)
            p = jnp.exp(s - top)
            total = jnp.sum(p, axis=0, keepdims=True)
            lse_ref[0, pl.ds(h, 1), pl.ds(b * width, width)] = top + jnp.log(total)
            vt = vts[pl.ds(pl.multiple_of(g * HEAD_SIZE, HEAD_SIZE), HEAD_SIZE), pl.ds(0, keys)]
            o = dot(vt, p.astype(BF)) / total
            ots[pl.ds(pl.multiple_of(h * HEAD_SIZE, HEAD_SIZE), HEAD_SIZE), pl.ds(b * width, width)] = o
            return 0
        lax.fori_loop(0, heads, one, 0)
    for j in range(group):
        o_ref[:, j * LANES : (j + 1) * LANES] = ots[pl.ds(j * LANES, LANES), :].T.astype(BF)


def attend(q, kv, far, begin, start, q_blocks=3):
    rows, q_width = q.shape
    kv_width = kv.shape[1] // 2
    pairs = kv_width // LANES
    group = q_width // kv_width
    spec = lambda off: pl.BlockSpec((rows, LANES), lambda i: (0, i + off))
    return pl.pallas_call(
        functools.partial(attend_kernel, group, q_blocks),
        grid=(pairs,),
        in_specs=[pl.BlockSpec(memory_space=pltpu.SMEM), pl.BlockSpec((1, rows), lambda i: (0, 0)),
                  pl.BlockSpec((rows, group * LANES), lambda i: (0, i)), spec(0), spec(pairs), spec(0), spec(pairs)],
        out_specs=[pl.BlockSpec((rows, group * LANES), lambda i: (0, i)), pl.BlockSpec((1, 8, rows), lambda i: (i, 0, 0))],
        out_shape=[jax.ShapeDtypeStruct((rows, q_width), BF), jax.ShapeDtypeStruct((pairs, 8, rows), F32)],
        scratch_shapes=[pltpu.VMEM((2 * rows, rows), F32), pltpu.VMEM((2, 2 * rows, HEAD_SIZE), BF), pltpu.VMEM((LANES, 2 * rows), BF),
                        pltpu.VMEM((2 * group, rows, HEAD_SIZE), BF), pltpu.VMEM((2 * group * HEAD_SIZE, rows), F32)],
        compiler_params=pltpu.CompilerParams(vmem_limit_bytes=50 << 20),
        cost_estimate=pl.CostEstimate(flops=8 * rows * rows * q_width, bytes_accessed=8 << 20, transcendentals=2 * rows * rows * 12),
    )(start, begin, q, kv, kv, far, far)


def attend_back_kernel(group, q_blocks, start_ref, begin_ref, q_ref, ko_ref, vo_ref, kf_ref, vf_ref, o_ref, do_ref, lse_ref,
                       dq_ref, dko_ref, dvo_ref, dkf_ref, dvf_ref, bias, ks, vs, kts, qs, dos, dqts, dks, dvs, deltas):
    rows = q_ref.shape[0]
    width = rows // q_blocks
    heads = 2 * group
    @pl.when(pl.program_id(0) == 0)
    def _():
        fill_bias(bias, start_ref, begin_ref, rows)
    split_heads(kf_ref, ks, 2, rows, 0)
    split_heads(ko_ref, ks, 2, rows, rows)
    split_heads(vf_ref, vs, 2, rows, 0)
    split_heads(vo_ref, vs, 2, rows, rows)
    split_heads(q_ref, qs, heads, rows, 0)
    split_heads(do_ref, dos, heads, rows, 0)
    kts[:, pl.ds(0, rows)] = kf_ref[...].astype(F32).T.astype(BF)
    kts[:, pl.ds(rows, rows)] = ko_ref[...].astype(F32).T.astype(BF)
    cols = heads * HEAD_SIZE
    pick = (lax.broadcasted_iota(jnp.int32, (8, cols), 1) // HEAD_SIZE == lax.broadcasted_iota(jnp.int32, (8, cols), 0)).astype(F32)
    prod = o_ref[...].astype(F32) * do_ref[...].astype(F32)
    deltas[...] = dot(pick, prod, ((1,), (1,)), lax.Precision.HIGHEST)
    dks[...] = jnp.zeros_like(dks)
    dvs[...] = jnp.zeros_like(dvs)
    for b in range(q_blocks):
        keys = rows + (b + 1) * width
        def one(h, _):
            g = h // group
            at = pl.ds(b * width, width)
            qb = qs[h, at, :]
            dob = dos[h, at, :]
            s = dot_t(ks[g, pl.ds(0, keys), :], qb) + bias[pl.ds(0, keys), at]
            p = jnp.exp(s - lse_ref[0, pl.ds(h, 1), at])
            dp = dot_t(vs[g, pl.ds(0, keys), :], dob)
            ds = (p * (dp - deltas[pl.ds(h, 1), at])).astype(BF)
            dvs[g, pl.ds(0, keys), :] += dot(p.astype(BF), dob)
            dks[g, pl.ds(0, keys), :] += dot(ds, qb)
            kt = kts[pl.ds(pl.multiple_of(g * HEAD_SIZE, HEAD_SIZE), HEAD_SIZE), pl.ds(0, keys)]
            dqts[pl.ds(pl.multiple_of(h * HEAD_SIZE, HEAD_SIZE), HEAD_SIZE), at] = dot(kt, ds) * 0.125
            return 0
        lax.fori_loop(0, heads, one, 0)
    for j in range(group):
        dq_ref[:, j * LANES : (j + 1) * LANES] = dqts[pl.ds(j * LANES, LANES), :].T
    for g in range(2):
        at = slice(g * HEAD_SIZE, (g + 1) * HEAD_SIZE)
        dkf_ref[:, at] = dks[g, pl.ds(0, rows), :].astype(BF)
        dko_ref[:, at] = dks[g, pl.ds(rows, rows), :]
        dvf_ref[:, at] = dvs[g, pl.ds(0, rows), :].astype(BF)
        dvo_ref[:, at] = dvs[g, pl.ds(rows, rows), :]


def attend_back(q, kv, far, begin, start, o, do, lse, q_blocks=3):
    rows, q_width = q.shape
    kv_width = kv.shape[1] // 2
    pairs = kv_width // LANES
    group = q_width // kv_width
    spec = lambda off: pl.BlockSpec((rows, LANES), lambda i: (0, i + off))
    wide = pl.BlockSpec((rows, group * LANES), lambda i: (0, i))
    sd = jax.ShapeDtypeStruct
    return pl.pallas_call(
        functools.partial(attend_back_kernel, group, q_blocks),
        grid=(pairs,),
        in_specs=[pl.BlockSpec(memory_space=pltpu.SMEM), pl.BlockSpec((1, rows), lambda i: (0, 0)),
                  wide, spec(0), spec(pairs), spec(0), spec(pairs), wide, wide, pl.BlockSpec((1, 8, rows), lambda i: (i, 0, 0))],
        out_specs=[wide, spec(0), spec(0), spec(0), spec(0)],
        out_shape=[sd((rows, q_width), F32), sd((rows, kv_width), F32), sd((rows, kv_width), F32), sd((rows, kv_width), BF), sd((rows, kv_width), BF)],
        scratch_shapes=[pltpu.VMEM((2 * rows, rows), F32), pltpu.VMEM((2, 2 * rows, HEAD_SIZE), BF), pltpu.VMEM((2, 2 * rows, HEAD_SIZE), BF), pltpu.VMEM((LANES, 2 * rows), BF),
                        pltpu.VMEM((2 * group, rows, HEAD_SIZE), BF), pltpu.VMEM((2 * group, rows, HEAD_SIZE), BF), pltpu.VMEM((2 * group * HEAD_SIZE, rows), F32),
                        pltpu.VMEM((2, 2 * rows, HEAD_SIZE), F32), pltpu.VMEM((2, 2 * rows, HEAD_SIZE), F32), pltpu.VMEM((8, rows), F32)],
        compiler_params=pltpu.CompilerParams(vmem_limit_bytes=56 << 20),
        cost_estimate=pl.CostEstimate(flops=20 * rows * rows * q_width, bytes_accessed=16 << 20, transcendentals=2 * rows * rows * 12),
    )(start, begin, q, kv, kv, far, far, o, do, lse)


def gather_kernel(n, count, *refs):
    ins, outs = refs[:count], refs[count : 2 * count]
    own_sem, z_send, z_recv, y_send, y_recv, x_send, x_recv = refs[2 * count :]
    outer, inner = levels(n)
    me = lax.axis_index("fsdp")
    ctx = lax.axis_index("ctx")
    z, y = me // inner, me % inner
    right = (z + 1) % outer * inner + y
    left = (z + outer - 1) % outer * inner + y

    def shard(do, dj):
        return (z + outer - do) % outer * inner + (y + inner - dj) % inner

    barrier = pltpu.get_barrier_semaphore()
    peers = [right, left] + [z * inner + (y + dj) % inner for dj in range(1, inner)]
    for peer in peers:
        pl.semaphore_signal(barrier, inc=1, device_id={"fsdp": peer}, device_id_type=MESH)
    pl.semaphore_signal(barrier, inc=1, device_id={"ctx": 1 - ctx}, device_id_type=MESH)
    pl.semaphore_wait(barrier, len(peers) + 1)

    def slab(a):
        third = ins[a].shape[0] // 3
        if third % 16:
            return pl.ds(0, ins[a].shape[0])
        return pl.ds(pl.multiple_of(ctx * third, 16), 2 * third)

    def tricked(a):
        return ins[a].shape[0] // 3 % 16 == 0

    def block(a, k, rows):
        return ins[a].at[rows] if k is None else outs[a].at[k, rows]

    def z_copy(a, k):
        src = shard(k - 1, 0)
        return pltpu.make_async_remote_copy(
            src_ref=block(a, None if k == 1 else src, slab(a)), dst_ref=outs[a].at[src, slab(a)],
            send_sem=z_send.at[a, k - 1], recv_sem=z_recv.at[a, k - 1], device_id={"fsdp": right}, device_id_type=MESH)

    def y_copy(a, do, dj):
        src = shard(do, 0)
        return pltpu.make_async_remote_copy(
            src_ref=block(a, None if do == 0 else src, slab(a)), dst_ref=outs[a].at[src, slab(a)],
            send_sem=y_send.at[a, do, dj - 1], recv_sem=y_recv.at[a, do, dj - 1],
            device_id={"fsdp": z * inner + (y + dj) % inner}, device_id_type=MESH)

    def x_copy(a, do, dj):
        src = shard(do, dj)
        third = ins[a].shape[0] // 3
        rows = pl.ds(pl.multiple_of(ctx * 2 * third, 16), third)
        return pltpu.make_async_remote_copy(
            src_ref=outs[a].at[src, rows], dst_ref=outs[a].at[src, rows],
            send_sem=x_send.at[a, do, dj], recv_sem=x_recv.at[a, do, dj], device_id={"ctx": 1 - ctx}, device_id_type=MESH)

    started = []

    def go(copy):
        copy.start()
        started.append(copy)

    own = [pltpu.make_async_copy(ins[a], outs[a].at[me], own_sem.at[a]) for a in range(count)]
    for a in range(count):
        go(z_copy(a, 1))
        for dj in range(1, inner):
            go(y_copy(a, 0, dj))
    for c in own:
        c.start()
    for do in range(1, outer + 1):
        if do < outer:
            for a in range(count):
                z_copy(a, do).wait_recv()
                if do + 1 < outer:
                    go(z_copy(a, do + 1))
                for dj in range(1, inner):
                    go(y_copy(a, do, dj))
                if tricked(a):
                    go(x_copy(a, do, 0))
        for a in range(count):
            for dj in range(1, inner):
                y_copy(a, do - 1, dj).wait_recv()
                if tricked(a):
                    go(x_copy(a, do - 1, dj))
    for a in range(count):
        if tricked(a):
            for do in range(outer):
                for dj in range(inner):
                    if do or dj:
                        x_copy(a, do, dj).wait_recv()
    for c in started:
        c.wait_send()
    for c in own:
        c.wait()


def gather_now(arrays, collective_id):
    n = lax.axis_size("fsdp")
    outer, inner = levels(n)
    count = len(arrays)
    dma = pltpu.SemaphoreType.DMA
    return pl.pallas_call(
        functools.partial(gather_kernel, n, count),
        in_specs=[pl.BlockSpec(memory_space=pl.ANY)] * count,
        out_specs=[pl.BlockSpec(memory_space=pl.ANY)] * count,
        out_shape=[jax.ShapeDtypeStruct((n,) + a.shape, a.dtype) for a in arrays],
        scratch_shapes=[
            dma((count,)), dma((count, outer - 1)), dma((count, outer - 1)),
            dma((count, outer, max(inner - 1, 1))), dma((count, outer, max(inner - 1, 1))),
            dma((count, outer, inner)), dma((count, outer, inner)),
        ],
        compiler_params=pltpu.CompilerParams(collective_id=collective_id, has_side_effects=True),
    )(*arrays)


def tp_sum(value):
    if lax.axis_size("tp") != 2:
        return lax.psum(value, "tp")
    return value + lax.ppermute(value, "tp", [(0, 1), (1, 0)])


def tiles(matrix):
    rows, cols = matrix.shape
    if cols % LANES:
        matrix = jnp.pad(matrix, ((0, 0), (0, LANES - cols % LANES)))
    return [matrix[:, i : i + LANES] for i in range(0, matrix.shape[1], LANES)]


def on_device(
    tokens, out_cotangent, lengths, adapter_of_doc, routes, attn_gain, ffn_gain,
    w_query, key_matrix, value_matrix, w_out, w_router, w_gate, w_up, w_down,
    a_query, b_query, a_key, key_second_factor, a_value, value_second_factor,
    a_out, b_out, a_router, b_router, a_gate, b_gate, a_up, b_up, a_down, b_down,
):
    rows, width = tokens.shape
    n = lax.axis_size("fsdp")
    n_tp = lax.axis_size("tp")
    tp_at = lax.axis_index("tp")
    ctx_at = lax.axis_index("ctx")
    group = rows * lax.axis_size("ctx")
    q_width = w_query.shape[1]
    kv_width = key_matrix.shape[1]
    ff_width = w_gate.shape[2]
    local_experts = w_gate.shape[0]
    experts = w_router.shape[1]
    ranks = a_query.shape[1]
    share = w_query.shape[0]
    low_rows = b_query.shape[0]

    def tp_cols(matrix, size):
        return lax.dynamic_slice_in_dim(matrix, tp_at * size, size, 1)

    def packed_low(parts, height):
        stack = jnp.concatenate(sum([tiles(p) for p in parts], []), axis=0)
        blocks = -(-stack.shape[0] // height)
        stack = jnp.pad(stack, ((0, blocks * height - stack.shape[0]), (0, 0)))
        return [stack[i * height : (i + 1) * height] for i in range(blocks)]

    first_low = [tp_cols(b_query, q_width), tp_cols(key_second_factor, kv_width), tp_cols(value_second_factor, kv_width)]
    second_low = [tp_cols(b_gate, ff_width), tp_cols(b_up, ff_width), b_out, b_down, b_router]
    base_one = [w_query, key_matrix, value_matrix, a_query, a_key, a_value]
    pack_one = jnp.concatenate(base_one + packed_low(first_low, share), axis=1)
    router_pad = jnp.pad(w_router, ((0, 0), (0, LANES - experts)))
    base_two = [w_out.T, a_router, a_gate, a_up, router_pad, a_out]
    pack_two = jnp.concatenate(base_two + packed_low(second_low + [a_down], share), axis=1)
    expert_block = jnp.concatenate([w_gate, w_up, jnp.swapaxes(w_down, 1, 2)], axis=2)

    (one,) = gather_now([pack_one], 0)
    one, pack_two, expert_block = lax.optimization_barrier((one, pack_two, expert_block))
    two = lax.all_gather(pack_two, "fsdp", axis=0, tiled=False)
    expert_parts = spread(expert_block)

    def unpack_low(whole, col, parts):
        flat = whole[:, :, col:]
        flat = flat.reshape(n, share, -1, LANES).transpose(0, 2, 1, 3).reshape(n, -1, LANES)
        found = []
        at = 0
        for height, cols in parts:
            count = -(-cols // LANES)
            piece = flat[:, at : at + count * height].reshape(n, count, height, LANES)
            found.append(piece.transpose(0, 2, 1, 3).reshape(n * height, count * LANES))
            at += count * height
        return found

    w_one = one.reshape(n * share, -1)
    cols_one = q_width + 2 * kv_width + 3 * ranks
    query_b, key_b, value_b = unpack_low(one, cols_one, [(low_rows, q_width), (low_rows, kv_width), (low_rows, kv_width)])
    w_two = two.reshape(n * share, -1)
    cols_two = q_width + 5 * ranks
    gate_b, up_b, out_b, down_b, router_b, down_a = unpack_low(
        two,
        cols_two,
        [(low_rows, ff_width), (low_rows, ff_width), (low_rows, width), (low_rows, width), (low_rows, experts), (a_down.shape[0], ranks)],
    )
    out_wt = w_two[:, :q_width]
    router_a = w_two[:, q_width : q_width + ranks]
    gate_a = w_two[:, q_width + ranks : q_width + 2 * ranks]
    up_a = w_two[:, q_width + 2 * ranks : q_width + 3 * ranks]
    router_w = w_two[:, q_width + 3 * ranks : q_width + 4 * ranks]
    out_a = lax.dynamic_slice_in_dim(w_two[:, q_width + 4 * ranks : q_width + 5 * ranks], tp_at * q_width, q_width, 0)
    down_at = lax.dynamic_slice_in_dim(down_a, tp_at * ff_width, ff_width, 0)

    ends = jnp.cumsum(lengths[0])
    starts = ends - lengths[0]
    place = jnp.arange(group, dtype=jnp.int32)
    doc = jnp.sum((place[:, None] >= ends[None, :]).astype(jnp.int32), axis=1)
    picked = (doc[:, None] == jnp.arange(lengths.shape[1], dtype=jnp.int32)[None, :]).astype(jnp.int32)
    begin = jnp.sum(picked * starts[None, :], axis=1)
    chosen = jnp.sum(picked * adapter_of_doc[0][None, :], axis=1)
    start = ctx_at * rows
    query_index = start + jnp.arange(rows, dtype=jnp.int32)
    begin_local = lax.dynamic_slice_in_dim(begin, start, rows)
    chosen_local = lax.dynamic_slice_in_dim(chosen, start, rows)
    mask = (chosen_local[:, None] == (jnp.arange(ranks, dtype=jnp.int32) // ADAPTER_RANK)[None, :]).astype(F32)
    half = HEAD_SIZE // 2
    freq = 10000.0 ** (-jnp.arange(half, dtype=F32) / half)
    angles = (query_index - begin_local).astype(F32)[:, None] * freq[None, :]
    cosine_table = jnp.cos(angles)[:, None, :]
    sine_table = jnp.sin(angles)[:, None, :]

    xfull = tokens.astype(F32)
    normed = rms_norm(xfull, attn_gain).astype(BF)
    raw = dot(normed, w_one[:, :cols_one])
    qkv = q_width + 2 * kv_width
    query_u = (raw[:, qkv : qkv + ranks] * mask).astype(BF)
    key_u = (raw[:, qkv + ranks : qkv + 2 * ranks] * mask).astype(BF)
    value_u = (raw[:, qkv + 2 * ranks : qkv + 3 * ranks] * mask).astype(BF)
    query_pre = raw[:, :q_width] + dot(query_u, query_b)
    key_pre = raw[:, q_width : q_width + kv_width] + dot(key_u, key_b)
    value_state = (raw[:, q_width + kv_width : qkv] + dot(value_u, value_b)).astype(BF)
    query_state = (
        rotary_apply(query_pre.reshape(rows, -1, HEAD_SIZE), cosine_table, sine_table).reshape(rows, q_width).astype(BF)
    )
    key = rotary_apply(key_pre.reshape(rows, -1, HEAD_SIZE), cosine_table, sine_table).reshape(rows, kv_width).astype(BF)
    far = lax.ppermute(jnp.concatenate([key, value_state], axis=1), "ctx", [(i, i + 1) for i in range(lax.axis_size("ctx") - 1)])
    kv = jnp.concatenate([key, value_state], axis=1)
    begin_row = begin_local[None, :]
    start_at = jnp.reshape(start, (1,)).astype(jnp.int32)
    query_state = (query_state.astype(F32) * 0.125).astype(BF)
    mixed_heads, log_total = attend(query_state, kv, far, begin_row, start_at)
    out_u = dot(mixed_heads, out_a) * mask
    attn_part = dot_t(mixed_heads, out_wt) + dot(out_u.astype(BF), out_b)
    hidden = xfull + tp_sum(attn_part)
    normed_two = rms_norm(hidden, ffn_gain).astype(BF)
    lows = dot(normed_two, w_two[:, q_width : q_width + 4 * ranks])
    router_u = (lows[:, :ranks] * mask).astype(BF)
    zin_gate = (lows[:, ranks : 2 * ranks] * mask).astype(BF)
    zin_up = (lows[:, 2 * ranks : 3 * ranks] * mask).astype(BF)
    logits = lows[:, 3 * ranks : 3 * ranks + experts] + dot(router_u, router_b)[:, :experts]
    selected = jnp.any(routes[:, :, None] == jnp.arange(experts, dtype=jnp.int32)[None, None, :], axis=1)
    gates = jax.nn.softmax(jnp.where(selected, logits, -jnp.inf), axis=-1)

    cot = out_cotangent
    dout = cot.astype(F32)
    gate_low = dot(zin_gate, gate_b)
    up_low = dot(zin_up, up_b)
    down_back = dot_t(cot, down_b) * mask
    act_low = dot_t(down_back.astype(BF), down_at)
    moe = jnp.zeros((rows, width), F32)
    dn2 = jnp.zeros((rows, width), F32)
    act_sum = jnp.zeros((rows, ff_width), F32)
    dg_sum = jnp.zeros((rows, ff_width), F32)
    du_sum = jnp.zeros((rows, ff_width), F32)
    dgate = jnp.zeros((rows, experts), F32)
    for owner, part in expert_parts:
        for j in range(local_experts):
            e = owner * local_experts + j
            w_gu = part[j][:, : 2 * ff_width]
            w_d = part[j][:, 2 * ff_width :]
            g = lax.dynamic_slice_in_dim(gates, e, 1, 1)
            pre = dot(normed_two, w_gu)
            gv = pre[:, :ff_width] + gate_low
            uv = pre[:, ff_width:] + up_low
            sig = jax.nn.sigmoid(gv)
            silu = gv * sig
            act = silu * uv
            back = dot(cot, w_d) + act_low
            col = jnp.sum(act * back, axis=1, keepdims=True)
            dgate = dgate + jnp.where(jnp.arange(experts)[None, :] == e, col, 0.0)
            act_g = (act * g).astype(BF)
            back = back * g
            dg = (back * uv * sig * (1.0 + gv * (1.0 - sig))).astype(BF)
            du = (back * silu).astype(BF)
            moe = moe + dot_t(act_g, w_d)
            dn2 = dn2 + dot_t(jnp.concatenate([dg, du], axis=1), w_gu)
            act_sum = act_sum + act_g.astype(F32)
            dg_sum = dg_sum + dg.astype(F32)
            du_sum = du_sum + du.astype(F32)
    down_low = (dot(act_sum.astype(BF), down_at) * mask).astype(BF)
    moe = moe + dot(down_low, down_b)
    output = (hidden + tp_sum(moe.astype(BF).astype(F32))).astype(BF)
    grad_bd = t_dot(down_low, cot)
    grad_ad = t_dot(act_sum.astype(BF), down_back.astype(BF))
    dg_sum = dg_sum.astype(BF)
    du_sum = du_sum.astype(BF)
    grad_bg = t_dot(zin_gate, dg_sum)
    grad_bu = t_dot(zin_up, du_sum)
    gate_du = (dot_t(dg_sum, gate_b) * mask).astype(BF)
    up_du = (dot_t(du_sum, up_b) * mask).astype(BF)
    dn2 = dn2 + dot_t(gate_du, gate_a) + dot_t(up_du, up_a)
    grad_ag = t_dot(normed_two, gate_du)
    grad_au = t_dot(normed_two, up_du)
    dn2, dgate = tp_sum(dn2), tp_sum(dgate)
    dlogits = (gates * (dgate - jnp.sum(gates * dgate, axis=-1, keepdims=True))).astype(BF)
    dlogits = jnp.pad(dlogits, ((0, 0), (0, LANES - experts)))
    router_du = (dot_t(dlogits, router_b) * mask).astype(BF)
    dn2 = dn2 + dot_t(dlogits, router_w) + dot_t(router_du, router_a)
    grad_br = t_dot(router_u, dlogits)[:, :experts]
    grad_ar = t_dot(normed_two, router_du)
    dhidden = dout + norm_back(hidden, ffn_gain, dn2)
    dattn = dhidden.astype(BF)
    out_du = (dot_t(dattn, out_b) * mask).astype(BF)
    dmixed = (dot(dattn, out_wt) + dot_t(out_du, out_a)).astype(BF)
    grad_bo = t_dot(out_u.astype(BF), dattn)
    grad_ao = t_dot(mixed_heads, out_du)
    dquery, dkey_own, dvalue_own, dkey_far, dvalue_far = attend_back(
        query_state, kv, far, begin_row, start_at, mixed_heads, dmixed, log_total
    )
    far_back = lax.ppermute(
        jnp.concatenate([dkey_far, dvalue_far], axis=1),
        "ctx",
        [(i + 1, i) for i in range(lax.axis_size("ctx") - 1)],
    ).astype(F32)
    dkey = dkey_own + far_back[:, :kv_width]
    dvalue = (dvalue_own + far_back[:, kv_width:]).astype(BF)
    dquery_pre = rotary_apply(dquery.reshape(rows, -1, HEAD_SIZE), cosine_table, -sine_table).reshape(rows, q_width).astype(BF)
    dkey_pre = rotary_apply(dkey.reshape(rows, -1, HEAD_SIZE), cosine_table, -sine_table).reshape(rows, kv_width).astype(BF)
    query_du = (dot_t(dquery_pre, query_b) * mask).astype(BF)
    key_du = (dot_t(dkey_pre, key_b) * mask).astype(BF)
    value_du = (dot_t(dvalue, value_b) * mask).astype(BF)
    everything = jnp.concatenate([dquery_pre, dkey_pre, dvalue, query_du, key_du, value_du], axis=1)
    dn1 = dot_t(everything, w_one[:, :cols_one])
    grad_a3 = t_dot(normed, everything[:, qkv:])
    grad_bq = t_dot(query_u, dquery_pre)
    grad_bk = t_dot(key_u, dkey_pre)
    grad_bv = t_dot(value_u, dvalue)
    dn1 = tp_sum(dn1)
    grad_tokens = (dhidden + norm_back(xfull, attn_gain, dn1)).astype(BF)

    def place_cols(piece, full_cols):
        blank = jnp.zeros((piece.shape[0], full_cols), F32)
        return lax.dynamic_update_slice_in_dim(blank, piece, tp_at * piece.shape[1], 1)

    def place_rows(piece, full_rows):
        blank = jnp.zeros((full_rows, piece.shape[1]), F32)
        return lax.dynamic_update_slice_in_dim(blank, piece, tp_at * piece.shape[0], 0)

    only_first = (tp_at == 0).astype(F32)
    grads = (
        grad_a3[:, :ranks],
        place_cols(grad_bq, q_width * n_tp),
        grad_a3[:, ranks : 2 * ranks],
        place_cols(grad_bk, kv_width * n_tp),
        grad_a3[:, 2 * ranks :],
        place_cols(grad_bv, kv_width * n_tp),
        place_rows(grad_ao, q_width * n_tp),
        grad_bo,
        grad_ar * only_first,
        grad_br * only_first,
        grad_ag,
        place_cols(grad_bg, ff_width * n_tp),
        grad_au,
        place_cols(grad_bu, ff_width * n_tp),
        place_rows(grad_ad, ff_width * n_tp),
        grad_bd,
    )
    def reduce_grads(some):
        flat = []
        for g in some:
            height, cols = g.shape[0] // n, g.shape[1]
            count = -(-cols // LANES)
            g = jnp.pad(g.astype(BF), ((0, 0), (0, count * LANES - cols)))
            flat.append(g.reshape(n, height, count, LANES).transpose(0, 2, 1, 3).reshape(n, count * height, LANES))
        flat = jnp.concatenate(flat, axis=1)
        mine = lax.psum_scatter(flat, "fsdp", scatter_dimension=0, tiled=False)
        mine = lax.psum(mine, ("ctx", "tp")).astype(F32)
        found = []
        at = 0
        for g in some:
            height, cols = g.shape[0] // n, g.shape[1]
            count = -(-cols // LANES)
            piece = mine[at : at + count * height].reshape(count, height, LANES).transpose(1, 0, 2).reshape(height, count * LANES)
            found.append(piece[:, :cols])
            at += count * height
        return found

    final = reduce_grads(grads[:6]) + reduce_grads(grads[6:])
    return (output, grad_tokens, *final)


def solution(mesh):
    both = P(("fsdp", "ctx"), None)
    split = P("fsdp", None)
    placed = (
        both, both, split, split, both, P(), P(),
        P("fsdp", "tp"), P("fsdp", "tp"), P("fsdp", "tp"), P("tp", "fsdp"), split,
        P("fsdp", None, "tp"), P("fsdp", None, "tp"), P("fsdp", "tp", None),
    ) + (split,) * 16
    return jax.shard_map(
        on_device, mesh=mesh, in_specs=placed, out_specs=(both, both) + (split,) * 16, check_vma=False
    )
```

```python
import functools

import jax
import jax.numpy as jnp
from jax import lax
from jax.experimental import pallas as pl
from jax.experimental.pallas import tpu as pltpu
from jax.sharding import PartitionSpec as P

HEAD_SIZE = 64
ADAPTER_RANK = 16
LANES = 128
norm_eps = 1e-05
BF = jnp.bfloat16
F32 = jnp.float32


MESH = pl.DeviceIdType.MESH


def dot(left, right, dims=((1,), (0,)), precision=None):
    return lax.dot_general(left, right, (dims, ((), ())), preferred_element_type=F32, precision=precision)


def dot_t(left, right):
    return dot(left, right, ((1,), (1,)))


def t_dot(left, right):
    return dot(left, right, ((0,), (0,)))


def rms_norm(values, gain):
    return values * lax.rsqrt(jnp.mean(values * values, axis=-1, keepdims=True) + norm_eps) * gain


def norm_back(values, gain, grad):
    unused, pull = jax.vjp(lambda inner: rms_norm(inner, gain), values)
    return pull(grad)[0]


def rotary_apply(values, cosine_table, sine_table):
    half = values.shape[-1] // 2
    first = values[..., :half]
    second = values[..., half:]
    return jnp.concatenate(
        [first * cosine_table - second * sine_table, first * sine_table + second * cosine_table],
        axis=-1,
    )


def levels(n):
    outer = 4 if n % 4 == 0 else n
    return outer, n // outer


def fill_bias(bias, start_ref, begin_ref, rows):
    step = rows // 3
    for at in range(0, 2 * rows, step):
        key = start_ref[0] - rows + at + lax.broadcasted_iota(jnp.int32, (step, rows), 0)
        query = start_ref[0] + lax.broadcasted_iota(jnp.int32, (step, rows), 1)
        ok = (key <= query) & (key >= begin_ref[...]) & (key >= 0)
        bias[pl.ds(at, step), :] = jnp.where(ok, 0.0, -1e30)


def split_heads(ref, out, count, rows, at=0):
    for h in range(count):
        out[h, pl.ds(at, rows), :] = ref[:, h * HEAD_SIZE : (h + 1) * HEAD_SIZE]


def attend_kernel(group, q_blocks, start_ref, begin_ref, q_ref, ko_ref, vo_ref, kf_ref, vf_ref, o_ref, lse_ref, bias, ks, vts, qs, ots):
    rows = q_ref.shape[0]
    width = rows // q_blocks
    heads = 2 * group
    @pl.when(pl.program_id(0) == 0)
    def _():
        fill_bias(bias, start_ref, begin_ref, rows)
    split_heads(kf_ref, ks, 2, rows, 0)
    split_heads(ko_ref, ks, 2, rows, rows)
    split_heads(q_ref, qs, heads, rows, 0)
    vts[:, pl.ds(0, rows)] = vf_ref[...].astype(F32).T.astype(BF)
    vts[:, pl.ds(rows, rows)] = vo_ref[...].astype(F32).T.astype(BF)
    for b in range(q_blocks):
        keys = rows + (b + 1) * width
        def one(h, _):
            g = h // group
            s = dot_t(ks[g, pl.ds(0, keys), :], qs[h, pl.ds(b * width, width), :]) + bias[pl.ds(0, keys), pl.ds(b * width, width)]
            top = jnp.max(s, axis=0, keepdims=True)
            p = jnp.exp(s - top)
            total = jnp.sum(p, axis=0, keepdims=True)
            lse_ref[0, pl.ds(h, 1), pl.ds(b * width, width)] = top + jnp.log(total)
            vt = vts[pl.ds(pl.multiple_of(g * HEAD_SIZE, HEAD_SIZE), HEAD_SIZE), pl.ds(0, keys)]
            o = dot(vt, p.astype(BF)) / total
            ots[pl.ds(pl.multiple_of(h * HEAD_SIZE, HEAD_SIZE), HEAD_SIZE), pl.ds(b * width, width)] = o
            return 0
        lax.fori_loop(0, heads, one, 0)
    for j in range(group):
        o_ref[:, j * LANES : (j + 1) * LANES] = ots[pl.ds(j * LANES, LANES), :].T.astype(BF)


def attend(q, kv, far, begin, start, q_blocks=3):
    rows, q_width = q.shape
    kv_width = kv.shape[1] // 2
    pairs = kv_width // LANES
    group = q_width // kv_width
    spec = lambda off: pl.BlockSpec((rows, LANES), lambda i: (0, i + off))
    return pl.pallas_call(
        functools.partial(attend_kernel, group, q_blocks),
        grid=(pairs,),
        in_specs=[pl.BlockSpec(memory_space=pltpu.SMEM), pl.BlockSpec((1, rows), lambda i: (0, 0)),
                  pl.BlockSpec((rows, group * LANES), lambda i: (0, i)), spec(0), spec(pairs), spec(0), spec(pairs)],
        out_specs=[pl.BlockSpec((rows, group * LANES), lambda i: (0, i)), pl.BlockSpec((1, 8, rows), lambda i: (i, 0, 0))],
        out_shape=[jax.ShapeDtypeStruct((rows, q_width), BF), jax.ShapeDtypeStruct((pairs, 8, rows), F32)],
        scratch_shapes=[pltpu.VMEM((2 * rows, rows), F32), pltpu.VMEM((2, 2 * rows, HEAD_SIZE), BF), pltpu.VMEM((LANES, 2 * rows), BF),
                        pltpu.VMEM((2 * group, rows, HEAD_SIZE), BF), pltpu.VMEM((2 * group * HEAD_SIZE, rows), F32)],
        compiler_params=pltpu.CompilerParams(vmem_limit_bytes=50 << 20),
        cost_estimate=pl.CostEstimate(flops=8 * rows * rows * q_width, bytes_accessed=8 << 20, transcendentals=2 * rows * rows * 12),
    )(start, begin, q, kv, kv, far, far)


def attend_back_kernel(group, q_blocks, start_ref, begin_ref, q_ref, ko_ref, vo_ref, kf_ref, vf_ref, o_ref, do_ref, lse_ref,
                       dq_ref, dko_ref, dvo_ref, dkf_ref, dvf_ref, bias, ks, vs, kts, qs, dos, dqts, dks, dvs, deltas):
    rows = q_ref.shape[0]
    width = rows // q_blocks
    heads = 2 * group
    @pl.when(pl.program_id(0) == 0)
    def _():
        fill_bias(bias, start_ref, begin_ref, rows)
    split_heads(kf_ref, ks, 2, rows, 0)
    split_heads(ko_ref, ks, 2, rows, rows)
    split_heads(vf_ref, vs, 2, rows, 0)
    split_heads(vo_ref, vs, 2, rows, rows)
    split_heads(q_ref, qs, heads, rows, 0)
    split_heads(do_ref, dos, heads, rows, 0)
    kts[:, pl.ds(0, rows)] = kf_ref[...].astype(F32).T.astype(BF)
    kts[:, pl.ds(rows, rows)] = ko_ref[...].astype(F32).T.astype(BF)
    cols = heads * HEAD_SIZE
    pick = (lax.broadcasted_iota(jnp.int32, (8, cols), 1) // HEAD_SIZE == lax.broadcasted_iota(jnp.int32, (8, cols), 0)).astype(F32)
    prod = o_ref[...].astype(F32) * do_ref[...].astype(F32)
    deltas[...] = dot(pick, prod, ((1,), (1,)), lax.Precision.HIGHEST)
    dks[...] = jnp.zeros_like(dks)
    dvs[...] = jnp.zeros_like(dvs)
    for b in range(q_blocks):
        keys = rows + (b + 1) * width
        def one(h, _):
            g = h // group
            at = pl.ds(b * width, width)
            qb = qs[h, at, :]
            dob = dos[h, at, :]
            s = dot_t(ks[g, pl.ds(0, keys), :], qb) + bias[pl.ds(0, keys), at]
            p = jnp.exp(s - lse_ref[0, pl.ds(h, 1), at])
            dp = dot_t(vs[g, pl.ds(0, keys), :], dob)
            ds = (p * (dp - deltas[pl.ds(h, 1), at])).astype(BF)
            dvs[g, pl.ds(0, keys), :] += dot(p.astype(BF), dob)
            dks[g, pl.ds(0, keys), :] += dot(ds, qb)
            kt = kts[pl.ds(pl.multiple_of(g * HEAD_SIZE, HEAD_SIZE), HEAD_SIZE), pl.ds(0, keys)]
            dqts[pl.ds(pl.multiple_of(h * HEAD_SIZE, HEAD_SIZE), HEAD_SIZE), at] = dot(kt, ds) * 0.125
            return 0
        lax.fori_loop(0, heads, one, 0)
    for j in range(group):
        dq_ref[:, j * LANES : (j + 1) * LANES] = dqts[pl.ds(j * LANES, LANES), :].T
    for g in range(2):
        at = slice(g * HEAD_SIZE, (g + 1) * HEAD_SIZE)
        dkf_ref[:, at] = dks[g, pl.ds(0, rows), :].astype(BF)
        dko_ref[:, at] = dks[g, pl.ds(rows, rows), :]
        dvf_ref[:, at] = dvs[g, pl.ds(0, rows), :].astype(BF)
        dvo_ref[:, at] = dvs[g, pl.ds(rows, rows), :]


def attend_back(q, kv, far, begin, start, o, do, lse, q_blocks=3):
    rows, q_width = q.shape
    kv_width = kv.shape[1] // 2
    pairs = kv_width // LANES
    group = q_width // kv_width
    spec = lambda off: pl.BlockSpec((rows, LANES), lambda i: (0, i + off))
    wide = pl.BlockSpec((rows, group * LANES), lambda i: (0, i))
    sd = jax.ShapeDtypeStruct
    return pl.pallas_call(
        functools.partial(attend_back_kernel, group, q_blocks),
        grid=(pairs,),
        in_specs=[pl.BlockSpec(memory_space=pltpu.SMEM), pl.BlockSpec((1, rows), lambda i: (0, 0)),
                  wide, spec(0), spec(pairs), spec(0), spec(pairs), wide, wide, pl.BlockSpec((1, 8, rows), lambda i: (i, 0, 0))],
        out_specs=[wide, spec(0), spec(0), spec(0), spec(0)],
        out_shape=[sd((rows, q_width), F32), sd((rows, kv_width), F32), sd((rows, kv_width), F32), sd((rows, kv_width), BF), sd((rows, kv_width), BF)],
        scratch_shapes=[pltpu.VMEM((2 * rows, rows), F32), pltpu.VMEM((2, 2 * rows, HEAD_SIZE), BF), pltpu.VMEM((2, 2 * rows, HEAD_SIZE), BF), pltpu.VMEM((LANES, 2 * rows), BF),
                        pltpu.VMEM((2 * group, rows, HEAD_SIZE), BF), pltpu.VMEM((2 * group, rows, HEAD_SIZE), BF), pltpu.VMEM((2 * group * HEAD_SIZE, rows), F32),
                        pltpu.VMEM((2, 2 * rows, HEAD_SIZE), F32), pltpu.VMEM((2, 2 * rows, HEAD_SIZE), F32), pltpu.VMEM((8, rows), F32)],
        compiler_params=pltpu.CompilerParams(vmem_limit_bytes=56 << 20),
        cost_estimate=pl.CostEstimate(flops=20 * rows * rows * q_width, bytes_accessed=16 << 20, transcendentals=2 * rows * rows * 12),
    )(start, begin, q, kv, kv, far, far, o, do, lse)


def slab_of(rows, ctx):
    edge = 3 * rows // 8 // 16 * 16
    take = rows - edge
    return pl.ds(pl.multiple_of(ctx * edge, 16), take), pl.ds(pl.multiple_of(ctx * take, 16), edge)


def gather_kernel(n, layout, *refs):
    total = sum(len(parts) for parts in layout)
    count = len(layout)
    ins, outs = refs[:total], refs[total : total + count]
    own_sem, z_send, z_recv, y_send, y_recv, x_send, x_recv = refs[total + count :]
    outer, inner = levels(n)
    me = lax.axis_index("fsdp")
    ctx = lax.axis_index("ctx")
    tp = lax.axis_index("tp")
    z, y = me // inner, me % inner
    right = (z + 1) % outer * inner + y
    left = (z + outer - 1) % outer * inner + y

    def shard(do, dj):
        return (z + outer - do) % outer * inner + (y + inner - dj) % inner

    own = []
    at = 0
    for a, parts in enumerate(layout):
        col = 0
        for cols, split in parts:
            src = ins[at].at[:, pl.ds(pl.multiple_of(tp * cols, LANES), cols)] if split else ins[at]
            own.append(pltpu.make_async_copy(src, outs[a].at[me, :, pl.ds(col, cols)], own_sem.at[at]))
            own[-1].start()
            col += cols
            at += 1

    barrier = pltpu.get_barrier_semaphore()
    peers = [right, left] + [z * inner + (y + dj) % inner for dj in range(1, inner)]
    for peer in peers:
        pl.semaphore_signal(barrier, inc=1, device_id={"fsdp": peer}, device_id_type=MESH)
    pl.semaphore_signal(barrier, inc=1, device_id={"ctx": 1 - ctx}, device_id_type=MESH)
    pl.semaphore_wait(barrier, len(peers) + 1)

    def cut(a):
        return 3 * outs[a].shape[1] // 8 >= 16

    def taken(a, k):
        if not cut(a):
            return outs[a].at[k]
        return outs[a].at[k, slab_of(outs[a].shape[1], ctx)[0]]

    def remote(part, send, recv, to):
        return pltpu.make_async_remote_copy(src_ref=part, dst_ref=part, send_sem=send, recv_sem=recv, device_id=to, device_id_type=MESH)

    def z_copy(a, k):
        return remote(taken(a, shard(k - 1, 0)), z_send.at[a, k - 1], z_recv.at[a, k - 1], {"fsdp": right})

    def y_copy(a, do, dj):
        to = {"fsdp": z * inner + (y + dj) % inner}
        return remote(taken(a, shard(do, 0)), y_send.at[a, do, dj - 1], y_recv.at[a, do, dj - 1], to)

    def x_copy(a, do, dj):
        part = outs[a].at[shard(do, dj), slab_of(outs[a].shape[1], ctx)[1]]
        return remote(part, x_send.at[a, do, dj], x_recv.at[a, do, dj], {"ctx": 1 - ctx})

    started = []

    def go(copy):
        copy.start()
        started.append(copy)

    for c in own:
        c.wait()
    for a in range(count):
        go(z_copy(a, 1))
        for dj in range(1, inner):
            go(y_copy(a, 0, dj))
    for do in range(1, outer + 1):
        for a in range(count):
            if do < outer:
                z_copy(a, do).wait_recv()
                if do + 1 < outer:
                    go(z_copy(a, do + 1))
                for dj in range(1, inner):
                    go(y_copy(a, do, dj))
                if cut(a):
                    go(x_copy(a, do, 0))
        for a in range(count):
            for dj in range(1, inner):
                y_copy(a, do - 1, dj).wait_recv()
                if cut(a):
                    go(x_copy(a, do - 1, dj))
    for a in range(count):
        if cut(a):
            for do in range(outer):
                for dj in range(inner):
                    if do or dj:
                        x_copy(a, do, dj).wait_recv()
    for c in started:
        c.wait_send()


def gather_packs(packs, collective_id):
    n = lax.axis_size("fsdp")
    outer, inner = levels(n)
    count = len(packs)
    layout = [[(cols, cols != a.shape[1]) for a, cols in parts] for parts in packs]
    arrays = [a for parts in packs for a, cols in parts]
    dma = pltpu.SemaphoreType.DMA
    anywhere = pl.BlockSpec(memory_space=pl.ANY)
    side = max(inner - 1, 1)
    return pl.pallas_call(
        functools.partial(gather_kernel, n, layout),
        in_specs=[anywhere] * len(arrays),
        out_specs=[anywhere] * count,
        out_shape=[jax.ShapeDtypeStruct((n, parts[0][0].shape[0], sum(cols for a, cols in parts)), BF) for parts in packs],
        scratch_shapes=[
            dma((len(arrays),)), dma((count, outer - 1)), dma((count, outer - 1)),
            dma((count, outer, side)), dma((count, outer, side)), dma((count, outer, inner)), dma((count, outer, inner)),
        ],
        compiler_params=pltpu.CompilerParams(collective_id=collective_id, has_side_effects=True),
    )(*arrays)


def moe_kernel(n, n2_ref, c_ref, gl_ref, ul_ref, al_ref, gates_ref, *refs):
    own, near, side = refs[0:3], refs[3:6], refs[6:9]
    moe_ref, dn2_ref, as_ref, gs_ref, us_ref, dgate_ref = refs[9:15]
    bufs = refs[15:18]
    wg, wu, wd, load_sem, z_send, z_recv, y_send, y_recv, x_send, x_recv = refs[18:]
    outer, inner = levels(n)
    me = lax.axis_index("fsdp")
    ctx = lax.axis_index("ctx")
    z, y = me // inner, me % inner
    right = (z + 1) % outer * inner + y
    left = (z + outer - 1) % outer * inner + y
    local = own[0].shape[0]
    rows = n2_ref.shape[0]
    experts = gates_ref.shape[1]
    chunks = [(j, a) for j in range(local) for a in range(3)]

    def shard(do, dj):
        return (z + outer - do) % outer * inner + (y + inner - dj) % inner

    def held(do, dj):
        if (do, dj) == (0, 0):
            return own
        if (do, dj) == (1, 0):
            return near
        if (do, dj) == (0, 1):
            return side
        at = shard(do, dj)
        return [b.at[at] for b in bufs]

    barrier = pltpu.get_barrier_semaphore()
    peers = [right, left] + [z * inner + (y + dj) % inner for dj in range(1, inner)]
    for peer in peers:
        pl.semaphore_signal(barrier, inc=1, device_id={"fsdp": peer}, device_id_type=MESH)
    pl.semaphore_signal(barrier, inc=1, device_id={"ctx": 1 - ctx}, device_id_type=MESH)
    pl.semaphore_wait(barrier, len(peers) + 1)

    def remote(src, dst, send, recv, to):
        return pltpu.make_async_remote_copy(
            src_ref=src, dst_ref=dst, send_sem=send, recv_sem=recv, device_id=to, device_id_type=MESH
        )

    def z_copy(do, i):
        j, a = chunks[i]
        take, unused = slab_of(own[a].shape[1], ctx)
        at = shard(do - 1, 0)
        return remote(held(do - 1, 0)[a].at[j, take], bufs[a].at[at, j, take], z_send.at[do, i], z_recv.at[do, i], {"fsdp": right})

    def y_copy(do, dj, i):
        j, a = chunks[i]
        take, unused = slab_of(own[a].shape[1], ctx)
        at = shard(do, 0)
        to = {"fsdp": z * inner + (y + dj) % inner}
        return remote(held(do, 0)[a].at[j, take], bufs[a].at[at, j, take], y_send.at[do, dj, i], y_recv.at[do, dj, i], to)

    def x_copy(do, dj, i):
        j, a = chunks[i]
        unused, edge = slab_of(own[a].shape[1], ctx)
        at = shard(do, dj)
        part = bufs[a].at[at, j, edge]
        return remote(part, part, x_send.at[do, dj, i], x_recv.at[do, dj, i], {"ctx": 1 - ctx})

    started = []

    def go(copy):
        copy.start()
        started.append(copy)

    for ref in (moe_ref, dn2_ref, as_ref, gs_ref, us_ref, dgate_ref):
        ref[...] = jnp.zeros_like(ref)

    step = rows // 3

    def compute(do, dj, j, slot):
        e = shard(do, dj) * local + j

        def block(b, carry):
            at = pl.ds(pl.multiple_of(b * step, step), step)
            xb = n2_ref[at, :]
            cb = c_ref[at, :]
            gv = dot(xb, wg[slot]) + gl_ref[at, :]
            uv = dot(xb, wu[slot]) + ul_ref[at, :]
            back = dot_t(cb, wd[slot]) + al_ref[at, :]
            hit = lax.broadcasted_iota(jnp.int32, (step, experts), 1) == e
            gate = jnp.sum(jnp.where(hit, gates_ref[at, :], 0.0), axis=1, keepdims=True)
            sig = 1.0 / (1.0 + jnp.exp(-gv))
            silu = gv * sig
            act = silu * uv
            col = jnp.sum(act * back, axis=1, keepdims=True)
            dgate_ref[at, :] += jnp.where(hit, col, 0.0)
            back = back * gate
            act = (act * gate).astype(BF)
            du = back * silu
            dg = back * uv * (sig + silu * (1.0 - sig))
            as_ref[at, :] += act.astype(F32)
            gs_ref[at, :] += dg
            us_ref[at, :] += du
            moe_ref[at, :] += dot(act, wd[slot])
            dn2_ref[at, :] += dot_t(dg.astype(BF), wg[slot]) + dot_t(du.astype(BF), wu[slot])
            return carry

        lax.fori_loop(0, 3, block, 0)

    queue = []

    def load(do, dj, j, slot):
        found = []
        for a, dst in enumerate((wg, wu, wd)):
            copy = pltpu.make_async_copy(held(do, dj)[a].at[j], dst.at[slot], load_sem.at[slot, a])
            copy.start()
            found.append(copy)
        return found

    pending = []
    turn = [0]

    def run_next():
        do, dj, j, slot, copies = pending.pop(0)
        for c in copies:
            c.wait()
        compute(do, dj, j, slot)

    def feed(do, dj, j):
        if len(pending) == 2:
            run_next()
        slot = turn[0] % 2
        turn[0] += 1
        pending.append((do, dj, j, slot, load(do, dj, j, slot)))

    def arrived(do, dj, j):
        for i, (jj, a) in enumerate(chunks):
            if jj == j:
                x_copy(do, dj, i).wait_recv()

    for i in range(len(chunks)):
        go(z_copy(2, i))
        for dj in range(1, inner):
            go(y_copy(1, dj, i))
        for dj in range(2, inner):
            go(y_copy(0, dj, i))

    ready = [(do, dj, j) for do, dj in ((0, 0), (1, 0), (0, 1)) for j in range(local)]
    for r in range(outer - 1):
        later = []
        for i, (j, a) in enumerate(chunks):
            if ready:
                do, dj, jj = ready.pop(0)
                if (do, dj) not in ((0, 0), (1, 0), (0, 1)):
                    arrived(do, dj, jj)
                feed(do, dj, jj)
            if r + 2 < outer:
                z_copy(r + 2, i).wait_recv()
                if r + 3 < outer:
                    go(z_copy(r + 3, i))
                for dj in range(1, inner):
                    go(y_copy(r + 2, dj, i))
                go(x_copy(r + 2, 0, i))
                if a == 2:
                    later.append((r + 2, 0, j))
            for do, dj in [(r + 1, dj) for dj in range(1, inner)] + ([(0, dj) for dj in range(2, inner)] if r == 0 else []):
                y_copy(do, dj, i).wait_recv()
                go(x_copy(do, dj, i))
                if a == 2:
                    later.append((do, dj, j))
        ready = ready + later
    for do, dj, j in ready:
        arrived(do, dj, j)
        feed(do, dj, j)
    while pending:
        run_next()
    for c in started:
        c.wait_send()


def moe_all(n2, cot, gate_low, up_low, act_low, gates, own, near, side, collective_id):
    n = lax.axis_size("fsdp")
    outer, inner = levels(n)
    rows, width = n2.shape
    ff = gate_low.shape[1]
    count = 3 * own[0].shape[0]
    dma = pltpu.SemaphoreType.DMA
    sd = jax.ShapeDtypeStruct
    vm = pl.BlockSpec(memory_space=pltpu.VMEM)
    anywhere = pl.BlockSpec(memory_space=pl.ANY)
    outs = pl.pallas_call(
        functools.partial(moe_kernel, n),
        in_specs=[vm] * 6 + [anywhere] * 9,
        out_specs=[vm] * 6 + [anywhere] * 3,
        out_shape=[sd((rows, width), F32), sd((rows, width), F32), sd((rows, ff), F32), sd((rows, ff), F32), sd((rows, ff), F32), sd(gates.shape, F32)]
        + [sd((n,) + a.shape, a.dtype) for a in own],
        scratch_shapes=[
            pltpu.VMEM((2, width, ff), BF), pltpu.VMEM((2, width, ff), BF), pltpu.VMEM((2, ff, width), BF), dma((2, 3)),
            dma((outer, count)), dma((outer, count)), dma((outer, inner, count)), dma((outer, inner, count)),
            dma((outer, inner, count)), dma((outer, inner, count)),
        ],
        compiler_params=pltpu.CompilerParams(collective_id=collective_id, has_side_effects=True, vmem_limit_bytes=56 << 20),
    )(n2, cot, gate_low, up_low, act_low, gates, *own, *near, *side)
    return outs[:6]


def tp_sum(value):
    if lax.axis_size("tp") != 2:
        return lax.psum(value, "tp")
    return value + lax.ppermute(value, "tp", [(0, 1), (1, 0)])


def on_device(
    tokens, out_cotangent, lengths, adapter_of_doc, routes, attn_gain, ffn_gain,
    w_query, key_matrix, value_matrix, w_out, w_router, w_gate, w_up, w_down,
    a_query, b_query, a_key, key_second_factor, a_value, value_second_factor,
    a_out, b_out, a_router, b_router, a_gate, b_gate, a_up, b_up, a_down, b_down,
):
    rows, width = tokens.shape
    n = lax.axis_size("fsdp")
    n_tp = lax.axis_size("tp")
    tp_at = lax.axis_index("tp")
    ctx_at = lax.axis_index("ctx")
    group = rows * lax.axis_size("ctx")
    q_width = w_query.shape[1]
    kv_width = key_matrix.shape[1]
    ff_width = w_gate.shape[2]
    local_experts = w_gate.shape[0]
    experts = w_router.shape[1]
    ranks = a_query.shape[1]
    share = w_query.shape[0]
    low_rows = b_query.shape[0]

    pad = ((0, 0), (0, LANES - experts))
    one, low_one = gather_packs(
        [
            [(a, a.shape[1]) for a in (w_query, key_matrix, value_matrix, a_query, a_key, a_value)],
            [(b_query, q_width), (key_second_factor, kv_width), (value_second_factor, kv_width)],
        ],
        0,
    )
    qkv = q_width + 2 * kv_width
    w_one = one.reshape(n * share, -1)
    low_one = low_one.reshape(n * low_rows, -1)
    query_b, key_b, value_b = low_one[:, :q_width], low_one[:, q_width : q_width + kv_width], low_one[:, q_width + kv_width :]

    ends = jnp.cumsum(lengths[0])
    starts = ends - lengths[0]
    place = jnp.arange(group, dtype=jnp.int32)
    doc = jnp.sum((place[:, None] >= ends[None, :]).astype(jnp.int32), axis=1)
    picked = (doc[:, None] == jnp.arange(lengths.shape[1], dtype=jnp.int32)[None, :]).astype(jnp.int32)
    begin = jnp.sum(picked * starts[None, :], axis=1)
    chosen = jnp.sum(picked * adapter_of_doc[0][None, :], axis=1)
    start = ctx_at * rows
    query_index = start + jnp.arange(rows, dtype=jnp.int32)
    begin_local = lax.dynamic_slice_in_dim(begin, start, rows)
    chosen_local = lax.dynamic_slice_in_dim(chosen, start, rows)
    mask = (chosen_local[:, None] == (jnp.arange(ranks, dtype=jnp.int32) // ADAPTER_RANK)[None, :]).astype(F32)
    half = HEAD_SIZE // 2
    freq = 10000.0 ** (-jnp.arange(half, dtype=F32) / half)
    angles = (query_index - begin_local).astype(F32)[:, None] * freq[None, :]
    cosine_table = jnp.cos(angles)[:, None, :]
    sine_table = jnp.sin(angles)[:, None, :]

    xfull = tokens.astype(F32)
    normed = rms_norm(xfull, attn_gain).astype(BF)
    raw = dot(normed, w_one)
    query_u = (raw[:, qkv : qkv + ranks] * mask).astype(BF)
    key_u = (raw[:, qkv + ranks : qkv + 2 * ranks] * mask).astype(BF)
    value_u = (raw[:, qkv + 2 * ranks : qkv + 3 * ranks] * mask).astype(BF)
    query_pre = raw[:, :q_width] + dot(query_u, query_b)
    key_pre = raw[:, q_width : q_width + kv_width] + dot(key_u, key_b)
    value_state = (raw[:, q_width + kv_width : qkv] + dot(value_u, value_b)).astype(BF)
    query_state = (
        rotary_apply(query_pre.reshape(rows, -1, HEAD_SIZE), cosine_table, sine_table).reshape(rows, q_width).astype(BF)
    )
    key = rotary_apply(key_pre.reshape(rows, -1, HEAD_SIZE), cosine_table, sine_table).reshape(rows, kv_width).astype(BF)
    kv = jnp.concatenate([key, value_state], axis=1)
    far = lax.ppermute(kv, "ctx", [(i, i + 1) for i in range(lax.axis_size("ctx") - 1)])
    w_out_t, kv = lax.optimization_barrier((w_out.T, kv))
    two, low_two, down_a = gather_packs(
        [
            [(a, a.shape[1]) for a in (w_out_t, a_router, a_gate, a_up, jnp.pad(w_router, pad), a_out)],
            [(b_gate, ff_width), (b_up, ff_width), (b_out, width), (b_down, width), (jnp.pad(b_router, pad), LANES)],
            [(a_down, ranks)],
        ],
        1,
    )
    near_w = lax.optimization_barrier((w_gate, w_up, w_down, two))[:3]
    outer, inner = levels(n)
    ring = [(i, (i + inner) % n) for i in range(n)]
    turn = [(i, i // inner * inner + (i % inner + 1) % inner) for i in range(n)]
    near = [lax.ppermute(a, "fsdp", ring) for a in near_w]
    beside = [lax.ppermute(a, "fsdp", turn) for a in near_w]
    far, two = lax.optimization_barrier((far, two))
    w_two = two.reshape(n * share, -1)
    low_two = low_two.reshape(n * low_rows, -1)
    gate_b, up_b = low_two[:, :ff_width], low_two[:, ff_width : 2 * ff_width]
    out_b = low_two[:, 2 * ff_width : 2 * ff_width + width]
    down_b = low_two[:, 2 * ff_width + width : 2 * ff_width + 2 * width]
    router_b = low_two[:, 2 * ff_width + 2 * width :]
    out_wt = w_two[:, :q_width]
    router_a = w_two[:, q_width : q_width + ranks]
    router_w = w_two[:, q_width + 3 * ranks : q_width + 4 * ranks]
    out_a = lax.dynamic_slice_in_dim(w_two[:, q_width + 4 * ranks : q_width + 5 * ranks], tp_at * q_width, q_width, 0)
    down_at = lax.dynamic_slice_in_dim(down_a.reshape(-1, ranks), tp_at * ff_width, ff_width, 0)
    begin_row = begin_local[None, :]
    start_at = jnp.reshape(start, (1,)).astype(jnp.int32)
    query_state = (query_state.astype(F32) * 0.125).astype(BF)
    mixed_heads, log_total = attend(query_state, kv, far, begin_row, start_at)
    out_u = dot(mixed_heads, out_a) * mask
    attn_part = dot_t(mixed_heads, out_wt) + dot(out_u.astype(BF), out_b)
    hidden = xfull + tp_sum(attn_part)
    normed_two = rms_norm(hidden, ffn_gain).astype(BF)
    lows = dot(normed_two, w_two[:, q_width : q_width + 4 * ranks])
    router_u = (lows[:, :ranks] * mask).astype(BF)
    zin_gate = (lows[:, ranks : 2 * ranks] * mask).astype(BF)
    zin_up = (lows[:, 2 * ranks : 3 * ranks] * mask).astype(BF)
    logits = lows[:, 3 * ranks : 3 * ranks + experts] + dot(router_u, router_b)[:, :experts]
    selected = jnp.any(routes[:, :, None] == jnp.arange(experts, dtype=jnp.int32)[None, None, :], axis=1)
    gates = jax.nn.softmax(jnp.where(selected, logits, -jnp.inf), axis=-1)

    cot = out_cotangent
    dout = cot.astype(F32)
    gate_low = dot(zin_gate, gate_b)
    up_low = dot(zin_up, up_b)
    down_back = dot_t(cot, down_b) * mask
    act_low = dot_t(down_back.astype(BF), down_at)
    moe, dn2, act_sum, dg_sum, du_sum, dgate = moe_all(
        normed_two, cot, gate_low, up_low, act_low, gates, (w_gate, w_up, w_down), near, beside, 2
    )
    down_low = (dot(act_sum.astype(BF), down_at) * mask).astype(BF)
    moe = moe + dot(down_low, down_b)
    output = (hidden + tp_sum(moe.astype(BF).astype(F32))).astype(BF)
    grad_bd = t_dot(down_low, cot)
    grad_ad = t_dot(act_sum.astype(BF), down_back.astype(BF))
    dg_sum = dg_sum.astype(BF)
    du_sum = du_sum.astype(BF)
    grad_bg = t_dot(zin_gate, dg_sum)
    grad_bu = t_dot(zin_up, du_sum)
    gate_du = (dot_t(dg_sum, gate_b) * mask).astype(BF)
    up_du = (dot_t(du_sum, up_b) * mask).astype(BF)
    gu_du = jnp.concatenate([gate_du, up_du], axis=1)
    dn2 = dn2 + dot_t(gu_du, w_two[:, q_width + ranks : q_width + 3 * ranks])
    grad_agu = t_dot(normed_two, gu_du)
    grad_ag, grad_au = grad_agu[:, :ranks], grad_agu[:, ranks:]
    dn2, dgate = tp_sum(dn2), tp_sum(dgate)
    dlogits = (gates * (dgate - jnp.sum(gates * dgate, axis=-1, keepdims=True))).astype(BF)
    dlogits = jnp.pad(dlogits, ((0, 0), (0, LANES - experts)))
    router_du = (dot_t(dlogits, router_b) * mask).astype(BF)
    dn2 = dn2 + dot_t(dlogits, router_w) + dot_t(router_du, router_a)
    grad_br = t_dot(router_u, dlogits)[:, :experts]
    grad_ar = t_dot(normed_two, router_du)
    dhidden = dout + norm_back(hidden, ffn_gain, dn2)
    dattn = dhidden.astype(BF)
    out_du = (dot_t(dattn, out_b) * mask).astype(BF)
    dmixed = (dot(dattn, out_wt) + dot_t(out_du, out_a)).astype(BF)
    grad_bo = t_dot(out_u.astype(BF), dattn)
    grad_ao = t_dot(mixed_heads, out_du)
    dquery, dkey_own, dvalue_own, dkey_far, dvalue_far = attend_back(
        query_state, kv, far, begin_row, start_at, mixed_heads, dmixed, log_total
    )
    far_back = lax.ppermute(
        jnp.concatenate([dkey_far, dvalue_far], axis=1),
        "ctx",
        [(i + 1, i) for i in range(lax.axis_size("ctx") - 1)],
    ).astype(F32)
    dkey = dkey_own + far_back[:, :kv_width]
    dvalue = (dvalue_own + far_back[:, kv_width:]).astype(BF)
    dquery_pre = rotary_apply(dquery.reshape(rows, -1, HEAD_SIZE), cosine_table, -sine_table).reshape(rows, q_width).astype(BF)
    dkey_pre = rotary_apply(dkey.reshape(rows, -1, HEAD_SIZE), cosine_table, -sine_table).reshape(rows, kv_width).astype(BF)
    query_du = (dot_t(dquery_pre, query_b) * mask).astype(BF)
    key_du = (dot_t(dkey_pre, key_b) * mask).astype(BF)
    value_du = (dot_t(dvalue, value_b) * mask).astype(BF)
    everything = jnp.concatenate([dquery_pre, dkey_pre, dvalue, query_du, key_du, value_du], axis=1)
    dn1 = dot_t(everything, w_one)
    grad_a3 = t_dot(normed, everything[:, qkv:])
    grad_bq = t_dot(query_u, dquery_pre)
    grad_bk = t_dot(key_u, dkey_pre)
    grad_bv = t_dot(value_u, dvalue)
    dn1 = tp_sum(dn1)
    grad_tokens = (dhidden + norm_back(xfull, attn_gain, dn1)).astype(BF)

    def place_cols(piece, full_cols):
        blank = jnp.zeros((piece.shape[0], full_cols), F32)
        return lax.dynamic_update_slice_in_dim(blank, piece, tp_at * piece.shape[1], 1)

    def place_rows(piece, full_rows):
        blank = jnp.zeros((full_rows, piece.shape[1]), F32)
        return lax.dynamic_update_slice_in_dim(blank, piece, tp_at * piece.shape[0], 0)

    only_first = (tp_at == 0).astype(F32)
    grads = (
        grad_a3[:, :ranks],
        place_cols(grad_bq, q_width * n_tp),
        grad_a3[:, ranks : 2 * ranks],
        place_cols(grad_bk, kv_width * n_tp),
        grad_a3[:, 2 * ranks :],
        place_cols(grad_bv, kv_width * n_tp),
        place_rows(grad_ao, q_width * n_tp),
        grad_bo,
        grad_ar * only_first,
        grad_br * only_first,
        grad_ag,
        place_cols(grad_bg, ff_width * n_tp),
        grad_au,
        place_cols(grad_bu, ff_width * n_tp),
        place_rows(grad_ad, ff_width * n_tp),
        grad_bd,
    )
    def reduce_grads(some):
        flat = []
        for g in some:
            height, cols = g.shape[0] // n, g.shape[1]
            count = -(-cols // LANES)
            g = jnp.pad(g.astype(BF), ((0, 0), (0, count * LANES - cols)))
            flat.append(g.reshape(n, height, count, LANES).transpose(0, 2, 1, 3).reshape(n, count * height, LANES))
        flat = jnp.concatenate(flat, axis=1)
        mine = lax.psum_scatter(flat, "fsdp", scatter_dimension=0, tiled=False)
        mine = lax.psum(mine, ("ctx", "tp")).astype(F32)
        found = []
        at = 0
        for g in some:
            height, cols = g.shape[0] // n, g.shape[1]
            count = -(-cols // LANES)
            piece = mine[at : at + count * height].reshape(count, height, LANES).transpose(1, 0, 2).reshape(height, count * LANES)
            found.append(piece[:, :cols])
            at += count * height
        return found

    final = reduce_grads(grads[:6]) + reduce_grads(grads[6:])
    return (output, grad_tokens, *final)


def solution(mesh):
    both = P(("fsdp", "ctx"), None)
    split = P("fsdp", None)
    placed = (
        both, both, split, split, both, P(), P(),
        P("fsdp", "tp"), P("fsdp", "tp"), P("fsdp", "tp"), P("tp", "fsdp"), split,
        P("fsdp", None, "tp"), P("fsdp", None, "tp"), P("fsdp", "tp", None),
    ) + (split,) * 16
    return jax.shard_map(
        on_device, mesh=mesh, in_specs=placed, out_specs=(both, both) + (split,) * 16, check_vma=False
    )
```

```python
import functools

import jax
import jax.numpy as jnp
from jax import lax
from jax.experimental import pallas as pl
from jax.experimental.pallas import tpu as pltpu
from jax.sharding import PartitionSpec as P

HEAD_SIZE = 64
ADAPTER_RANK = 16
LANES = 128
norm_eps = 1e-05
BF = jnp.bfloat16
F32 = jnp.float32


MESH = pl.DeviceIdType.MESH


def dot(left, right, dims=((1,), (0,)), precision=None):
    return lax.dot_general(left, right, (dims, ((), ())), preferred_element_type=F32, precision=precision)


def dot_t(left, right):
    return dot(left, right, ((1,), (1,)))


def t_dot(left, right):
    return dot(left, right, ((0,), (0,)))


def rms_norm(values, gain):
    return values * lax.rsqrt(jnp.mean(values * values, axis=-1, keepdims=True) + norm_eps) * gain


def norm_back(values, gain, grad):
    unused, pull = jax.vjp(lambda inner: rms_norm(inner, gain), values)
    return pull(grad)[0]


def rotary_apply(values, cosine_table, sine_table):
    half = values.shape[-1] // 2
    first = values[..., :half]
    second = values[..., half:]
    return jnp.concatenate(
        [first * cosine_table - second * sine_table, first * sine_table + second * cosine_table],
        axis=-1,
    )


def levels(n):
    outer = 4 if n % 4 == 0 else n
    return outer, n // outer


def fill_bias(bias, start_ref, begin_ref, rows):
    step = rows // 3
    for at in range(0, 2 * rows, step):
        key = start_ref[0] - rows + at + lax.broadcasted_iota(jnp.int32, (step, rows), 0)
        query = start_ref[0] + lax.broadcasted_iota(jnp.int32, (step, rows), 1)
        ok = (key <= query) & (key >= begin_ref[...]) & (key >= 0)
        bias[pl.ds(at, step), :] = jnp.where(ok, 0.0, -1e30)


def split_heads(ref, out, count, rows, at=0):
    for h in range(count):
        out[h, pl.ds(at, rows), :] = ref[:, h * HEAD_SIZE : (h + 1) * HEAD_SIZE]


def attend_kernel(group, q_blocks, start_ref, begin_ref, q_ref, ko_ref, vo_ref, kf_ref, vf_ref, o_ref, lse_ref, bias, ks, vts, qs, ots):
    rows = q_ref.shape[0]
    width = rows // q_blocks
    heads = 2 * group
    @pl.when(pl.program_id(0) == 0)
    def _():
        fill_bias(bias, start_ref, begin_ref, rows)
    split_heads(kf_ref, ks, 2, rows, 0)
    split_heads(ko_ref, ks, 2, rows, rows)
    split_heads(q_ref, qs, heads, rows, 0)
    vts[:, pl.ds(0, rows)] = vf_ref[...].astype(F32).T.astype(BF)
    vts[:, pl.ds(rows, rows)] = vo_ref[...].astype(F32).T.astype(BF)
    for b in range(q_blocks):
        keys = rows + (b + 1) * width
        def one(h, _):
            g = h // group
            s = dot_t(ks[g, pl.ds(0, keys), :], qs[h, pl.ds(b * width, width), :]) + bias[pl.ds(0, keys), pl.ds(b * width, width)]
            top = jnp.max(s, axis=0, keepdims=True)
            p = jnp.exp(s - top)
            total = jnp.sum(p, axis=0, keepdims=True)
            lse_ref[0, pl.ds(h, 1), pl.ds(b * width, width)] = top + jnp.log(total)
            vt = vts[pl.ds(pl.multiple_of(g * HEAD_SIZE, HEAD_SIZE), HEAD_SIZE), pl.ds(0, keys)]
            o = dot(vt, p.astype(BF)) / total
            ots[pl.ds(pl.multiple_of(h * HEAD_SIZE, HEAD_SIZE), HEAD_SIZE), pl.ds(b * width, width)] = o
            return 0
        lax.fori_loop(0, heads, one, 0)
    for j in range(group):
        o_ref[:, j * LANES : (j + 1) * LANES] = ots[pl.ds(j * LANES, LANES), :].T.astype(BF)


def attend(q, kv, far, begin, start, q_blocks=3):
    rows, q_width = q.shape
    kv_width = kv.shape[1] // 2
    pairs = kv_width // LANES
    group = q_width // kv_width
    spec = lambda off: pl.BlockSpec((rows, LANES), lambda i: (0, i + off))
    return pl.pallas_call(
        functools.partial(attend_kernel, group, q_blocks),
        grid=(pairs,),
        in_specs=[pl.BlockSpec(memory_space=pltpu.SMEM), pl.BlockSpec((1, rows), lambda i: (0, 0)),
                  pl.BlockSpec((rows, group * LANES), lambda i: (0, i)), spec(0), spec(pairs), spec(0), spec(pairs)],
        out_specs=[pl.BlockSpec((rows, group * LANES), lambda i: (0, i)), pl.BlockSpec((1, 8, rows), lambda i: (i, 0, 0))],
        out_shape=[jax.ShapeDtypeStruct((rows, q_width), BF), jax.ShapeDtypeStruct((pairs, 8, rows), F32)],
        scratch_shapes=[pltpu.VMEM((2 * rows, rows), F32), pltpu.VMEM((2, 2 * rows, HEAD_SIZE), BF), pltpu.VMEM((LANES, 2 * rows), BF),
                        pltpu.VMEM((2 * group, rows, HEAD_SIZE), BF), pltpu.VMEM((2 * group * HEAD_SIZE, rows), F32)],
        compiler_params=pltpu.CompilerParams(vmem_limit_bytes=50 << 20),
        cost_estimate=pl.CostEstimate(flops=8 * rows * rows * q_width, bytes_accessed=8 << 20, transcendentals=2 * rows * rows * 12),
    )(start, begin, q, kv, kv, far, far)


def attend_back_kernel(group, q_blocks, start_ref, begin_ref, q_ref, ko_ref, vo_ref, kf_ref, vf_ref, o_ref, do_ref, lse_ref,
                       dq_ref, dko_ref, dvo_ref, dkf_ref, dvf_ref, bias, ks, vs, kts, qs, dos, dqts, dks, dvs, deltas):
    rows = q_ref.shape[0]
    width = rows // q_blocks
    heads = 2 * group
    @pl.when(pl.program_id(0) == 0)
    def _():
        fill_bias(bias, start_ref, begin_ref, rows)
    split_heads(kf_ref, ks, 2, rows, 0)
    split_heads(ko_ref, ks, 2, rows, rows)
    split_heads(vf_ref, vs, 2, rows, 0)
    split_heads(vo_ref, vs, 2, rows, rows)
    split_heads(q_ref, qs, heads, rows, 0)
    split_heads(do_ref, dos, heads, rows, 0)
    kts[:, pl.ds(0, rows)] = kf_ref[...].astype(F32).T.astype(BF)
    kts[:, pl.ds(rows, rows)] = ko_ref[...].astype(F32).T.astype(BF)
    cols = heads * HEAD_SIZE
    pick = (lax.broadcasted_iota(jnp.int32, (8, cols), 1) // HEAD_SIZE == lax.broadcasted_iota(jnp.int32, (8, cols), 0)).astype(F32)
    prod = o_ref[...].astype(F32) * do_ref[...].astype(F32)
    deltas[...] = dot(pick, prod, ((1,), (1,)), lax.Precision.HIGHEST)
    dks[...] = jnp.zeros_like(dks)
    dvs[...] = jnp.zeros_like(dvs)
    for b in range(q_blocks):
        keys = rows + (b + 1) * width
        def one(h, _):
            g = h // group
            at = pl.ds(b * width, width)
            qb = qs[h, at, :]
            dob = dos[h, at, :]
            s = dot_t(ks[g, pl.ds(0, keys), :], qb) + bias[pl.ds(0, keys), at]
            p = jnp.exp(s - lse_ref[0, pl.ds(h, 1), at])
            dp = dot_t(vs[g, pl.ds(0, keys), :], dob)
            ds = (p * (dp - deltas[pl.ds(h, 1), at])).astype(BF)
            dvs[g, pl.ds(0, keys), :] += dot(p.astype(BF), dob)
            dks[g, pl.ds(0, keys), :] += dot(ds, qb)
            kt = kts[pl.ds(pl.multiple_of(g * HEAD_SIZE, HEAD_SIZE), HEAD_SIZE), pl.ds(0, keys)]
            dqts[pl.ds(pl.multiple_of(h * HEAD_SIZE, HEAD_SIZE), HEAD_SIZE), at] = dot(kt, ds) * 0.125
            return 0
        lax.fori_loop(0, heads, one, 0)
    for j in range(group):
        dq_ref[:, j * LANES : (j + 1) * LANES] = dqts[pl.ds(j * LANES, LANES), :].T
    for g in range(2):
        at = slice(g * HEAD_SIZE, (g + 1) * HEAD_SIZE)
        dkf_ref[:, at] = dks[g, pl.ds(0, rows), :].astype(BF)
        dko_ref[:, at] = dks[g, pl.ds(rows, rows), :]
        dvf_ref[:, at] = dvs[g, pl.ds(0, rows), :].astype(BF)
        dvo_ref[:, at] = dvs[g, pl.ds(rows, rows), :]


def attend_back(q, kv, far, begin, start, o, do, lse, q_blocks=3):
    rows, q_width = q.shape
    kv_width = kv.shape[1] // 2
    pairs = kv_width // LANES
    group = q_width // kv_width
    spec = lambda off: pl.BlockSpec((rows, LANES), lambda i: (0, i + off))
    wide = pl.BlockSpec((rows, group * LANES), lambda i: (0, i))
    sd = jax.ShapeDtypeStruct
    return pl.pallas_call(
        functools.partial(attend_back_kernel, group, q_blocks),
        grid=(pairs,),
        in_specs=[pl.BlockSpec(memory_space=pltpu.SMEM), pl.BlockSpec((1, rows), lambda i: (0, 0)),
                  wide, spec(0), spec(pairs), spec(0), spec(pairs), wide, wide, pl.BlockSpec((1, 8, rows), lambda i: (i, 0, 0))],
        out_specs=[wide, spec(0), spec(0), spec(0), spec(0)],
        out_shape=[sd((rows, q_width), F32), sd((rows, kv_width), F32), sd((rows, kv_width), F32), sd((rows, kv_width), BF), sd((rows, kv_width), BF)],
        scratch_shapes=[pltpu.VMEM((2 * rows, rows), F32), pltpu.VMEM((2, 2 * rows, HEAD_SIZE), BF), pltpu.VMEM((2, 2 * rows, HEAD_SIZE), BF), pltpu.VMEM((LANES, 2 * rows), BF),
                        pltpu.VMEM((2 * group, rows, HEAD_SIZE), BF), pltpu.VMEM((2 * group, rows, HEAD_SIZE), BF), pltpu.VMEM((2 * group * HEAD_SIZE, rows), F32),
                        pltpu.VMEM((2, 2 * rows, HEAD_SIZE), F32), pltpu.VMEM((2, 2 * rows, HEAD_SIZE), F32), pltpu.VMEM((8, rows), F32)],
        compiler_params=pltpu.CompilerParams(vmem_limit_bytes=56 << 20),
        cost_estimate=pl.CostEstimate(flops=20 * rows * rows * q_width, bytes_accessed=16 << 20, transcendentals=2 * rows * rows * 12),
    )(start, begin, q, kv, kv, far, far, o, do, lse)


def slab_of(rows, ctx):
    edge = 3 * rows // 8 // 16 * 16
    take = rows - edge
    return pl.ds(pl.multiple_of(ctx * edge, 16), take), pl.ds(pl.multiple_of(ctx * take, 16), edge)


def gather_kernel(n, layout, *refs):
    total = sum(len(parts) for parts in layout)
    count = len(layout)
    ins, outs = refs[:total], refs[total : total + count]
    own_sem, z_send, z_recv, y_send, y_recv, x_send, x_recv = refs[total + count :]
    outer, inner = levels(n)
    me = lax.axis_index("fsdp")
    ctx = lax.axis_index("ctx")
    tp = lax.axis_index("tp")
    z, y = me // inner, me % inner
    right = (z + 1) % outer * inner + y
    left = (z + outer - 1) % outer * inner + y

    def shard(do, dj):
        return (z + outer - do) % outer * inner + (y + inner - dj) % inner

    own = []
    at = 0
    for a, parts in enumerate(layout):
        col = 0
        for cols, split in parts:
            src = ins[at].at[:, pl.ds(pl.multiple_of(tp * cols, LANES), cols)] if split else ins[at]
            own.append(pltpu.make_async_copy(src, outs[a].at[me, :, pl.ds(col, cols)], own_sem.at[at]))
            own[-1].start()
            col += cols
            at += 1

    barrier = pltpu.get_barrier_semaphore()
    peers = [right, left] + [z * inner + (y + dj) % inner for dj in range(1, inner)]
    for peer in peers:
        pl.semaphore_signal(barrier, inc=1, device_id={"fsdp": peer}, device_id_type=MESH)
    pl.semaphore_signal(barrier, inc=1, device_id={"ctx": 1 - ctx}, device_id_type=MESH)
    pl.semaphore_wait(barrier, len(peers) + 1)

    def cut(a):
        return 3 * outs[a].shape[1] // 8 >= 16

    def taken(a, k):
        if not cut(a):
            return outs[a].at[k]
        return outs[a].at[k, slab_of(outs[a].shape[1], ctx)[0]]

    def remote(part, send, recv, to):
        return pltpu.make_async_remote_copy(src_ref=part, dst_ref=part, send_sem=send, recv_sem=recv, device_id=to, device_id_type=MESH)

    def z_copy(a, k):
        return remote(taken(a, shard(k - 1, 0)), z_send.at[a, k - 1], z_recv.at[a, k - 1], {"fsdp": right})

    def y_copy(a, do, dj):
        to = {"fsdp": z * inner + (y + dj) % inner}
        return remote(taken(a, shard(do, 0)), y_send.at[a, do, dj - 1], y_recv.at[a, do, dj - 1], to)

    def x_copy(a, do, dj):
        part = outs[a].at[shard(do, dj), slab_of(outs[a].shape[1], ctx)[1]]
        return remote(part, x_send.at[a, do, dj], x_recv.at[a, do, dj], {"ctx": 1 - ctx})

    started = []

    def go(copy):
        copy.start()
        started.append(copy)

    for c in own:
        c.wait()
    for a in range(count):
        go(z_copy(a, 1))
        for dj in range(1, inner):
            go(y_copy(a, 0, dj))
    for do in range(1, outer + 1):
        for a in range(count):
            if do < outer:
                z_copy(a, do).wait_recv()
                if do + 1 < outer:
                    go(z_copy(a, do + 1))
                for dj in range(1, inner):
                    go(y_copy(a, do, dj))
                if cut(a):
                    go(x_copy(a, do, 0))
        for a in range(count):
            for dj in range(1, inner):
                y_copy(a, do - 1, dj).wait_recv()
                if cut(a):
                    go(x_copy(a, do - 1, dj))
    for a in range(count):
        if cut(a):
            for do in range(outer):
                for dj in range(inner):
                    if do or dj:
                        x_copy(a, do, dj).wait_recv()
    for c in started:
        c.wait_send()


def gather_packs(packs, collective_id):
    n = lax.axis_size("fsdp")
    outer, inner = levels(n)
    count = len(packs)
    layout = [[(cols, cols != a.shape[1]) for a, cols in parts] for parts in packs]
    arrays = [a for parts in packs for a, cols in parts]
    dma = pltpu.SemaphoreType.DMA
    anywhere = pl.BlockSpec(memory_space=pl.ANY)
    side = max(inner - 1, 1)
    return pl.pallas_call(
        functools.partial(gather_kernel, n, layout),
        in_specs=[anywhere] * len(arrays),
        out_specs=[anywhere] * count,
        out_shape=[jax.ShapeDtypeStruct((n, parts[0][0].shape[0], sum(cols for a, cols in parts)), BF) for parts in packs],
        scratch_shapes=[
            dma((len(arrays),)), dma((count, outer - 1)), dma((count, outer - 1)),
            dma((count, outer, side)), dma((count, outer, side)), dma((count, outer, inner)), dma((count, outer, inner)),
        ],
        compiler_params=pltpu.CompilerParams(collective_id=collective_id, has_side_effects=True),
    )(*arrays)


def t_dot_k(left, right):
    return dot(left, right, ((0,), (0,)))


def expert_kernel(experts, count, ids_ref, t_ref, c_ref, *refs):
    w_refs = refs[:count]
    ga_ref, ua_ref, gb_ref, ub_ref, db_ref, da_ref = refs[count : count + 6]
    prior = refs[count + 6 : count + 11]
    early = refs[count + 11 : -9]
    r_ref, m_ref = refs[-9:-7]
    sums = refs[-7:-2]
    moe_acc, dn2_acc = refs[-2:]
    rows, width = c_ref.shape
    ff = gb_ref.shape[1]
    spare = r_ref.shape[1] - width
    lanes = t_ref.shape[1] - width

    @pl.when(pl.program_id(0) == 0)
    def _():
        for old, new in zip(prior, sums):
            new[...] = old[...]

    n2 = t_ref[:, :width]
    cot = c_ref[...]
    extra = t_ref[:, width:].astype(F32)
    lane = lax.broadcasted_iota(jnp.int32, (rows, lanes), 1)
    chosen = jnp.sum(jnp.where(lane == 2 * experts, extra, 0.0), axis=1, keepdims=True)
    low_lane = lax.broadcasted_iota(jnp.int32, (rows, LANES), 1)
    mask = ((low_lane // ADAPTER_RANK).astype(F32) == chosen).astype(F32)
    zg = (dot(n2, ga_ref[...]) * mask).astype(BF)
    zu = (dot(n2, ua_ref[...]) * mask).astype(BF)
    gl = dot(zg, gb_ref[...])
    ul = dot(zu, ub_ref[...])
    down_back = (dot_t(cot, db_ref[...]) * mask).astype(BF)
    al = dot_t(down_back, da_ref[...])
    back_lane = lax.broadcasted_iota(jnp.int32, (rows, spare), 1)
    dgate = jnp.zeros((rows, spare), F32)
    act_sum = dg_sum = du_sum = None
    for k in range(count):
        e = ids_ref[k]
        w = w_refs[k]
        gate = jnp.sum(jnp.where((lane == e) | (lane == experts + e), extra, 0.0), axis=1, keepdims=True)
        gv = dot(n2, w[:, :ff]) + gl
        uv = dot(n2, w[:, ff : 2 * ff]) + ul
        back = dot(cot, w[:, 2 * ff :]) + al
        sig = 1.0 / (1.0 + jnp.exp(-gv))
        silu = gv * sig
        act = silu * uv
        col = jnp.sum(act * back, axis=1, keepdims=True)
        high = col.astype(BF).astype(F32)
        at = e + ids_ref[count]
        dgate = dgate + jnp.where(back_lane == at, high, 0.0) + jnp.where(back_lane == at + experts, col - high, 0.0)
        back = back * gate
        act = act * gate
        du = back * silu
        dg = back * uv * (sig + silu * (1.0 - sig))
        act_sum = act if k == 0 else act_sum + act
        dg_sum = dg if k == 0 else dg_sum + dg
        du_sum = du if k == 0 else du_sum + du
        moe = dot_t(act.astype(BF), w[:, 2 * ff :])
        dn2 = dot_t(jnp.concatenate([dg.astype(BF), du.astype(BF)], axis=1), w[:, : 2 * ff])
        if k == 0:
            moe_acc[...] = moe
            dn2_acc[...] = dn2
        else:
            moe_acc[...] += moe
            dn2_acc[...] += dn2
    act_sum, dg_sum, du_sum = act_sum.astype(BF), dg_sum.astype(BF), du_sum.astype(BF)
    low = (dot(act_sum, da_ref[...]) * mask).astype(BF)
    gdu = (dot_t(dg_sum, gb_ref[...]) * mask).astype(BF)
    udu = (dot_t(du_sum, ub_ref[...]) * mask).astype(BF)
    moe = moe_acc[...] + dot(low, db_ref[...])
    dn2 = dn2_acc[...] + dot_t(gdu, ga_ref[...]) + dot_t(udu, ua_ref[...])
    if early:
        moe = moe + early[1][...].astype(F32)
        dn2 = dn2 + early[0][:, :width].astype(F32)
        dgate = dgate + early[0][:, width:].astype(F32)
    m_ref[...] = moe.astype(BF)
    r_ref[:, :width] = dn2.astype(BF)
    r_ref[:, width:] = dgate.astype(BF)
    bd_ref, ad_ref, bg_ref, bu_ref, a_ref = sums
    bd_ref[...] += t_dot_k(low, cot)
    ad_ref[...] += t_dot_k(act_sum, down_back)
    bg_ref[...] += t_dot_k(zg, dg_sum)
    bu_ref[...] += t_dot_k(zu, du_sum)
    a_ref[...] += t_dot_k(n2, jnp.concatenate([gdu, udu], axis=1))


def experts_on(ids, experts, spare, t, cot, weights, w_two, first, low_two, down_b, down_at, prior, early=()):
    rows, width = cot.shape
    ff = down_at.shape[0]
    step = 256
    sd = jax.ShapeDtypeStruct
    whole = lambda a: pl.BlockSpec(a.shape, lambda i: (0, 0))
    by_row = lambda cols: pl.BlockSpec((step, cols), lambda i: (i, 0))
    column = lambda height, cols, at: pl.BlockSpec((height, cols), lambda i: (0, at))
    low_rows = low_two.shape[0]
    count = len(weights)
    flops = 2 * rows * width * ff * 7 * count
    outs = pl.pallas_call(
        functools.partial(expert_kernel, experts, count),
        grid=(rows // step,),
        in_specs=[pl.BlockSpec(memory_space=pltpu.SMEM), by_row(t.shape[1]), by_row(width)]
        + [pl.BlockSpec(w.shape, lambda i: (0, 0), pipeline_mode=pl.Buffered(1)) for w in weights]
        + [column(width, LANES, first), column(width, LANES, first + 1), column(low_rows, ff, 0), column(low_rows, ff, 1), whole(down_b), whole(down_at)]
        + [whole(p) for p in prior] + [by_row(e.shape[1]) for e in early],
        out_specs=[by_row(width + spare), by_row(width)] + [whole(p) for p in prior],
        out_shape=[sd((rows, width + spare), BF), sd((rows, width), BF)] + [sd(p.shape, F32) for p in prior],
        scratch_shapes=[pltpu.VMEM((step, width), F32), pltpu.VMEM((step, width), F32)],
        input_output_aliases={3 + count + 6 + i: 2 + i for i in range(len(prior))},
        compiler_params=pltpu.CompilerParams(vmem_limit_bytes=58 << 20),
        cost_estimate=pl.CostEstimate(flops=flops, bytes_accessed=24 << 20, transcendentals=rows * ff * count),
    )(ids, t, cot, *weights, w_two, w_two, low_two, low_two, down_b, down_at, *prior, *early)
    return outs[0], outs[1], outs[2:]


class Crossing:
    def __init__(self):
        self.n_ctx, self.n_tp = lax.axis_size("ctx"), lax.axis_size("tp")
        self.tp_at = lax.axis_index("tp")

    def pairs(self, by):
        return [(c, (c + by) % self.n_ctx) for c in range(self.n_ctx)]

    def half(self, block):
        if self.n_tp != 2:
            return block
        size = block.shape[0] // 2
        return lax.dynamic_slice_in_dim(block, self.tp_at * size, size, 0)

    def other_half(self, block):
        size = block.shape[0] // 2
        return lax.dynamic_slice_in_dim(block, (1 - self.tp_at) * size, size, 0)

    def joined(self, half):
        if self.n_tp != 2:
            return half
        other = lax.ppermute(half, "tp", [(0, 1), (1, 0)])
        size = half.shape[0]
        whole = lax.dynamic_update_slice_in_dim(jnp.zeros((2 * size,) + half.shape[1:], half.dtype), half, self.tp_at * size, 0)
        return lax.dynamic_update_slice_in_dim(whole, other, (1 - self.tp_at) * size, 0)

    def fetch(self, block):
        half = self.half(block)
        return [lax.ppermute(half, "ctx", self.pairs(by)) for by in range(1, self.n_ctx)]

    def summed_half(self, block):
        if self.n_tp != 2:
            return block.astype(F32)
        return self.half(block).astype(F32) + lax.ppermute(self.other_half(block), "tp", [(0, 1), (1, 0)]).astype(F32)

    def give(self, block, by):
        return lax.ppermute(self.summed_half(block).astype(BF), "ctx", self.pairs(-by))

    def total(self, own, parts):
        found = self.summed_half(own)
        for part in parts:
            found = found + part.astype(F32)
        if self.n_tp != 2:
            return lax.psum(found, "tp")
        return self.joined(found.astype(BF)).astype(F32)


def tp_sum(value):
    if lax.axis_size("tp") != 2:
        return lax.psum(value, "tp")
    return value + lax.ppermute(value, "tp", [(0, 1), (1, 0)])


def on_device(
    tokens, out_cotangent, lengths, adapter_of_doc, routes, attn_gain, ffn_gain,
    w_query, key_matrix, value_matrix, w_out, w_router, w_gate, w_up, w_down,
    a_query, b_query, a_key, key_second_factor, a_value, value_second_factor,
    a_out, b_out, a_router, b_router, a_gate, b_gate, a_up, b_up, a_down, b_down,
):
    rows, width = tokens.shape
    n = lax.axis_size("fsdp")
    n_tp = lax.axis_size("tp")
    tp_at = lax.axis_index("tp")
    ctx_at = lax.axis_index("ctx")
    group = rows * lax.axis_size("ctx")
    q_width = w_query.shape[1]
    kv_width = key_matrix.shape[1]
    ff_width = w_gate.shape[2]
    local_experts = w_gate.shape[0]
    experts = w_router.shape[1]
    ranks = a_query.shape[1]
    share = w_query.shape[0]
    low_rows = b_query.shape[0]

    pad = ((0, 0), (0, LANES - experts))
    one, low_one = gather_packs(
        [
            [(a, a.shape[1]) for a in (w_query, key_matrix, value_matrix, a_query, a_key, a_value)],
            [(b_query, q_width), (key_second_factor, kv_width), (value_second_factor, kv_width)],
        ],
        0,
    )
    qkv = q_width + 2 * kv_width
    w_one = one.reshape(n * share, -1)
    low_one = low_one.reshape(n * low_rows, -1)
    query_b, key_b, value_b = low_one[:, :q_width], low_one[:, q_width : q_width + kv_width], low_one[:, q_width + kv_width :]

    ends = jnp.cumsum(lengths[0])
    starts = ends - lengths[0]
    place = jnp.arange(group, dtype=jnp.int32)
    doc = jnp.sum((place[:, None] >= ends[None, :]).astype(jnp.int32), axis=1)
    picked = (doc[:, None] == jnp.arange(lengths.shape[1], dtype=jnp.int32)[None, :]).astype(jnp.int32)
    begin = jnp.sum(picked * starts[None, :], axis=1)
    chosen = jnp.sum(picked * adapter_of_doc[0][None, :], axis=1)
    start = ctx_at * rows
    query_index = start + jnp.arange(rows, dtype=jnp.int32)
    begin_local = lax.dynamic_slice_in_dim(begin, start, rows)
    chosen_local = lax.dynamic_slice_in_dim(chosen, start, rows)
    mask = (chosen_local[:, None] == (jnp.arange(ranks, dtype=jnp.int32) // ADAPTER_RANK)[None, :]).astype(F32)
    half = HEAD_SIZE // 2
    freq = 10000.0 ** (-jnp.arange(half, dtype=F32) / half)
    angles = (query_index - begin_local).astype(F32)[:, None] * freq[None, :]
    cosine_table = jnp.cos(angles)[:, None, :]
    sine_table = jnp.sin(angles)[:, None, :]

    xfull = tokens.astype(F32)
    normed = rms_norm(xfull, attn_gain).astype(BF)
    raw = dot(normed, w_one)
    query_u = (raw[:, qkv : qkv + ranks] * mask).astype(BF)
    key_u = (raw[:, qkv + ranks : qkv + 2 * ranks] * mask).astype(BF)
    value_u = (raw[:, qkv + 2 * ranks : qkv + 3 * ranks] * mask).astype(BF)
    query_pre = raw[:, :q_width] + dot(query_u, query_b)
    key_pre = raw[:, q_width : q_width + kv_width] + dot(key_u, key_b)
    value_state = (raw[:, q_width + kv_width : qkv] + dot(value_u, value_b)).astype(BF)
    query_state = (
        rotary_apply(query_pre.reshape(rows, -1, HEAD_SIZE), cosine_table, sine_table).reshape(rows, q_width).astype(BF)
    )
    key = rotary_apply(key_pre.reshape(rows, -1, HEAD_SIZE), cosine_table, sine_table).reshape(rows, kv_width).astype(BF)
    kv = jnp.concatenate([key, value_state], axis=1)
    cross = Crossing()
    outer, inner = levels(n)
    me = lax.axis_index("fsdp")
    ring = [(i, (i + inner) % n) for i in range(n)]
    turns = [[(i, i // inner * inner + (i % inner + dj) % inner) for i in range(n)] for dj in range(1, inner)]
    local = local_experts // cross.n_ctx
    mine = [lax.dynamic_slice_in_dim(a, ctx_at * local, local, 0) for a in (w_gate, w_up, w_down)]
    block = jnp.concatenate([mine[0], mine[1], jnp.swapaxes(mine[2], 1, 2)], axis=2)
    brought = {(0, 0): block}

    def bring(do, after):
        last = [brought[(do, 0)]] + [brought[(do - 1, dj)] for dj in range(1, inner) if do]
        last, after = lax.optimization_barrier((last, after))
        brought[(do, 0)] = last[0]
        for dj, value in zip(range(1, inner), last[1:]):
            brought[(do - 1, dj)] = value
        if do + 1 < outer:
            brought[(do + 1, 0)] = lax.ppermute(last[0], "fsdp", ring)
        for dj in range(1, inner):
            brought[(do, dj)] = lax.ppermute(last[0], "fsdp", turns[dj - 1])
        return after

    one = bring(0, one)
    far = lax.ppermute(kv, "ctx", [(i, i + 1) for i in range(lax.axis_size("ctx") - 1)])
    w_out_t, kv = lax.optimization_barrier((w_out.T, kv))
    two, low_two, down_a = gather_packs(
        [
            [(a, a.shape[1]) for a in (w_out_t, a_router, a_gate, a_up, jnp.pad(w_router, pad), a_out)],
            [(b_gate, ff_width), (b_up, ff_width), (b_out, width), (b_down, width), (jnp.pad(b_router, pad), LANES)],
            [(a_down, ranks)],
        ],
        1,
    )
    two = bring(1, two)
    cot = lax.optimization_barrier((out_cotangent, two))[0]
    cot_halves = cross.fetch(cot)
    far, two = lax.optimization_barrier((far, two))
    w_two = two.reshape(n * share, -1)
    low_two = low_two.reshape(n * low_rows, -1)
    out_b = low_two[:, 2 * ff_width : 2 * ff_width + width]
    down_b = low_two[:, 2 * ff_width + width : 2 * ff_width + 2 * width]
    router_b = low_two[:, 2 * ff_width + 2 * width :]
    out_wt = w_two[:, :q_width]
    router_a = w_two[:, q_width : q_width + ranks]
    router_w = w_two[:, q_width + 3 * ranks : q_width + 4 * ranks]
    out_a = lax.dynamic_slice_in_dim(w_two[:, q_width + 4 * ranks : q_width + 5 * ranks], tp_at * q_width, q_width, 0)
    down_at = lax.dynamic_slice_in_dim(down_a.reshape(-1, ranks), tp_at * ff_width, ff_width, 0)
    begin_row = begin_local[None, :]
    start_at = jnp.reshape(start, (1,)).astype(jnp.int32)
    query_state = (query_state.astype(F32) * 0.125).astype(BF)
    mixed_heads, log_total = attend(query_state, kv, far, begin_row, start_at)
    mixed_heads = bring(2, mixed_heads)
    cot_halves, mixed_heads = lax.optimization_barrier((cot_halves, mixed_heads))
    out_u = dot(mixed_heads, out_a) * mask
    attn_part = dot_t(mixed_heads, out_wt) + dot(out_u.astype(BF), out_b)
    hidden = xfull + tp_sum(attn_part)
    normed_two = rms_norm(hidden, ffn_gain).astype(BF)
    lows = dot(normed_two, jnp.concatenate([router_a, router_w], axis=1))
    router_u = (lows[:, :ranks] * mask).astype(BF)
    logits = lows[:, ranks : ranks + experts] + dot(router_u, router_b)[:, :experts]
    selected = jnp.any(routes[:, :, None] == jnp.arange(experts, dtype=jnp.int32)[None, None, :], axis=1)
    gates = jax.nn.softmax(jnp.where(selected, logits, -jnp.inf), axis=-1)

    dout = cot.astype(F32)
    high = gates.astype(BF)
    spare = -(-2 * experts * n_tp // LANES) * LANES
    carried = jnp.concatenate(
        [
            normed_two,
            high,
            (gates - high.astype(F32)).astype(BF),
            chosen_local[:, None].astype(BF),
            jnp.zeros((rows, LANES - 2 * experts - 1), BF),
        ],
        axis=1,
    )
    halves = cross.fetch(carried)
    for do in range(3, outer):
        carried = bring(do, carried)
    early = [(0, 0), (1, 0)] + [(0, dj) for dj in range(1, inner)] + [(2, 0)] + [(1, dj) for dj in range(1, inner)]
    late = [(do, 0) for do in range(3, outer)] + [(do, dj) for do in range(2, outer) for dj in range(1, inner)]

    def weights_of(keys):
        ids = [((me // inner + outer - do) % outer * inner + (me % inner + inner - dj) % inner) * local_experts + ctx_at * local + j for do, dj in keys for j in range(local)]
        return jnp.stack(ids + [tp_at * 2 * experts]).astype(jnp.int32), [brought[k][j] for k in keys for j in range(local)]

    sums = [jnp.zeros(shape, F32) for shape in ((ranks, width), (ff_width, ranks), (ranks, ff_width), (ranks, ff_width), (width, 2 * ranks))]
    at = q_width // LANES + 1
    work = [(carried, cot)] + [(None, None)] * (cross.n_ctx - 1)
    partial = []
    ids, weights = weights_of(early)
    for by in range(cross.n_ctx):
        if by:
            work[by] = (cross.joined(halves[by - 1]), cross.joined(cot_halves[by - 1]))
        r, m, sums = experts_on(ids, experts, spare, *work[by], weights, w_two, at, low_two, down_b, down_at, sums)
        if by == 0:
            halves, cot_halves, r = lax.optimization_barrier((halves, cot_halves, r))
        partial.append((r, m))
    ids, weights = weights_of(late)
    back_parts, moe_parts = [], []
    for by in list(range(1, cross.n_ctx)) + [0]:
        r, m, sums = experts_on(ids, experts, spare, *work[by], weights, w_two, at, low_two, down_b, down_at, sums, partial[by])
        moe_parts.append(m)
        if by:
            half = cross.summed_half(r).astype(BF)
            half, carried = lax.optimization_barrier((half, work[0][0]))
            work[0] = (carried, cot)
            back_parts.append(lax.ppermute(half, "ctx", cross.pairs(-by)))
    r, back_parts = lax.optimization_barrier((r, back_parts))
    back = cross.total(r, back_parts)
    dn2 = back[:, :width]
    dgate = jnp.sum(back[:, width : width + 2 * experts * n_tp].reshape(rows, 2 * n_tp, experts), axis=1)
    grad_bd, grad_ad, grad_bg, grad_bu, grad_agu = sums
    grad_ag, grad_au = grad_agu[:, :ranks], grad_agu[:, ranks:]
    dlogits = (gates * (dgate - jnp.sum(gates * dgate, axis=-1, keepdims=True))).astype(BF)
    dlogits = jnp.pad(dlogits, ((0, 0), (0, LANES - experts)))
    router_du = (dot_t(dlogits, router_b) * mask).astype(BF)
    dn2 = dn2 + dot_t(dlogits, router_w) + dot_t(router_du, router_a)
    grad_br = t_dot(router_u, dlogits)[:, :experts]
    grad_ar = t_dot(normed_two, router_du)
    dhidden = dout + norm_back(hidden, ffn_gain, dn2)
    dattn = dhidden.astype(BF)
    out_du = (dot_t(dattn, out_b) * mask).astype(BF)
    dmixed = (dot(dattn, out_wt) + dot_t(out_du, out_a)).astype(BF)
    grad_bo = t_dot(out_u.astype(BF), dattn)
    grad_ao = t_dot(mixed_heads, out_du)
    dquery, dkey_own, dvalue_own, dkey_far, dvalue_far = attend_back(
        query_state, kv, far, begin_row, start_at, mixed_heads, dmixed, log_total
    )
    moe_parts, dquery = lax.optimization_barrier((moe_parts, dquery))
    moe = cross.total(moe_parts[-1], [cross.give(p, by) for by, p in zip(range(1, cross.n_ctx), moe_parts)])
    output = (hidden + moe).astype(BF)
    far_back = lax.ppermute(
        jnp.concatenate([dkey_far, dvalue_far], axis=1),
        "ctx",
        [(i + 1, i) for i in range(lax.axis_size("ctx") - 1)],
    ).astype(F32)
    dkey = dkey_own + far_back[:, :kv_width]
    dvalue = (dvalue_own + far_back[:, kv_width:]).astype(BF)
    dquery_pre = rotary_apply(dquery.reshape(rows, -1, HEAD_SIZE), cosine_table, -sine_table).reshape(rows, q_width).astype(BF)
    dkey_pre = rotary_apply(dkey.reshape(rows, -1, HEAD_SIZE), cosine_table, -sine_table).reshape(rows, kv_width).astype(BF)
    query_du = (dot_t(dquery_pre, query_b) * mask).astype(BF)
    key_du = (dot_t(dkey_pre, key_b) * mask).astype(BF)
    value_du = (dot_t(dvalue, value_b) * mask).astype(BF)
    everything = jnp.concatenate([dquery_pre, dkey_pre, dvalue, query_du, key_du, value_du], axis=1)
    dn1 = dot_t(everything, w_one)
    grad_a3 = t_dot(normed, everything[:, qkv:])
    grad_bq = t_dot(query_u, dquery_pre)
    grad_bk = t_dot(key_u, dkey_pre)
    grad_bv = t_dot(value_u, dvalue)
    dn1 = tp_sum(dn1)
    grad_tokens = (dhidden + norm_back(xfull, attn_gain, dn1)).astype(BF)

    def place_cols(piece, full_cols):
        blank = jnp.zeros((piece.shape[0], full_cols), F32)
        return lax.dynamic_update_slice_in_dim(blank, piece, tp_at * piece.shape[1], 1)

    def place_rows(piece, full_rows):
        blank = jnp.zeros((full_rows, piece.shape[1]), F32)
        return lax.dynamic_update_slice_in_dim(blank, piece, tp_at * piece.shape[0], 0)

    only_first = (tp_at == 0).astype(F32)
    grads = (
        grad_a3[:, :ranks],
        place_cols(grad_bq, q_width * n_tp),
        grad_a3[:, ranks : 2 * ranks],
        place_cols(grad_bk, kv_width * n_tp),
        grad_a3[:, 2 * ranks :],
        place_cols(grad_bv, kv_width * n_tp),
        place_rows(grad_ao, q_width * n_tp),
        grad_bo,
        grad_ar * only_first,
        grad_br * only_first,
        grad_ag,
        place_cols(grad_bg, ff_width * n_tp),
        grad_au,
        place_cols(grad_bu, ff_width * n_tp),
        place_rows(grad_ad, ff_width * n_tp),
        grad_bd,
    )
    def reduce_grads(some):
        flat = []
        for g in some:
            height, cols = g.shape[0] // n, g.shape[1]
            count = -(-cols // LANES)
            g = jnp.pad(g.astype(BF), ((0, 0), (0, count * LANES - cols)))
            flat.append(g.reshape(n, height, count, LANES).transpose(0, 2, 1, 3).reshape(n, count * height, LANES))
        flat = jnp.concatenate(flat, axis=1)
        mine = lax.psum_scatter(flat, "fsdp", scatter_dimension=0, tiled=False)
        mine = lax.psum(mine, ("ctx", "tp")).astype(F32)
        found = []
        at = 0
        for g in some:
            height, cols = g.shape[0] // n, g.shape[1]
            count = -(-cols // LANES)
            piece = mine[at : at + count * height].reshape(count, height, LANES).transpose(1, 0, 2).reshape(height, count * LANES)
            found.append(piece[:, :cols])
            at += count * height
        return found

    final = reduce_grads(grads[:6]) + reduce_grads(grads[6:])
    return (output, grad_tokens, *final)


def solution(mesh):
    both = P(("fsdp", "ctx"), None)
    split = P("fsdp", None)
    placed = (
        both, both, split, split, both, P(), P(),
        P("fsdp", "tp"), P("fsdp", "tp"), P("fsdp", "tp"), P("tp", "fsdp"), split,
        P("fsdp", None, "tp"), P("fsdp", None, "tp"), P("fsdp", "tp", None),
    ) + (split,) * 16
    return jax.shard_map(
        on_device, mesh=mesh, in_specs=placed, out_specs=(both, both) + (split,) * 16, check_vma=False
    )
```

```python
import functools

import jax
import jax.numpy as jnp
from jax import lax
from jax.experimental import pallas as pl
from jax.experimental.pallas import tpu as pltpu
from jax.sharding import PartitionSpec as P

HEAD_SIZE = 64
ADAPTER_RANK = 16
LANES = 128
norm_eps = 1e-05
BF = jnp.bfloat16
F32 = jnp.float32


MESH = pl.DeviceIdType.MESH


def dot(left, right, dims=((1,), (0,)), precision=None):
    return lax.dot_general(left, right, (dims, ((), ())), preferred_element_type=F32, precision=precision)


def dot_t(left, right):
    return dot(left, right, ((1,), (1,)))


def t_dot(left, right):
    return dot(left, right, ((0,), (0,)))


def rms_norm(values, gain):
    return values * lax.rsqrt(jnp.mean(values * values, axis=-1, keepdims=True) + norm_eps) * gain


def norm_back(values, gain, grad):
    unused, pull = jax.vjp(lambda inner: rms_norm(inner, gain), values)
    return pull(grad)[0]


def rotary_apply(values, cosine_table, sine_table):
    half = values.shape[-1] // 2
    first = values[..., :half]
    second = values[..., half:]
    return jnp.concatenate(
        [first * cosine_table - second * sine_table, first * sine_table + second * cosine_table],
        axis=-1,
    )


def levels(n):
    outer = 4 if n % 4 == 0 else n
    return outer, n // outer


def fill_bias(bias, start_ref, begin_ref, rows):
    step = rows // 3
    for at in range(0, 2 * rows, step):
        key = start_ref[0] - rows + at + lax.broadcasted_iota(jnp.int32, (step, rows), 0)
        query = start_ref[0] + lax.broadcasted_iota(jnp.int32, (step, rows), 1)
        ok = (key <= query) & (key >= begin_ref[...]) & (key >= 0)
        bias[pl.ds(at, step), :] = jnp.where(ok, 0.0, -1e30)


def split_heads(ref, out, count, rows, at=0):
    for h in range(count):
        out[h, pl.ds(at, rows), :] = ref[:, h * HEAD_SIZE : (h + 1) * HEAD_SIZE]


def attend_kernel(group, q_blocks, start_ref, begin_ref, q_ref, ko_ref, vo_ref, kf_ref, vf_ref, o_ref, lse_ref, bias, ks, vts, qs, ots):
    rows = q_ref.shape[0]
    width = rows // q_blocks
    heads = 2 * group
    @pl.when(pl.program_id(0) == 0)
    def _():
        fill_bias(bias, start_ref, begin_ref, rows)
    split_heads(kf_ref, ks, 2, rows, 0)
    split_heads(ko_ref, ks, 2, rows, rows)
    split_heads(q_ref, qs, heads, rows, 0)
    vts[:, pl.ds(0, rows)] = vf_ref[...].astype(F32).T.astype(BF)
    vts[:, pl.ds(rows, rows)] = vo_ref[...].astype(F32).T.astype(BF)
    for b in range(q_blocks):
        keys = rows + (b + 1) * width
        def one(h, _):
            g = h // group
            s = dot_t(ks[g, pl.ds(0, keys), :], qs[h, pl.ds(b * width, width), :]) + bias[pl.ds(0, keys), pl.ds(b * width, width)]
            top = jnp.max(s, axis=0, keepdims=True)
            p = jnp.exp(s - top)
            total = jnp.sum(p, axis=0, keepdims=True)
            lse_ref[0, pl.ds(h, 1), pl.ds(b * width, width)] = top + jnp.log(total)
            vt = vts[pl.ds(pl.multiple_of(g * HEAD_SIZE, HEAD_SIZE), HEAD_SIZE), pl.ds(0, keys)]
            o = dot(vt, p.astype(BF)) / total
            ots[pl.ds(pl.multiple_of(h * HEAD_SIZE, HEAD_SIZE), HEAD_SIZE), pl.ds(b * width, width)] = o
            return 0
        lax.fori_loop(0, heads, one, 0)
    for j in range(group):
        o_ref[:, j * LANES : (j + 1) * LANES] = ots[pl.ds(j * LANES, LANES), :].T.astype(BF)


def attend(q, kv, far, begin, start, q_blocks=3):
    rows, q_width = q.shape
    kv_width = kv.shape[1] // 2
    pairs = kv_width // LANES
    group = q_width // kv_width
    spec = lambda off: pl.BlockSpec((rows, LANES), lambda i: (0, i + off))
    return pl.pallas_call(
        functools.partial(attend_kernel, group, q_blocks),
        grid=(pairs,),
        in_specs=[pl.BlockSpec(memory_space=pltpu.SMEM), pl.BlockSpec((1, rows), lambda i: (0, 0)),
                  pl.BlockSpec((rows, group * LANES), lambda i: (0, i)), spec(0), spec(pairs), spec(0), spec(pairs)],
        out_specs=[pl.BlockSpec((rows, group * LANES), lambda i: (0, i)), pl.BlockSpec((1, 8, rows), lambda i: (i, 0, 0))],
        out_shape=[jax.ShapeDtypeStruct((rows, q_width), BF), jax.ShapeDtypeStruct((pairs, 8, rows), F32)],
        scratch_shapes=[pltpu.VMEM((2 * rows, rows), F32), pltpu.VMEM((2, 2 * rows, HEAD_SIZE), BF), pltpu.VMEM((LANES, 2 * rows), BF),
                        pltpu.VMEM((2 * group, rows, HEAD_SIZE), BF), pltpu.VMEM((2 * group * HEAD_SIZE, rows), F32)],
        compiler_params=pltpu.CompilerParams(vmem_limit_bytes=50 << 20),
        cost_estimate=pl.CostEstimate(flops=8 * rows * rows * q_width, bytes_accessed=8 << 20, transcendentals=2 * rows * rows * 12),
    )(start, begin, q, kv, kv, far, far)


def attend_back_kernel(group, q_blocks, start_ref, begin_ref, q_ref, ko_ref, vo_ref, kf_ref, vf_ref, o_ref, do_ref, lse_ref,
                       dq_ref, dko_ref, dvo_ref, dkf_ref, dvf_ref, bias, ks, vs, kts, qs, dos, dqts, dks, dvs, deltas):
    rows = q_ref.shape[0]
    width = rows // q_blocks
    heads = 2 * group
    @pl.when(pl.program_id(0) == 0)
    def _():
        fill_bias(bias, start_ref, begin_ref, rows)
    split_heads(kf_ref, ks, 2, rows, 0)
    split_heads(ko_ref, ks, 2, rows, rows)
    split_heads(vf_ref, vs, 2, rows, 0)
    split_heads(vo_ref, vs, 2, rows, rows)
    split_heads(q_ref, qs, heads, rows, 0)
    split_heads(do_ref, dos, heads, rows, 0)
    kts[:, pl.ds(0, rows)] = kf_ref[...].astype(F32).T.astype(BF)
    kts[:, pl.ds(rows, rows)] = ko_ref[...].astype(F32).T.astype(BF)
    cols = heads * HEAD_SIZE
    pick = (lax.broadcasted_iota(jnp.int32, (8, cols), 1) // HEAD_SIZE == lax.broadcasted_iota(jnp.int32, (8, cols), 0)).astype(F32)
    prod = o_ref[...].astype(F32) * do_ref[...].astype(F32)
    deltas[...] = dot(pick, prod, ((1,), (1,)), lax.Precision.HIGHEST)
    dks[...] = jnp.zeros_like(dks)
    dvs[...] = jnp.zeros_like(dvs)
    for b in range(q_blocks):
        keys = rows + (b + 1) * width
        def one(h, _):
            g = h // group
            at = pl.ds(b * width, width)
            qb = qs[h, at, :]
            dob = dos[h, at, :]
            s = dot_t(ks[g, pl.ds(0, keys), :], qb) + bias[pl.ds(0, keys), at]
            p = jnp.exp(s - lse_ref[0, pl.ds(h, 1), at])
            dp = dot_t(vs[g, pl.ds(0, keys), :], dob)
            ds = (p * (dp - deltas[pl.ds(h, 1), at])).astype(BF)
            dvs[g, pl.ds(0, keys), :] += dot(p.astype(BF), dob)
            dks[g, pl.ds(0, keys), :] += dot(ds, qb)
            kt = kts[pl.ds(pl.multiple_of(g * HEAD_SIZE, HEAD_SIZE), HEAD_SIZE), pl.ds(0, keys)]
            dqts[pl.ds(pl.multiple_of(h * HEAD_SIZE, HEAD_SIZE), HEAD_SIZE), at] = dot(kt, ds) * 0.125
            return 0
        lax.fori_loop(0, heads, one, 0)
    for j in range(group):
        dq_ref[:, j * LANES : (j + 1) * LANES] = dqts[pl.ds(j * LANES, LANES), :].T
    for g in range(2):
        at = slice(g * HEAD_SIZE, (g + 1) * HEAD_SIZE)
        dkf_ref[:, at] = dks[g, pl.ds(0, rows), :].astype(BF)
        dko_ref[:, at] = dks[g, pl.ds(rows, rows), :]
        dvf_ref[:, at] = dvs[g, pl.ds(0, rows), :].astype(BF)
        dvo_ref[:, at] = dvs[g, pl.ds(rows, rows), :]


def attend_back(q, kv, far, begin, start, o, do, lse, q_blocks=3):
    rows, q_width = q.shape
    kv_width = kv.shape[1] // 2
    pairs = kv_width // LANES
    group = q_width // kv_width
    spec = lambda off: pl.BlockSpec((rows, LANES), lambda i: (0, i + off))
    wide = pl.BlockSpec((rows, group * LANES), lambda i: (0, i))
    sd = jax.ShapeDtypeStruct
    return pl.pallas_call(
        functools.partial(attend_back_kernel, group, q_blocks),
        grid=(pairs,),
        in_specs=[pl.BlockSpec(memory_space=pltpu.SMEM), pl.BlockSpec((1, rows), lambda i: (0, 0)),
                  wide, spec(0), spec(pairs), spec(0), spec(pairs), wide, wide, pl.BlockSpec((1, 8, rows), lambda i: (i, 0, 0))],
        out_specs=[wide, spec(0), spec(0), spec(0), spec(0)],
        out_shape=[sd((rows, q_width), F32), sd((rows, kv_width), F32), sd((rows, kv_width), F32), sd((rows, kv_width), BF), sd((rows, kv_width), BF)],
        scratch_shapes=[pltpu.VMEM((2 * rows, rows), F32), pltpu.VMEM((2, 2 * rows, HEAD_SIZE), BF), pltpu.VMEM((2, 2 * rows, HEAD_SIZE), BF), pltpu.VMEM((LANES, 2 * rows), BF),
                        pltpu.VMEM((2 * group, rows, HEAD_SIZE), BF), pltpu.VMEM((2 * group, rows, HEAD_SIZE), BF), pltpu.VMEM((2 * group * HEAD_SIZE, rows), F32),
                        pltpu.VMEM((2, 2 * rows, HEAD_SIZE), F32), pltpu.VMEM((2, 2 * rows, HEAD_SIZE), F32), pltpu.VMEM((8, rows), F32)],
        compiler_params=pltpu.CompilerParams(vmem_limit_bytes=56 << 20),
        cost_estimate=pl.CostEstimate(flops=20 * rows * rows * q_width, bytes_accessed=16 << 20, transcendentals=2 * rows * rows * 12),
    )(start, begin, q, kv, kv, far, far, o, do, lse)


def slab_of(rows, ctx):
    edge = 3 * rows // 8 // 16 * 16
    take = rows - edge
    return pl.ds(pl.multiple_of(ctx * edge, 16), take), pl.ds(pl.multiple_of(ctx * take, 16), edge)


def gather_kernel(n, count, *refs):
    ins, outs = refs[:count], refs[count : 2 * count]
    own_sem, z_send, z_recv, y_send, y_recv, x_send, x_recv = refs[2 * count :]
    outer, inner = levels(n)
    me = lax.axis_index("fsdp")
    ctx = lax.axis_index("ctx")
    z, y = me // inner, me % inner
    right = (z + 1) % outer * inner + y
    left = (z + outer - 1) % outer * inner + y

    def shard(do, dj):
        return (z + outer - do) % outer * inner + (y + inner - dj) % inner

    own = [pltpu.make_async_copy(ins[a], outs[a].at[me], own_sem.at[a]) for a in range(count)]
    barrier = pltpu.get_barrier_semaphore()
    peers = [right, left] + [z * inner + (y + dj) % inner for dj in range(1, inner)]
    for peer in peers:
        pl.semaphore_signal(barrier, inc=1, device_id={"fsdp": peer}, device_id_type=MESH)
    pl.semaphore_signal(barrier, inc=1, device_id={"ctx": 1 - ctx}, device_id_type=MESH)
    pl.semaphore_wait(barrier, len(peers) + 1)

    def cut(a):
        return 3 * outs[a].shape[1] // 8 >= 16

    def taken(a, k):
        if not cut(a):
            return outs[a].at[k]
        return outs[a].at[k, slab_of(outs[a].shape[1], ctx)[0]]

    def remote(part, send, recv, to, src=None):
        src = part if src is None else src
        return pltpu.make_async_remote_copy(src_ref=src, dst_ref=part, send_sem=send, recv_sem=recv, device_id=to, device_id_type=MESH)

    def from_own(a):
        return ins[a].at[slab_of(ins[a].shape[0], ctx)[0]] if cut(a) else ins[a]

    def z_copy(a, k):
        src = from_own(a) if k == 1 else None
        return remote(taken(a, shard(k - 1, 0)), z_send.at[a, k - 1], z_recv.at[a, k - 1], {"fsdp": right}, src)

    def y_copy(a, do, dj):
        to = {"fsdp": z * inner + (y + dj) % inner}
        src = from_own(a) if do == 0 else None
        return remote(taken(a, shard(do, 0)), y_send.at[a, do, dj - 1], y_recv.at[a, do, dj - 1], to, src)

    def x_copy(a, do, dj):
        part = outs[a].at[shard(do, dj), slab_of(outs[a].shape[1], ctx)[1]]
        return remote(part, x_send.at[a, do, dj], x_recv.at[a, do, dj], {"ctx": 1 - ctx})

    started = []

    def go(copy):
        copy.start()
        started.append(copy)

    for a in range(count):
        go(z_copy(a, 1))
        for dj in range(1, inner):
            go(y_copy(a, 0, dj))
    for c in own:
        c.start()
    for do in range(1, outer + 1):
        for a in range(count):
            if do < outer:
                z_copy(a, do).wait_recv()
                if do + 1 < outer:
                    go(z_copy(a, do + 1))
                for dj in range(1, inner):
                    go(y_copy(a, do, dj))
                if cut(a):
                    go(x_copy(a, do, 0))
        for a in range(count):
            for dj in range(1, inner):
                y_copy(a, do - 1, dj).wait_recv()
                if cut(a):
                    go(x_copy(a, do - 1, dj))
    for a in range(count):
        if cut(a):
            for do in range(outer):
                for dj in range(inner):
                    if do or dj:
                        x_copy(a, do, dj).wait_recv()
    for c in started:
        c.wait_send()
    for c in own:
        c.wait()


def gather_packs(packs, collective_id):
    n = lax.axis_size("fsdp")
    outer, inner = levels(n)
    count = len(packs)
    tp_at = lax.axis_index("tp")
    arrays = []
    for parts in packs:
        cut = [a if cols == a.shape[1] else lax.dynamic_slice_in_dim(a, tp_at * cols, cols, 1) for a, cols in parts]
        arrays.append(jnp.concatenate(cut, axis=1) if len(cut) > 1 else cut[0])
    dma = pltpu.SemaphoreType.DMA
    anywhere = pl.BlockSpec(memory_space=pl.ANY)
    side = max(inner - 1, 1)
    return pl.pallas_call(
        functools.partial(gather_kernel, n, count),
        in_specs=[anywhere] * count,
        out_specs=[anywhere] * count,
        out_shape=[jax.ShapeDtypeStruct((n,) + a.shape, a.dtype) for a in arrays],
        scratch_shapes=[
            dma((count,)), dma((count, outer - 1)), dma((count, outer - 1)),
            dma((count, outer, side)), dma((count, outer, side)), dma((count, outer, inner)), dma((count, outer, inner)),
        ],
        compiler_params=pltpu.CompilerParams(collective_id=collective_id, has_side_effects=True),
    )(*arrays)


def t_dot_k(left, right):
    return dot(left, right, ((0,), (0,)))


def expert_kernel(experts, count, ids_ref, t_ref, c_ref, *refs):
    w_refs = refs[:count]
    ga_ref, ua_ref, gb_ref, ub_ref, db_ref, da_ref = refs[count : count + 6]
    prior = refs[count + 6 : count + 11]
    early = refs[count + 11 : -9]
    r_ref, m_ref = refs[-9:-7]
    sums = refs[-7:-2]
    moe_acc, dn2_acc = refs[-2:]
    rows, width = c_ref.shape
    ff = gb_ref.shape[1]
    spare = r_ref.shape[1] - width
    lanes = t_ref.shape[1] - width

    @pl.when(pl.program_id(0) == 0)
    def _():
        for old, new in zip(prior, sums):
            new[...] = old[...]

    n2 = t_ref[:, :width]
    cot = c_ref[...]
    extra = t_ref[:, width:].astype(F32)
    lane = lax.broadcasted_iota(jnp.int32, (rows, lanes), 1)
    chosen = jnp.sum(jnp.where(lane == 2 * experts, extra, 0.0), axis=1, keepdims=True)
    low_lane = lax.broadcasted_iota(jnp.int32, (rows, LANES), 1)
    mask = ((low_lane // ADAPTER_RANK).astype(F32) == chosen).astype(F32)
    zg = (dot(n2, ga_ref[...]) * mask).astype(BF)
    zu = (dot(n2, ua_ref[...]) * mask).astype(BF)
    gl = dot(zg, gb_ref[...])
    ul = dot(zu, ub_ref[...])
    down_back = (dot_t(cot, db_ref[...]) * mask).astype(BF)
    al = dot_t(down_back, da_ref[...])
    back_lane = lax.broadcasted_iota(jnp.int32, (rows, spare), 1)
    dgate = jnp.zeros((rows, spare), F32)
    act_sum = dg_sum = du_sum = None
    for k in range(count):
        e = ids_ref[k]
        w = w_refs[k]
        gate = jnp.sum(jnp.where((lane == e) | (lane == experts + e), extra, 0.0), axis=1, keepdims=True)
        gv = dot(n2, w[:, :ff]) + gl
        uv = dot(n2, w[:, ff : 2 * ff]) + ul
        back = dot(cot, w[:, 2 * ff :]) + al
        sig = 1.0 / (1.0 + jnp.exp(-gv))
        silu = gv * sig
        act = silu * uv
        col = jnp.sum(act * back, axis=1, keepdims=True)
        high = col.astype(BF).astype(F32)
        at = e + ids_ref[count]
        dgate = dgate + jnp.where(back_lane == at, high, 0.0) + jnp.where(back_lane == at + experts, col - high, 0.0)
        back = back * gate
        act = act * gate
        du = back * silu
        dg = back * uv * (sig + silu * (1.0 - sig))
        act_sum = act if k == 0 else act_sum + act
        dg_sum = dg if k == 0 else dg_sum + dg
        du_sum = du if k == 0 else du_sum + du
        moe = dot_t(act.astype(BF), w[:, 2 * ff :])
        dn2 = dot_t(jnp.concatenate([dg.astype(BF), du.astype(BF)], axis=1), w[:, : 2 * ff])
        if k == 0:
            moe_acc[...] = moe
            dn2_acc[...] = dn2
        else:
            moe_acc[...] += moe
            dn2_acc[...] += dn2
    act_sum, dg_sum, du_sum = act_sum.astype(BF), dg_sum.astype(BF), du_sum.astype(BF)
    low = (dot(act_sum, da_ref[...]) * mask).astype(BF)
    gdu = (dot_t(dg_sum, gb_ref[...]) * mask).astype(BF)
    udu = (dot_t(du_sum, ub_ref[...]) * mask).astype(BF)
    moe = moe_acc[...] + dot(low, db_ref[...])
    dn2 = dn2_acc[...] + dot_t(gdu, ga_ref[...]) + dot_t(udu, ua_ref[...])
    if early:
        moe = moe + early[1][...].astype(F32)
        dn2 = dn2 + early[0][:, :width].astype(F32)
        dgate = dgate + early[0][:, width:].astype(F32)
    m_ref[...] = moe.astype(BF)
    r_ref[:, :width] = dn2.astype(BF)
    r_ref[:, width:] = dgate.astype(BF)
    bd_ref, ad_ref, bg_ref, bu_ref, a_ref = sums
    bd_ref[...] += t_dot_k(low, cot)
    ad_ref[...] += t_dot_k(act_sum, down_back)
    bg_ref[...] += t_dot_k(zg, dg_sum)
    bu_ref[...] += t_dot_k(zu, du_sum)
    a_ref[...] += t_dot_k(n2, jnp.concatenate([gdu, udu], axis=1))


def experts_on(ids, experts, spare, t, cot, weights, w_two, first, low_two, down_b, down_at, prior, early=()):
    rows, width = cot.shape
    ff = down_at.shape[0]
    step = 256
    sd = jax.ShapeDtypeStruct
    whole = lambda a: pl.BlockSpec(a.shape, lambda i: (0, 0))
    by_row = lambda cols: pl.BlockSpec((step, cols), lambda i: (i, 0))
    column = lambda height, cols, at: pl.BlockSpec((height, cols), lambda i: (0, at))
    low_rows = low_two.shape[0]
    count = len(weights)
    flops = 2 * rows * width * ff * 7 * count
    outs = pl.pallas_call(
        functools.partial(expert_kernel, experts, count),
        grid=(rows // step,),
        in_specs=[pl.BlockSpec(memory_space=pltpu.SMEM), by_row(t.shape[1]), by_row(width)]
        + [pl.BlockSpec(w.shape, lambda i: (0, 0), pipeline_mode=pl.Buffered(1)) for w in weights]
        + [column(width, LANES, first), column(width, LANES, first + 1), column(low_rows, ff, 0), column(low_rows, ff, 1), whole(down_b), whole(down_at)]
        + [whole(p) for p in prior] + [by_row(e.shape[1]) for e in early],
        out_specs=[by_row(width + spare), by_row(width)] + [whole(p) for p in prior],
        out_shape=[sd((rows, width + spare), BF), sd((rows, width), BF)] + [sd(p.shape, F32) for p in prior],
        scratch_shapes=[pltpu.VMEM((step, width), F32), pltpu.VMEM((step, width), F32)],
        input_output_aliases={3 + count + 6 + i: 2 + i for i in range(len(prior))},
        compiler_params=pltpu.CompilerParams(vmem_limit_bytes=58 << 20),
        cost_estimate=pl.CostEstimate(flops=flops, bytes_accessed=24 << 20, transcendentals=rows * ff * count),
    )(ids, t, cot, *weights, w_two, w_two, low_two, low_two, down_b, down_at, *prior, *early)
    return outs[0], outs[1], outs[2:]


class Crossing:
    def __init__(self):
        self.n_ctx, self.n_tp = lax.axis_size("ctx"), lax.axis_size("tp")
        self.tp_at = lax.axis_index("tp")

    def pairs(self, by):
        return [(c, (c + by) % self.n_ctx) for c in range(self.n_ctx)]

    def half(self, block):
        if self.n_tp != 2:
            return block
        size = block.shape[0] // 2
        return lax.dynamic_slice_in_dim(block, self.tp_at * size, size, 0)

    def other_half(self, block):
        size = block.shape[0] // 2
        return lax.dynamic_slice_in_dim(block, (1 - self.tp_at) * size, size, 0)

    def joined(self, half):
        if self.n_tp != 2:
            return half
        other = lax.ppermute(half, "tp", [(0, 1), (1, 0)])
        size = half.shape[0]
        whole = lax.dynamic_update_slice_in_dim(jnp.zeros((2 * size,) + half.shape[1:], half.dtype), half, self.tp_at * size, 0)
        return lax.dynamic_update_slice_in_dim(whole, other, (1 - self.tp_at) * size, 0)

    def fetch(self, block):
        half = self.half(block)
        return [lax.ppermute(half, "ctx", self.pairs(by)) for by in range(1, self.n_ctx)]

    def summed_half(self, block):
        if self.n_tp != 2:
            return block.astype(F32)
        return self.half(block).astype(F32) + lax.ppermute(self.other_half(block), "tp", [(0, 1), (1, 0)]).astype(F32)

    def swapped(self, blocks):
        if self.n_tp != 2:
            return [jnp.zeros_like(b) for b in blocks]
        return [lax.ppermute(self.other_half(b), "tp", [(0, 1), (1, 0)]) for b in blocks]

    def halves_of_total(self, own, parts):
        found = self.summed_half(own)
        for part in parts:
            found = found + part.astype(F32)
        if self.n_tp != 2:
            found = lax.psum(found, "tp").astype(BF)
            size = found.shape[0] // 2
            return found[:size], found[size:], 0
        found = found.astype(BF)
        return found, lax.ppermute(found, "tp", [(0, 1), (1, 0)]), self.tp_at


def put_rows(pack, value, at, height):
    for f in range(pack.shape[0]):
        pack[f, pl.ds(at, height), :] = value[f * height : (f + 1) * height, :]


def put_cols(pack, value, at, height, first):
    for i in range(value.shape[1] // LANES):
        for f in range(pack.shape[0]):
            spot = pl.ds(pl.multiple_of(at + (first + i) * height, 8), height)
            pack[f, spot, :] = value[f * height : (f + 1) * height, i * LANES : (i + 1) * LANES]


def adapter_mask(chosen_ref):
    rows = chosen_ref.shape[0]
    return (lax.broadcasted_iota(jnp.int32, (rows, LANES), 1) // ADAPTER_RANK == chosen_ref[...]).astype(F32)


def qkv_back_kernel(n_tp, low_rows, share, tp_ref, dq_ref, dko_ref, dvo_ref, fb_ref, cos_ref, sin_ref, n1_ref, u_ref, chosen_ref, w_ref, lb_ref, dn1_ref, pack_ref, a_acc, b_acc):
    q_width, kv_width = dq_ref.shape[1], dko_ref.shape[1]
    ranks = LANES
    rows = dq_ref.shape[0]
    step = pl.program_id(0)
    mask = adapter_mask(chosen_ref)
    head = lax.broadcasted_iota(jnp.int32, (rows, LANES), 1) % HEAD_SIZE < HEAD_SIZE // 2

    def turned_back(v):
        swapped = jnp.where(head, pltpu.roll(v, LANES - HEAD_SIZE // 2, 1), pltpu.roll(v, HEAD_SIZE // 2, 1))
        return (v * cos_ref[...] - swapped * sin_ref[...]).astype(BF)

    dq = [turned_back(dq_ref[:, i : i + LANES]) for i in range(0, q_width, LANES)]
    dk = [turned_back(dko_ref[:, i : i + LANES] + fb_ref[:, i : i + LANES].astype(F32)) for i in range(0, kv_width, LANES)]
    dv = (dvo_ref[...] + fb_ref[:, kv_width:].astype(F32)).astype(BF)
    dq = jnp.concatenate(dq, axis=1)
    dk = jnp.concatenate(dk, axis=1) if len(dk) > 1 else dk[0]
    lows = []
    at = 0
    for d in (dq, dk, dv):
        lows.append((dot_t(d, lb_ref[:, at : at + d.shape[1]]) * mask).astype(BF))
        at += d.shape[1]
    lows = jnp.concatenate(lows, axis=1)
    dn1_ref[...] = dot_t(jnp.concatenate([dq, dk, dv, lows], axis=1), w_ref[...]).astype(BF)
    n1 = n1_ref[...]
    parts = [
        (a_acc, slice(0, 3 * ranks), t_dot_k(n1, lows)),
        (b_acc, slice(0, q_width), t_dot_k(u_ref[:, :ranks], dq)),
        (b_acc, slice(q_width, q_width + kv_width), t_dot_k(u_ref[:, ranks : 2 * ranks], dk)),
        (b_acc, slice(q_width + kv_width, q_width + 2 * kv_width), t_dot_k(u_ref[:, 2 * ranks :], dv)),
    ]

    @pl.when(step == 0)
    def _():
        for acc, cols, value in parts:
            acc[:, cols] = value

    @pl.when(step > 0)
    def _():
        for acc, cols, value in parts:
            acc[:, cols] += value

    @pl.when(step == pl.num_programs(0) - 1)
    def _():
        pack_ref[...] = jnp.zeros_like(pack_ref)
        at, col = 0, 0
        for i, cols in enumerate((q_width, kv_width, kv_width)):
            put_rows(pack_ref, a_acc[:, i * ranks : (i + 1) * ranks], at, share)
            at += share
            put_cols(pack_ref, b_acc[:, col : col + cols], at, low_rows, tp_ref[0] * (cols // LANES))
            at += cols * n_tp // LANES * low_rows
            col += cols


def qkv_back(n, n_tp, low_rows, share, tp_at, dq, dko, dvo, fb, cos, sin, n1, u3, chosen, w_one, low_one, height):
    rows, q_width = dq.shape
    width = n1.shape[1]
    step = 256
    by_row = lambda a: pl.BlockSpec((step, a.shape[1]), lambda i: (i, 0))
    whole = lambda a: pl.BlockSpec(a.shape, lambda i: (0, 0), pipeline_mode=pl.Buffered(1))
    sd = jax.ShapeDtypeStruct
    return pl.pallas_call(
        functools.partial(qkv_back_kernel, n_tp, low_rows, share),
        grid=(rows // step,),
        in_specs=[pl.BlockSpec(memory_space=pltpu.SMEM)] + [by_row(a) for a in (dq, dko, dvo, fb, cos, sin, n1, u3, chosen)] + [whole(w_one), whole(low_one)],
        out_specs=[pl.BlockSpec((step, width), lambda i: (i, 0)), pl.BlockSpec((n, height, LANES), lambda i: (0, 0, 0))],
        out_shape=[sd((rows, width), BF), sd((n, height, LANES), F32)],
        scratch_shapes=[pltpu.VMEM((width, 3 * LANES), F32), pltpu.VMEM((LANES, low_one.shape[1]), F32)],
        compiler_params=pltpu.CompilerParams(vmem_limit_bytes=50 << 20),
        cost_estimate=pl.CostEstimate(flops=4 * rows * width * w_one.shape[1], bytes_accessed=24 << 20, transcendentals=0),
    )(tp_at, dq, dko, dvo, fb, cos, sin, n1, u3, chosen, w_one, low_one)


def mid_back_kernel(n, n_tp, experts, share, low_rows, sel_ref, mine_ref, other_ref, h_ref, c_ref, t_ref, o_ref, ou_ref, ru_ref, chosen_ref, gain_ref,
                    w_ref, low_ref, oa_ref, bd_ref, ad_ref, bg_ref, bu_ref, agu_ref, dh_ref, do_ref, pack_ref, ar_acc, ao_acc, bo_acc, br_acc):
    width = h_ref.shape[1]
    q_width = o_ref.shape[1]
    ff = bg_ref.shape[1]
    spare = mine_ref.shape[1] - width
    step = pl.program_id(0)
    mask = adapter_mask(chosen_ref)
    picked = step == sel_ref[0]

    def fold(height, top):
        lane = lax.broadcasted_iota(jnp.int32, (height, LANES), 0)
        return ((lane % experts == lax.broadcasted_iota(jnp.int32, (height, LANES), 1)) & (lane < top)).astype(BF)

    back = jnp.where(picked, mine_ref[:, :width].astype(F32), other_ref[:, :width].astype(F32))
    tail = jnp.where(picked, mine_ref[:, width:].astype(F32), other_ref[:, width:].astype(F32)).astype(BF)
    dgate = dot(tail, fold(spare, 2 * experts * n_tp))
    gates = dot(t_ref[:, width:], fold(LANES, 2 * experts))
    n2 = t_ref[:, :width]
    router_a, router_w = w_ref[:, q_width : q_width + LANES], w_ref[:, q_width + 3 * LANES : q_width + 4 * LANES]
    out_b, router_b = low_ref[:, 2 * ff : 2 * ff + width], low_ref[:, 2 * ff + 2 * width :]
    dlog = (gates * (dgate - jnp.sum(gates * dgate, axis=1, keepdims=True))).astype(BF)
    rdu = (dot_t(dlog, router_b) * mask).astype(BF)
    dn2 = back + dot_t(dlog, router_w) + dot_t(rdu, router_a)
    h = h_ref[...]
    r = lax.rsqrt(jnp.mean(h * h, axis=1, keepdims=True) + norm_eps)
    gd = dn2 * gain_ref[...]
    dh = c_ref[...].astype(F32) + r * gd - h * (r * r * r * jnp.mean(gd * h, axis=1, keepdims=True))
    dh_ref[...] = dh
    dattn = dh.astype(BF)
    odu = (dot_t(dattn, out_b) * mask).astype(BF)
    do_ref[...] = (dot(dattn, w_ref[:, :q_width]) + dot_t(odu, oa_ref[...])).astype(BF)
    parts = [
        (ar_acc, t_dot_k(n2, rdu)),
        (ao_acc, t_dot_k(o_ref[...], odu)),
        (bo_acc, t_dot_k(ou_ref[...], dattn)),
        (br_acc, t_dot_k(ru_ref[...], dlog)),
    ]

    @pl.when(step == 0)
    def _():
        for acc, value in parts:
            acc[...] = value

    @pl.when(step > 0)
    def _():
        for acc, value in parts:
            acc[...] += value

    @pl.when(step == pl.num_programs(0) - 1)
    def _():
        pack_ref[...] = jnp.zeros_like(pack_ref)
        tp = sel_ref[1]
        first = (tp == 0).astype(F32)
        own = n // n_tp
        at = 0
        for k in range(own):
            pack_ref[tp * own + k, pl.ds(at, share), :] = ao_acc[k * share : (k + 1) * share, :]
        at += share
        put_cols(pack_ref, bo_acc, at, low_rows, 0)
        at += width // LANES * low_rows
        ar_acc[...] = ar_acc[...] * first
        put_rows(pack_ref, ar_acc, at, share)
        at += share
        br_acc[...] = br_acc[...] * first
        put_cols(pack_ref, br_acc, at, low_rows, 0)
        at += low_rows
        for i, ref in enumerate((bg_ref, bu_ref)):
            put_rows(pack_ref, agu_ref[:, i * LANES : (i + 1) * LANES], at, share)
            at += share
            put_cols(pack_ref, ref, at, low_rows, tp * (ff // LANES))
            at += ff * n_tp // LANES * low_rows
        size = ad_ref.shape[0] // own
        for k in range(own):
            pack_ref[tp * own + k, pl.ds(at, size), :] = ad_ref[k * size : (k + 1) * size, :]
        at += size
        put_cols(pack_ref, bd_ref, at, low_rows, 0)


def mid_back(n, n_tp, experts, share, low_rows, sel, mine, other, hidden, cot, carried, mixed, out_u, router_u, chosen, gain, w_two, low_two, out_a, sums, height):
    rows, width = hidden.shape
    q_width = mixed.shape[1]
    step = rows // 2
    sd = jax.ShapeDtypeStruct
    by_row = lambda a: pl.BlockSpec((step, a.shape[1]), lambda i: (i, 0))
    whole = lambda a: pl.BlockSpec(a.shape, lambda i: (0, 0), pipeline_mode=pl.Buffered(1))
    return pl.pallas_call(
        functools.partial(mid_back_kernel, n, n_tp, experts, share, low_rows),
        grid=(2,),
        in_specs=[pl.BlockSpec(memory_space=pltpu.SMEM), whole(mine), whole(other)]
        + [by_row(a) for a in (hidden, cot, carried, mixed, out_u, router_u, chosen)]
        + [whole(a) for a in (gain, w_two, low_two, out_a, *sums)],
        out_specs=[by_row(hidden), by_row(mixed), pl.BlockSpec((n, height, LANES), lambda i: (0, 0, 0))],
        out_shape=[sd((rows, width), F32), sd((rows, q_width), BF), sd((n, height, LANES), F32)],
        scratch_shapes=[pltpu.VMEM((width, LANES), F32), pltpu.VMEM((q_width, LANES), F32), pltpu.VMEM((LANES, width), F32), pltpu.VMEM((LANES, LANES), F32)],
        compiler_params=pltpu.CompilerParams(vmem_limit_bytes=58 << 20),
        cost_estimate=pl.CostEstimate(flops=8 * rows * width * q_width, bytes_accessed=32 << 20, transcendentals=0),
    )(sel, mine, other, hidden, cot, carried, mixed, out_u, router_u, chosen, gain, w_two, low_two, out_a, *sums)


def reduce_kernel(n, pack_ref, side_ref, out_ref, side_out, side_in, side_snd, snd1, rcv1, acc, snd2, rcv2, acc2, snd3, rcv3, fin, sems, send3, recv3):
    me = lax.axis_index("fsdp")
    ctx = lax.axis_index("ctx")
    tp = lax.axis_index("tp")
    half = pack_ref.shape[1] // 2
    part = half // 2
    barrier = pltpu.get_barrier_semaphore()
    pl.semaphore_signal(barrier, inc=1, device_id={"tp": 1 - tp}, device_id_type=MESH)
    pl.semaphore_signal(barrier, inc=1, device_id={"ctx": 1 - ctx}, device_id_type=MESH)
    for k in range(1, n):
        pl.semaphore_signal(barrier, inc=1, device_id={"fsdp": (me + k) % n}, device_id_type=MESH)
    snd1[...] = pack_ref[:, pl.ds(pl.multiple_of((1 - tp) * half, 16), half), :].astype(BF)
    pl.semaphore_wait(barrier, n + 1)

    def swap(src, dst, i, to):
        copy = pltpu.make_async_remote_copy(src_ref=src, dst_ref=dst, send_sem=sems.at[0, i], recv_sem=sems.at[1, i], device_id=to, device_id_type=MESH)
        copy.start()
        return copy

    copy = swap(snd1, rcv1, 0, {"tp": 1 - tp})
    side = swap(side_ref, side_in.at[0], 4, {"tp": 1 - tp})
    copy.wait()
    acc[...] = pack_ref[:, pl.ds(pl.multiple_of(tp * half, 16), half), :] + rcv1[...].astype(F32)
    snd2[...] = acc[:, pl.ds(pl.multiple_of((1 - ctx) * part, 16), part), :].astype(BF)
    copy = swap(snd2, rcv2, 1, {"ctx": 1 - ctx})
    side.wait()
    side_snd[...] = (side_ref[...].astype(F32) + side_in[0].astype(F32)).astype(BF)
    side = swap(side_snd, side_in.at[1], 5, {"ctx": 1 - ctx})
    copy.wait()
    acc2[...] = acc[:, pl.ds(pl.multiple_of(ctx * part, 16), part), :] + rcv2[...].astype(F32)
    snd3[...] = acc2[...].astype(BF)

    def ship(k):
        to = (me + k) % n
        return pltpu.make_async_remote_copy(
            src_ref=snd3.at[to], dst_ref=rcv3.at[me], send_sem=send3.at[k], recv_sem=recv3.at[k], device_id={"fsdp": to}, device_id_type=MESH
        )

    def came(k):
        return pltpu.make_async_remote_copy(
            src_ref=snd3.at[me], dst_ref=rcv3.at[(me + n - k) % n], send_sem=send3.at[k], recv_sem=recv3.at[k],
            device_id={"fsdp": (me + k) % n}, device_id_type=MESH,
        )

    for k in range(1, n):
        ship(k).start()
    total = acc2[me]
    for k in range(1, n):
        came(k).wait_recv()
        total = total + rcv3[(me + n - k) % n].astype(F32)
    for k in range(1, n):
        ship(k).wait_send()
    spot = tp * 2 + ctx
    fin[spot] = total.astype(BF)
    copy = swap(fin.at[spot], fin.at[spot], 2, {"ctx": 1 - ctx})
    copy.wait()
    both = fin.at[pl.ds(tp * 2, 2)]
    copy = swap(both, both, 3, {"tp": 1 - tp})
    copy.wait()
    for i in range(4):
        out_ref[pl.ds(i * part, part), :] = fin[i].astype(F32)
    side.wait()
    side_out[...] = side_snd[...].astype(F32) + side_in[1].astype(F32)


def reduce_pack(pack, side, collective_id):
    n, height = pack.shape[:2]
    if lax.axis_size("tp") != 2 or lax.axis_size("ctx") != 2 or height % 64 or side.shape[0] % 16:
        mine = lax.psum_scatter(pack.astype(BF), "fsdp", scatter_dimension=0, tiled=False)
        return lax.psum(mine, ("ctx", "tp")).astype(F32), lax.psum(side, ("ctx", "tp")).astype(F32)
    half, part = height // 2, height // 4
    vm = pltpu.VMEM
    dma = pltpu.SemaphoreType.DMA
    return pl.pallas_call(
        functools.partial(reduce_kernel, n),
        in_specs=[pl.BlockSpec(memory_space=vm)] * 2,
        out_specs=[pl.BlockSpec(memory_space=vm)] * 2,
        out_shape=[jax.ShapeDtypeStruct((height, LANES), F32), jax.ShapeDtypeStruct(side.shape, F32)],
        scratch_shapes=[
            vm((2,) + side.shape, BF), vm(side.shape, BF), vm((n, half, LANES), BF), vm((n, half, LANES), BF), vm((n, half, LANES), F32),
            vm((n, part, LANES), BF), vm((n, part, LANES), BF), vm((n, part, LANES), F32),
            vm((n, part, LANES), BF), vm((n, part, LANES), BF), vm((4, part, LANES), BF),
            dma((2, 6)), dma((n,)), dma((n,)),
        ],
        compiler_params=pltpu.CompilerParams(collective_id=collective_id, has_side_effects=True, vmem_limit_bytes=48 << 20),
    )(pack, side)


def tp_sum(value):
    if lax.axis_size("tp") != 2:
        return lax.psum(value, "tp")
    return value + lax.ppermute(value, "tp", [(0, 1), (1, 0)])


def on_device(
    tokens, out_cotangent, lengths, adapter_of_doc, routes, attn_gain, ffn_gain,
    w_query, key_matrix, value_matrix, w_out, w_router, w_gate, w_up, w_down,
    a_query, b_query, a_key, key_second_factor, a_value, value_second_factor,
    a_out, b_out, a_router, b_router, a_gate, b_gate, a_up, b_up, a_down, b_down,
):
    rows, width = tokens.shape
    n = lax.axis_size("fsdp")
    n_tp = lax.axis_size("tp")
    tp_at = lax.axis_index("tp")
    ctx_at = lax.axis_index("ctx")
    group = rows * lax.axis_size("ctx")
    q_width = w_query.shape[1]
    kv_width = key_matrix.shape[1]
    ff_width = w_gate.shape[2]
    local_experts = w_gate.shape[0]
    experts = w_router.shape[1]
    ranks = a_query.shape[1]
    share = w_query.shape[0]
    low_rows = b_query.shape[0]

    pad = ((0, 0), (0, LANES - experts))
    one, low_one = gather_packs(
        [
            [(a, a.shape[1]) for a in (w_query, key_matrix, value_matrix, a_query, a_key, a_value)],
            [(b_query, q_width), (key_second_factor, kv_width), (value_second_factor, kv_width)],
        ],
        0,
    )
    qkv = q_width + 2 * kv_width
    w_one = one.reshape(n * share, -1)
    low_one = low_one.reshape(n * low_rows, -1)
    query_b, key_b, value_b = low_one[:, :q_width], low_one[:, q_width : q_width + kv_width], low_one[:, q_width + kv_width :]

    ends = jnp.cumsum(lengths[0])
    starts = ends - lengths[0]
    place = jnp.arange(group, dtype=jnp.int32)
    doc = jnp.sum((place[:, None] >= ends[None, :]).astype(jnp.int32), axis=1)
    picked = (doc[:, None] == jnp.arange(lengths.shape[1], dtype=jnp.int32)[None, :]).astype(jnp.int32)
    begin = jnp.sum(picked * starts[None, :], axis=1)
    chosen = jnp.sum(picked * adapter_of_doc[0][None, :], axis=1)
    start = ctx_at * rows
    query_index = start + jnp.arange(rows, dtype=jnp.int32)
    begin_local = lax.dynamic_slice_in_dim(begin, start, rows)
    chosen_local = lax.dynamic_slice_in_dim(chosen, start, rows)
    mask = (chosen_local[:, None] == (jnp.arange(ranks, dtype=jnp.int32) // ADAPTER_RANK)[None, :]).astype(F32)
    half = HEAD_SIZE // 2
    freq = 10000.0 ** (-jnp.arange(half, dtype=F32) / half)
    angles = (query_index - begin_local).astype(F32)[:, None] * freq[None, :]
    cosine_table = jnp.cos(angles)[:, None, :]
    sine_table = jnp.sin(angles)[:, None, :]

    xfull = tokens.astype(F32)
    normed = rms_norm(xfull, attn_gain).astype(BF)
    raw = dot(normed, w_one)
    query_u = (raw[:, qkv : qkv + ranks] * mask).astype(BF)
    key_u = (raw[:, qkv + ranks : qkv + 2 * ranks] * mask).astype(BF)
    value_u = (raw[:, qkv + 2 * ranks : qkv + 3 * ranks] * mask).astype(BF)
    query_pre = raw[:, :q_width] + dot(query_u, query_b)
    key_pre = raw[:, q_width : q_width + kv_width] + dot(key_u, key_b)
    value_state = (raw[:, q_width + kv_width : qkv] + dot(value_u, value_b)).astype(BF)
    query_state = (
        rotary_apply(query_pre.reshape(rows, -1, HEAD_SIZE), cosine_table, sine_table).reshape(rows, q_width).astype(BF)
    )
    key = rotary_apply(key_pre.reshape(rows, -1, HEAD_SIZE), cosine_table, sine_table).reshape(rows, kv_width).astype(BF)
    kv = jnp.concatenate([key, value_state], axis=1)
    cross = Crossing()
    outer, inner = levels(n)
    me = lax.axis_index("fsdp")
    ring = [(i, (i + inner) % n) for i in range(n)]
    turns = [[(i, i // inner * inner + (i % inner + dj) % inner) for i in range(n)] for dj in range(1, inner)]
    local = local_experts // cross.n_ctx
    mine = [lax.dynamic_slice_in_dim(a, ctx_at * local, local, 0) for a in (w_gate, w_up, w_down)]
    block = jnp.concatenate([mine[0], mine[1], jnp.swapaxes(mine[2], 1, 2)], axis=2)
    brought = {(0, 0): block}

    def bring(do, after):
        last = [brought[(do, 0)]] + [brought[(do - 1, dj)] for dj in range(1, inner) if do]
        last, after = lax.optimization_barrier((last, after))
        brought[(do, 0)] = last[0]
        for dj, value in zip(range(1, inner), last[1:]):
            brought[(do - 1, dj)] = value
        if do + 1 < outer:
            brought[(do + 1, 0)] = lax.ppermute(last[0], "fsdp", ring)
        for dj in range(1, inner):
            brought[(do, dj)] = lax.ppermute(last[0], "fsdp", turns[dj - 1])
        return after

    one = bring(0, one)
    far = lax.ppermute(kv, "ctx", [(i, i + 1) for i in range(lax.axis_size("ctx") - 1)])
    w_out_t, kv = lax.optimization_barrier((w_out.T, kv))
    two, low_two, down_a = gather_packs(
        [
            [(a, a.shape[1]) for a in (w_out_t, a_router, a_gate, a_up, jnp.pad(w_router, pad), a_out)],
            [(b_gate, ff_width), (b_up, ff_width), (b_out, width), (b_down, width), (jnp.pad(b_router, pad), LANES)],
            [(a_down, ranks)],
        ],
        1,
    )
    two = bring(1, two)
    cot = lax.optimization_barrier((out_cotangent, two))[0]
    cot_halves = cross.fetch(cot)
    far, two = lax.optimization_barrier((far, two))
    w_two = two.reshape(n * share, -1)
    low_two = low_two.reshape(n * low_rows, -1)
    out_b = low_two[:, 2 * ff_width : 2 * ff_width + width]
    down_b = low_two[:, 2 * ff_width + width : 2 * ff_width + 2 * width]
    router_b = low_two[:, 2 * ff_width + 2 * width :]
    out_wt = w_two[:, :q_width]
    router_a = w_two[:, q_width : q_width + ranks]
    router_w = w_two[:, q_width + 3 * ranks : q_width + 4 * ranks]
    out_a = lax.dynamic_slice_in_dim(w_two[:, q_width + 4 * ranks : q_width + 5 * ranks], tp_at * q_width, q_width, 0)
    down_at = lax.dynamic_slice_in_dim(down_a.reshape(-1, ranks), tp_at * ff_width, ff_width, 0)
    begin_row = begin_local[None, :]
    start_at = jnp.reshape(start, (1,)).astype(jnp.int32)
    query_state = (query_state.astype(F32) * 0.125).astype(BF)
    mixed_heads, log_total = attend(query_state, kv, far, begin_row, start_at)
    mixed_heads = bring(2, mixed_heads)
    cot_halves, mixed_heads = lax.optimization_barrier((cot_halves, mixed_heads))
    out_u = dot(mixed_heads, out_a) * mask
    attn_part = dot_t(mixed_heads, out_wt) + dot(out_u.astype(BF), out_b)
    hidden = xfull + tp_sum(attn_part)
    normed_two = rms_norm(hidden, ffn_gain).astype(BF)
    lows = dot(normed_two, jnp.concatenate([router_a, router_w], axis=1))
    router_u = (lows[:, :ranks] * mask).astype(BF)
    logits = lows[:, ranks : ranks + experts] + dot(router_u, router_b)[:, :experts]
    selected = jnp.any(routes[:, :, None] == jnp.arange(experts, dtype=jnp.int32)[None, None, :], axis=1)
    gates = jax.nn.softmax(jnp.where(selected, logits, -jnp.inf), axis=-1)

    high = gates.astype(BF)
    spare = -(-2 * experts * n_tp // LANES) * LANES
    carried = jnp.concatenate(
        [
            normed_two,
            high,
            (gates - high.astype(F32)).astype(BF),
            chosen_local[:, None].astype(BF),
            jnp.zeros((rows, LANES - 2 * experts - 1), BF),
        ],
        axis=1,
    )
    halves = cross.fetch(carried)
    early = [(0, 0), (1, 0)] + [(0, dj) for dj in range(1, inner)] + [(2, 0)] + [(1, dj) for dj in range(1, inner)]
    late = [(do, 0) for do in range(3, outer)] + [(do, dj) for do in range(2, outer) for dj in range(1, inner)]

    def weights_of(keys):
        ids = [((me // inner + outer - do) % outer * inner + (me % inner + inner - dj) % inner) * local_experts + ctx_at * local + j for do, dj in keys for j in range(local)]
        return jnp.stack(ids + [tp_at * 2 * experts]).astype(jnp.int32), [brought[k][j] for k in keys for j in range(local)]

    sums = [jnp.zeros(shape, F32) for shape in ((ranks, width), (ff_width, ranks), (ranks, ff_width), (ranks, ff_width), (width, 2 * ranks))]
    at = q_width // LANES + 1
    work = [(carried, cot)] + [(None, None)] * (cross.n_ctx - 1)
    partial = []
    ids, weights = weights_of(early)
    for by in range(cross.n_ctx):
        if by:
            work[by] = (cross.joined(halves[by - 1]), cross.joined(cot_halves[by - 1]))
        r, m, sums = experts_on(ids, experts, spare, *work[by], weights, w_two, at, low_two, down_b, down_at, sums)
        if by == 0:
            for do in range(3, outer):
                r = bring(do, r)
            halves, cot_halves, r = lax.optimization_barrier((halves, cot_halves, r))
        partial.append((r, m))
    ids, weights = weights_of(late)
    back_parts, moe_parts = [], []
    for by in list(range(1, cross.n_ctx)) + [0]:
        r, m, sums = experts_on(ids, experts, spare, *work[by], weights, w_two, at, low_two, down_b, down_at, sums, partial[by])
        moe_parts.append(m)
        if by:
            half = cross.summed_half(r).astype(BF)
            half, carried = lax.optimization_barrier((half, work[0][0]))
            work[0] = (carried, cot)
            back_parts.append(lax.ppermute(half, "ctx", cross.pairs(-by)))
    r, back_parts = lax.optimization_barrier((r, back_parts))
    mine_half, other, first = cross.halves_of_total(r, back_parts)
    swapped = cross.swapped(moe_parts)
    early_shapes = [
        (share, ranks), (low_rows, width), (share, ranks), (low_rows, experts), (share, ranks), (low_rows, ff_width * n_tp),
        (share, ranks), (low_rows, ff_width * n_tp), (a_down.shape[0], ranks), (low_rows, width),
    ]
    height = sum(-(-cols // LANES) * tall for tall, cols in early_shapes)
    sel = jnp.stack([jnp.asarray(first, jnp.int32), tp_at.astype(jnp.int32)])
    dhidden, dmixed, early_pack = mid_back(
        n, n_tp, experts, share, low_rows, sel, mine_half, other, hidden, cot, carried, mixed_heads, out_u.astype(BF), router_u,
        chosen_local[:, None], ffn_gain[None, :], w_two, low_two, out_a, sums, height,
    )
    early_pack, dmixed, swapped = lax.optimization_barrier((early_pack.astype(BF), dmixed, swapped))
    moe_halves = [cross.half(p).astype(F32) + q.astype(F32) for p, q in zip(moe_parts, swapped)]
    moe_got = [lax.ppermute(p.astype(BF), "ctx", cross.pairs(-by)) for by, p in zip(range(1, cross.n_ctx), moe_halves)]
    early_sum = lax.psum_scatter(early_pack, "fsdp", scatter_dimension=0, tiled=False)
    dquery, dkey_own, dvalue_own, dkey_far, dvalue_far = attend_back(
        query_state, kv, far, begin_row, start_at, mixed_heads, dmixed, log_total
    )
    moe_got, dquery = lax.optimization_barrier((moe_got, dquery))
    moe = moe_halves[-1]
    for part in moe_got:
        moe = moe + part.astype(F32)
    moe = cross.joined(moe.astype(BF)).astype(F32) if n_tp == 2 else lax.psum(moe, "tp")
    output = (hidden + moe).astype(BF)
    far_back = lax.ppermute(
        jnp.concatenate([dkey_far, dvalue_far], axis=1),
        "ctx",
        [(i + 1, i) for i in range(lax.axis_size("ctx") - 1)],
    )
    height = 3 * share + low_rows * n_tp * qkv // LANES
    cosine_wide = jnp.tile(cosine_table[:, 0, :], (1, 2 * LANES // HEAD_SIZE))
    sine_wide = jnp.tile(jnp.concatenate([-sine_table[:, 0, :], sine_table[:, 0, :]], axis=1), (1, LANES // HEAD_SIZE))
    dn1, pack = qkv_back(
        n, n_tp, low_rows, share, jnp.reshape(tp_at, (1,)).astype(jnp.int32), dquery, dkey_own, dvalue_own, far_back,
        cosine_wide, sine_wide, normed, jnp.concatenate([query_u, key_u, value_u], axis=1), chosen_local[:, None], w_one, low_one, height,
    )
    early_sum, dn1, pack = lax.optimization_barrier((early_sum, dn1, pack))
    late, early_sum = reduce_pack(pack, early_sum, 2)
    dn1 = tp_sum(dn1.astype(F32)) if n_tp != 2 else dn1.astype(F32) + lax.ppermute(dn1, "tp", [(0, 1), (1, 0)]).astype(F32)
    grad_tokens = (dhidden + norm_back(xfull, attn_gain, dn1)).astype(BF)

    def unpack(mine, shapes):
        found = []
        at = 0
        for height, cols in shapes:
            count = -(-cols // LANES)
            piece = mine[at : at + count * height].reshape(count, height, LANES).transpose(1, 0, 2).reshape(height, count * LANES)
            found.append(piece[:, :cols])
            at += count * height
        return found

    first_shapes = [(share, ranks), (low_rows, q_width * n_tp), (share, ranks), (low_rows, kv_width * n_tp), (share, ranks), (low_rows, kv_width * n_tp)]
    final = unpack(late, first_shapes) + unpack(early_sum, early_shapes)
    return (output, grad_tokens, *final)


def solution(mesh):
    both = P(("fsdp", "ctx"), None)
    split = P("fsdp", None)
    placed = (
        both, both, split, split, both, P(), P(),
        P("fsdp", "tp"), P("fsdp", "tp"), P("fsdp", "tp"), P("tp", "fsdp"), split,
        P("fsdp", None, "tp"), P("fsdp", None, "tp"), P("fsdp", "tp", None),
    ) + (split,) * 16
    return jax.shard_map(
        on_device, mesh=mesh, in_specs=placed, out_specs=(both, both) + (split,) * 16, check_vma=False
    )
```

```python
import functools

import jax
import jax.numpy as jnp
from jax import lax
from jax.experimental import pallas as pl
from jax.experimental.pallas import tpu as pltpu
from jax.sharding import PartitionSpec as P

HEAD_SIZE = 64
ADAPTER_RANK = 16
LANES = 128
norm_eps = 1e-05
BF = jnp.bfloat16
F32 = jnp.float32


MESH = pl.DeviceIdType.MESH


def dot(left, right, dims=((1,), (0,)), precision=None):
    return lax.dot_general(left, right, (dims, ((), ())), preferred_element_type=F32, precision=precision)


def dot_t(left, right):
    return dot(left, right, ((1,), (1,)))


def t_dot(left, right):
    return dot(left, right, ((0,), (0,)))


def rms_norm(values, gain):
    return values * lax.rsqrt(jnp.mean(values * values, axis=-1, keepdims=True) + norm_eps) * gain


def norm_back(values, gain, grad):
    unused, pull = jax.vjp(lambda inner: rms_norm(inner, gain), values)
    return pull(grad)[0]


def levels(n):
    outer = 4 if n % 4 == 0 else n
    return outer, n // outer


def fill_bias(bias, start_ref, begin_ref, rows):
    step = rows // 3
    for at in range(0, 2 * rows, step):
        key = start_ref[0] - rows + at + lax.broadcasted_iota(jnp.int32, (step, rows), 0)
        query = start_ref[0] + lax.broadcasted_iota(jnp.int32, (step, rows), 1)
        ok = (key <= query) & (key >= begin_ref[...]) & (key >= 0)
        bias[pl.ds(at, step), :] = jnp.where(ok, 0.0, -1e30)


def split_heads(ref, out, count, rows, at=0):
    for h in range(count):
        out[h, pl.ds(at, rows), :] = ref[:, h * HEAD_SIZE : (h + 1) * HEAD_SIZE]


def attend_kernel(group, q_blocks, start_ref, begin_ref, q_ref, ko_ref, vo_ref, kf_ref, vf_ref, o_ref, lse_ref, bias, ks, vts, qs, ots):
    rows = q_ref.shape[0]
    width = rows // q_blocks
    heads = 2 * group
    @pl.when(pl.program_id(0) == 0)
    def _():
        fill_bias(bias, start_ref, begin_ref, rows)
    split_heads(kf_ref, ks, 2, rows, 0)
    split_heads(ko_ref, ks, 2, rows, rows)
    split_heads(q_ref, qs, heads, rows, 0)
    vts[:, pl.ds(0, rows)] = vf_ref[...].astype(F32).T.astype(BF)
    vts[:, pl.ds(rows, rows)] = vo_ref[...].astype(F32).T.astype(BF)
    for b in range(q_blocks):
        keys = rows + (b + 1) * width
        def one(h, _):
            g = h // group
            s = dot_t(ks[g, pl.ds(0, keys), :], qs[h, pl.ds(b * width, width), :]) + bias[pl.ds(0, keys), pl.ds(b * width, width)]
            top = jnp.max(s, axis=0, keepdims=True)
            p = jnp.exp(s - top)
            total = jnp.sum(p, axis=0, keepdims=True)
            lse_ref[0, pl.ds(h, 1), pl.ds(b * width, width)] = top + jnp.log(total)
            vt = vts[pl.ds(pl.multiple_of(g * HEAD_SIZE, HEAD_SIZE), HEAD_SIZE), pl.ds(0, keys)]
            o = dot(vt, p.astype(BF)) / total
            ots[pl.ds(pl.multiple_of(h * HEAD_SIZE, HEAD_SIZE), HEAD_SIZE), pl.ds(b * width, width)] = o
            return 0
        lax.fori_loop(0, heads, one, 0)
    for j in range(group):
        o_ref[:, j * LANES : (j + 1) * LANES] = ots[pl.ds(j * LANES, LANES), :].T.astype(BF)


def attend(q, kv, far, begin, start, q_blocks=3):
    rows, q_width = q.shape
    kv_width = kv.shape[1] // 2
    pairs = kv_width // LANES
    group = q_width // kv_width
    spec = lambda off: pl.BlockSpec((rows, LANES), lambda i: (0, i + off))
    return pl.pallas_call(
        functools.partial(attend_kernel, group, q_blocks),
        grid=(pairs,),
        in_specs=[pl.BlockSpec(memory_space=pltpu.SMEM), pl.BlockSpec((1, rows), lambda i: (0, 0)),
                  pl.BlockSpec((rows, group * LANES), lambda i: (0, i)), spec(0), spec(pairs), spec(0), spec(pairs)],
        out_specs=[pl.BlockSpec((rows, group * LANES), lambda i: (0, i)), pl.BlockSpec((1, 8, rows), lambda i: (i, 0, 0))],
        out_shape=[jax.ShapeDtypeStruct((rows, q_width), BF), jax.ShapeDtypeStruct((pairs, 8, rows), F32)],
        scratch_shapes=[pltpu.VMEM((2 * rows, rows), F32), pltpu.VMEM((2, 2 * rows, HEAD_SIZE), BF), pltpu.VMEM((LANES, 2 * rows), BF),
                        pltpu.VMEM((2 * group, rows, HEAD_SIZE), BF), pltpu.VMEM((2 * group * HEAD_SIZE, rows), F32)],
        compiler_params=pltpu.CompilerParams(vmem_limit_bytes=50 << 20),
        cost_estimate=pl.CostEstimate(flops=8 * rows * rows * q_width, bytes_accessed=8 << 20, transcendentals=2 * rows * rows * 12),
    )(start, begin, q, kv, kv, far, far)


def attend_back_kernel(group, q_blocks, start_ref, begin_ref, q_ref, ko_ref, vo_ref, kf_ref, vf_ref, o_ref, do_ref, lse_ref,
                       dq_ref, dko_ref, dvo_ref, dkf_ref, dvf_ref, bias, ks, vs, kts, qs, dos, dqts, dks, dvs, deltas):
    rows = q_ref.shape[0]
    width = rows // q_blocks
    heads = 2 * group
    @pl.when(pl.program_id(0) == 0)
    def _():
        fill_bias(bias, start_ref, begin_ref, rows)
    split_heads(kf_ref, ks, 2, rows, 0)
    split_heads(ko_ref, ks, 2, rows, rows)
    split_heads(vf_ref, vs, 2, rows, 0)
    split_heads(vo_ref, vs, 2, rows, rows)
    split_heads(q_ref, qs, heads, rows, 0)
    split_heads(do_ref, dos, heads, rows, 0)
    kts[:, pl.ds(0, rows)] = kf_ref[...].astype(F32).T.astype(BF)
    kts[:, pl.ds(rows, rows)] = ko_ref[...].astype(F32).T.astype(BF)
    cols = heads * HEAD_SIZE
    pick = (lax.broadcasted_iota(jnp.int32, (8, cols), 1) // HEAD_SIZE == lax.broadcasted_iota(jnp.int32, (8, cols), 0)).astype(F32)
    prod = o_ref[...].astype(F32) * do_ref[...].astype(F32)
    deltas[...] = dot(pick, prod, ((1,), (1,)), lax.Precision.HIGHEST)
    dks[...] = jnp.zeros_like(dks)
    dvs[...] = jnp.zeros_like(dvs)
    for b in range(q_blocks):
        keys = rows + (b + 1) * width
        def one(h, _):
            g = h // group
            at = pl.ds(b * width, width)
            qb = qs[h, at, :]
            dob = dos[h, at, :]
            s = dot_t(ks[g, pl.ds(0, keys), :], qb) + bias[pl.ds(0, keys), at]
            p = jnp.exp(s - lse_ref[0, pl.ds(h, 1), at])
            dp = dot_t(vs[g, pl.ds(0, keys), :], dob)
            ds = (p * (dp - deltas[pl.ds(h, 1), at])).astype(BF)
            dvs[g, pl.ds(0, keys), :] += dot(p.astype(BF), dob)
            dks[g, pl.ds(0, keys), :] += dot(ds, qb)
            kt = kts[pl.ds(pl.multiple_of(g * HEAD_SIZE, HEAD_SIZE), HEAD_SIZE), pl.ds(0, keys)]
            dqts[pl.ds(pl.multiple_of(h * HEAD_SIZE, HEAD_SIZE), HEAD_SIZE), at] = dot(kt, ds) * 0.125
            return 0
        lax.fori_loop(0, heads, one, 0)
    for j in range(group):
        dq_ref[:, j * LANES : (j + 1) * LANES] = dqts[pl.ds(j * LANES, LANES), :].T
    for g in range(2):
        at = slice(g * HEAD_SIZE, (g + 1) * HEAD_SIZE)
        dkf_ref[:, at] = dks[g, pl.ds(0, rows), :].astype(BF)
        dko_ref[:, at] = dks[g, pl.ds(rows, rows), :]
        dvf_ref[:, at] = dvs[g, pl.ds(0, rows), :].astype(BF)
        dvo_ref[:, at] = dvs[g, pl.ds(rows, rows), :]


def attend_back(q, kv, far, begin, start, o, do, lse, q_blocks=3):
    rows, q_width = q.shape
    kv_width = kv.shape[1] // 2
    pairs = kv_width // LANES
    group = q_width // kv_width
    spec = lambda off: pl.BlockSpec((rows, LANES), lambda i: (0, i + off))
    wide = pl.BlockSpec((rows, group * LANES), lambda i: (0, i))
    sd = jax.ShapeDtypeStruct
    return pl.pallas_call(
        functools.partial(attend_back_kernel, group, q_blocks),
        grid=(pairs,),
        in_specs=[pl.BlockSpec(memory_space=pltpu.SMEM), pl.BlockSpec((1, rows), lambda i: (0, 0)),
                  wide, spec(0), spec(pairs), spec(0), spec(pairs), wide, wide, pl.BlockSpec((1, 8, rows), lambda i: (i, 0, 0))],
        out_specs=[wide, spec(0), spec(0), spec(0), spec(0)],
        out_shape=[sd((rows, q_width), F32), sd((rows, kv_width), F32), sd((rows, kv_width), F32), sd((rows, kv_width), BF), sd((rows, kv_width), BF)],
        scratch_shapes=[pltpu.VMEM((2 * rows, rows), F32), pltpu.VMEM((2, 2 * rows, HEAD_SIZE), BF), pltpu.VMEM((2, 2 * rows, HEAD_SIZE), BF), pltpu.VMEM((LANES, 2 * rows), BF),
                        pltpu.VMEM((2 * group, rows, HEAD_SIZE), BF), pltpu.VMEM((2 * group, rows, HEAD_SIZE), BF), pltpu.VMEM((2 * group * HEAD_SIZE, rows), F32),
                        pltpu.VMEM((2, 2 * rows, HEAD_SIZE), F32), pltpu.VMEM((2, 2 * rows, HEAD_SIZE), F32), pltpu.VMEM((8, rows), F32)],
        compiler_params=pltpu.CompilerParams(vmem_limit_bytes=56 << 20),
        cost_estimate=pl.CostEstimate(flops=20 * rows * rows * q_width, bytes_accessed=16 << 20, transcendentals=2 * rows * rows * 12),
    )(start, begin, q, kv, kv, far, far, o, do, lse)


def slab_of(rows, ctx):
    edge = 3 * rows // 8 // 16 * 16
    take = rows - edge
    return pl.ds(pl.multiple_of(ctx * edge, 16), take), pl.ds(pl.multiple_of(ctx * take, 16), edge)


def gather_kernel(n, count, extra, *refs):
    total = count + extra
    ins, outs = refs[:total], refs[total : 2 * total]
    own_sem, z_send, z_recv, y_send, y_recv, x_send, x_recv, extra_sem = refs[2 * total :]
    outer, inner = levels(n)
    me = lax.axis_index("fsdp")
    ctx = lax.axis_index("ctx")
    z, y = me // inner, me % inner
    right = (z + 1) % outer * inner + y
    left = (z + outer - 1) % outer * inner + y

    def shard(do, dj):
        return (z + outer - do) % outer * inner + (y + inner - dj) % inner

    own = [pltpu.make_async_copy(ins[a], outs[a].at[me], own_sem.at[a]) for a in range(count)]
    barrier = pltpu.get_barrier_semaphore()
    peers = [right, left] + [z * inner + (y + dj) % inner for dj in range(1, inner)]
    for peer in peers:
        pl.semaphore_signal(barrier, inc=1, device_id={"fsdp": peer}, device_id_type=MESH)
    pl.semaphore_signal(barrier, inc=1, device_id={"ctx": 1 - ctx}, device_id_type=MESH)
    pl.semaphore_wait(barrier, len(peers) + 1)

    def cut(a):
        return 3 * outs[a].shape[1] // 8 >= 16

    def taken(a, k):
        if not cut(a):
            return outs[a].at[k]
        return outs[a].at[k, slab_of(outs[a].shape[1], ctx)[0]]

    def remote(part, send, recv, to, src=None):
        src = part if src is None else src
        return pltpu.make_async_remote_copy(src_ref=src, dst_ref=part, send_sem=send, recv_sem=recv, device_id=to, device_id_type=MESH)

    def from_own(a):
        return ins[a].at[slab_of(ins[a].shape[0], ctx)[0]] if cut(a) else ins[a]

    def z_copy(a, k):
        src = from_own(a) if k == 1 else None
        return remote(taken(a, shard(k - 1, 0)), z_send.at[a, k - 1], z_recv.at[a, k - 1], {"fsdp": right}, src)

    def y_copy(a, do, dj):
        to = {"fsdp": z * inner + (y + dj) % inner}
        src = from_own(a) if do == 0 else None
        return remote(taken(a, shard(do, 0)), y_send.at[a, do, dj - 1], y_recv.at[a, do, dj - 1], to, src)

    def x_copy(a, do, dj):
        part = outs[a].at[shard(do, dj), slab_of(outs[a].shape[1], ctx)[1]]
        return remote(part, x_send.at[a, do, dj], x_recv.at[a, do, dj], {"ctx": 1 - ctx})

    started = []

    def go(copy):
        copy.start()
        started.append(copy)

    straight = [
        pltpu.make_async_remote_copy(
            src_ref=ins[count + i], dst_ref=outs[count + i], send_sem=extra_sem.at[0, i], recv_sem=extra_sem.at[1, i],
            device_id={"ctx": 1 - ctx}, device_id_type=MESH,
        )
        for i in range(extra)
    ]
    for c in straight:
        c.start()
    for a in range(count):
        go(z_copy(a, 1))
        for dj in range(1, inner):
            go(y_copy(a, 0, dj))
    for c in own:
        c.start()
    for do in range(1, outer + 1):
        for a in range(count):
            if do < outer:
                z_copy(a, do).wait_recv()
                if do + 1 < outer:
                    go(z_copy(a, do + 1))
                for dj in range(1, inner):
                    go(y_copy(a, do, dj))
                if cut(a):
                    go(x_copy(a, do, 0))
        for a in range(count):
            for dj in range(1, inner):
                y_copy(a, do - 1, dj).wait_recv()
                if cut(a):
                    go(x_copy(a, do - 1, dj))
    for a in range(count):
        if cut(a):
            for do in range(outer):
                for dj in range(inner):
                    if do or dj:
                        x_copy(a, do, dj).wait_recv()
    for c in started:
        c.wait_send()
    for c in straight:
        c.wait()
    for c in own:
        c.wait()


def gather_packs(packs, extra, collective_id):
    n = lax.axis_size("fsdp")
    outer, inner = levels(n)
    count = len(packs)
    tp_at = lax.axis_index("tp")
    arrays = []
    for parts in packs:
        cut = [a if cols == a.shape[1] else lax.dynamic_slice_in_dim(a, tp_at * cols, cols, 1) for a, cols in parts]
        arrays.append(jnp.concatenate(cut, axis=1) if len(cut) > 1 else cut[0])
    dma = pltpu.SemaphoreType.DMA
    anywhere = pl.BlockSpec(memory_space=pl.ANY)
    side = max(inner - 1, 1)
    return pl.pallas_call(
        functools.partial(gather_kernel, n, count, len(extra)),
        in_specs=[anywhere] * (count + len(extra)),
        out_specs=[anywhere] * (count + len(extra)),
        out_shape=[jax.ShapeDtypeStruct((n,) + a.shape, a.dtype) for a in arrays]
        + [jax.ShapeDtypeStruct(a.shape, a.dtype) for a in extra],
        scratch_shapes=[
            dma((count,)), dma((count, outer - 1)), dma((count, outer - 1)),
            dma((count, outer, side)), dma((count, outer, side)), dma((count, outer, inner)), dma((count, outer, inner)),
            dma((2, max(len(extra), 1))),
        ],
        compiler_params=pltpu.CompilerParams(collective_id=collective_id, has_side_effects=True),
    )(*arrays, *extra)


def t_dot_k(left, right):
    return dot(left, right, ((0,), (0,)))


def expert_kernel(experts, count, ids_ref, t_ref, c_ref, *refs):
    w_refs = refs[:count]
    ga_ref, ua_ref, gb_ref, ub_ref, db_ref, da_ref = refs[count : count + 6]
    prior = refs[count + 6 : count + 11]
    early = refs[count + 11 : -9]
    r_ref, m_ref = refs[-9:-7]
    sums = refs[-7:-2]
    moe_acc, dn2_acc = refs[-2:]
    rows, width = c_ref.shape
    ff = gb_ref.shape[1]
    spare = r_ref.shape[1] - width
    lanes = t_ref.shape[1] - width

    @pl.when(pl.program_id(0) == 0)
    def _():
        for old, new in zip(prior, sums):
            new[...] = old[...]

    n2 = t_ref[:, :width]
    cot = c_ref[...]
    extra = t_ref[:, width:].astype(F32)
    lane = lax.broadcasted_iota(jnp.int32, (rows, lanes), 1)
    chosen = jnp.sum(jnp.where(lane == 2 * experts, extra, 0.0), axis=1, keepdims=True)
    low_lane = lax.broadcasted_iota(jnp.int32, (rows, LANES), 1)
    mask = ((low_lane // ADAPTER_RANK).astype(F32) == chosen).astype(F32)
    zg = (dot(n2, ga_ref[...]) * mask).astype(BF)
    zu = (dot(n2, ua_ref[...]) * mask).astype(BF)
    gl = dot(zg, gb_ref[...])
    ul = dot(zu, ub_ref[...])
    down_back = (dot_t(cot, db_ref[...]) * mask).astype(BF)
    al = dot_t(down_back, da_ref[...])
    back_lane = lax.broadcasted_iota(jnp.int32, (rows, spare), 1)
    dgate = jnp.zeros((rows, spare), F32)
    act_sum = dg_sum = du_sum = None
    for k in range(count):
        e = ids_ref[k]
        w = w_refs[k]
        gate = jnp.sum(jnp.where((lane == e) | (lane == experts + e), extra, 0.0), axis=1, keepdims=True)
        gv = dot(n2, w[:, :ff]) + gl
        uv = dot(n2, w[:, ff : 2 * ff]) + ul
        back = dot(cot, w[:, 2 * ff :]) + al
        sig = 1.0 / (1.0 + jnp.exp(-gv))
        silu = gv * sig
        act = silu * uv
        col = jnp.sum(act * back, axis=1, keepdims=True)
        high = col.astype(BF).astype(F32)
        at = e + ids_ref[count]
        dgate = dgate + jnp.where(back_lane == at, high, 0.0) + jnp.where(back_lane == at + experts, col - high, 0.0)
        back = back * gate
        act = act * gate
        du = back * silu
        dg = back * uv * (sig + silu * (1.0 - sig))
        act_sum = act if k == 0 else act_sum + act
        dg_sum = dg if k == 0 else dg_sum + dg
        du_sum = du if k == 0 else du_sum + du
        moe = dot_t(act.astype(BF), w[:, 2 * ff :])
        dn2 = dot_t(jnp.concatenate([dg.astype(BF), du.astype(BF)], axis=1), w[:, : 2 * ff])
        if k == 0:
            moe_acc[...] = moe
            dn2_acc[...] = dn2
        else:
            moe_acc[...] += moe
            dn2_acc[...] += dn2
    act_sum, dg_sum, du_sum = act_sum.astype(BF), dg_sum.astype(BF), du_sum.astype(BF)
    low = (dot(act_sum, da_ref[...]) * mask).astype(BF)
    gdu = (dot_t(dg_sum, gb_ref[...]) * mask).astype(BF)
    udu = (dot_t(du_sum, ub_ref[...]) * mask).astype(BF)
    moe = moe_acc[...] + dot(low, db_ref[...])
    dn2 = dn2_acc[...] + dot_t(gdu, ga_ref[...]) + dot_t(udu, ua_ref[...])
    if early:
        moe = moe + early[1][...].astype(F32)
        dn2 = dn2 + early[0][:, :width].astype(F32)
        dgate = dgate + early[0][:, width:].astype(F32)
    m_ref[...] = moe.astype(BF)
    r_ref[:, :width] = dn2.astype(BF)
    r_ref[:, width:] = dgate.astype(BF)
    bd_ref, ad_ref, bg_ref, bu_ref, a_ref = sums
    bd_ref[...] += t_dot_k(low, cot)
    ad_ref[...] += t_dot_k(act_sum, down_back)
    bg_ref[...] += t_dot_k(zg, dg_sum)
    bu_ref[...] += t_dot_k(zu, du_sum)
    a_ref[...] += t_dot_k(n2, jnp.concatenate([gdu, udu], axis=1))


def experts_on(ids, experts, spare, t, cot, weights, w_two, first, low_two, down_b, down_at, prior, early=()):
    rows, width = cot.shape
    ff = down_at.shape[0]
    step = 256
    sd = jax.ShapeDtypeStruct
    whole = lambda a: pl.BlockSpec(a.shape, lambda i: (0, 0))
    by_row = lambda cols: pl.BlockSpec((step, cols), lambda i: (i, 0))
    column = lambda height, cols, at: pl.BlockSpec((height, cols), lambda i: (0, at))
    low_rows = low_two.shape[0]
    count = len(weights)
    flops = 2 * rows * width * ff * 7 * count
    outs = pl.pallas_call(
        functools.partial(expert_kernel, experts, count),
        grid=(rows // step,),
        in_specs=[pl.BlockSpec(memory_space=pltpu.SMEM), by_row(t.shape[1]), by_row(width)]
        + [pl.BlockSpec(w.shape, lambda i: (0, 0), pipeline_mode=pl.Buffered(1)) for w in weights]
        + [column(width, LANES, first), column(width, LANES, first + 1), column(low_rows, ff, 0), column(low_rows, ff, 1), whole(down_b), whole(down_at)]
        + [whole(p) for p in prior] + [by_row(e.shape[1]) for e in early],
        out_specs=[by_row(width + spare), by_row(width)] + [whole(p) for p in prior],
        out_shape=[sd((rows, width + spare), BF), sd((rows, width), BF)] + [sd(p.shape, F32) for p in prior],
        scratch_shapes=[pltpu.VMEM((step, width), F32), pltpu.VMEM((step, width), F32)],
        input_output_aliases={3 + count + 6 + i: 2 + i for i in range(len(prior))},
        compiler_params=pltpu.CompilerParams(vmem_limit_bytes=58 << 20),
        cost_estimate=pl.CostEstimate(flops=flops, bytes_accessed=24 << 20, transcendentals=rows * ff * count),
    )(ids, t, cot, *weights, w_two, w_two, low_two, low_two, down_b, down_at, *prior, *early)
    return outs[0], outs[1], outs[2:]


class Crossing:
    def __init__(self):
        self.n_ctx, self.n_tp = lax.axis_size("ctx"), lax.axis_size("tp")
        self.tp_at = lax.axis_index("tp")

    def pairs(self, by):
        return [(c, (c + by) % self.n_ctx) for c in range(self.n_ctx)]

    def half(self, block):
        if self.n_tp != 2:
            return block
        size = block.shape[0] // 2
        return lax.dynamic_slice_in_dim(block, self.tp_at * size, size, 0)

    def other_half(self, block):
        size = block.shape[0] // 2
        return lax.dynamic_slice_in_dim(block, (1 - self.tp_at) * size, size, 0)

    def joined(self, half):
        if self.n_tp != 2:
            return half
        other = lax.ppermute(half, "tp", [(0, 1), (1, 0)])
        size = half.shape[0]
        whole = lax.dynamic_update_slice_in_dim(jnp.zeros((2 * size,) + half.shape[1:], half.dtype), half, self.tp_at * size, 0)
        return lax.dynamic_update_slice_in_dim(whole, other, (1 - self.tp_at) * size, 0)

    def fetch(self, block):
        half = self.half(block)
        return [lax.ppermute(half, "ctx", self.pairs(by)) for by in range(1, self.n_ctx)]

    def summed_half(self, block):
        if self.n_tp != 2:
            return block.astype(F32)
        return self.half(block).astype(F32) + lax.ppermute(self.other_half(block), "tp", [(0, 1), (1, 0)]).astype(F32)

    def swapped(self, blocks):
        if self.n_tp != 2:
            return [jnp.zeros_like(b) for b in blocks]
        return [lax.ppermute(self.other_half(b), "tp", [(0, 1), (1, 0)]) for b in blocks]

    def halves_of_total(self, own, parts):
        found = self.summed_half(own)
        for part in parts:
            found = found + part.astype(F32)
        if self.n_tp != 2:
            found = lax.psum(found, "tp").astype(BF)
            size = found.shape[0] // 2
            return found[:size], found[size:], 0
        found = found.astype(BF)
        return found, lax.ppermute(found, "tp", [(0, 1), (1, 0)]), self.tp_at


def put_rows(pack, value, at, height):
    for f in range(pack.shape[0]):
        pack[f, pl.ds(at, height), :] = value[f * height : (f + 1) * height, :].astype(pack.dtype)


def put_cols(pack, value, at, height, first):
    for i in range(value.shape[1] // LANES):
        for f in range(pack.shape[0]):
            spot = pl.ds(pl.multiple_of(at + (first + i) * height, 8 if height % 16 else 16), height)
            pack[f, spot, :] = value[f * height : (f + 1) * height, i * LANES : (i + 1) * LANES].astype(pack.dtype)


def adapter_mask(chosen_ref):
    rows = chosen_ref.shape[0]
    return (lax.broadcasted_iota(jnp.int32, (rows, LANES), 1) // ADAPTER_RANK == chosen_ref[...]).astype(F32)


def qkv_back_kernel(n_tp, low_rows, share, tp_ref, dq_ref, dko_ref, dvo_ref, fb_ref, cos_ref, sin_ref, n1_ref, u_ref, chosen_ref, w_ref, lb_ref, dn1_ref, pack_ref, a_acc, b_acc):
    q_width, kv_width = dq_ref.shape[1], dko_ref.shape[1]
    ranks = LANES
    rows = dq_ref.shape[0]
    step = pl.program_id(0)
    mask = adapter_mask(chosen_ref)
    head = lax.broadcasted_iota(jnp.int32, (rows, LANES), 1) % HEAD_SIZE < HEAD_SIZE // 2

    def turned_back(v):
        swapped = jnp.where(head, pltpu.roll(v, LANES - HEAD_SIZE // 2, 1), pltpu.roll(v, HEAD_SIZE // 2, 1))
        return (v * cos_ref[...] - swapped * sin_ref[...]).astype(BF)

    dq = [turned_back(dq_ref[:, i : i + LANES]) for i in range(0, q_width, LANES)]
    dk = [turned_back(dko_ref[:, i : i + LANES] + fb_ref[:, i : i + LANES].astype(F32)) for i in range(0, kv_width, LANES)]
    dv = (dvo_ref[...] + fb_ref[:, kv_width:].astype(F32)).astype(BF)
    dq = jnp.concatenate(dq, axis=1)
    dk = jnp.concatenate(dk, axis=1) if len(dk) > 1 else dk[0]
    lows = []
    at = 0
    for d in (dq, dk, dv):
        lows.append((dot_t(d, lb_ref[:, at : at + d.shape[1]]) * mask).astype(BF))
        at += d.shape[1]
    lows = jnp.concatenate(lows, axis=1)
    dn1_ref[...] = dot_t(jnp.concatenate([dq, dk, dv, lows], axis=1), w_ref[...]).astype(BF)
    n1 = n1_ref[...]
    parts = [
        (a_acc, slice(0, 3 * ranks), t_dot_k(n1, lows)),
        (b_acc, slice(0, q_width), t_dot_k(u_ref[:, :ranks], dq)),
        (b_acc, slice(q_width, q_width + kv_width), t_dot_k(u_ref[:, ranks : 2 * ranks], dk)),
        (b_acc, slice(q_width + kv_width, q_width + 2 * kv_width), t_dot_k(u_ref[:, 2 * ranks :], dv)),
    ]

    @pl.when(step == 0)
    def _():
        for acc, cols, value in parts:
            acc[:, cols] = value

    @pl.when(step > 0)
    def _():
        for acc, cols, value in parts:
            acc[:, cols] += value

    @pl.when(step == pl.num_programs(0) - 1)
    def _():
        pack_ref[...] = jnp.zeros_like(pack_ref)
        at, col = 0, 0
        for i, cols in enumerate((q_width, kv_width, kv_width)):
            put_rows(pack_ref, a_acc[:, i * ranks : (i + 1) * ranks], at, share)
            at += share
            put_cols(pack_ref, b_acc[:, col : col + cols], at, low_rows, tp_ref[0] * (cols // LANES))
            at += cols * n_tp // LANES * low_rows
            col += cols


def qkv_back(n, n_tp, low_rows, share, tp_at, dq, dko, dvo, fb, cos, sin, n1, u3, chosen, w_one, low_one, height):
    rows, q_width = dq.shape
    width = n1.shape[1]
    step = 256
    by_row = lambda a: pl.BlockSpec((step, a.shape[1]), lambda i: (i, 0))
    whole = lambda a: pl.BlockSpec(a.shape, lambda i: (0, 0), pipeline_mode=pl.Buffered(1))
    sd = jax.ShapeDtypeStruct
    return pl.pallas_call(
        functools.partial(qkv_back_kernel, n_tp, low_rows, share),
        grid=(rows // step,),
        in_specs=[pl.BlockSpec(memory_space=pltpu.SMEM)] + [by_row(a) for a in (dq, dko, dvo, fb, cos, sin, n1, u3, chosen)] + [whole(w_one), whole(low_one)],
        out_specs=[pl.BlockSpec((step, width), lambda i: (i, 0)), pl.BlockSpec((n, height, LANES), lambda i: (0, 0, 0))],
        out_shape=[sd((rows, width), BF), sd((n, height, LANES), F32)],
        scratch_shapes=[pltpu.VMEM((width, 3 * LANES), F32), pltpu.VMEM((LANES, low_one.shape[1]), F32)],
        compiler_params=pltpu.CompilerParams(vmem_limit_bytes=50 << 20),
        cost_estimate=pl.CostEstimate(flops=4 * rows * width * w_one.shape[1], bytes_accessed=24 << 20, transcendentals=0),
    )(tp_at, dq, dko, dvo, fb, cos, sin, n1, u3, chosen, w_one, low_one)


def normed_rows(v, gain):
    return v * lax.rsqrt(jnp.mean(v * v, axis=1, keepdims=True) + norm_eps) * gain


def turned(v, cos, sin):
    head = lax.broadcasted_iota(jnp.int32, v.shape, 1) % HEAD_SIZE < HEAD_SIZE // 2
    swapped = jnp.where(head, pltpu.roll(v, LANES - HEAD_SIZE // 2, 1), pltpu.roll(v, HEAD_SIZE // 2, 1))
    return v * cos + swapped * sin


def kv_kernel(q_width, x_ref, chosen_ref, cos_ref, sin_ref, gain_ref, w_ref, low_ref, n1_ref, u_ref, kv_ref):
    kv_width = kv_ref.shape[1] // 2
    mask = adapter_mask(chosen_ref)
    n1 = normed_rows(x_ref[...].astype(F32), gain_ref[...]).astype(BF)
    n1_ref[...] = n1
    raw = dot(n1, w_ref[:, q_width:])
    lows = (raw[:, 2 * kv_width :] * jnp.concatenate([mask] * 3, axis=1)).astype(BF)
    u_ref[...] = lows
    key = raw[:, :kv_width] + dot(lows[:, LANES : 2 * LANES], low_ref[:, q_width : q_width + kv_width])
    for i in range(0, kv_width, LANES):
        kv_ref[:, i : i + LANES] = turned(key[:, i : i + LANES], cos_ref[...], sin_ref[...]).astype(BF)
    value = raw[:, kv_width : 2 * kv_width] + dot(lows[:, 2 * LANES :], low_ref[:, q_width + kv_width :])
    kv_ref[:, kv_width:] = value.astype(BF)


def q_kernel(n1_ref, u_ref, cos_ref, sin_ref, w_ref, low_ref, q_ref):
    q_width = q_ref.shape[1]
    q = dot(n1_ref[...], w_ref[:, :q_width]) + dot(u_ref[:, :LANES], low_ref[:, :q_width])
    for i in range(0, q_width, LANES):
        q_ref[:, i : i + LANES] = (turned(q[:, i : i + LANES], cos_ref[...], sin_ref[...]) * 0.125).astype(BF)


def out_kernel(o_ref, chosen_ref, w_ref, oa_ref, low_ref, part_ref, u_ref):
    q_width, width = o_ref.shape[1], part_ref.shape[1]
    ff2 = low_ref.shape[1] - 2 * width - LANES
    o = o_ref[...]
    u = (dot(o, oa_ref[...]) * adapter_mask(chosen_ref)).astype(BF)
    u_ref[...] = u
    part_ref[...] = (dot_t(o, w_ref[:, :q_width]) + dot(u, low_ref[:, ff2 : ff2 + width])).astype(BF)


def route_kernel(experts, q_width, x_ref, one_ref, other_ref, chosen_ref, routes_ref, gain_ref, w_ref, low_ref, h_ref, t_ref, u_ref):
    width = h_ref.shape[1]
    rows = h_ref.shape[0]
    h = x_ref[...].astype(F32) + (one_ref[...].astype(F32) + other_ref[...].astype(F32))
    h_ref[...] = h
    n2 = normed_rows(h, gain_ref[...]).astype(BF)
    t_ref[:, :width] = n2
    u = (dot(n2, w_ref[:, q_width : q_width + LANES]) * adapter_mask(chosen_ref)).astype(BF)
    u_ref[...] = u
    logits = dot(n2, w_ref[:, q_width + 3 * LANES : q_width + 4 * LANES]) + dot(u, low_ref[:, low_ref.shape[1] - LANES :])
    lane = lax.broadcasted_iota(jnp.int32, (rows, LANES), 1)
    selected = lane == routes_ref[:, 0:1]
    for k in range(1, routes_ref.shape[1]):
        selected = selected | (lane == routes_ref[:, k : k + 1])
    top = jnp.max(jnp.where(selected, logits, -jnp.inf), axis=1, keepdims=True)
    gates = jnp.where(selected, jnp.exp(jnp.where(selected, logits - top, 0.0)), 0.0)
    gates = gates / jnp.sum(gates, axis=1, keepdims=True)
    high = gates.astype(BF).astype(F32)
    extra = high + pltpu.roll(gates - high, experts, 1) + jnp.where(lane == 2 * experts, chosen_ref[...].astype(F32), 0.0)
    t_ref[:, width:] = extra.astype(BF)


def by_rows(kernel, step, rowed, whole, outs, flops):
    rows = rowed[0].shape[0]
    block = lambda cols: pl.BlockSpec((step, cols), lambda i: (i, 0))
    return pl.pallas_call(
        kernel,
        grid=(rows // step,),
        in_specs=[block(a.shape[1]) for a in rowed] + [pl.BlockSpec(a.shape, lambda i: (0, 0), pipeline_mode=pl.Buffered(1)) for a in whole],
        out_specs=[block(cols) for cols, kind in outs],
        out_shape=[jax.ShapeDtypeStruct((rows, cols), kind) for cols, kind in outs],
        compiler_params=pltpu.CompilerParams(vmem_limit_bytes=48 << 20),
        cost_estimate=pl.CostEstimate(flops=flops, bytes_accessed=1 << 20, transcendentals=0),
    )(*rowed, *whole)


def mid_back_kernel(n, n_tp, experts, share, low_rows, sel_ref, mine_ref, other_ref, h_ref, c_ref, t_ref, o_ref, ou_ref, ru_ref, chosen_ref, gain_ref,
                    w_ref, low_ref, oa_ref, bd_ref, ad_ref, bg_ref, bu_ref, agu_ref, dh_ref, do_ref, pack_ref, ar_acc, ao_acc, bo_acc, br_acc):
    width = h_ref.shape[1]
    q_width = o_ref.shape[1]
    ff = bg_ref.shape[1]
    spare = mine_ref.shape[1] - width
    step = pl.program_id(0)
    mask = adapter_mask(chosen_ref)
    picked = step == sel_ref[0]

    def fold(height, top):
        lane = lax.broadcasted_iota(jnp.int32, (height, LANES), 0)
        return ((lane % experts == lax.broadcasted_iota(jnp.int32, (height, LANES), 1)) & (lane < top)).astype(BF)

    back = jnp.where(picked, mine_ref[:, :width].astype(F32), other_ref[:, :width].astype(F32))
    tail = jnp.where(picked, mine_ref[:, width:].astype(F32), other_ref[:, width:].astype(F32)).astype(BF)
    dgate = dot(tail, fold(spare, 2 * experts * n_tp))
    gates = dot(t_ref[:, width:], fold(LANES, 2 * experts))
    n2 = t_ref[:, :width]
    router_a, router_w = w_ref[:, q_width : q_width + LANES], w_ref[:, q_width + 3 * LANES : q_width + 4 * LANES]
    out_b, router_b = low_ref[:, 2 * ff : 2 * ff + width], low_ref[:, 2 * ff + 2 * width :]
    dlog = (gates * (dgate - jnp.sum(gates * dgate, axis=1, keepdims=True))).astype(BF)
    rdu = (dot_t(dlog, router_b) * mask).astype(BF)
    dn2 = back + dot_t(dlog, router_w) + dot_t(rdu, router_a)
    h = h_ref[...]
    r = lax.rsqrt(jnp.mean(h * h, axis=1, keepdims=True) + norm_eps)
    gd = dn2 * gain_ref[...]
    dh = c_ref[...].astype(F32) + r * gd - h * (r * r * r * jnp.mean(gd * h, axis=1, keepdims=True))
    dh_ref[...] = dh
    dattn = dh.astype(BF)
    odu = (dot_t(dattn, out_b) * mask).astype(BF)
    do_ref[...] = (dot(dattn, w_ref[:, :q_width]) + dot_t(odu, oa_ref[...])).astype(BF)
    parts = [
        (ar_acc, t_dot_k(n2, rdu)),
        (ao_acc, t_dot_k(o_ref[...], odu)),
        (bo_acc, t_dot_k(ou_ref[...], dattn)),
        (br_acc, t_dot_k(ru_ref[...], dlog)),
    ]

    @pl.when(step == 0)
    def _():
        for acc, value in parts:
            acc[...] = value

    @pl.when(step > 0)
    def _():
        for acc, value in parts:
            acc[...] += value

    @pl.when(step == pl.num_programs(0) - 1)
    def _():
        pack_ref[...] = jnp.zeros_like(pack_ref)
        tp = sel_ref[1]
        first = (tp == 0).astype(F32)
        own = n // n_tp
        at = 0
        for k in range(own):
            pack_ref[tp * own + k, pl.ds(at, share), :] = ao_acc[k * share : (k + 1) * share, :].astype(pack_ref.dtype)
        at += share
        put_cols(pack_ref, bo_acc, at, low_rows, 0)
        at += width // LANES * low_rows
        ar_acc[...] = ar_acc[...] * first
        put_rows(pack_ref, ar_acc, at, share)
        at += share
        br_acc[...] = br_acc[...] * first
        put_cols(pack_ref, br_acc, at, low_rows, 0)
        at += low_rows
        for i, ref in enumerate((bg_ref, bu_ref)):
            put_rows(pack_ref, agu_ref[:, i * LANES : (i + 1) * LANES], at, share)
            at += share
            put_cols(pack_ref, ref, at, low_rows, tp * (ff // LANES))
            at += ff * n_tp // LANES * low_rows
        size = ad_ref.shape[0] // own
        for k in range(own):
            pack_ref[tp * own + k, pl.ds(at, size), :] = ad_ref[k * size : (k + 1) * size, :].astype(pack_ref.dtype)
        at += size
        put_cols(pack_ref, bd_ref, at, low_rows, 0)


def mid_back(n, n_tp, experts, share, low_rows, sel, mine, other, hidden, cot, carried, mixed, out_u, router_u, chosen, gain, w_two, low_two, out_a, sums, height):
    rows, width = hidden.shape
    q_width = mixed.shape[1]
    step = rows // 2
    sd = jax.ShapeDtypeStruct
    by_row = lambda a: pl.BlockSpec((step, a.shape[1]), lambda i: (i, 0))
    whole = lambda a: pl.BlockSpec(a.shape, lambda i: (0, 0), pipeline_mode=pl.Buffered(1))
    return pl.pallas_call(
        functools.partial(mid_back_kernel, n, n_tp, experts, share, low_rows),
        grid=(2,),
        in_specs=[pl.BlockSpec(memory_space=pltpu.SMEM), whole(mine), whole(other)]
        + [by_row(a) for a in (hidden, cot, carried, mixed, out_u, router_u, chosen)]
        + [whole(a) for a in (gain, w_two, low_two, out_a, *sums)],
        out_specs=[by_row(hidden), by_row(mixed), pl.BlockSpec((n, height, LANES), lambda i: (0, 0, 0))],
        out_shape=[sd((rows, width), F32), sd((rows, q_width), BF), sd((n, height, LANES), F32 if low_rows % 16 else BF)],
        scratch_shapes=[pltpu.VMEM((width, LANES), F32), pltpu.VMEM((q_width, LANES), F32), pltpu.VMEM((LANES, width), F32), pltpu.VMEM((LANES, LANES), F32)],
        compiler_params=pltpu.CompilerParams(vmem_limit_bytes=58 << 20),
        cost_estimate=pl.CostEstimate(flops=8 * rows * width * q_width, bytes_accessed=32 << 20, transcendentals=0),
    )(sel, mine, other, hidden, cot, carried, mixed, out_u, router_u, chosen, gain, w_two, low_two, out_a, *sums)


def reduce_kernel(n, pack_ref, side_ref, out_ref, side_out, side_in, side_snd, snd1, rcv1, acc, snd2, rcv2, acc2, snd3, rcv3, fin, sems, send3, recv3):
    me = lax.axis_index("fsdp")
    ctx = lax.axis_index("ctx")
    tp = lax.axis_index("tp")
    half = pack_ref.shape[1] // 2
    part = half // 2
    barrier = pltpu.get_barrier_semaphore()
    pl.semaphore_signal(barrier, inc=1, device_id={"tp": 1 - tp}, device_id_type=MESH)
    pl.semaphore_signal(barrier, inc=1, device_id={"ctx": 1 - ctx}, device_id_type=MESH)
    for k in range(1, n):
        pl.semaphore_signal(barrier, inc=1, device_id={"fsdp": (me + k) % n}, device_id_type=MESH)
    snd1[...] = pack_ref[:, pl.ds(pl.multiple_of((1 - tp) * half, 16), half), :].astype(BF)
    pl.semaphore_wait(barrier, n + 1)

    def swap(src, dst, i, to):
        copy = pltpu.make_async_remote_copy(src_ref=src, dst_ref=dst, send_sem=sems.at[0, i], recv_sem=sems.at[1, i], device_id=to, device_id_type=MESH)
        copy.start()
        return copy

    copy = swap(snd1, rcv1, 0, {"tp": 1 - tp})
    side = swap(side_ref, side_in.at[0], 4, {"tp": 1 - tp})
    copy.wait()
    acc[...] = pack_ref[:, pl.ds(pl.multiple_of(tp * half, 16), half), :] + rcv1[...].astype(F32)
    snd2[...] = acc[:, pl.ds(pl.multiple_of((1 - ctx) * part, 16), part), :].astype(BF)
    copy = swap(snd2, rcv2, 1, {"ctx": 1 - ctx})
    side.wait()
    side_snd[...] = (side_ref[...].astype(F32) + side_in[0].astype(F32)).astype(BF)
    side = swap(side_snd, side_in.at[1], 5, {"ctx": 1 - ctx})
    copy.wait()
    acc2[...] = acc[:, pl.ds(pl.multiple_of(ctx * part, 16), part), :] + rcv2[...].astype(F32)
    snd3[...] = acc2[...].astype(BF)

    def ship(k):
        to = (me + k) % n
        return pltpu.make_async_remote_copy(
            src_ref=snd3.at[to], dst_ref=rcv3.at[me], send_sem=send3.at[k], recv_sem=recv3.at[k], device_id={"fsdp": to}, device_id_type=MESH
        )

    def came(k):
        return pltpu.make_async_remote_copy(
            src_ref=snd3.at[me], dst_ref=rcv3.at[(me + n - k) % n], send_sem=send3.at[k], recv_sem=recv3.at[k],
            device_id={"fsdp": (me + k) % n}, device_id_type=MESH,
        )

    for k in range(1, n):
        ship(k).start()
    total = acc2[me]
    for k in range(1, n):
        came(k).wait_recv()
        total = total + rcv3[(me + n - k) % n].astype(F32)
    for k in range(1, n):
        ship(k).wait_send()
    spot = tp * 2 + ctx
    fin[spot] = total.astype(BF)
    copy = swap(fin.at[spot], fin.at[spot], 2, {"ctx": 1 - ctx})
    copy.wait()
    both = fin.at[pl.ds(tp * 2, 2)]
    copy = swap(both, both, 3, {"tp": 1 - tp})
    copy.wait()
    for i in range(4):
        out_ref[pl.ds(i * part, part), :] = fin[i].astype(F32)
    side.wait()
    side_out[...] = side_snd[...].astype(F32) + side_in[1].astype(F32)


def reduce_pack(pack, side, collective_id):
    n, height = pack.shape[:2]
    if lax.axis_size("tp") != 2 or lax.axis_size("ctx") != 2 or height % 64 or side.shape[0] % 16:
        mine = lax.psum_scatter(pack.astype(BF), "fsdp", scatter_dimension=0, tiled=False)
        return lax.psum(mine, ("ctx", "tp")).astype(F32), lax.psum(side, ("ctx", "tp")).astype(F32)
    half, part = height // 2, height // 4
    vm = pltpu.VMEM
    dma = pltpu.SemaphoreType.DMA
    return pl.pallas_call(
        functools.partial(reduce_kernel, n),
        in_specs=[pl.BlockSpec(memory_space=vm)] * 2,
        out_specs=[pl.BlockSpec(memory_space=vm)] * 2,
        out_shape=[jax.ShapeDtypeStruct((height, LANES), F32), jax.ShapeDtypeStruct(side.shape, F32)],
        scratch_shapes=[
            vm((2,) + side.shape, BF), vm(side.shape, BF), vm((n, half, LANES), BF), vm((n, half, LANES), BF), vm((n, half, LANES), F32),
            vm((n, part, LANES), BF), vm((n, part, LANES), BF), vm((n, part, LANES), F32),
            vm((n, part, LANES), BF), vm((n, part, LANES), BF), vm((4, part, LANES), BF),
            dma((2, 6)), dma((n,)), dma((n,)),
        ],
        compiler_params=pltpu.CompilerParams(collective_id=collective_id, has_side_effects=True, vmem_limit_bytes=48 << 20),
    )(pack, side)


def tp_sum(value):
    if lax.axis_size("tp") != 2:
        return lax.psum(value, "tp")
    return value + lax.ppermute(value, "tp", [(0, 1), (1, 0)])


def on_device(
    tokens, out_cotangent, lengths, adapter_of_doc, routes, attn_gain, ffn_gain,
    w_query, key_matrix, value_matrix, w_out, w_router, w_gate, w_up, w_down,
    a_query, b_query, a_key, key_second_factor, a_value, value_second_factor,
    a_out, b_out, a_router, b_router, a_gate, b_gate, a_up, b_up, a_down, b_down,
):
    rows, width = tokens.shape
    n = lax.axis_size("fsdp")
    n_tp = lax.axis_size("tp")
    tp_at = lax.axis_index("tp")
    ctx_at = lax.axis_index("ctx")
    group = rows * lax.axis_size("ctx")
    q_width = w_query.shape[1]
    kv_width = key_matrix.shape[1]
    ff_width = w_gate.shape[2]
    local_experts = w_gate.shape[0]
    experts = w_router.shape[1]
    ranks = a_query.shape[1]
    share = w_query.shape[0]
    low_rows = b_query.shape[0]

    pad = ((0, 0), (0, LANES - experts))
    one, low_one = gather_packs(
        [
            [(a, a.shape[1]) for a in (w_query, key_matrix, value_matrix, a_query, a_key, a_value)],
            [(b_query, q_width), (key_second_factor, kv_width), (value_second_factor, kv_width)],
        ],
        (),
        0,
    )
    qkv = q_width + 2 * kv_width
    w_one = one.reshape(n * share, -1)
    low_one = low_one.reshape(n * low_rows, -1)

    ends = jnp.cumsum(lengths[0])
    starts = ends - lengths[0]
    place = jnp.arange(group, dtype=jnp.int32)
    doc = jnp.sum((place[:, None] >= ends[None, :]).astype(jnp.int32), axis=1)
    picked = (doc[:, None] == jnp.arange(lengths.shape[1], dtype=jnp.int32)[None, :]).astype(jnp.int32)
    begin = jnp.sum(picked * starts[None, :], axis=1)
    chosen = jnp.sum(picked * adapter_of_doc[0][None, :], axis=1)
    start = ctx_at * rows
    query_index = start + jnp.arange(rows, dtype=jnp.int32)
    begin_local = lax.dynamic_slice_in_dim(begin, start, rows)
    chosen_local = lax.dynamic_slice_in_dim(chosen, start, rows)
    freq = 10000.0 ** (-jnp.arange(HEAD_SIZE // 2, dtype=F32) / (HEAD_SIZE // 2))
    angles = (query_index - begin_local).astype(F32)[:, None] * freq[None, :]
    cosine, sine = jnp.cos(angles), jnp.sin(angles)
    cosine_wide = jnp.tile(cosine, (1, 2 * LANES // HEAD_SIZE))
    sine_wide = jnp.tile(jnp.concatenate([-sine, sine], axis=1), (1, LANES // HEAD_SIZE))
    chosen_col = chosen_local[:, None]
    gain_one, gain_two = attn_gain[None, :], ffn_gain[None, :]
    normed, low_u, kv = by_rows(
        functools.partial(kv_kernel, q_width), 256, (tokens, chosen_col, cosine_wide, sine_wide), (gain_one, w_one, low_one),
        ((width, BF), (3 * ranks, BF), (2 * kv_width, BF)), 2 * rows * width * (w_one.shape[1] - q_width),
    )
    cross = Crossing()
    outer, inner = levels(n)
    me = lax.axis_index("fsdp")
    ring = [(i, (i + inner) % n) for i in range(n)]
    turns = [[(i, i // inner * inner + (i % inner + dj) % inner) for i in range(n)] for dj in range(1, inner)]
    local = local_experts // cross.n_ctx
    mine = [lax.dynamic_slice_in_dim(a, ctx_at * local, local, 0) for a in (w_gate, w_up, w_down)]
    block = jnp.concatenate([mine[0], mine[1], jnp.swapaxes(mine[2], 1, 2)], axis=2)
    brought = {(0, 0): block}

    def bring(do, after):
        last = [brought[(do, 0)]] + [brought[(do - 1, dj)] for dj in range(1, inner) if do]
        last, after = lax.optimization_barrier((last, after))
        brought[(do, 0)] = last[0]
        for dj, value in zip(range(1, inner), last[1:]):
            brought[(do - 1, dj)] = value
        if do + 1 < outer:
            brought[(do + 1, 0)] = lax.ppermute(last[0], "fsdp", ring)
        for dj in range(1, inner):
            brought[(do, dj)] = lax.ppermute(last[0], "fsdp", turns[dj - 1])
        return after

    one = bring(0, one)
    (query_state,) = by_rows(
        q_kernel, 256, (normed, low_u, cosine_wide, sine_wide), (w_one, low_one), ((q_width, BF),), 2 * rows * width * q_width
    )
    w_out, w_router, b_router, query_state = lax.optimization_barrier((w_out, w_router, b_router, query_state))
    two, low_two, down_a, far = gather_packs(
        [
            [(a, a.shape[1]) for a in (w_out.T, a_router, a_gate, a_up, jnp.pad(w_router, pad), a_out)],
            [(b_gate, ff_width), (b_up, ff_width), (b_out, width), (b_down, width), (jnp.pad(b_router, pad), LANES)],
            [(a_down, ranks)],
        ],
        (kv,),
        1,
    )
    cot = lax.optimization_barrier((out_cotangent, two))[0]
    cot_halves = cross.fetch(cot)
    far = bring(1, far)
    w_two = two.reshape(n * share, -1)
    low_two = low_two.reshape(n * low_rows, -1)
    down_b = low_two[:, 2 * ff_width + width : 2 * ff_width + 2 * width]
    out_a = lax.dynamic_slice_in_dim(w_two[:, q_width + 4 * ranks : q_width + 5 * ranks], tp_at * q_width, q_width, 0)
    down_at = lax.dynamic_slice_in_dim(down_a.reshape(-1, ranks), tp_at * ff_width, ff_width, 0)
    begin_row = begin_local[None, :]
    start_at = jnp.reshape(start, (1,)).astype(jnp.int32)
    mixed_heads, log_total = attend(query_state, kv, far, begin_row, start_at)
    mixed_heads = bring(2, mixed_heads)
    cot_halves, mixed_heads = lax.optimization_barrier((cot_halves, mixed_heads))
    attn_part, out_u = by_rows(
        out_kernel, 256, (mixed_heads, chosen_col), (w_two, out_a, low_two), ((width, BF), (ranks, BF)), 0
    )
    if n_tp == 2:
        attn_other = lax.ppermute(attn_part, "tp", [(0, 1), (1, 0)])
    else:
        attn_part, attn_other = lax.psum(attn_part.astype(F32), "tp"), jnp.zeros_like(attn_part)
    spare = -(-2 * experts * n_tp // LANES) * LANES
    hidden, carried, router_u = by_rows(
        functools.partial(route_kernel, experts, q_width), 256, (tokens, attn_part, attn_other, chosen_col, routes), (gain_two, w_two, low_two),
        ((width, F32), (width + LANES, BF), (ranks, BF)), 0,
    )
    halves = cross.fetch(carried)
    early = [(0, 0), (1, 0)] + [(0, dj) for dj in range(1, inner)] + [(2, 0)] + [(1, dj) for dj in range(1, inner)]
    late = [(do, 0) for do in range(3, outer)] + [(do, dj) for do in range(2, outer) for dj in range(1, inner)]

    def weights_of(keys):
        ids = [((me // inner + outer - do) % outer * inner + (me % inner + inner - dj) % inner) * local_experts + ctx_at * local + j for do, dj in keys for j in range(local)]
        return jnp.stack(ids + [tp_at * 2 * experts]).astype(jnp.int32), [brought[k][j] for k in keys for j in range(local)]

    sums = [jnp.zeros(shape, F32) for shape in ((ranks, width), (ff_width, ranks), (ranks, ff_width), (ranks, ff_width), (width, 2 * ranks))]
    at = q_width // LANES + 1
    work = [(carried, cot)] + [(None, None)] * (cross.n_ctx - 1)
    partial = []
    ids, weights = weights_of(early)
    for by in range(cross.n_ctx):
        if by:
            work[by] = (cross.joined(halves[by - 1]), cross.joined(cot_halves[by - 1]))
        r, m, sums = experts_on(ids, experts, spare, *work[by], weights, w_two, at, low_two, down_b, down_at, sums)
        if by == 0:
            for do in range(3, outer):
                r = bring(do, r)
            halves, cot_halves, r = lax.optimization_barrier((halves, cot_halves, r))
        partial.append((r, m))
    ids, weights = weights_of(late)
    back_parts, moe_parts = [], []
    for by in list(range(1, cross.n_ctx)) + [0]:
        r, m, sums = experts_on(ids, experts, spare, *work[by], weights, w_two, at, low_two, down_b, down_at, sums, partial[by])
        moe_parts.append(m)
        if by:
            half = cross.summed_half(r).astype(BF)
            half, carried = lax.optimization_barrier((half, work[0][0]))
            work[0] = (carried, cot)
            back_parts.append(lax.ppermute(half, "ctx", cross.pairs(-by)))
    r, back_parts = lax.optimization_barrier((r, back_parts))
    mine_half, other, first = cross.halves_of_total(r, back_parts)
    swapped = cross.swapped(moe_parts)
    early_shapes = [
        (share, ranks), (low_rows, width), (share, ranks), (low_rows, experts), (share, ranks), (low_rows, ff_width * n_tp),
        (share, ranks), (low_rows, ff_width * n_tp), (a_down.shape[0], ranks), (low_rows, width),
    ]
    height = sum(-(-cols // LANES) * tall for tall, cols in early_shapes)
    sel = jnp.stack([jnp.asarray(first, jnp.int32), tp_at.astype(jnp.int32)])
    dhidden, dmixed, early_pack = mid_back(
        n, n_tp, experts, share, low_rows, sel, mine_half, other, hidden, cot, carried, mixed_heads, out_u, router_u,
        chosen_col, gain_two, w_two, low_two, out_a, sums, height,
    )
    early_pack, dmixed, swapped = lax.optimization_barrier((early_pack.astype(BF), dmixed, swapped))
    moe_halves = [cross.half(p).astype(F32) + q.astype(F32) for p, q in zip(moe_parts, swapped)]
    moe_got = [lax.ppermute(p.astype(BF), "ctx", cross.pairs(-by)) for by, p in zip(range(1, cross.n_ctx), moe_halves)]
    early_sum = lax.psum_scatter(early_pack, "fsdp", scatter_dimension=0, tiled=False)
    dquery, dkey_own, dvalue_own, dkey_far, dvalue_far = attend_back(
        query_state, kv, far, begin_row, start_at, mixed_heads, dmixed, log_total
    )
    moe_got, dquery = lax.optimization_barrier((moe_got, dquery))
    moe = moe_halves[-1]
    for part in moe_got:
        moe = moe + part.astype(F32)
    moe = cross.joined(moe.astype(BF)).astype(F32) if n_tp == 2 else lax.psum(moe, "tp")
    output = (hidden + moe).astype(BF)
    far_back = lax.ppermute(
        jnp.concatenate([dkey_far, dvalue_far], axis=1),
        "ctx",
        [(i + 1, i) for i in range(lax.axis_size("ctx") - 1)],
    )
    height = 3 * share + low_rows * n_tp * qkv // LANES
    dn1, pack = qkv_back(
        n, n_tp, low_rows, share, jnp.reshape(tp_at, (1,)).astype(jnp.int32), dquery, dkey_own, dvalue_own, far_back,
        cosine_wide, sine_wide, normed, low_u, chosen_col, w_one, low_one, height,
    )
    early_sum, dn1, pack = lax.optimization_barrier((early_sum, dn1, pack))
    late, early_sum = reduce_pack(pack, early_sum, 2)
    dn1 = tp_sum(dn1.astype(F32)) if n_tp != 2 else dn1.astype(F32) + lax.ppermute(dn1, "tp", [(0, 1), (1, 0)]).astype(F32)
    grad_tokens = (dhidden + norm_back(tokens.astype(F32), attn_gain, dn1)).astype(BF)

    def unpack(mine, shapes):
        found = []
        at = 0
        for height, cols in shapes:
            count = -(-cols // LANES)
            piece = mine[at : at + count * height].reshape(count, height, LANES).transpose(1, 0, 2).reshape(height, count * LANES)
            found.append(piece[:, :cols])
            at += count * height
        return found

    first_shapes = [(share, ranks), (low_rows, q_width * n_tp), (share, ranks), (low_rows, kv_width * n_tp), (share, ranks), (low_rows, kv_width * n_tp)]
    final = unpack(late, first_shapes) + unpack(early_sum, early_shapes)
    return (output, grad_tokens, *final)


def solution(mesh):
    both = P(("fsdp", "ctx"), None)
    split = P("fsdp", None)
    placed = (
        both, both, split, split, both, P(), P(),
        P("fsdp", "tp"), P("fsdp", "tp"), P("fsdp", "tp"), P("tp", "fsdp"), split,
        P("fsdp", None, "tp"), P("fsdp", None, "tp"), P("fsdp", "tp", None),
    ) + (split,) * 16
    return jax.shard_map(
        on_device, mesh=mesh, in_specs=placed, out_specs=(both, both) + (split,) * 16, check_vma=False
    )
```

```python
import functools

import jax
import jax.numpy as jnp
from jax import lax
from jax.experimental import pallas as pl
from jax.experimental.pallas import tpu as pltpu
from jax.sharding import PartitionSpec as P

HEAD_SIZE = 64
ADAPTER_RANK = 16
LANES = 128
norm_eps = 1e-05
BF = jnp.bfloat16
F32 = jnp.float32


MESH = pl.DeviceIdType.MESH


def dot(left, right, dims=((1,), (0,)), precision=None):
    return lax.dot_general(left, right, (dims, ((), ())), preferred_element_type=F32, precision=precision)


def dot_t(left, right):
    return dot(left, right, ((1,), (1,)))


def t_dot(left, right):
    return dot(left, right, ((0,), (0,)))


def rms_norm(values, gain):
    return values * lax.rsqrt(jnp.mean(values * values, axis=-1, keepdims=True) + norm_eps) * gain


def norm_back(values, gain, grad):
    unused, pull = jax.vjp(lambda inner: rms_norm(inner, gain), values)
    return pull(grad)[0]


def levels(n):
    outer = 4 if n % 4 == 0 else n
    return outer, n // outer


def fill_bias(bias, start_ref, begin_ref, rows):
    step = rows // 3
    for at in range(0, 2 * rows, step):
        key = start_ref[0] - rows + at + lax.broadcasted_iota(jnp.int32, (step, rows), 0)
        query = start_ref[0] + lax.broadcasted_iota(jnp.int32, (step, rows), 1)
        ok = (key <= query) & (key >= begin_ref[...]) & (key >= 0)
        bias[pl.ds(at, step), :] = jnp.where(ok, 0.0, -1e30)


def split_heads(ref, out, count, rows, at=0):
    for h in range(count):
        out[h, pl.ds(at, rows), :] = ref[:, h * HEAD_SIZE : (h + 1) * HEAD_SIZE]


def attend_kernel(group, q_blocks, start_ref, begin_ref, q_ref, ko_ref, vo_ref, kf_ref, vf_ref, o_ref, lse_ref, bias, ks, vts, qs, ots):
    rows = q_ref.shape[0]
    width = rows // q_blocks
    heads = 2 * group
    @pl.when(pl.program_id(0) == 0)
    def _():
        fill_bias(bias, start_ref, begin_ref, rows)
    split_heads(kf_ref, ks, 2, rows, 0)
    split_heads(ko_ref, ks, 2, rows, rows)
    split_heads(q_ref, qs, heads, rows, 0)
    vts[:, pl.ds(0, rows)] = vf_ref[...].astype(F32).T.astype(BF)
    vts[:, pl.ds(rows, rows)] = vo_ref[...].astype(F32).T.astype(BF)
    for b in range(q_blocks):
        keys = rows + (b + 1) * width
        def one(h, _):
            g = h // group
            s = dot_t(ks[g, pl.ds(0, keys), :], qs[h, pl.ds(b * width, width), :]) + bias[pl.ds(0, keys), pl.ds(b * width, width)]
            top = jnp.max(s, axis=0, keepdims=True)
            p = jnp.exp(s - top)
            total = jnp.sum(p, axis=0, keepdims=True)
            lse_ref[0, pl.ds(h, 1), pl.ds(b * width, width)] = top + jnp.log(total)
            vt = vts[pl.ds(pl.multiple_of(g * HEAD_SIZE, HEAD_SIZE), HEAD_SIZE), pl.ds(0, keys)]
            o = dot(vt, p.astype(BF)) / total
            ots[pl.ds(pl.multiple_of(h * HEAD_SIZE, HEAD_SIZE), HEAD_SIZE), pl.ds(b * width, width)] = o
            return 0
        lax.fori_loop(0, heads, one, 0)
    for j in range(group):
        o_ref[:, j * LANES : (j + 1) * LANES] = ots[pl.ds(j * LANES, LANES), :].T.astype(BF)


def attend(q, kv, far, begin, start, q_blocks=3):
    rows, q_width = q.shape
    kv_width = kv.shape[1] // 2
    pairs = kv_width // LANES
    group = q_width // kv_width
    spec = lambda off: pl.BlockSpec((rows, LANES), lambda i: (0, i + off))
    return pl.pallas_call(
        functools.partial(attend_kernel, group, q_blocks),
        grid=(pairs,),
        in_specs=[pl.BlockSpec(memory_space=pltpu.SMEM), pl.BlockSpec((1, rows), lambda i: (0, 0)),
                  pl.BlockSpec((rows, group * LANES), lambda i: (0, i)), spec(0), spec(pairs), spec(0), spec(pairs)],
        out_specs=[pl.BlockSpec((rows, group * LANES), lambda i: (0, i)), pl.BlockSpec((1, 8, rows), lambda i: (i, 0, 0))],
        out_shape=[jax.ShapeDtypeStruct((rows, q_width), BF), jax.ShapeDtypeStruct((pairs, 8, rows), F32)],
        scratch_shapes=[pltpu.VMEM((2 * rows, rows), F32), pltpu.VMEM((2, 2 * rows, HEAD_SIZE), BF), pltpu.VMEM((LANES, 2 * rows), BF),
                        pltpu.VMEM((2 * group, rows, HEAD_SIZE), BF), pltpu.VMEM((2 * group * HEAD_SIZE, rows), F32)],
        compiler_params=pltpu.CompilerParams(vmem_limit_bytes=50 << 20),
        cost_estimate=pl.CostEstimate(flops=8 * rows * rows * q_width, bytes_accessed=8 << 20, transcendentals=2 * rows * rows * 12),
    )(start, begin, q, kv, kv, far, far)


def attend_back_kernel(group, q_blocks, far, *refs):
    if far:
        start_ref, begin_ref, q_ref, k_ref, v_ref, o_ref, do_ref, lse_ref = refs[:8]
        dq_far = None
    else:
        start_ref, begin_ref, q_ref, k_ref, v_ref, o_ref, do_ref, lse_ref, dq_far = refs[:9]
    dq_ref, dk_ref, dv_ref, bias, ks, vs, kts, qs, dos, dqts, dks, dvs, deltas = refs[-13:]
    rows = q_ref.shape[0]
    width = rows // q_blocks
    heads = 2 * group

    @pl.when(pl.program_id(0) == 0)
    def _():
        first = start_ref[0] - rows if far else start_ref[0]
        for at in range(0, rows, width):
            key = first + at + lax.broadcasted_iota(jnp.int32, (width, rows), 0)
            query = start_ref[0] + lax.broadcasted_iota(jnp.int32, (width, rows), 1)
            ok = (key <= query) & (key >= begin_ref[...]) & (key >= 0)
            bias[pl.ds(at, width), :] = jnp.where(ok, 0.0, -1e30)

    split_heads(k_ref, ks, 2, rows, 0)
    split_heads(v_ref, vs, 2, rows, 0)
    split_heads(q_ref, qs, heads, rows, 0)
    split_heads(do_ref, dos, heads, rows, 0)
    kts[...] = k_ref[...].astype(F32).T.astype(BF)
    cols = heads * HEAD_SIZE
    pick = (
        lax.broadcasted_iota(jnp.int32, (8, cols), 1) // HEAD_SIZE == lax.broadcasted_iota(jnp.int32, (8, cols), 0)
    ).astype(F32)
    prod = o_ref[...].astype(F32) * do_ref[...].astype(F32)
    deltas[...] = dot(pick, prod, ((1,), (1,)), lax.Precision.HIGHEST)
    dks[...] = jnp.zeros_like(dks)
    dvs[...] = jnp.zeros_like(dvs)
    for b in range(q_blocks):
        keys = rows if far else (b + 1) * width

        def one(h, _):
            g = h // group
            at = pl.ds(b * width, width)
            qb = qs[h, at, :]
            dob = dos[h, at, :]
            s = dot_t(ks[g, pl.ds(0, keys), :], qb) + bias[pl.ds(0, keys), at]
            p = jnp.exp(s - lse_ref[0, pl.ds(h, 1), at])
            dp = dot_t(vs[g, pl.ds(0, keys), :], dob)
            ds = (p * (dp - deltas[pl.ds(h, 1), at])).astype(BF)
            dvs[g, pl.ds(0, keys), :] += dot(p.astype(BF), dob)
            dks[g, pl.ds(0, keys), :] += dot(ds, qb)
            kt = kts[pl.ds(pl.multiple_of(g * HEAD_SIZE, HEAD_SIZE), HEAD_SIZE), pl.ds(0, keys)]
            dqts[pl.ds(pl.multiple_of(h * HEAD_SIZE, HEAD_SIZE), HEAD_SIZE), at] = dot(kt, ds) * 0.125
            return 0

        lax.fori_loop(0, heads, one, 0)
    for j in range(group):
        at = slice(j * LANES, (j + 1) * LANES)
        part = dqts[pl.ds(j * LANES, LANES), :].T
        dq_ref[:, at] = part if far else part + dq_far[:, at]
    for g in range(2):
        at = slice(g * HEAD_SIZE, (g + 1) * HEAD_SIZE)
        dk_ref[:, at] = dks[g].astype(dk_ref.dtype)
        dv_ref[:, at] = dvs[g].astype(dv_ref.dtype)


def attend_back(q, keys, begin, start, o, do, lse, dq_far=None, q_blocks=3):
    far = dq_far is None
    rows, q_width = q.shape
    kv_width = keys.shape[1] // 2
    pairs = kv_width // LANES
    group = q_width // kv_width
    spec = lambda off: pl.BlockSpec((rows, LANES), lambda i: (0, i + off))
    wide = pl.BlockSpec((rows, group * LANES), lambda i: (0, i))
    sd = jax.ShapeDtypeStruct
    kind = BF if far else F32
    vm = pltpu.VMEM
    return pl.pallas_call(
        functools.partial(attend_back_kernel, group, q_blocks, far),
        grid=(pairs,),
        in_specs=[pl.BlockSpec(memory_space=pltpu.SMEM), pl.BlockSpec((1, rows), lambda i: (0, 0)), wide, spec(0), spec(pairs), wide, wide]
        + [pl.BlockSpec((1, 8, rows), lambda i: (i, 0, 0))] + ([] if far else [wide]),
        out_specs=[wide, spec(0), spec(0)],
        out_shape=[sd((rows, q_width), F32), sd((rows, kv_width), kind), sd((rows, kv_width), kind)],
        scratch_shapes=[
            vm((rows, rows), F32), vm((2, rows, HEAD_SIZE), BF), vm((2, rows, HEAD_SIZE), BF), vm((LANES, rows), BF),
            vm((2 * group, rows, HEAD_SIZE), BF), vm((2 * group, rows, HEAD_SIZE), BF), vm((2 * group * HEAD_SIZE, rows), F32),
            vm((2, rows, HEAD_SIZE), F32), vm((2, rows, HEAD_SIZE), F32), vm((8, rows), F32),
        ],
        compiler_params=pltpu.CompilerParams(vmem_limit_bytes=56 << 20),
        cost_estimate=pl.CostEstimate(flops=12 * rows * rows * q_width, bytes_accessed=16 << 20, transcendentals=rows * rows * 12),
    )(start, begin, q, keys, keys, o, do, lse, *(() if far else (dq_far,)))


def slab_of(rows, ctx):
    edge = 3 * rows // 8 // 16 * 16
    take = rows - edge
    return pl.ds(pl.multiple_of(ctx * edge, 16), take), pl.ds(pl.multiple_of(ctx * take, 16), edge)


def gather_kernel(n, count, extra, *refs):
    total = count + extra
    ins, outs = refs[:total], refs[total : 2 * total]
    own_sem, z_send, z_recv, y_send, y_recv, x_send, x_recv, extra_sem = refs[2 * total :]
    outer, inner = levels(n)
    me = lax.axis_index("fsdp")
    ctx = lax.axis_index("ctx")
    z, y = me // inner, me % inner
    right = (z + 1) % outer * inner + y
    left = (z + outer - 1) % outer * inner + y

    def shard(do, dj):
        return (z + outer - do) % outer * inner + (y + inner - dj) % inner

    own = [pltpu.make_async_copy(ins[a], outs[a].at[me], own_sem.at[a]) for a in range(count)]
    barrier = pltpu.get_barrier_semaphore()
    peers = [right, left] + [z * inner + (y + dj) % inner for dj in range(1, inner)]
    for peer in peers:
        pl.semaphore_signal(barrier, inc=1, device_id={"fsdp": peer}, device_id_type=MESH)
    pl.semaphore_signal(barrier, inc=1, device_id={"ctx": 1 - ctx}, device_id_type=MESH)
    pl.semaphore_wait(barrier, len(peers) + 1)

    def cut(a):
        return 3 * outs[a].shape[1] // 8 >= 16

    def taken(a, k):
        if not cut(a):
            return outs[a].at[k]
        return outs[a].at[k, slab_of(outs[a].shape[1], ctx)[0]]

    def remote(part, send, recv, to, src=None):
        src = part if src is None else src
        return pltpu.make_async_remote_copy(src_ref=src, dst_ref=part, send_sem=send, recv_sem=recv, device_id=to, device_id_type=MESH)

    def from_own(a):
        return ins[a].at[slab_of(ins[a].shape[0], ctx)[0]] if cut(a) else ins[a]

    def z_copy(a, k):
        src = from_own(a) if k == 1 else None
        return remote(taken(a, shard(k - 1, 0)), z_send.at[a, k - 1], z_recv.at[a, k - 1], {"fsdp": right}, src)

    def y_copy(a, do, dj):
        to = {"fsdp": z * inner + (y + dj) % inner}
        src = from_own(a) if do == 0 else None
        return remote(taken(a, shard(do, 0)), y_send.at[a, do, dj - 1], y_recv.at[a, do, dj - 1], to, src)

    def x_copy(a, do, dj):
        part = outs[a].at[shard(do, dj), slab_of(outs[a].shape[1], ctx)[1]]
        return remote(part, x_send.at[a, do, dj], x_recv.at[a, do, dj], {"ctx": 1 - ctx})

    started = []

    def go(copy):
        copy.start()
        started.append(copy)

    straight = [
        pltpu.make_async_remote_copy(
            src_ref=ins[count + i], dst_ref=outs[count + i], send_sem=extra_sem.at[0, i], recv_sem=extra_sem.at[1, i],
            device_id={"ctx": 1 - ctx}, device_id_type=MESH,
        )
        for i in range(extra)
    ]
    for c in straight:
        c.start()
    for a in range(count):
        go(z_copy(a, 1))
        for dj in range(1, inner):
            go(y_copy(a, 0, dj))
    for c in own:
        c.start()
    for do in range(1, outer + 1):
        for a in range(count):
            if do < outer:
                z_copy(a, do).wait_recv()
                if do + 1 < outer:
                    go(z_copy(a, do + 1))
                for dj in range(1, inner):
                    go(y_copy(a, do, dj))
                if cut(a):
                    go(x_copy(a, do, 0))
        for a in range(count):
            for dj in range(1, inner):
                y_copy(a, do - 1, dj).wait_recv()
                if cut(a):
                    go(x_copy(a, do - 1, dj))
    for a in range(count):
        if cut(a):
            for do in range(outer):
                for dj in range(inner):
                    if do or dj:
                        x_copy(a, do, dj).wait_recv()
    for c in started:
        c.wait_send()
    for c in straight:
        c.wait()
    for c in own:
        c.wait()


def gather_packs(packs, extra, collective_id):
    n = lax.axis_size("fsdp")
    outer, inner = levels(n)
    count = len(packs)
    tp_at = lax.axis_index("tp")
    arrays = []
    for parts in packs:
        cut = [a if cols == a.shape[1] else lax.dynamic_slice_in_dim(a, tp_at * cols, cols, 1) for a, cols in parts]
        arrays.append(jnp.concatenate(cut, axis=1) if len(cut) > 1 else cut[0])
    dma = pltpu.SemaphoreType.DMA
    anywhere = pl.BlockSpec(memory_space=pl.ANY)
    side = max(inner - 1, 1)
    return pl.pallas_call(
        functools.partial(gather_kernel, n, count, len(extra)),
        in_specs=[anywhere] * (count + len(extra)),
        out_specs=[anywhere] * (count + len(extra)),
        out_shape=[jax.ShapeDtypeStruct((n,) + a.shape, a.dtype) for a in arrays]
        + [jax.ShapeDtypeStruct(a.shape, a.dtype) for a in extra],
        scratch_shapes=[
            dma((count,)), dma((count, outer - 1)), dma((count, outer - 1)),
            dma((count, outer, side)), dma((count, outer, side)), dma((count, outer, inner)), dma((count, outer, inner)),
            dma((2, max(len(extra), 1))),
        ],
        compiler_params=pltpu.CompilerParams(collective_id=collective_id, has_side_effects=True),
    )(*arrays, *extra)


def t_dot_k(left, right):
    return dot(left, right, ((0,), (0,)))


def expert_loop(experts, ids_ref, t_ref, c_ref, w_refs, lows, kept, moe_acc, dn2_acc, spare):
    rows, width = c_ref.shape
    count = len(w_refs)
    ff = lows[0].shape[1]
    gl, ul, al = lows
    n2 = t_ref[:, :width]
    cot = c_ref[...]
    extra = t_ref[:, width:].astype(F32)
    lane = lax.broadcasted_iota(jnp.int32, extra.shape, 1)
    back_lane = lax.broadcasted_iota(jnp.int32, (rows, spare), 1)
    dgate = jnp.zeros((rows, spare), F32)
    act_sum, dg_sum, du_sum = kept
    for k in range(count):
        e = ids_ref[k]
        w = w_refs[k]
        gate = jnp.sum(jnp.where((lane == e) | (lane == experts + e), extra, 0.0), axis=1, keepdims=True)
        gv = dot(n2, w[:, :ff]) + gl
        uv = dot(n2, w[:, ff : 2 * ff]) + ul
        back = dot(cot, w[:, 2 * ff :]) + al
        sig = 1.0 / (1.0 + jnp.exp(-gv))
        silu = gv * sig
        act = silu * uv
        col = jnp.sum(act * back, axis=1, keepdims=True)
        high = col.astype(BF).astype(F32)
        at = e + ids_ref[count]
        dgate = dgate + jnp.where(back_lane == at, high, 0.0) + jnp.where(back_lane == at + experts, col - high, 0.0)
        back = back * gate
        act = act * gate
        du = back * silu
        dg = back * uv * (sig + silu * (1.0 - sig))
        act_sum = act if act_sum is None else act_sum + act
        dg_sum = dg if dg_sum is None else dg_sum + dg
        du_sum = du if du_sum is None else du_sum + du
        moe = dot_t(act.astype(BF), w[:, 2 * ff :])
        dn2 = dot_t(jnp.concatenate([dg.astype(BF), du.astype(BF)], axis=1), w[:, : 2 * ff])
        if k == 0:
            moe_acc[...] = moe
            dn2_acc[...] = dn2
        else:
            moe_acc[...] += moe
            dn2_acc[...] += dn2
    return dgate, act_sum, dg_sum, du_sum


def row_mask(experts, t_ref, width):
    extra = t_ref[:, width:].astype(F32)
    lane = lax.broadcasted_iota(jnp.int32, extra.shape, 1)
    chosen = jnp.sum(jnp.where(lane == 2 * experts, extra, 0.0), axis=1, keepdims=True)
    low_lane = lax.broadcasted_iota(jnp.int32, (extra.shape[0], LANES), 1)
    return ((low_lane // ADAPTER_RANK).astype(F32) == chosen).astype(F32)


def first_experts_kernel(experts, count, ids_ref, t_ref, c_ref, *refs):
    w_refs = refs[:count]
    ga_ref, ua_ref, gb_ref, ub_ref, db_ref, da_ref, r_ref, m_ref, wide_ref, thin_ref, moe_acc, dn2_acc = refs[count:]
    width = c_ref.shape[1]
    mask = row_mask(experts, t_ref, width)
    n2 = t_ref[:, :width]
    zg = (dot(n2, ga_ref[...]) * mask).astype(BF)
    zu = (dot(n2, ua_ref[...]) * mask).astype(BF)
    down_back = (dot_t(c_ref[...], db_ref[...]) * mask).astype(BF)
    lows = (dot(zg, gb_ref[...]), dot(zu, ub_ref[...]), dot_t(down_back, da_ref[...]))
    dgate, *sums = expert_loop(experts, ids_ref, t_ref, c_ref, w_refs, lows, (None, None, None), moe_acc, dn2_acc, r_ref.shape[1] - width)
    thin_ref[...] = jnp.concatenate([zg, zu, down_back], axis=1)
    wide_ref[...] = jnp.concatenate([*lows, *sums], axis=1)
    m_ref[...] = moe_acc[...].astype(BF)
    r_ref[:, :width] = dn2_acc[...].astype(BF)
    r_ref[:, width:] = dgate.astype(BF)


def last_experts_kernel(experts, count, ids_ref, t_ref, c_ref, *refs):
    w_refs = refs[:count]
    ga_ref, ua_ref, gb_ref, ub_ref, db_ref, da_ref = refs[count : count + 6]
    prior = refs[count + 6 : count + 11]
    r1_ref, m1_ref, wide_ref, thin_ref, r_ref, m_ref = refs[count + 11 : count + 17]
    sums = refs[count + 17 : count + 22]
    moe_acc, dn2_acc = refs[count + 22 :]
    width = c_ref.shape[1]
    ff = gb_ref.shape[1]

    @pl.when(pl.program_id(0) == 0)
    def _():
        for old, new in zip(prior, sums):
            new[...] = old[...]

    mask = row_mask(experts, t_ref, width)
    parts = [wide_ref[:, i * ff : (i + 1) * ff] for i in range(6)]
    dgate, act_sum, dg_sum, du_sum = expert_loop(
        experts, ids_ref, t_ref, c_ref, w_refs, parts[:3], parts[3:], moe_acc, dn2_acc, r_ref.shape[1] - width
    )
    zg, zu, down_back = thin_ref[:, :LANES], thin_ref[:, LANES : 2 * LANES], thin_ref[:, 2 * LANES :]
    act_sum, dg_sum, du_sum = act_sum.astype(BF), dg_sum.astype(BF), du_sum.astype(BF)
    low = (dot(act_sum, da_ref[...]) * mask).astype(BF)
    gdu = (dot_t(dg_sum, gb_ref[...]) * mask).astype(BF)
    udu = (dot_t(du_sum, ub_ref[...]) * mask).astype(BF)
    m_ref[...] = (moe_acc[...] + dot(low, db_ref[...]) + m1_ref[...].astype(F32)).astype(BF)
    dn2 = dn2_acc[...] + dot_t(gdu, ga_ref[...]) + dot_t(udu, ua_ref[...])
    r_ref[:, :width] = (dn2 + r1_ref[:, :width].astype(F32)).astype(BF)
    r_ref[:, width:] = (dgate + r1_ref[:, width:].astype(F32)).astype(BF)
    bd_ref, ad_ref, bg_ref, bu_ref, a_ref = sums
    cot = c_ref[...]
    bd_ref[...] += t_dot_k(low, cot)
    ad_ref[...] += t_dot_k(act_sum, down_back)
    bg_ref[...] += t_dot_k(zg, dg_sum)
    bu_ref[...] += t_dot_k(zu, du_sum)
    a_ref[...] += t_dot_k(t_ref[:, :width], jnp.concatenate([gdu, udu], axis=1))


def experts_on(ids, experts, spare, t, cot, weights, w_two, first, low_two, down_b, down_at, prior=(), early=()):
    rows, width = cot.shape
    ff = down_at.shape[0]
    step = 256
    sd = jax.ShapeDtypeStruct
    whole = lambda a: pl.BlockSpec(a.shape, lambda i: (0, 0))
    once = lambda a: pl.BlockSpec(a.shape, lambda i: (0, 0), pipeline_mode=pl.Buffered(1))
    by_row = lambda cols: pl.BlockSpec((step, cols), lambda i: (i, 0))
    column = lambda height, cols, at: pl.BlockSpec((height, cols), lambda i: (0, at))
    low_rows = low_two.shape[0]
    count = len(weights)
    flops = 2 * rows * width * ff * 7 * count
    out_specs = [by_row(width + spare), by_row(width)]
    out_shape = [sd((rows, width + spare), BF), sd((rows, width), BF)]
    if early:
        out_specs += [whole(p) for p in prior]
        out_shape += [sd(p.shape, F32) for p in prior]
    else:
        out_specs += [by_row(6 * ff), by_row(3 * LANES)]
        out_shape += [sd((rows, 6 * ff), F32), sd((rows, 3 * LANES), BF)]
    outs = pl.pallas_call(
        functools.partial(last_experts_kernel if early else first_experts_kernel, experts, count),
        grid=(rows // step,),
        in_specs=[pl.BlockSpec(memory_space=pltpu.SMEM), by_row(t.shape[1]), by_row(width)]
        + [once(w) for w in weights]
        + [column(width, LANES, first), column(width, LANES, first + 1), column(low_rows, ff, 0), column(low_rows, ff, 1), whole(down_b), whole(down_at)]
        + [once(p) for p in prior] + [by_row(e.shape[1]) for e in early],
        out_specs=out_specs,
        out_shape=out_shape,
        scratch_shapes=[pltpu.VMEM((step, width), F32), pltpu.VMEM((step, width), F32)],
        input_output_aliases={3 + count + 6 + i: 2 + i for i in range(len(prior))},
        compiler_params=pltpu.CompilerParams(vmem_limit_bytes=58 << 20),
        cost_estimate=pl.CostEstimate(flops=flops, bytes_accessed=24 << 20, transcendentals=rows * ff * count),
    )(ids, t, cot, *weights, w_two, w_two, low_two, low_two, down_b, down_at, *prior, *early)
    return outs


class Crossing:
    def __init__(self):
        self.n_ctx, self.n_tp = lax.axis_size("ctx"), lax.axis_size("tp")
        self.tp_at = lax.axis_index("tp")

    def pairs(self, by):
        return [(c, (c + by) % self.n_ctx) for c in range(self.n_ctx)]

    def half(self, block):
        if self.n_tp != 2:
            return block
        size = block.shape[0] // 2
        return lax.dynamic_slice_in_dim(block, self.tp_at * size, size, 0)

    def other_half(self, block):
        size = block.shape[0] // 2
        return lax.dynamic_slice_in_dim(block, (1 - self.tp_at) * size, size, 0)

    def joined(self, half):
        if self.n_tp != 2:
            return half
        other = lax.ppermute(half, "tp", [(0, 1), (1, 0)])
        size = half.shape[0]
        whole = lax.dynamic_update_slice_in_dim(jnp.zeros((2 * size,) + half.shape[1:], half.dtype), half, self.tp_at * size, 0)
        return lax.dynamic_update_slice_in_dim(whole, other, (1 - self.tp_at) * size, 0)

    def fetch(self, block):
        half = self.half(block)
        return [lax.ppermute(half, "ctx", self.pairs(by)) for by in range(1, self.n_ctx)]

    def summed_half(self, block):
        if self.n_tp != 2:
            return block.astype(F32)
        return self.half(block).astype(F32) + lax.ppermute(self.other_half(block), "tp", [(0, 1), (1, 0)]).astype(F32)

    def swapped(self, blocks):
        if self.n_tp != 2:
            return [jnp.zeros_like(b) for b in blocks]
        return [lax.ppermute(self.other_half(b), "tp", [(0, 1), (1, 0)]) for b in blocks]

    def halves_of_total(self, own, parts):
        found = self.summed_half(own)
        for part in parts:
            found = found + part.astype(F32)
        if self.n_tp != 2:
            found = lax.psum(found, "tp").astype(BF)
            size = found.shape[0] // 2
            return found[:size], found[size:], 0
        found = found.astype(BF)
        return found, lax.ppermute(found, "tp", [(0, 1), (1, 0)]), self.tp_at


def put_rows(pack, value, at, height):
    for f in range(pack.shape[0]):
        pack[f, pl.ds(at, height), :] = value[f * height : (f + 1) * height, :].astype(pack.dtype)


def put_cols(pack, value, at, height, first):
    for i in range(value.shape[1] // LANES):
        for f in range(pack.shape[0]):
            spot = pl.ds(pl.multiple_of(at + (first + i) * height, 8 if height % 16 else 16), height)
            pack[f, spot, :] = value[f * height : (f + 1) * height, i * LANES : (i + 1) * LANES].astype(pack.dtype)


def adapter_mask(chosen_ref):
    rows = chosen_ref.shape[0]
    return (lax.broadcasted_iota(jnp.int32, (rows, LANES), 1) // ADAPTER_RANK == chosen_ref[...]).astype(F32)


def qkv_back_kernel(n_tp, low_rows, share, tp_ref, dq_ref, dko_ref, dvo_ref, fb_ref, cos_ref, sin_ref, n1_ref, u_ref, chosen_ref, w_ref, lb_ref, dn1_ref, pack_ref, a_acc, b_acc):
    q_width, kv_width = dq_ref.shape[1], dko_ref.shape[1]
    ranks = LANES
    rows = dq_ref.shape[0]
    step = pl.program_id(0)
    mask = adapter_mask(chosen_ref)
    head = lax.broadcasted_iota(jnp.int32, (rows, LANES), 1) % HEAD_SIZE < HEAD_SIZE // 2

    def turned_back(v):
        swapped = jnp.where(head, pltpu.roll(v, LANES - HEAD_SIZE // 2, 1), pltpu.roll(v, HEAD_SIZE // 2, 1))
        return (v * cos_ref[...] - swapped * sin_ref[...]).astype(BF)

    dq = [turned_back(dq_ref[:, i : i + LANES]) for i in range(0, q_width, LANES)]
    dk = [turned_back(dko_ref[:, i : i + LANES] + fb_ref[:, i : i + LANES].astype(F32)) for i in range(0, kv_width, LANES)]
    dv = (dvo_ref[...] + fb_ref[:, kv_width:].astype(F32)).astype(BF)
    dq = jnp.concatenate(dq, axis=1)
    dk = jnp.concatenate(dk, axis=1) if len(dk) > 1 else dk[0]
    lows = []
    at = 0
    for d in (dq, dk, dv):
        lows.append((dot_t(d, lb_ref[:, at : at + d.shape[1]]) * mask).astype(BF))
        at += d.shape[1]
    lows = jnp.concatenate(lows, axis=1)
    dn1_ref[...] = dot_t(jnp.concatenate([dq, dk, dv, lows], axis=1), w_ref[...]).astype(BF)
    n1 = n1_ref[...]
    parts = [
        (a_acc, slice(0, 3 * ranks), t_dot_k(n1, lows)),
        (b_acc, slice(0, q_width), t_dot_k(u_ref[:, :ranks], dq)),
        (b_acc, slice(q_width, q_width + kv_width), t_dot_k(u_ref[:, ranks : 2 * ranks], dk)),
        (b_acc, slice(q_width + kv_width, q_width + 2 * kv_width), t_dot_k(u_ref[:, 2 * ranks :], dv)),
    ]

    @pl.when(step == 0)
    def _():
        for acc, cols, value in parts:
            acc[:, cols] = value

    @pl.when(step > 0)
    def _():
        for acc, cols, value in parts:
            acc[:, cols] += value

    @pl.when(step == pl.num_programs(0) - 1)
    def _():
        pack_ref[...] = jnp.zeros_like(pack_ref)
        at, col = 0, 0
        for i, cols in enumerate((q_width, kv_width, kv_width)):
            put_rows(pack_ref, a_acc[:, i * ranks : (i + 1) * ranks], at, share)
            at += share
            put_cols(pack_ref, b_acc[:, col : col + cols], at, low_rows, tp_ref[0] * (cols // LANES))
            at += cols * n_tp // LANES * low_rows
            col += cols


def qkv_back(n, n_tp, low_rows, share, tp_at, dq, dko, dvo, fb, cos, sin, n1, u3, chosen, w_one, low_one, height):
    rows, q_width = dq.shape
    width = n1.shape[1]
    step = 256
    by_row = lambda a: pl.BlockSpec((step, a.shape[1]), lambda i: (i, 0))
    whole = lambda a: pl.BlockSpec(a.shape, lambda i: (0, 0), pipeline_mode=pl.Buffered(1))
    sd = jax.ShapeDtypeStruct
    return pl.pallas_call(
        functools.partial(qkv_back_kernel, n_tp, low_rows, share),
        grid=(rows // step,),
        in_specs=[pl.BlockSpec(memory_space=pltpu.SMEM)] + [by_row(a) for a in (dq, dko, dvo, fb, cos, sin, n1, u3, chosen)] + [whole(w_one), whole(low_one)],
        out_specs=[pl.BlockSpec((step, width), lambda i: (i, 0)), pl.BlockSpec((n, height, LANES), lambda i: (0, 0, 0))],
        out_shape=[sd((rows, width), BF), sd((n, height, LANES), F32)],
        scratch_shapes=[pltpu.VMEM((width, 3 * LANES), F32), pltpu.VMEM((LANES, low_one.shape[1]), F32)],
        compiler_params=pltpu.CompilerParams(vmem_limit_bytes=50 << 20),
        cost_estimate=pl.CostEstimate(flops=4 * rows * width * w_one.shape[1], bytes_accessed=24 << 20, transcendentals=0),
    )(tp_at, dq, dko, dvo, fb, cos, sin, n1, u3, chosen, w_one, low_one)


def normed_rows(v, gain):
    return v * lax.rsqrt(jnp.mean(v * v, axis=1, keepdims=True) + norm_eps) * gain


def turned(v, cos, sin):
    head = lax.broadcasted_iota(jnp.int32, v.shape, 1) % HEAD_SIZE < HEAD_SIZE // 2
    swapped = jnp.where(head, pltpu.roll(v, LANES - HEAD_SIZE // 2, 1), pltpu.roll(v, HEAD_SIZE // 2, 1))
    return v * cos + swapped * sin


def kv_kernel(q_width, x_ref, chosen_ref, cos_ref, sin_ref, gain_ref, w_ref, low_ref, n1_ref, u_ref, kv_ref):
    kv_width = kv_ref.shape[1] // 2
    mask = adapter_mask(chosen_ref)
    n1 = normed_rows(x_ref[...].astype(F32), gain_ref[...]).astype(BF)
    n1_ref[...] = n1
    raw = dot(n1, w_ref[:, q_width:])
    lows = (raw[:, 2 * kv_width :] * jnp.concatenate([mask] * 3, axis=1)).astype(BF)
    u_ref[...] = lows
    key = raw[:, :kv_width] + dot(lows[:, LANES : 2 * LANES], low_ref[:, q_width : q_width + kv_width])
    for i in range(0, kv_width, LANES):
        kv_ref[:, i : i + LANES] = turned(key[:, i : i + LANES], cos_ref[...], sin_ref[...]).astype(BF)
    value = raw[:, kv_width : 2 * kv_width] + dot(lows[:, 2 * LANES :], low_ref[:, q_width + kv_width :])
    kv_ref[:, kv_width:] = value.astype(BF)


def q_kernel(n1_ref, u_ref, cos_ref, sin_ref, w_ref, low_ref, q_ref):
    q_width = q_ref.shape[1]
    q = dot(n1_ref[...], w_ref[:, :q_width]) + dot(u_ref[:, :LANES], low_ref[:, :q_width])
    for i in range(0, q_width, LANES):
        q_ref[:, i : i + LANES] = (turned(q[:, i : i + LANES], cos_ref[...], sin_ref[...]) * 0.125).astype(BF)


def out_kernel(o_ref, chosen_ref, w_ref, oa_ref, low_ref, part_ref, u_ref):
    q_width, width = o_ref.shape[1], part_ref.shape[1]
    ff2 = low_ref.shape[1] - 2 * width - LANES
    o = o_ref[...]
    u = (dot(o, oa_ref[...]) * adapter_mask(chosen_ref)).astype(BF)
    u_ref[...] = u
    part_ref[...] = (dot_t(o, w_ref[:, :q_width]) + dot(u, low_ref[:, ff2 : ff2 + width])).astype(BF)


def route_kernel(experts, q_width, x_ref, one_ref, other_ref, chosen_ref, routes_ref, gain_ref, w_ref, low_ref, h_ref, t_ref, u_ref):
    width = h_ref.shape[1]
    rows = h_ref.shape[0]
    h = x_ref[...].astype(F32) + (one_ref[...].astype(F32) + other_ref[...].astype(F32))
    h_ref[...] = h
    n2 = normed_rows(h, gain_ref[...]).astype(BF)
    t_ref[:, :width] = n2
    u = (dot(n2, w_ref[:, q_width : q_width + LANES]) * adapter_mask(chosen_ref)).astype(BF)
    u_ref[...] = u
    logits = dot(n2, w_ref[:, q_width + 3 * LANES : q_width + 4 * LANES]) + dot(u, low_ref[:, low_ref.shape[1] - LANES :])
    lane = lax.broadcasted_iota(jnp.int32, (rows, LANES), 1)
    selected = lane == routes_ref[:, 0:1]
    for k in range(1, routes_ref.shape[1]):
        selected = selected | (lane == routes_ref[:, k : k + 1])
    top = jnp.max(jnp.where(selected, logits, -jnp.inf), axis=1, keepdims=True)
    gates = jnp.where(selected, jnp.exp(jnp.where(selected, logits - top, 0.0)), 0.0)
    gates = gates / jnp.sum(gates, axis=1, keepdims=True)
    high = gates.astype(BF).astype(F32)
    extra = high + pltpu.roll(gates - high, experts, 1) + jnp.where(lane == 2 * experts, chosen_ref[...].astype(F32), 0.0)
    t_ref[:, width:] = extra.astype(BF)


def by_rows(kernel, step, rowed, whole, outs, flops):
    rows = rowed[0].shape[0]
    block = lambda cols: pl.BlockSpec((step, cols), lambda i: (i, 0))
    return pl.pallas_call(
        kernel,
        grid=(rows // step,),
        in_specs=[block(a.shape[1]) for a in rowed] + [pl.BlockSpec(a.shape, lambda i: (0, 0), pipeline_mode=pl.Buffered(1)) for a in whole],
        out_specs=[block(cols) for cols, kind in outs],
        out_shape=[jax.ShapeDtypeStruct((rows, cols), kind) for cols, kind in outs],
        compiler_params=pltpu.CompilerParams(vmem_limit_bytes=48 << 20),
        cost_estimate=pl.CostEstimate(flops=flops, bytes_accessed=1 << 20, transcendentals=0),
    )(*rowed, *whole)


def mid_back_kernel(n, n_tp, experts, share, low_rows, sel_ref, mine_ref, other_ref, h_ref, c_ref, t_ref, o_ref, ou_ref, ru_ref, chosen_ref, gain_ref,
                    w_ref, low_ref, oa_ref, bd_ref, ad_ref, bg_ref, bu_ref, agu_ref, dh_ref, do_ref, pack_ref, ar_acc, ao_acc, bo_acc, br_acc):
    width = h_ref.shape[1]
    q_width = o_ref.shape[1]
    ff = bg_ref.shape[1]
    spare = mine_ref.shape[1] - width
    step = pl.program_id(0)
    mask = adapter_mask(chosen_ref)
    picked = step == sel_ref[0]

    def fold(height, top):
        lane = lax.broadcasted_iota(jnp.int32, (height, LANES), 0)
        return ((lane % experts == lax.broadcasted_iota(jnp.int32, (height, LANES), 1)) & (lane < top)).astype(BF)

    back = jnp.where(picked, mine_ref[:, :width].astype(F32), other_ref[:, :width].astype(F32))
    tail = jnp.where(picked, mine_ref[:, width:].astype(F32), other_ref[:, width:].astype(F32)).astype(BF)
    dgate = dot(tail, fold(spare, 2 * experts * n_tp))
    gates = dot(t_ref[:, width:], fold(LANES, 2 * experts))
    n2 = t_ref[:, :width]
    router_a, router_w = w_ref[:, q_width : q_width + LANES], w_ref[:, q_width + 3 * LANES : q_width + 4 * LANES]
    out_b, router_b = low_ref[:, 2 * ff : 2 * ff + width], low_ref[:, 2 * ff + 2 * width :]
    dlog = (gates * (dgate - jnp.sum(gates * dgate, axis=1, keepdims=True))).astype(BF)
    rdu = (dot_t(dlog, router_b) * mask).astype(BF)
    dn2 = back + dot_t(dlog, router_w) + dot_t(rdu, router_a)
    h = h_ref[...]
    r = lax.rsqrt(jnp.mean(h * h, axis=1, keepdims=True) + norm_eps)
    gd = dn2 * gain_ref[...]
    dh = c_ref[...].astype(F32) + r * gd - h * (r * r * r * jnp.mean(gd * h, axis=1, keepdims=True))
    dh_ref[...] = dh
    dattn = dh.astype(BF)
    odu = (dot_t(dattn, out_b) * mask).astype(BF)
    do_ref[...] = (dot(dattn, w_ref[:, :q_width]) + dot_t(odu, oa_ref[...])).astype(BF)
    parts = [
        (ar_acc, t_dot_k(n2, rdu)),
        (ao_acc, t_dot_k(o_ref[...], odu)),
        (bo_acc, t_dot_k(ou_ref[...], dattn)),
        (br_acc, t_dot_k(ru_ref[...], dlog)),
    ]

    @pl.when(step == 0)
    def _():
        for acc, value in parts:
            acc[...] = value

    @pl.when(step > 0)
    def _():
        for acc, value in parts:
            acc[...] += value

    @pl.when(step == pl.num_programs(0) - 1)
    def _():
        pack_ref[...] = jnp.zeros_like(pack_ref)
        tp = sel_ref[1]
        first = (tp == 0).astype(F32)
        own = n // n_tp
        at = 0
        for k in range(own):
            pack_ref[tp * own + k, pl.ds(at, share), :] = ao_acc[k * share : (k + 1) * share, :].astype(pack_ref.dtype)
        at += share
        put_cols(pack_ref, bo_acc, at, low_rows, 0)
        at += width // LANES * low_rows
        ar_acc[...] = ar_acc[...] * first
        put_rows(pack_ref, ar_acc, at, share)
        at += share
        br_acc[...] = br_acc[...] * first
        put_cols(pack_ref, br_acc, at, low_rows, 0)
        at += low_rows
        for i, ref in enumerate((bg_ref, bu_ref)):
            put_rows(pack_ref, agu_ref[:, i * LANES : (i + 1) * LANES], at, share)
            at += share
            put_cols(pack_ref, ref, at, low_rows, tp * (ff // LANES))
            at += ff * n_tp // LANES * low_rows
        size = ad_ref.shape[0] // own
        for k in range(own):
            pack_ref[tp * own + k, pl.ds(at, size), :] = ad_ref[k * size : (k + 1) * size, :].astype(pack_ref.dtype)
        at += size
        put_cols(pack_ref, bd_ref, at, low_rows, 0)


def mid_back(n, n_tp, experts, share, low_rows, sel, mine, other, hidden, cot, carried, mixed, out_u, router_u, chosen, gain, w_two, low_two, out_a, sums, height):
    rows, width = hidden.shape
    q_width = mixed.shape[1]
    step = rows // 2
    sd = jax.ShapeDtypeStruct
    by_row = lambda a: pl.BlockSpec((step, a.shape[1]), lambda i: (i, 0))
    whole = lambda a: pl.BlockSpec(a.shape, lambda i: (0, 0), pipeline_mode=pl.Buffered(1))
    return pl.pallas_call(
        functools.partial(mid_back_kernel, n, n_tp, experts, share, low_rows),
        grid=(2,),
        in_specs=[pl.BlockSpec(memory_space=pltpu.SMEM), whole(mine), whole(other)]
        + [by_row(a) for a in (hidden, cot, carried, mixed, out_u, router_u, chosen)]
        + [whole(a) for a in (gain, w_two, low_two, out_a, *sums)],
        out_specs=[by_row(hidden), by_row(mixed), pl.BlockSpec((n, height, LANES), lambda i: (0, 0, 0))],
        out_shape=[sd((rows, width), F32), sd((rows, q_width), BF), sd((n, height, LANES), F32 if low_rows % 16 else BF)],
        scratch_shapes=[pltpu.VMEM((width, LANES), F32), pltpu.VMEM((q_width, LANES), F32), pltpu.VMEM((LANES, width), F32), pltpu.VMEM((LANES, LANES), F32)],
        compiler_params=pltpu.CompilerParams(vmem_limit_bytes=58 << 20),
        cost_estimate=pl.CostEstimate(flops=8 * rows * width * q_width, bytes_accessed=32 << 20, transcendentals=0),
    )(sel, mine, other, hidden, cot, carried, mixed, out_u, router_u, chosen, gain, w_two, low_two, out_a, *sums)


def reduce_kernel(n, pack_ref, side_ref, out_ref, side_out, side_in, side_snd, snd1, rcv1, acc, snd2, rcv2, acc2, snd3, rcv3, fin, sems, send3, recv3):
    me = lax.axis_index("fsdp")
    ctx = lax.axis_index("ctx")
    tp = lax.axis_index("tp")
    half = pack_ref.shape[1] // 2
    part = half // 2
    barrier = pltpu.get_barrier_semaphore()
    pl.semaphore_signal(barrier, inc=1, device_id={"tp": 1 - tp}, device_id_type=MESH)
    pl.semaphore_signal(barrier, inc=1, device_id={"ctx": 1 - ctx}, device_id_type=MESH)
    for k in range(1, n):
        pl.semaphore_signal(barrier, inc=1, device_id={"fsdp": (me + k) % n}, device_id_type=MESH)
    snd1[...] = pack_ref[:, pl.ds(pl.multiple_of((1 - tp) * half, 16), half), :].astype(BF)
    pl.semaphore_wait(barrier, n + 1)

    def swap(src, dst, i, to):
        copy = pltpu.make_async_remote_copy(src_ref=src, dst_ref=dst, send_sem=sems.at[0, i], recv_sem=sems.at[1, i], device_id=to, device_id_type=MESH)
        copy.start()
        return copy

    copy = swap(snd1, rcv1, 0, {"tp": 1 - tp})
    side = swap(side_ref, side_in.at[0], 4, {"tp": 1 - tp})
    copy.wait()
    acc[...] = pack_ref[:, pl.ds(pl.multiple_of(tp * half, 16), half), :] + rcv1[...].astype(F32)
    snd2[...] = acc[:, pl.ds(pl.multiple_of((1 - ctx) * part, 16), part), :].astype(BF)
    copy = swap(snd2, rcv2, 1, {"ctx": 1 - ctx})
    side.wait()
    side_snd[...] = (side_ref[...].astype(F32) + side_in[0].astype(F32)).astype(BF)
    side = swap(side_snd, side_in.at[1], 5, {"ctx": 1 - ctx})
    copy.wait()
    acc2[...] = acc[:, pl.ds(pl.multiple_of(ctx * part, 16), part), :] + rcv2[...].astype(F32)
    snd3[...] = acc2[...].astype(BF)

    def ship(k):
        to = (me + k) % n
        return pltpu.make_async_remote_copy(
            src_ref=snd3.at[to], dst_ref=rcv3.at[me], send_sem=send3.at[k], recv_sem=recv3.at[k], device_id={"fsdp": to}, device_id_type=MESH
        )

    def came(k):
        return pltpu.make_async_remote_copy(
            src_ref=snd3.at[me], dst_ref=rcv3.at[(me + n - k) % n], send_sem=send3.at[k], recv_sem=recv3.at[k],
            device_id={"fsdp": (me + k) % n}, device_id_type=MESH,
        )

    for k in range(1, n):
        ship(k).start()
    total = acc2[me]
    for k in range(1, n):
        came(k).wait_recv()
        total = total + rcv3[(me + n - k) % n].astype(F32)
    for k in range(1, n):
        ship(k).wait_send()
    spot = tp * 2 + ctx
    fin[spot] = total.astype(BF)
    copy = swap(fin.at[spot], fin.at[spot], 2, {"ctx": 1 - ctx})
    copy.wait()
    both = fin.at[pl.ds(tp * 2, 2)]
    copy = swap(both, both, 3, {"tp": 1 - tp})
    copy.wait()
    for i in range(4):
        out_ref[pl.ds(i * part, part), :] = fin[i].astype(F32)
    side.wait()
    side_out[...] = side_snd[...].astype(F32) + side_in[1].astype(F32)


def reduce_pack(pack, side, collective_id):
    n, height = pack.shape[:2]
    if lax.axis_size("tp") != 2 or lax.axis_size("ctx") != 2 or height % 64 or side.shape[0] % 16:
        mine = lax.psum_scatter(pack.astype(BF), "fsdp", scatter_dimension=0, tiled=False)
        return lax.psum(mine, ("ctx", "tp")).astype(F32), lax.psum(side, ("ctx", "tp")).astype(F32)
    half, part = height // 2, height // 4
    vm = pltpu.VMEM
    dma = pltpu.SemaphoreType.DMA
    return pl.pallas_call(
        functools.partial(reduce_kernel, n),
        in_specs=[pl.BlockSpec(memory_space=vm)] * 2,
        out_specs=[pl.BlockSpec(memory_space=vm)] * 2,
        out_shape=[jax.ShapeDtypeStruct((height, LANES), F32), jax.ShapeDtypeStruct(side.shape, F32)],
        scratch_shapes=[
            vm((2,) + side.shape, BF), vm(side.shape, BF), vm((n, half, LANES), BF), vm((n, half, LANES), BF), vm((n, half, LANES), F32),
            vm((n, part, LANES), BF), vm((n, part, LANES), BF), vm((n, part, LANES), F32),
            vm((n, part, LANES), BF), vm((n, part, LANES), BF), vm((4, part, LANES), BF),
            dma((2, 6)), dma((n,)), dma((n,)),
        ],
        compiler_params=pltpu.CompilerParams(collective_id=collective_id, has_side_effects=True, vmem_limit_bytes=48 << 20),
    )(pack, side)


def tp_sum(value):
    if lax.axis_size("tp") != 2:
        return lax.psum(value, "tp")
    return value + lax.ppermute(value, "tp", [(0, 1), (1, 0)])


def on_device(
    tokens, out_cotangent, lengths, adapter_of_doc, routes, attn_gain, ffn_gain,
    w_query, key_matrix, value_matrix, w_out, w_router, w_gate, w_up, w_down,
    a_query, b_query, a_key, key_second_factor, a_value, value_second_factor,
    a_out, b_out, a_router, b_router, a_gate, b_gate, a_up, b_up, a_down, b_down,
):
    rows, width = tokens.shape
    n = lax.axis_size("fsdp")
    n_tp = lax.axis_size("tp")
    tp_at = lax.axis_index("tp")
    ctx_at = lax.axis_index("ctx")
    group = rows * lax.axis_size("ctx")
    q_width = w_query.shape[1]
    kv_width = key_matrix.shape[1]
    ff_width = w_gate.shape[2]
    local_experts = w_gate.shape[0]
    experts = w_router.shape[1]
    ranks = a_query.shape[1]
    share = w_query.shape[0]
    low_rows = b_query.shape[0]

    pad = ((0, 0), (0, LANES - experts))
    one, low_one = gather_packs(
        [
            [(a, a.shape[1]) for a in (w_query, key_matrix, value_matrix, a_query, a_key, a_value)],
            [(b_query, q_width), (key_second_factor, kv_width), (value_second_factor, kv_width)],
        ],
        (),
        0,
    )
    qkv = q_width + 2 * kv_width
    w_one = one.reshape(n * share, -1)
    low_one = low_one.reshape(n * low_rows, -1)

    ends = jnp.cumsum(lengths[0])
    starts = ends - lengths[0]
    place = jnp.arange(group, dtype=jnp.int32)
    doc = jnp.sum((place[:, None] >= ends[None, :]).astype(jnp.int32), axis=1)
    picked = (doc[:, None] == jnp.arange(lengths.shape[1], dtype=jnp.int32)[None, :]).astype(jnp.int32)
    begin = jnp.sum(picked * starts[None, :], axis=1)
    chosen = jnp.sum(picked * adapter_of_doc[0][None, :], axis=1)
    start = ctx_at * rows
    query_index = start + jnp.arange(rows, dtype=jnp.int32)
    begin_local = lax.dynamic_slice_in_dim(begin, start, rows)
    chosen_local = lax.dynamic_slice_in_dim(chosen, start, rows)
    freq = 10000.0 ** (-jnp.arange(HEAD_SIZE // 2, dtype=F32) / (HEAD_SIZE // 2))
    angles = (query_index - begin_local).astype(F32)[:, None] * freq[None, :]
    cosine, sine = jnp.cos(angles), jnp.sin(angles)
    cosine_wide = jnp.tile(cosine, (1, 2 * LANES // HEAD_SIZE))
    sine_wide = jnp.tile(jnp.concatenate([-sine, sine], axis=1), (1, LANES // HEAD_SIZE))
    chosen_col = chosen_local[:, None]
    gain_one, gain_two = attn_gain[None, :], ffn_gain[None, :]
    normed, low_u, kv = by_rows(
        functools.partial(kv_kernel, q_width), 256, (tokens, chosen_col, cosine_wide, sine_wide), (gain_one, w_one, low_one),
        ((width, BF), (3 * ranks, BF), (2 * kv_width, BF)), 2 * rows * width * (w_one.shape[1] - q_width),
    )
    cross = Crossing()
    outer, inner = levels(n)
    me = lax.axis_index("fsdp")
    ring = [(i, (i + inner) % n) for i in range(n)]
    turns = [[(i, i // inner * inner + (i % inner + dj) % inner) for i in range(n)] for dj in range(1, inner)]
    local = local_experts // cross.n_ctx
    mine = [lax.dynamic_slice_in_dim(a, ctx_at * local, local, 0) for a in (w_gate, w_up, w_down)]
    block = jnp.concatenate([mine[0], mine[1], jnp.swapaxes(mine[2], 1, 2)], axis=2)
    brought = {(0, 0): block}

    def bring(do, after):
        last = [brought[(do, 0)]] + [brought[(do - 1, dj)] for dj in range(1, inner) if do]
        last, after = lax.optimization_barrier((last, after))
        brought[(do, 0)] = last[0]
        for dj, value in zip(range(1, inner), last[1:]):
            brought[(do - 1, dj)] = value
        if do + 1 < outer:
            brought[(do + 1, 0)] = lax.ppermute(last[0], "fsdp", ring)
        for dj in range(1, inner):
            brought[(do, dj)] = lax.ppermute(last[0], "fsdp", turns[dj - 1])
        return after

    one = bring(0, one)
    (query_state,) = by_rows(
        q_kernel, 256, (normed, low_u, cosine_wide, sine_wide), (w_one, low_one), ((q_width, BF),), 2 * rows * width * q_width
    )
    w_out, w_router, b_router, query_state = lax.optimization_barrier((w_out, w_router, b_router, query_state))
    two, low_two, down_a, far = gather_packs(
        [
            [(a, a.shape[1]) for a in (w_out.T, a_router, a_gate, a_up, jnp.pad(w_router, pad), a_out)],
            [(b_gate, ff_width), (b_up, ff_width), (b_out, width), (b_down, width), (jnp.pad(b_router, pad), LANES)],
            [(a_down, ranks)],
        ],
        (kv,),
        1,
    )
    cot = lax.optimization_barrier((out_cotangent, two))[0]
    cot_halves = cross.fetch(cot)
    far = bring(1, far)
    w_two = two.reshape(n * share, -1)
    low_two = low_two.reshape(n * low_rows, -1)
    down_b = low_two[:, 2 * ff_width + width : 2 * ff_width + 2 * width]
    out_a = lax.dynamic_slice_in_dim(w_two[:, q_width + 4 * ranks : q_width + 5 * ranks], tp_at * q_width, q_width, 0)
    down_at = lax.dynamic_slice_in_dim(down_a.reshape(-1, ranks), tp_at * ff_width, ff_width, 0)
    begin_row = begin_local[None, :]
    start_at = jnp.reshape(start, (1,)).astype(jnp.int32)
    mixed_heads, log_total = attend(query_state, kv, far, begin_row, start_at)
    cot_halves, mixed_heads = lax.optimization_barrier((cot_halves, mixed_heads))
    attn_part, out_u = by_rows(
        out_kernel, 256, (mixed_heads, chosen_col), (w_two, out_a, low_two), ((width, BF), (ranks, BF)), 0
    )
    attn_part = bring(2, attn_part)
    if n_tp == 2:
        attn_other = lax.ppermute(attn_part, "tp", [(0, 1), (1, 0)])
    else:
        attn_part, attn_other = lax.psum(attn_part.astype(F32), "tp"), jnp.zeros_like(attn_part)
    spare = -(-2 * experts * n_tp // LANES) * LANES
    hidden, carried, router_u = by_rows(
        functools.partial(route_kernel, experts, q_width), 256, (tokens, attn_part, attn_other, chosen_col, routes), (gain_two, w_two, low_two),
        ((width, F32), (width + LANES, BF), (ranks, BF)), 0,
    )
    halves = cross.fetch(carried)
    early = [(0, 0), (1, 0)] + [(0, dj) for dj in range(1, inner)] + [(2, 0)] + [(1, dj) for dj in range(1, inner)]
    late = [(do, 0) for do in range(3, outer)] + [(do, dj) for do in range(2, outer) for dj in range(1, inner)]

    def weights_of(keys):
        ids = [((me // inner + outer - do) % outer * inner + (me % inner + inner - dj) % inner) * local_experts + ctx_at * local + j for do, dj in keys for j in range(local)]
        return jnp.stack(ids + [tp_at * 2 * experts]).astype(jnp.int32), [brought[k][j] for k in keys for j in range(local)]

    sums = [jnp.zeros(shape, F32) for shape in ((ranks, width), (ff_width, ranks), (ranks, ff_width), (ranks, ff_width), (width, 2 * ranks))]
    at = q_width // LANES + 1
    work = [(carried, cot)] + [(None, None)] * (cross.n_ctx - 1)
    partial = []
    ids, weights = weights_of(early)
    for by in range(cross.n_ctx):
        if by:
            work[by] = (cross.joined(halves[by - 1]), cross.joined(cot_halves[by - 1]))
        r, m, wide, thin = experts_on(ids, experts, spare, *work[by], weights, w_two, at, low_two, down_b, down_at)
        if by == 0:
            for do in range(3, outer):
                r = bring(do, r)
            halves, cot_halves, r = lax.optimization_barrier((halves, cot_halves, r))
        partial.append((r, m, wide, thin))
    ids, weights = weights_of(late)
    back_parts, moe_parts = [], []
    for by in list(range(1, cross.n_ctx)) + [0]:
        r, m, *sums = experts_on(ids, experts, spare, *work[by], weights, w_two, at, low_two, down_b, down_at, sums, partial[by])
        moe_parts.append(m)
        if by:
            half = cross.summed_half(r).astype(BF)
            half, carried = lax.optimization_barrier((half, work[0][0]))
            work[0] = (carried, cot)
            back_parts.append(lax.ppermute(half, "ctx", cross.pairs(-by)))
    r, back_parts = lax.optimization_barrier((r, back_parts))
    mine_half, other, first = cross.halves_of_total(r, back_parts)
    swapped = cross.swapped(moe_parts)
    early_shapes = [
        (share, ranks), (low_rows, width), (share, ranks), (low_rows, experts), (share, ranks), (low_rows, ff_width * n_tp),
        (share, ranks), (low_rows, ff_width * n_tp), (a_down.shape[0], ranks), (low_rows, width),
    ]
    height = sum(-(-cols // LANES) * tall for tall, cols in early_shapes)
    sel = jnp.stack([jnp.asarray(first, jnp.int32), tp_at.astype(jnp.int32)])
    dhidden, dmixed, early_pack = mid_back(
        n, n_tp, experts, share, low_rows, sel, mine_half, other, hidden, cot, carried, mixed_heads, out_u, router_u,
        chosen_col, gain_two, w_two, low_two, out_a, sums, height,
    )
    early_pack, dmixed, swapped = lax.optimization_barrier((early_pack.astype(BF), dmixed, swapped))
    moe_halves = [cross.half(p).astype(F32) + q.astype(F32) for p, q in zip(moe_parts, swapped)]
    moe_got = [lax.ppermute(p.astype(BF), "ctx", cross.pairs(-by)) for by, p in zip(range(1, cross.n_ctx), moe_halves)]
    early_sum = lax.psum_scatter(early_pack, "fsdp", scatter_dimension=0, tiled=False)
    dq_far, dkey_far, dvalue_far = attend_back(query_state, far, begin_row, start_at, mixed_heads, dmixed, log_total)
    far_back = lax.ppermute(
        jnp.concatenate([dkey_far, dvalue_far], axis=1), "ctx", [(i + 1, i) for i in range(lax.axis_size("ctx") - 1)]
    )
    dquery, dkey_own, dvalue_own = attend_back(query_state, kv, begin_row, start_at, mixed_heads, dmixed, log_total, dq_far)
    far_back, moe_got, dquery = lax.optimization_barrier((far_back, moe_got, dquery))
    moe = moe_halves[-1]
    for part in moe_got:
        moe = moe + part.astype(F32)
    moe = cross.joined(moe.astype(BF)).astype(F32) if n_tp == 2 else lax.psum(moe, "tp")
    output = (hidden + moe).astype(BF)
    height = 3 * share + low_rows * n_tp * qkv // LANES
    dn1, pack = qkv_back(
        n, n_tp, low_rows, share, jnp.reshape(tp_at, (1,)).astype(jnp.int32), dquery, dkey_own, dvalue_own, far_back,
        cosine_wide, sine_wide, normed, low_u, chosen_col, w_one, low_one, height,
    )
    early_sum, dn1, pack = lax.optimization_barrier((early_sum, dn1, pack))
    late, early_sum = reduce_pack(pack, early_sum, 2)
    dn1 = tp_sum(dn1.astype(F32)) if n_tp != 2 else dn1.astype(F32) + lax.ppermute(dn1, "tp", [(0, 1), (1, 0)]).astype(F32)
    grad_tokens = (dhidden + norm_back(tokens.astype(F32), attn_gain, dn1)).astype(BF)

    def unpack(mine, shapes):
        found = []
        at = 0
        for height, cols in shapes:
            count = -(-cols // LANES)
            piece = mine[at : at + count * height].reshape(count, height, LANES).transpose(1, 0, 2).reshape(height, count * LANES)
            found.append(piece[:, :cols])
            at += count * height
        return found

    first_shapes = [(share, ranks), (low_rows, q_width * n_tp), (share, ranks), (low_rows, kv_width * n_tp), (share, ranks), (low_rows, kv_width * n_tp)]
    final = unpack(late, first_shapes) + unpack(early_sum, early_shapes)
    return (output, grad_tokens, *final)


def solution(mesh):
    both = P(("fsdp", "ctx"), None)
    split = P("fsdp", None)
    placed = (
        both, both, split, split, both, P(), P(),
        P("fsdp", "tp"), P("fsdp", "tp"), P("fsdp", "tp"), P("tp", "fsdp"), split,
        P("fsdp", None, "tp"), P("fsdp", None, "tp"), P("fsdp", "tp", None),
    ) + (split,) * 16
    return jax.shard_map(
        on_device, mesh=mesh, in_specs=placed, out_specs=(both, both) + (split,) * 16, check_vma=False
    )
```

```python
import functools

import jax
import jax.numpy as jnp
from jax import lax
from jax.experimental import pallas as pl
from jax.experimental.pallas import tpu as pltpu
from jax.sharding import PartitionSpec as P

HEAD_SIZE = 64
ADAPTER_RANK = 16
LANES = 128
norm_eps = 1e-05
BF = jnp.bfloat16
F32 = jnp.float32


MESH = pl.DeviceIdType.MESH


def dot(left, right, dims=((1,), (0,)), precision=None):
    return lax.dot_general(left, right, (dims, ((), ())), preferred_element_type=F32, precision=precision)


def dot_t(left, right):
    return dot(left, right, ((1,), (1,)))


def t_dot(left, right):
    return dot(left, right, ((0,), (0,)))


def rms_norm(values, gain):
    return values * lax.rsqrt(jnp.mean(values * values, axis=-1, keepdims=True) + norm_eps) * gain


def norm_back(values, gain, grad):
    unused, pull = jax.vjp(lambda inner: rms_norm(inner, gain), values)
    return pull(grad)[0]


def levels(n):
    outer = 4 if n % 4 == 0 else n
    return outer, n // outer


def fill_bias(bias, start_ref, begin_ref, rows):
    step = rows // 3
    for at in range(0, 2 * rows, step):
        key = start_ref[0] - rows + at + lax.broadcasted_iota(jnp.int32, (step, rows), 0)
        query = start_ref[0] + lax.broadcasted_iota(jnp.int32, (step, rows), 1)
        ok = (key <= query) & (key >= begin_ref[...]) & (key >= 0)
        bias[pl.ds(at, step), :] = jnp.where(ok, 0.0, -1e30)


def split_heads(ref, out, count, rows, at=0):
    for h in range(count):
        out[h, pl.ds(at, rows), :] = ref[:, h * HEAD_SIZE : (h + 1) * HEAD_SIZE]


def attend_kernel(group, q_blocks, start_ref, begin_ref, q_ref, ko_ref, vo_ref, kf_ref, vf_ref, o_ref, lse_ref, bias, ks, vts, qs, ots):
    rows = q_ref.shape[0]
    width = rows // q_blocks
    heads = 2 * group
    @pl.when(pl.program_id(0) == 0)
    def _():
        fill_bias(bias, start_ref, begin_ref, rows)
    split_heads(kf_ref, ks, 2, rows, 0)
    split_heads(ko_ref, ks, 2, rows, rows)
    split_heads(q_ref, qs, heads, rows, 0)
    vts[:, pl.ds(0, rows)] = vf_ref[...].astype(F32).T.astype(BF)
    vts[:, pl.ds(rows, rows)] = vo_ref[...].astype(F32).T.astype(BF)
    for b in range(q_blocks):
        keys = rows + (b + 1) * width
        def one(h, _):
            g = h // group
            s = dot_t(ks[g, pl.ds(0, keys), :], qs[h, pl.ds(b * width, width), :]) + bias[pl.ds(0, keys), pl.ds(b * width, width)]
            top = jnp.max(s, axis=0, keepdims=True)
            p = jnp.exp(s - top)
            total = jnp.sum(p, axis=0, keepdims=True)
            lse_ref[0, pl.ds(h, 1), pl.ds(b * width, width)] = top + jnp.log(total)
            vt = vts[pl.ds(pl.multiple_of(g * HEAD_SIZE, HEAD_SIZE), HEAD_SIZE), pl.ds(0, keys)]
            o = dot(vt, p.astype(BF)) / total
            ots[pl.ds(pl.multiple_of(h * HEAD_SIZE, HEAD_SIZE), HEAD_SIZE), pl.ds(b * width, width)] = o
            return 0
        lax.fori_loop(0, heads, one, 0)
    for j in range(group):
        o_ref[:, j * LANES : (j + 1) * LANES] = ots[pl.ds(j * LANES, LANES), :].T.astype(BF)


def attend(q, kv, far, begin, start, q_blocks=3):
    rows, q_width = q.shape
    kv_width = kv.shape[1] // 2
    pairs = kv_width // LANES
    group = q_width // kv_width
    spec = lambda off: pl.BlockSpec((rows, LANES), lambda i: (0, i + off))
    return pl.pallas_call(
        functools.partial(attend_kernel, group, q_blocks),
        grid=(pairs,),
        in_specs=[pl.BlockSpec(memory_space=pltpu.SMEM), pl.BlockSpec((1, rows), lambda i: (0, 0)),
                  pl.BlockSpec((rows, group * LANES), lambda i: (0, i)), spec(0), spec(pairs), spec(0), spec(pairs)],
        out_specs=[pl.BlockSpec((rows, group * LANES), lambda i: (0, i)), pl.BlockSpec((1, 8, rows), lambda i: (i, 0, 0))],
        out_shape=[jax.ShapeDtypeStruct((rows, q_width), BF), jax.ShapeDtypeStruct((pairs, 8, rows), F32)],
        scratch_shapes=[pltpu.VMEM((2 * rows, rows), F32), pltpu.VMEM((2, 2 * rows, HEAD_SIZE), BF), pltpu.VMEM((LANES, 2 * rows), BF),
                        pltpu.VMEM((2 * group, rows, HEAD_SIZE), BF), pltpu.VMEM((2 * group * HEAD_SIZE, rows), F32)],
        compiler_params=pltpu.CompilerParams(vmem_limit_bytes=50 << 20),
        cost_estimate=pl.CostEstimate(flops=8 * rows * rows * q_width, bytes_accessed=8 << 20, transcendentals=2 * rows * rows * 12),
    )(start, begin, q, kv, kv, far, far)


def attend_back_kernel(group, q_blocks, far, *refs):
    if far:
        start_ref, begin_ref, q_ref, k_ref, v_ref, o_ref, do_ref, lse_ref = refs[:8]
        dq_far = None
    else:
        start_ref, begin_ref, q_ref, k_ref, v_ref, o_ref, do_ref, lse_ref, dq_far = refs[:9]
    dq_ref, dk_ref, dv_ref, bias, ks, vs, kts, qs, dos, dqts, dks, dvs, deltas = refs[-13:]
    rows = q_ref.shape[0]
    width = rows // q_blocks
    heads = 2 * group

    @pl.when(pl.program_id(0) == 0)
    def _():
        first = start_ref[0] - rows if far else start_ref[0]
        for at in range(0, rows, width):
            key = first + at + lax.broadcasted_iota(jnp.int32, (width, rows), 0)
            query = start_ref[0] + lax.broadcasted_iota(jnp.int32, (width, rows), 1)
            ok = (key <= query) & (key >= begin_ref[...]) & (key >= 0)
            bias[pl.ds(at, width), :] = jnp.where(ok, 0.0, -1e30)

    split_heads(k_ref, ks, 2, rows, 0)
    split_heads(v_ref, vs, 2, rows, 0)
    split_heads(q_ref, qs, heads, rows, 0)
    split_heads(do_ref, dos, heads, rows, 0)
    kts[...] = k_ref[...].astype(F32).T.astype(BF)
    cols = heads * HEAD_SIZE
    pick = (
        lax.broadcasted_iota(jnp.int32, (8, cols), 1) // HEAD_SIZE == lax.broadcasted_iota(jnp.int32, (8, cols), 0)
    ).astype(F32)
    prod = o_ref[...].astype(F32) * do_ref[...].astype(F32)
    deltas[...] = dot(pick, prod, ((1,), (1,)), lax.Precision.HIGHEST)
    dks[...] = jnp.zeros_like(dks)
    dvs[...] = jnp.zeros_like(dvs)
    for b in range(q_blocks):
        keys = rows if far else (b + 1) * width

        def one(h, _):
            g = h // group
            at = pl.ds(b * width, width)
            qb = qs[h, at, :]
            dob = dos[h, at, :]
            s = dot_t(ks[g, pl.ds(0, keys), :], qb) + bias[pl.ds(0, keys), at]
            p = jnp.exp(s - lse_ref[0, pl.ds(h, 1), at])
            dp = dot_t(vs[g, pl.ds(0, keys), :], dob)
            ds = (p * (dp - deltas[pl.ds(h, 1), at])).astype(BF)
            dvs[g, pl.ds(0, keys), :] += dot(p.astype(BF), dob)
            dks[g, pl.ds(0, keys), :] += dot(ds, qb)
            kt = kts[pl.ds(pl.multiple_of(g * HEAD_SIZE, HEAD_SIZE), HEAD_SIZE), pl.ds(0, keys)]
            dqts[pl.ds(pl.multiple_of(h * HEAD_SIZE, HEAD_SIZE), HEAD_SIZE), at] = dot(kt, ds) * 0.125
            return 0

        lax.fori_loop(0, heads, one, 0)
    for j in range(group):
        at = slice(j * LANES, (j + 1) * LANES)
        part = dqts[pl.ds(j * LANES, LANES), :].T
        dq_ref[:, at] = part if far else part + dq_far[:, at]
    for g in range(2):
        at = slice(g * HEAD_SIZE, (g + 1) * HEAD_SIZE)
        dk_ref[:, at] = dks[g].astype(dk_ref.dtype)
        dv_ref[:, at] = dvs[g].astype(dv_ref.dtype)


def attend_back(q, keys, begin, start, o, do, lse, dq_far=None, q_blocks=3):
    far = dq_far is None
    rows, q_width = q.shape
    kv_width = keys.shape[1] // 2
    pairs = kv_width // LANES
    group = q_width // kv_width
    spec = lambda off: pl.BlockSpec((rows, LANES), lambda i: (0, i + off))
    wide = pl.BlockSpec((rows, group * LANES), lambda i: (0, i))
    sd = jax.ShapeDtypeStruct
    kind = BF if far else F32
    vm = pltpu.VMEM
    return pl.pallas_call(
        functools.partial(attend_back_kernel, group, q_blocks, far),
        grid=(pairs,),
        in_specs=[pl.BlockSpec(memory_space=pltpu.SMEM), pl.BlockSpec((1, rows), lambda i: (0, 0)), wide, spec(0), spec(pairs), wide, wide]
        + [pl.BlockSpec((1, 8, rows), lambda i: (i, 0, 0))] + ([] if far else [wide]),
        out_specs=[wide, spec(0), spec(0)],
        out_shape=[sd((rows, q_width), F32), sd((rows, kv_width), kind), sd((rows, kv_width), kind)],
        scratch_shapes=[
            vm((rows, rows), F32), vm((2, rows, HEAD_SIZE), BF), vm((2, rows, HEAD_SIZE), BF), vm((LANES, rows), BF),
            vm((2 * group, rows, HEAD_SIZE), BF), vm((2 * group, rows, HEAD_SIZE), BF), vm((2 * group * HEAD_SIZE, rows), F32),
            vm((2, rows, HEAD_SIZE), F32), vm((2, rows, HEAD_SIZE), F32), vm((8, rows), F32),
        ],
        compiler_params=pltpu.CompilerParams(vmem_limit_bytes=56 << 20),
        cost_estimate=pl.CostEstimate(flops=12 * rows * rows * q_width, bytes_accessed=16 << 20, transcendentals=rows * rows * 12),
    )(start, begin, q, keys, keys, o, do, lse, *(() if far else (dq_far,)))


def slab_of(rows, ctx):
    edge = 3 * rows // 8 // 16 * 16
    take = rows - edge
    return pl.ds(pl.multiple_of(ctx * edge, 16), take), pl.ds(pl.multiple_of(ctx * take, 16), edge)


def gather_kernel(n, count, extra, *refs):
    total = count + extra
    ins, outs = refs[:total], refs[total : 2 * total]
    own_sem, z_send, z_recv, y_send, y_recv, x_send, x_recv, extra_sem = refs[2 * total :]
    outer, inner = levels(n)
    me = lax.axis_index("fsdp")
    ctx = lax.axis_index("ctx")
    z, y = me // inner, me % inner
    right = (z + 1) % outer * inner + y
    left = (z + outer - 1) % outer * inner + y

    def shard(do, dj):
        return (z + outer - do) % outer * inner + (y + inner - dj) % inner

    own = [pltpu.make_async_copy(ins[a], outs[a].at[me], own_sem.at[a]) for a in range(count)]
    barrier = pltpu.get_barrier_semaphore()
    peers = [right, left] + [z * inner + (y + dj) % inner for dj in range(1, inner)]
    for peer in peers:
        pl.semaphore_signal(barrier, inc=1, device_id={"fsdp": peer}, device_id_type=MESH)
    pl.semaphore_signal(barrier, inc=1, device_id={"ctx": 1 - ctx}, device_id_type=MESH)
    pl.semaphore_wait(barrier, len(peers) + 1)

    def cut(a):
        return 3 * outs[a].shape[1] // 8 >= 16

    def taken(a, k):
        if not cut(a):
            return outs[a].at[k]
        return outs[a].at[k, slab_of(outs[a].shape[1], ctx)[0]]

    def remote(part, send, recv, to, src=None):
        src = part if src is None else src
        return pltpu.make_async_remote_copy(src_ref=src, dst_ref=part, send_sem=send, recv_sem=recv, device_id=to, device_id_type=MESH)

    def from_own(a):
        return ins[a].at[slab_of(ins[a].shape[0], ctx)[0]] if cut(a) else ins[a]

    def z_copy(a, k):
        src = from_own(a) if k == 1 else None
        return remote(taken(a, shard(k - 1, 0)), z_send.at[a, k - 1], z_recv.at[a, k - 1], {"fsdp": right}, src)

    def y_copy(a, do, dj):
        to = {"fsdp": z * inner + (y + dj) % inner}
        src = from_own(a) if do == 0 else None
        return remote(taken(a, shard(do, 0)), y_send.at[a, do, dj - 1], y_recv.at[a, do, dj - 1], to, src)

    def x_copy(a, do, dj):
        part = outs[a].at[shard(do, dj), slab_of(outs[a].shape[1], ctx)[1]]
        return remote(part, x_send.at[a, do, dj], x_recv.at[a, do, dj], {"ctx": 1 - ctx})

    started = []

    def go(copy):
        copy.start()
        started.append(copy)

    straight = [
        pltpu.make_async_remote_copy(
            src_ref=ins[count + i], dst_ref=outs[count + i], send_sem=extra_sem.at[0, i], recv_sem=extra_sem.at[1, i],
            device_id={"ctx": 1 - ctx}, device_id_type=MESH,
        )
        for i in range(extra)
    ]
    for c in straight:
        c.start()
    for a in range(count):
        go(z_copy(a, 1))
        for dj in range(1, inner):
            go(y_copy(a, 0, dj))
    for c in own:
        c.start()
    for do in range(1, outer + 1):
        for a in range(count):
            if do < outer:
                z_copy(a, do).wait_recv()
                if do + 1 < outer:
                    go(z_copy(a, do + 1))
                for dj in range(1, inner):
                    go(y_copy(a, do, dj))
                if cut(a):
                    go(x_copy(a, do, 0))
        for a in range(count):
            for dj in range(1, inner):
                y_copy(a, do - 1, dj).wait_recv()
                if cut(a):
                    go(x_copy(a, do - 1, dj))
    for a in range(count):
        if cut(a):
            for do in range(outer):
                for dj in range(inner):
                    if do or dj:
                        x_copy(a, do, dj).wait_recv()
    for c in started:
        c.wait_send()
    for c in straight:
        c.wait()
    for c in own:
        c.wait()


def gather_packs(packs, extra, collective_id):
    n = lax.axis_size("fsdp")
    outer, inner = levels(n)
    count = len(packs)
    tp_at = lax.axis_index("tp")
    arrays = []
    for parts in packs:
        cut = [a if cols == a.shape[1] else lax.dynamic_slice_in_dim(a, tp_at * cols, cols, 1) for a, cols in parts]
        arrays.append(jnp.concatenate(cut, axis=1) if len(cut) > 1 else cut[0])
    dma = pltpu.SemaphoreType.DMA
    anywhere = pl.BlockSpec(memory_space=pl.ANY)
    side = max(inner - 1, 1)
    return pl.pallas_call(
        functools.partial(gather_kernel, n, count, len(extra)),
        in_specs=[anywhere] * (count + len(extra)),
        out_specs=[anywhere] * (count + len(extra)),
        out_shape=[jax.ShapeDtypeStruct((n,) + a.shape, a.dtype) for a in arrays]
        + [jax.ShapeDtypeStruct(a.shape, a.dtype) for a in extra],
        scratch_shapes=[
            dma((count,)), dma((count, outer - 1)), dma((count, outer - 1)),
            dma((count, outer, side)), dma((count, outer, side)), dma((count, outer, inner)), dma((count, outer, inner)),
            dma((2, max(len(extra), 1))),
        ],
        compiler_params=pltpu.CompilerParams(collective_id=collective_id, has_side_effects=True),
    )(*arrays, *extra)


def t_dot_k(left, right):
    return dot(left, right, ((0,), (0,)))


def expert_loop(experts, ids_ref, t_ref, c_ref, w_refs, lows, kept, moe_acc, dn2_acc, spare):
    rows, width = c_ref.shape
    count = len(w_refs)
    ff = lows[0].shape[1]
    gl, ul, al = lows
    n2 = t_ref[:, :width]
    cot = c_ref[...]
    extra = t_ref[:, width:].astype(F32)
    lane = lax.broadcasted_iota(jnp.int32, extra.shape, 1)
    back_lane = lax.broadcasted_iota(jnp.int32, (rows, spare), 1)
    dgate = jnp.zeros((rows, spare), F32)
    act_sum, dg_sum, du_sum = kept
    for k in range(count):
        e = ids_ref[k]
        w = w_refs[k]
        gate = jnp.sum(jnp.where((lane == e) | (lane == experts + e), extra, 0.0), axis=1, keepdims=True)
        gv = dot(n2, w[:, :ff]) + gl
        uv = dot(n2, w[:, ff : 2 * ff]) + ul
        back = dot(cot, w[:, 2 * ff :]) + al
        sig = 1.0 / (1.0 + jnp.exp(-gv))
        silu = gv * sig
        act = silu * uv
        col = jnp.sum(act * back, axis=1, keepdims=True)
        high = col.astype(BF).astype(F32)
        at = e + ids_ref[count]
        dgate = dgate + jnp.where(back_lane == at, high, 0.0) + jnp.where(back_lane == at + experts, col - high, 0.0)
        back = back * gate
        act = act * gate
        du = back * silu
        dg = back * uv * (sig + silu * (1.0 - sig))
        act_sum = act if act_sum is None else act_sum + act
        dg_sum = dg if dg_sum is None else dg_sum + dg
        du_sum = du if du_sum is None else du_sum + du
        moe = dot_t(act.astype(BF), w[:, 2 * ff :])
        dn2 = dot_t(jnp.concatenate([dg.astype(BF), du.astype(BF)], axis=1), w[:, : 2 * ff])
        if k == 0:
            moe_acc[...] = moe
            dn2_acc[...] = dn2
        else:
            moe_acc[...] += moe
            dn2_acc[...] += dn2
    return dgate, act_sum, dg_sum, du_sum


def row_mask(experts, t_ref, width):
    extra = t_ref[:, width:].astype(F32)
    lane = lax.broadcasted_iota(jnp.int32, extra.shape, 1)
    chosen = jnp.sum(jnp.where(lane == 2 * experts, extra, 0.0), axis=1, keepdims=True)
    low_lane = lax.broadcasted_iota(jnp.int32, (extra.shape[0], LANES), 1)
    return ((low_lane // ADAPTER_RANK).astype(F32) == chosen).astype(F32)


def first_experts_kernel(experts, count, ids_ref, t_ref, c_ref, *refs):
    w_refs = refs[:count]
    ga_ref, ua_ref, gb_ref, ub_ref, db_ref, da_ref, r_ref, m_ref, wide_ref, thin_ref, moe_acc, dn2_acc = refs[count:]
    width = c_ref.shape[1]
    mask = row_mask(experts, t_ref, width)
    n2 = t_ref[:, :width]
    zg = (dot(n2, ga_ref[...]) * mask).astype(BF)
    zu = (dot(n2, ua_ref[...]) * mask).astype(BF)
    down_back = (dot_t(c_ref[...], db_ref[...]) * mask).astype(BF)
    lows = (dot(zg, gb_ref[...]), dot(zu, ub_ref[...]), dot_t(down_back, da_ref[...]))
    dgate, *sums = expert_loop(experts, ids_ref, t_ref, c_ref, w_refs, lows, (None, None, None), moe_acc, dn2_acc, r_ref.shape[1] - width)
    thin_ref[...] = jnp.concatenate([zg, zu, down_back], axis=1)
    wide_ref[...] = jnp.concatenate([*lows, *sums], axis=1)
    m_ref[...] = moe_acc[...].astype(BF)
    r_ref[:, :width] = dn2_acc[...].astype(BF)
    r_ref[:, width:] = dgate.astype(BF)


def last_experts_kernel(experts, count, ids_ref, t_ref, c_ref, *refs):
    w_refs = refs[:count]
    ga_ref, ua_ref, gb_ref, ub_ref, db_ref, da_ref = refs[count : count + 6]
    prior = refs[count + 6 : count + 11]
    r1_ref, m1_ref, wide_ref, thin_ref, r_ref, m_ref = refs[count + 11 : count + 17]
    sums = refs[count + 17 : count + 22]
    moe_acc, dn2_acc = refs[count + 22 :]
    width = c_ref.shape[1]
    ff = gb_ref.shape[1]

    @pl.when(pl.program_id(0) == 0)
    def _():
        for old, new in zip(prior, sums):
            new[...] = old[...]

    mask = row_mask(experts, t_ref, width)
    parts = [wide_ref[:, i * ff : (i + 1) * ff] for i in range(6)]
    dgate, act_sum, dg_sum, du_sum = expert_loop(
        experts, ids_ref, t_ref, c_ref, w_refs, parts[:3], parts[3:], moe_acc, dn2_acc, r_ref.shape[1] - width
    )
    zg, zu, down_back = thin_ref[:, :LANES], thin_ref[:, LANES : 2 * LANES], thin_ref[:, 2 * LANES :]
    act_sum, dg_sum, du_sum = act_sum.astype(BF), dg_sum.astype(BF), du_sum.astype(BF)
    low = (dot(act_sum, da_ref[...]) * mask).astype(BF)
    gdu = (dot_t(dg_sum, gb_ref[...]) * mask).astype(BF)
    udu = (dot_t(du_sum, ub_ref[...]) * mask).astype(BF)
    m_ref[...] = (moe_acc[...] + dot(low, db_ref[...]) + m1_ref[...].astype(F32)).astype(BF)
    dn2 = dn2_acc[...] + dot_t(gdu, ga_ref[...]) + dot_t(udu, ua_ref[...])
    r_ref[:, :width] = (dn2 + r1_ref[:, :width].astype(F32)).astype(BF)
    r_ref[:, width:] = (dgate + r1_ref[:, width:].astype(F32)).astype(BF)
    bd_ref, ad_ref, bg_ref, bu_ref, a_ref = sums
    cot = c_ref[...]
    bd_ref[...] += t_dot_k(low, cot)
    ad_ref[...] += t_dot_k(act_sum, down_back)
    bg_ref[...] += t_dot_k(zg, dg_sum)
    bu_ref[...] += t_dot_k(zu, du_sum)
    a_ref[...] += t_dot_k(t_ref[:, :width], jnp.concatenate([gdu, udu], axis=1))


def experts_on(ids, experts, spare, t, cot, weights, w_two, first, low_two, down_b, down_at, prior=(), early=()):
    rows, width = cot.shape
    ff = down_at.shape[0]
    step = 256
    sd = jax.ShapeDtypeStruct
    whole = lambda a: pl.BlockSpec(a.shape, lambda i: (0, 0))
    once = lambda a: pl.BlockSpec(a.shape, lambda i: (0, 0), pipeline_mode=pl.Buffered(1))
    by_row = lambda cols: pl.BlockSpec((step, cols), lambda i: (i, 0))
    column = lambda height, cols, at: pl.BlockSpec((height, cols), lambda i: (0, at))
    low_rows = low_two.shape[0]
    count = len(weights)
    flops = 2 * rows * width * ff * 7 * count
    out_specs = [by_row(width + spare), by_row(width)]
    out_shape = [sd((rows, width + spare), BF), sd((rows, width), BF)]
    if early:
        out_specs += [whole(p) for p in prior]
        out_shape += [sd(p.shape, F32) for p in prior]
    else:
        out_specs += [by_row(6 * ff), by_row(3 * LANES)]
        out_shape += [sd((rows, 6 * ff), F32), sd((rows, 3 * LANES), BF)]
    outs = pl.pallas_call(
        functools.partial(last_experts_kernel if early else first_experts_kernel, experts, count),
        grid=(rows // step,),
        in_specs=[pl.BlockSpec(memory_space=pltpu.SMEM), by_row(t.shape[1]), by_row(width)]
        + [once(w) for w in weights]
        + [column(width, LANES, first), column(width, LANES, first + 1), column(low_rows, ff, 0), column(low_rows, ff, 1), whole(down_b), whole(down_at)]
        + [once(p) for p in prior] + [by_row(e.shape[1]) for e in early],
        out_specs=out_specs,
        out_shape=out_shape,
        scratch_shapes=[pltpu.VMEM((step, width), F32), pltpu.VMEM((step, width), F32)],
        input_output_aliases={3 + count + 6 + i: 2 + i for i in range(len(prior))},
        compiler_params=pltpu.CompilerParams(vmem_limit_bytes=58 << 20),
        cost_estimate=pl.CostEstimate(flops=flops, bytes_accessed=24 << 20, transcendentals=rows * ff * count),
    )(ids, t, cot, *weights, w_two, w_two, low_two, low_two, down_b, down_at, *prior, *early)
    return outs


class Crossing:
    def __init__(self):
        self.n_ctx, self.n_tp = lax.axis_size("ctx"), lax.axis_size("tp")
        self.tp_at = lax.axis_index("tp")

    def pairs(self, by):
        return [(c, (c + by) % self.n_ctx) for c in range(self.n_ctx)]

    def half(self, block):
        if self.n_tp != 2:
            return block
        size = block.shape[0] // 2
        return lax.dynamic_slice_in_dim(block, self.tp_at * size, size, 0)

    def other_half(self, block):
        size = block.shape[0] // 2
        return lax.dynamic_slice_in_dim(block, (1 - self.tp_at) * size, size, 0)

    def joined(self, half):
        if self.n_tp != 2:
            return half
        other = lax.ppermute(half, "tp", [(0, 1), (1, 0)])
        size = half.shape[0]
        whole = lax.dynamic_update_slice_in_dim(jnp.zeros((2 * size,) + half.shape[1:], half.dtype), half, self.tp_at * size, 0)
        return lax.dynamic_update_slice_in_dim(whole, other, (1 - self.tp_at) * size, 0)

    def fetch(self, block):
        half = self.half(block)
        return [lax.ppermute(half, "ctx", self.pairs(by)) for by in range(1, self.n_ctx)]

    def summed_half(self, block):
        if self.n_tp != 2:
            return block.astype(F32)
        return self.half(block).astype(F32) + lax.ppermute(self.other_half(block), "tp", [(0, 1), (1, 0)]).astype(F32)

    def swapped(self, blocks):
        if self.n_tp != 2:
            return [jnp.zeros_like(b) for b in blocks]
        return [lax.ppermute(self.other_half(b), "tp", [(0, 1), (1, 0)]) for b in blocks]

    def halves_of_total(self, own, parts):
        found = self.summed_half(own)
        for part in parts:
            found = found + part.astype(F32)
        if self.n_tp != 2:
            found = lax.psum(found, "tp").astype(BF)
            size = found.shape[0] // 2
            return found[:size], found[size:], 0
        found = found.astype(BF)
        return found, lax.ppermute(found, "tp", [(0, 1), (1, 0)]), self.tp_at


def put_rows(pack, value, at, height):
    for f in range(pack.shape[0]):
        pack[f, pl.ds(at, height), :] = value[f * height : (f + 1) * height, :].astype(pack.dtype)


def put_cols(pack, value, at, height, first):
    for i in range(value.shape[1] // LANES):
        for f in range(pack.shape[0]):
            spot = pl.ds(pl.multiple_of(at + (first + i) * height, 8 if height % 16 else 16), height)
            pack[f, spot, :] = value[f * height : (f + 1) * height, i * LANES : (i + 1) * LANES].astype(pack.dtype)


def adapter_mask(chosen_ref):
    rows = chosen_ref.shape[0]
    return (lax.broadcasted_iota(jnp.int32, (rows, LANES), 1) // ADAPTER_RANK == chosen_ref[...]).astype(F32)


def qkv_back_kernel(n_tp, low_rows, share, tp_ref, dq_ref, dko_ref, dvo_ref, fb_ref, cos_ref, sin_ref, n1_ref, u_ref, chosen_ref, w_ref, lb_ref, dn1_ref, pack_ref, a_acc, b_acc):
    q_width, kv_width = dq_ref.shape[1], dko_ref.shape[1]
    ranks = LANES
    rows = dq_ref.shape[0]
    step = pl.program_id(0)
    mask = adapter_mask(chosen_ref)
    head = lax.broadcasted_iota(jnp.int32, (rows, LANES), 1) % HEAD_SIZE < HEAD_SIZE // 2

    def turned_back(v):
        swapped = jnp.where(head, pltpu.roll(v, LANES - HEAD_SIZE // 2, 1), pltpu.roll(v, HEAD_SIZE // 2, 1))
        return (v * cos_ref[...] - swapped * sin_ref[...]).astype(BF)

    dq = [turned_back(dq_ref[:, i : i + LANES]) for i in range(0, q_width, LANES)]
    dk = [turned_back(dko_ref[:, i : i + LANES] + fb_ref[:, i : i + LANES].astype(F32)) for i in range(0, kv_width, LANES)]
    dv = (dvo_ref[...] + fb_ref[:, kv_width:].astype(F32)).astype(BF)
    dq = jnp.concatenate(dq, axis=1)
    dk = jnp.concatenate(dk, axis=1) if len(dk) > 1 else dk[0]
    lows = []
    at = 0
    for d in (dq, dk, dv):
        lows.append((dot_t(d, lb_ref[:, at : at + d.shape[1]]) * mask).astype(BF))
        at += d.shape[1]
    lows = jnp.concatenate(lows, axis=1)
    dn1_ref[...] = dot_t(jnp.concatenate([dq, dk, dv, lows], axis=1), w_ref[...]).astype(BF)
    n1 = n1_ref[...]
    parts = [
        (a_acc, slice(0, 3 * ranks), t_dot_k(n1, lows)),
        (b_acc, slice(0, q_width), t_dot_k(u_ref[:, :ranks], dq)),
        (b_acc, slice(q_width, q_width + kv_width), t_dot_k(u_ref[:, ranks : 2 * ranks], dk)),
        (b_acc, slice(q_width + kv_width, q_width + 2 * kv_width), t_dot_k(u_ref[:, 2 * ranks :], dv)),
    ]

    @pl.when(step == 0)
    def _():
        for acc, cols, value in parts:
            acc[:, cols] = value

    @pl.when(step > 0)
    def _():
        for acc, cols, value in parts:
            acc[:, cols] += value

    @pl.when(step == pl.num_programs(0) - 1)
    def _():
        pack_ref[...] = jnp.zeros_like(pack_ref)
        at, col = 0, 0
        for i, cols in enumerate((q_width, kv_width, kv_width)):
            put_rows(pack_ref, a_acc[:, i * ranks : (i + 1) * ranks], at, share)
            at += share
            put_cols(pack_ref, b_acc[:, col : col + cols], at, low_rows, tp_ref[0] * (cols // LANES))
            at += cols * n_tp // LANES * low_rows
            col += cols


def qkv_back(n, n_tp, low_rows, share, tp_at, dq, dko, dvo, fb, cos, sin, n1, u3, chosen, w_one, low_one, height):
    rows, q_width = dq.shape
    width = n1.shape[1]
    step = 256
    by_row = lambda a: pl.BlockSpec((step, a.shape[1]), lambda i: (i, 0))
    whole = lambda a: pl.BlockSpec(a.shape, lambda i: (0, 0), pipeline_mode=pl.Buffered(1))
    sd = jax.ShapeDtypeStruct
    return pl.pallas_call(
        functools.partial(qkv_back_kernel, n_tp, low_rows, share),
        grid=(rows // step,),
        in_specs=[pl.BlockSpec(memory_space=pltpu.SMEM)] + [by_row(a) for a in (dq, dko, dvo, fb, cos, sin, n1, u3, chosen)] + [whole(w_one), whole(low_one)],
        out_specs=[pl.BlockSpec((step, width), lambda i: (i, 0)), pl.BlockSpec((n, height, LANES), lambda i: (0, 0, 0))],
        out_shape=[sd((rows, width), BF), sd((n, height, LANES), F32)],
        scratch_shapes=[pltpu.VMEM((width, 3 * LANES), F32), pltpu.VMEM((LANES, low_one.shape[1]), F32)],
        compiler_params=pltpu.CompilerParams(vmem_limit_bytes=50 << 20),
        cost_estimate=pl.CostEstimate(flops=4 * rows * width * w_one.shape[1], bytes_accessed=24 << 20, transcendentals=0),
    )(tp_at, dq, dko, dvo, fb, cos, sin, n1, u3, chosen, w_one, low_one)


def normed_rows(v, gain):
    return v * lax.rsqrt(jnp.mean(v * v, axis=1, keepdims=True) + norm_eps) * gain


def turned(v, cos, sin):
    head = lax.broadcasted_iota(jnp.int32, v.shape, 1) % HEAD_SIZE < HEAD_SIZE // 2
    swapped = jnp.where(head, pltpu.roll(v, LANES - HEAD_SIZE // 2, 1), pltpu.roll(v, HEAD_SIZE // 2, 1))
    return v * cos + swapped * sin


def kv_kernel(q_width, x_ref, chosen_ref, cos_ref, sin_ref, gain_ref, w_ref, low_ref, n1_ref, u_ref, kv_ref):
    kv_width = kv_ref.shape[1] // 2
    mask = adapter_mask(chosen_ref)
    n1 = normed_rows(x_ref[...].astype(F32), gain_ref[...]).astype(BF)
    n1_ref[...] = n1
    raw = dot(n1, w_ref[:, q_width:])
    lows = (raw[:, 2 * kv_width :] * jnp.concatenate([mask] * 3, axis=1)).astype(BF)
    u_ref[...] = lows
    key = raw[:, :kv_width] + dot(lows[:, LANES : 2 * LANES], low_ref[:, q_width : q_width + kv_width])
    for i in range(0, kv_width, LANES):
        kv_ref[:, i : i + LANES] = turned(key[:, i : i + LANES], cos_ref[...], sin_ref[...]).astype(BF)
    value = raw[:, kv_width : 2 * kv_width] + dot(lows[:, 2 * LANES :], low_ref[:, q_width + kv_width :])
    kv_ref[:, kv_width:] = value.astype(BF)


def q_kernel(n1_ref, u_ref, cos_ref, sin_ref, w_ref, low_ref, q_ref):
    q_width = q_ref.shape[1]
    q = dot(n1_ref[...], w_ref[:, :q_width]) + dot(u_ref[:, :LANES], low_ref[:, :q_width])
    for i in range(0, q_width, LANES):
        q_ref[:, i : i + LANES] = (turned(q[:, i : i + LANES], cos_ref[...], sin_ref[...]) * 0.125).astype(BF)


def out_kernel(o_ref, chosen_ref, w_ref, oa_ref, low_ref, part_ref, u_ref):
    q_width, width = o_ref.shape[1], part_ref.shape[1]
    ff2 = low_ref.shape[1] - 2 * width - LANES
    o = o_ref[...]
    u = (dot(o, oa_ref[...]) * adapter_mask(chosen_ref)).astype(BF)
    u_ref[...] = u
    part_ref[...] = (dot_t(o, w_ref[:, :q_width]) + dot(u, low_ref[:, ff2 : ff2 + width])).astype(BF)


def route_kernel(experts, q_width, x_ref, one_ref, other_ref, chosen_ref, routes_ref, gain_ref, w_ref, low_ref, h_ref, t_ref, u_ref):
    width = h_ref.shape[1]
    rows = h_ref.shape[0]
    h = x_ref[...].astype(F32) + (one_ref[...].astype(F32) + other_ref[...].astype(F32))
    h_ref[...] = h
    n2 = normed_rows(h, gain_ref[...]).astype(BF)
    t_ref[:, :width] = n2
    u = (dot(n2, w_ref[:, q_width : q_width + LANES]) * adapter_mask(chosen_ref)).astype(BF)
    u_ref[...] = u
    logits = dot(n2, w_ref[:, q_width + 3 * LANES : q_width + 4 * LANES]) + dot(u, low_ref[:, low_ref.shape[1] - LANES :])
    lane = lax.broadcasted_iota(jnp.int32, (rows, LANES), 1)
    selected = lane == routes_ref[:, 0:1]
    for k in range(1, routes_ref.shape[1]):
        selected = selected | (lane == routes_ref[:, k : k + 1])
    top = jnp.max(jnp.where(selected, logits, -jnp.inf), axis=1, keepdims=True)
    gates = jnp.where(selected, jnp.exp(jnp.where(selected, logits - top, 0.0)), 0.0)
    gates = gates / jnp.sum(gates, axis=1, keepdims=True)
    high = gates.astype(BF).astype(F32)
    extra = high + pltpu.roll(gates - high, experts, 1) + jnp.where(lane == 2 * experts, chosen_ref[...].astype(F32), 0.0)
    t_ref[:, width:] = extra.astype(BF)


def by_rows(kernel, step, rowed, whole, outs, flops):
    rows = rowed[0].shape[0]
    block = lambda cols: pl.BlockSpec((step, cols), lambda i: (i, 0))
    return pl.pallas_call(
        kernel,
        grid=(rows // step,),
        in_specs=[block(a.shape[1]) for a in rowed] + [pl.BlockSpec(a.shape, lambda i: (0, 0), pipeline_mode=pl.Buffered(1)) for a in whole],
        out_specs=[block(cols) for cols, kind in outs],
        out_shape=[jax.ShapeDtypeStruct((rows, cols), kind) for cols, kind in outs],
        compiler_params=pltpu.CompilerParams(vmem_limit_bytes=48 << 20),
        cost_estimate=pl.CostEstimate(flops=flops, bytes_accessed=1 << 20, transcendentals=0),
    )(*rowed, *whole)


def mid_back_kernel(n, n_tp, experts, share, low_rows, sel_ref, mine_ref, other_ref, h_ref, c_ref, t_ref, o_ref, ou_ref, ru_ref, chosen_ref, gain_ref,
                    w_ref, low_ref, oa_ref, bd_ref, ad_ref, bg_ref, bu_ref, agu_ref, dh_ref, do_ref, pack_ref, ar_acc, ao_acc, bo_acc, br_acc):
    width = h_ref.shape[1]
    q_width = o_ref.shape[1]
    ff = bg_ref.shape[1]
    spare = mine_ref.shape[1] - width
    step = pl.program_id(0)
    mask = adapter_mask(chosen_ref)
    picked = step == sel_ref[0]

    def fold(height, top):
        lane = lax.broadcasted_iota(jnp.int32, (height, LANES), 0)
        return ((lane % experts == lax.broadcasted_iota(jnp.int32, (height, LANES), 1)) & (lane < top)).astype(BF)

    back = jnp.where(picked, mine_ref[:, :width].astype(F32), other_ref[:, :width].astype(F32))
    tail = jnp.where(picked, mine_ref[:, width:].astype(F32), other_ref[:, width:].astype(F32)).astype(BF)
    dgate = dot(tail, fold(spare, 2 * experts * n_tp))
    gates = dot(t_ref[:, width:], fold(LANES, 2 * experts))
    n2 = t_ref[:, :width]
    router_a, router_w = w_ref[:, q_width : q_width + LANES], w_ref[:, q_width + 3 * LANES : q_width + 4 * LANES]
    out_b, router_b = low_ref[:, 2 * ff : 2 * ff + width], low_ref[:, 2 * ff + 2 * width :]
    dlog = (gates * (dgate - jnp.sum(gates * dgate, axis=1, keepdims=True))).astype(BF)
    rdu = (dot_t(dlog, router_b) * mask).astype(BF)
    dn2 = back + dot_t(dlog, router_w) + dot_t(rdu, router_a)
    h = h_ref[...]
    r = lax.rsqrt(jnp.mean(h * h, axis=1, keepdims=True) + norm_eps)
    gd = dn2 * gain_ref[...]
    dh = c_ref[...].astype(F32) + r * gd - h * (r * r * r * jnp.mean(gd * h, axis=1, keepdims=True))
    dh_ref[...] = dh
    dattn = dh.astype(BF)
    odu = (dot_t(dattn, out_b) * mask).astype(BF)
    do_ref[...] = (dot(dattn, w_ref[:, :q_width]) + dot_t(odu, oa_ref[...])).astype(BF)
    parts = [
        (ar_acc, t_dot_k(n2, rdu)),
        (ao_acc, t_dot_k(o_ref[...], odu)),
        (bo_acc, t_dot_k(ou_ref[...], dattn)),
        (br_acc, t_dot_k(ru_ref[...], dlog)),
    ]

    @pl.when(step == 0)
    def _():
        for acc, value in parts:
            acc[...] = value

    @pl.when(step > 0)
    def _():
        for acc, value in parts:
            acc[...] += value

    @pl.when(step == pl.num_programs(0) - 1)
    def _():
        pack_ref[...] = jnp.zeros_like(pack_ref)
        tp = sel_ref[1]
        first = (tp == 0).astype(F32)
        own = n // n_tp
        at = 0
        for k in range(own):
            pack_ref[tp * own + k, pl.ds(at, share), :] = ao_acc[k * share : (k + 1) * share, :].astype(pack_ref.dtype)
        at += share
        put_cols(pack_ref, bo_acc, at, low_rows, 0)
        at += width // LANES * low_rows
        ar_acc[...] = ar_acc[...] * first
        put_rows(pack_ref, ar_acc, at, share)
        at += share
        br_acc[...] = br_acc[...] * first
        put_cols(pack_ref, br_acc, at, low_rows, 0)
        at += low_rows
        for i, ref in enumerate((bg_ref, bu_ref)):
            put_rows(pack_ref, agu_ref[:, i * LANES : (i + 1) * LANES], at, share)
            at += share
            put_cols(pack_ref, ref, at, low_rows, tp * (ff // LANES))
            at += ff * n_tp // LANES * low_rows
        size = ad_ref.shape[0] // own
        for k in range(own):
            pack_ref[tp * own + k, pl.ds(at, size), :] = ad_ref[k * size : (k + 1) * size, :].astype(pack_ref.dtype)
        at += size
        put_cols(pack_ref, bd_ref, at, low_rows, 0)


def mid_back(n, n_tp, experts, share, low_rows, sel, mine, other, hidden, cot, carried, mixed, out_u, router_u, chosen, gain, w_two, low_two, out_a, sums, height):
    rows, width = hidden.shape
    q_width = mixed.shape[1]
    step = rows // 2
    sd = jax.ShapeDtypeStruct
    by_row = lambda a: pl.BlockSpec((step, a.shape[1]), lambda i: (i, 0))
    whole = lambda a: pl.BlockSpec(a.shape, lambda i: (0, 0), pipeline_mode=pl.Buffered(1))
    return pl.pallas_call(
        functools.partial(mid_back_kernel, n, n_tp, experts, share, low_rows),
        grid=(2,),
        in_specs=[pl.BlockSpec(memory_space=pltpu.SMEM), whole(mine), whole(other)]
        + [by_row(a) for a in (hidden, cot, carried, mixed, out_u, router_u, chosen)]
        + [whole(a) for a in (gain, w_two, low_two, out_a, *sums)],
        out_specs=[by_row(hidden), by_row(mixed), pl.BlockSpec((n, height, LANES), lambda i: (0, 0, 0))],
        out_shape=[sd((rows, width), F32), sd((rows, q_width), BF), sd((n, height, LANES), F32 if low_rows % 16 else BF)],
        scratch_shapes=[pltpu.VMEM((width, LANES), F32), pltpu.VMEM((q_width, LANES), F32), pltpu.VMEM((LANES, width), F32), pltpu.VMEM((LANES, LANES), F32)],
        compiler_params=pltpu.CompilerParams(vmem_limit_bytes=58 << 20),
        cost_estimate=pl.CostEstimate(flops=8 * rows * width * q_width, bytes_accessed=32 << 20, transcendentals=0),
    )(sel, mine, other, hidden, cot, carried, mixed, out_u, router_u, chosen, gain, w_two, low_two, out_a, *sums)


def reduce_kernel(n, pack_ref, side_ref, out_ref, side_out, side_in, side_snd, snd1, rcv1, acc, snd2, rcv2, acc2, snd3, rcv3, fin, sems, send3, recv3):
    me = lax.axis_index("fsdp")
    ctx = lax.axis_index("ctx")
    tp = lax.axis_index("tp")
    half = pack_ref.shape[1] // 2
    part = half // 2
    barrier = pltpu.get_barrier_semaphore()
    pl.semaphore_signal(barrier, inc=1, device_id={"tp": 1 - tp}, device_id_type=MESH)
    pl.semaphore_signal(barrier, inc=1, device_id={"ctx": 1 - ctx}, device_id_type=MESH)
    for k in range(1, n):
        pl.semaphore_signal(barrier, inc=1, device_id={"fsdp": (me + k) % n}, device_id_type=MESH)
    snd1[...] = pack_ref[:, pl.ds(pl.multiple_of((1 - tp) * half, 16), half), :].astype(BF)
    pl.semaphore_wait(barrier, n + 1)

    def swap(src, dst, i, to):
        copy = pltpu.make_async_remote_copy(src_ref=src, dst_ref=dst, send_sem=sems.at[0, i], recv_sem=sems.at[1, i], device_id=to, device_id_type=MESH)
        copy.start()
        return copy

    copy = swap(snd1, rcv1, 0, {"tp": 1 - tp})
    side = swap(side_ref, side_in.at[0], 4, {"tp": 1 - tp})
    copy.wait()
    acc[...] = pack_ref[:, pl.ds(pl.multiple_of(tp * half, 16), half), :] + rcv1[...].astype(F32)
    snd2[...] = acc[:, pl.ds(pl.multiple_of((1 - ctx) * part, 16), part), :].astype(BF)
    copy = swap(snd2, rcv2, 1, {"ctx": 1 - ctx})
    side.wait()
    side_snd[...] = (side_ref[...].astype(F32) + side_in[0].astype(F32)).astype(BF)
    side = swap(side_snd, side_in.at[1], 5, {"ctx": 1 - ctx})
    copy.wait()
    acc2[...] = acc[:, pl.ds(pl.multiple_of(ctx * part, 16), part), :] + rcv2[...].astype(F32)
    snd3[...] = acc2[...].astype(BF)

    def ship(k):
        to = (me + k) % n
        return pltpu.make_async_remote_copy(
            src_ref=snd3.at[to], dst_ref=rcv3.at[me], send_sem=send3.at[k], recv_sem=recv3.at[k], device_id={"fsdp": to}, device_id_type=MESH
        )

    def came(k):
        return pltpu.make_async_remote_copy(
            src_ref=snd3.at[me], dst_ref=rcv3.at[(me + n - k) % n], send_sem=send3.at[k], recv_sem=recv3.at[k],
            device_id={"fsdp": (me + k) % n}, device_id_type=MESH,
        )

    for k in range(1, n):
        ship(k).start()
    total = acc2[me]
    for k in range(1, n):
        came(k).wait_recv()
        total = total + rcv3[(me + n - k) % n].astype(F32)
    for k in range(1, n):
        ship(k).wait_send()
    spot = tp * 2 + ctx
    fin[spot] = total.astype(BF)
    copy = swap(fin.at[spot], fin.at[spot], 2, {"ctx": 1 - ctx})
    copy.wait()
    both = fin.at[pl.ds(tp * 2, 2)]
    copy = swap(both, both, 3, {"tp": 1 - tp})
    copy.wait()
    for i in range(4):
        out_ref[pl.ds(i * part, part), :] = fin[i].astype(F32)
    side.wait()
    side_out[...] = side_snd[...].astype(F32) + side_in[1].astype(F32)


def reduce_pack(pack, side, collective_id):
    n, height = pack.shape[:2]
    if lax.axis_size("tp") != 2 or lax.axis_size("ctx") != 2 or height % 64 or side.shape[0] % 16:
        mine = lax.psum_scatter(pack.astype(BF), "fsdp", scatter_dimension=0, tiled=False)
        return lax.psum(mine, ("ctx", "tp")).astype(F32), lax.psum(side, ("ctx", "tp")).astype(F32)
    half, part = height // 2, height // 4
    vm = pltpu.VMEM
    dma = pltpu.SemaphoreType.DMA
    return pl.pallas_call(
        functools.partial(reduce_kernel, n),
        in_specs=[pl.BlockSpec(memory_space=vm)] * 2,
        out_specs=[pl.BlockSpec(memory_space=vm)] * 2,
        out_shape=[jax.ShapeDtypeStruct((height, LANES), F32), jax.ShapeDtypeStruct(side.shape, F32)],
        scratch_shapes=[
            vm((2,) + side.shape, BF), vm(side.shape, BF), vm((n, half, LANES), BF), vm((n, half, LANES), BF), vm((n, half, LANES), F32),
            vm((n, part, LANES), BF), vm((n, part, LANES), BF), vm((n, part, LANES), F32),
            vm((n, part, LANES), BF), vm((n, part, LANES), BF), vm((4, part, LANES), BF),
            dma((2, 6)), dma((n,)), dma((n,)),
        ],
        compiler_params=pltpu.CompilerParams(collective_id=collective_id, has_side_effects=True, vmem_limit_bytes=48 << 20),
    )(pack, side)


def tp_sum(value):
    if lax.axis_size("tp") != 2:
        return lax.psum(value, "tp")
    return value + lax.ppermute(value, "tp", [(0, 1), (1, 0)])


def on_device(
    tokens, out_cotangent, lengths, adapter_of_doc, routes, attn_gain, ffn_gain,
    w_query, key_matrix, value_matrix, w_out, w_router, w_gate, w_up, w_down,
    a_query, b_query, a_key, key_second_factor, a_value, value_second_factor,
    a_out, b_out, a_router, b_router, a_gate, b_gate, a_up, b_up, a_down, b_down,
):
    rows, width = tokens.shape
    n = lax.axis_size("fsdp")
    n_tp = lax.axis_size("tp")
    tp_at = lax.axis_index("tp")
    ctx_at = lax.axis_index("ctx")
    group = rows * lax.axis_size("ctx")
    q_width = w_query.shape[1]
    kv_width = key_matrix.shape[1]
    ff_width = w_gate.shape[2]
    local_experts = w_gate.shape[0]
    experts = w_router.shape[1]
    ranks = a_query.shape[1]
    share = w_query.shape[0]
    low_rows = b_query.shape[0]

    pad = ((0, 0), (0, LANES - experts))
    one, low_one = gather_packs(
        [
            [(a, a.shape[1]) for a in (w_query, key_matrix, value_matrix, a_query, a_key, a_value)],
            [(b_query, q_width), (key_second_factor, kv_width), (value_second_factor, kv_width)],
        ],
        (),
        0,
    )
    qkv = q_width + 2 * kv_width
    w_one = one.reshape(n * share, -1)
    low_one = low_one.reshape(n * low_rows, -1)

    ends = jnp.cumsum(lengths[0])
    starts = ends - lengths[0]
    place = jnp.arange(group, dtype=jnp.int32)
    doc = jnp.sum((place[:, None] >= ends[None, :]).astype(jnp.int32), axis=1)
    picked = (doc[:, None] == jnp.arange(lengths.shape[1], dtype=jnp.int32)[None, :]).astype(jnp.int32)
    begin = jnp.sum(picked * starts[None, :], axis=1)
    chosen = jnp.sum(picked * adapter_of_doc[0][None, :], axis=1)
    start = ctx_at * rows
    query_index = start + jnp.arange(rows, dtype=jnp.int32)
    begin_local = lax.dynamic_slice_in_dim(begin, start, rows)
    chosen_local = lax.dynamic_slice_in_dim(chosen, start, rows)
    freq = 10000.0 ** (-jnp.arange(HEAD_SIZE // 2, dtype=F32) / (HEAD_SIZE // 2))
    angles = (query_index - begin_local).astype(F32)[:, None] * freq[None, :]
    cosine, sine = jnp.cos(angles), jnp.sin(angles)
    cosine_wide = jnp.tile(cosine, (1, 2 * LANES // HEAD_SIZE))
    sine_wide = jnp.tile(jnp.concatenate([-sine, sine], axis=1), (1, LANES // HEAD_SIZE))
    chosen_col = chosen_local[:, None]
    gain_one, gain_two = attn_gain[None, :], ffn_gain[None, :]
    normed, low_u, kv = by_rows(
        functools.partial(kv_kernel, q_width), 256, (tokens, chosen_col, cosine_wide, sine_wide), (gain_one, w_one, low_one),
        ((width, BF), (3 * ranks, BF), (2 * kv_width, BF)), 2 * rows * width * (w_one.shape[1] - q_width),
    )
    cross = Crossing()
    outer, inner = levels(n)
    me = lax.axis_index("fsdp")
    ring = [(i, (i + inner) % n) for i in range(n)]
    turns = [[(i, i // inner * inner + (i % inner + dj) % inner) for i in range(n)] for dj in range(1, inner)]
    local = local_experts // cross.n_ctx
    mine = [lax.dynamic_slice_in_dim(a, ctx_at * local, local, 0) for a in (w_gate, w_up, w_down)]
    block = jnp.concatenate([mine[0], mine[1], jnp.swapaxes(mine[2], 1, 2)], axis=2)
    brought = {(0, 0): block}

    def bring(do, after):
        last = [brought[(do, 0)]] + [brought[(do - 1, dj)] for dj in range(1, inner) if do]
        last, after = lax.optimization_barrier((last, after))
        brought[(do, 0)] = last[0]
        for dj, value in zip(range(1, inner), last[1:]):
            brought[(do - 1, dj)] = value
        if do + 1 < outer:
            brought[(do + 1, 0)] = lax.ppermute(last[0], "fsdp", ring)
        for dj in range(1, inner):
            brought[(do, dj)] = lax.ppermute(last[0], "fsdp", turns[dj - 1])
        return after

    one = bring(0, one)
    (query_state,) = by_rows(
        q_kernel, 256, (normed, low_u, cosine_wide, sine_wide), (w_one, low_one), ((q_width, BF),), 2 * rows * width * q_width
    )
    w_out, w_router, b_router, query_state = lax.optimization_barrier((w_out, w_router, b_router, query_state))
    two, low_two, down_a, far = gather_packs(
        [
            [(a, a.shape[1]) for a in (w_out.T, a_router, a_gate, a_up, jnp.pad(w_router, pad), a_out)],
            [(b_gate, ff_width), (b_up, ff_width), (b_out, width), (b_down, width), (jnp.pad(b_router, pad), LANES)],
            [(a_down, ranks)],
        ],
        (kv,),
        1,
    )
    cot = lax.optimization_barrier((out_cotangent, two))[0]
    cot_halves = cross.fetch(cot)
    far = bring(1, far)
    w_two = two.reshape(n * share, -1)
    low_two = low_two.reshape(n * low_rows, -1)
    down_b = low_two[:, 2 * ff_width + width : 2 * ff_width + 2 * width]
    out_a = lax.dynamic_slice_in_dim(w_two[:, q_width + 4 * ranks : q_width + 5 * ranks], tp_at * q_width, q_width, 0)
    down_at = lax.dynamic_slice_in_dim(down_a.reshape(-1, ranks), tp_at * ff_width, ff_width, 0)
    begin_row = begin_local[None, :]
    start_at = jnp.reshape(start, (1,)).astype(jnp.int32)
    mixed_heads, log_total = attend(query_state, kv, far, begin_row, start_at)
    cot_halves, mixed_heads = lax.optimization_barrier((cot_halves, mixed_heads))
    attn_part, out_u = by_rows(
        out_kernel, 256, (mixed_heads, chosen_col), (w_two, out_a, low_two), ((width, BF), (ranks, BF)), 0
    )
    attn_part = bring(2, attn_part)
    if n_tp == 2:
        attn_other = lax.ppermute(attn_part, "tp", [(0, 1), (1, 0)])
    else:
        attn_part, attn_other = lax.psum(attn_part.astype(F32), "tp"), jnp.zeros_like(attn_part)
    spare = -(-2 * experts * n_tp // LANES) * LANES
    hidden, carried, router_u = by_rows(
        functools.partial(route_kernel, experts, q_width), 256, (tokens, attn_part, attn_other, chosen_col, routes), (gain_two, w_two, low_two),
        ((width, F32), (width + LANES, BF), (ranks, BF)), 0,
    )
    halves = cross.fetch(carried)
    early = [(0, 0), (1, 0)] + [(0, dj) for dj in range(1, inner)] + [(2, 0)] + [(1, dj) for dj in range(1, inner)]
    late = [(do, 0) for do in range(3, outer)] + [(do, dj) for do in range(2, outer) for dj in range(1, inner)]
    last = [k for k in late if k[0] == outer - 1 and k[1]]
    between = [k for k in late if k not in last]

    def weights_of(keys):
        ids = [((me // inner + outer - do) % outer * inner + (me % inner + inner - dj) % inner) * local_experts + ctx_at * local + j for do, dj in keys for j in range(local)]
        return jnp.stack(ids + [tp_at * 2 * experts]).astype(jnp.int32), [brought[k][j] for k in keys for j in range(local)]

    sums = [jnp.zeros(shape, F32) for shape in ((ranks, width), (ff_width, ranks), (ranks, ff_width), (ranks, ff_width), (width, 2 * ranks))]
    at = q_width // LANES + 1
    work = [(carried, cot)] + [(None, None)] * (cross.n_ctx - 1)
    partial = []
    for by in range(cross.n_ctx):
        ids, weights = weights_of(early + between if by else early)
        if by:
            work[by] = (cross.joined(halves[by - 1]), cross.joined(cot_halves[by - 1]))
        r, m, wide, thin = experts_on(ids, experts, spare, *work[by], weights, w_two, at, low_two, down_b, down_at)
        if by == 0:
            for do in range(3, outer):
                r = bring(do, r)
            halves, cot_halves, r = lax.optimization_barrier((halves, cot_halves, r))
        partial.append((r, m, wide, thin))
    back_parts, moe_parts = [], []
    for by in list(range(1, cross.n_ctx)) + [0]:
        ids, weights = weights_of(last if by else late)
        r, m, *sums = experts_on(ids, experts, spare, *work[by], weights, w_two, at, low_two, down_b, down_at, sums, partial[by])
        moe_parts.append(m)
        if by:
            half = cross.summed_half(r).astype(BF)
            half, carried = lax.optimization_barrier((half, work[0][0]))
            work[0] = (carried, cot)
            back_parts.append(lax.ppermute(half, "ctx", cross.pairs(-by)))
    r, back_parts = lax.optimization_barrier((r, back_parts))
    mine_half, other, first = cross.halves_of_total(r, back_parts)
    swapped = cross.swapped(moe_parts)
    early_shapes = [
        (share, ranks), (low_rows, width), (share, ranks), (low_rows, experts), (share, ranks), (low_rows, ff_width * n_tp),
        (share, ranks), (low_rows, ff_width * n_tp), (a_down.shape[0], ranks), (low_rows, width),
    ]
    height = sum(-(-cols // LANES) * tall for tall, cols in early_shapes)
    sel = jnp.stack([jnp.asarray(first, jnp.int32), tp_at.astype(jnp.int32)])
    dhidden, dmixed, early_pack = mid_back(
        n, n_tp, experts, share, low_rows, sel, mine_half, other, hidden, cot, carried, mixed_heads, out_u, router_u,
        chosen_col, gain_two, w_two, low_two, out_a, sums, height,
    )
    early_pack, dmixed, swapped = lax.optimization_barrier((early_pack.astype(BF), dmixed, swapped))
    moe_halves = [cross.half(p).astype(F32) + q.astype(F32) for p, q in zip(moe_parts, swapped)]
    moe_got = [lax.ppermute(p.astype(BF), "ctx", cross.pairs(-by)) for by, p in zip(range(1, cross.n_ctx), moe_halves)]
    early_sum = lax.psum_scatter(early_pack, "fsdp", scatter_dimension=0, tiled=False)
    dq_far, dkey_far, dvalue_far = attend_back(query_state, far, begin_row, start_at, mixed_heads, dmixed, log_total)
    far_back = lax.ppermute(
        jnp.concatenate([dkey_far, dvalue_far], axis=1), "ctx", [(i + 1, i) for i in range(lax.axis_size("ctx") - 1)]
    )
    dquery, dkey_own, dvalue_own = attend_back(query_state, kv, begin_row, start_at, mixed_heads, dmixed, log_total, dq_far)
    far_back, moe_got, dquery = lax.optimization_barrier((far_back, moe_got, dquery))
    moe = moe_halves[-1]
    for part in moe_got:
        moe = moe + part.astype(F32)
    moe = cross.joined(moe.astype(BF)).astype(F32) if n_tp == 2 else lax.psum(moe, "tp")
    output = (hidden + moe).astype(BF)
    height = 3 * share + low_rows * n_tp * qkv // LANES
    dn1, pack = qkv_back(
        n, n_tp, low_rows, share, jnp.reshape(tp_at, (1,)).astype(jnp.int32), dquery, dkey_own, dvalue_own, far_back,
        cosine_wide, sine_wide, normed, low_u, chosen_col, w_one, low_one, height,
    )
    early_sum, dn1, pack = lax.optimization_barrier((early_sum, dn1, pack))
    late, early_sum = reduce_pack(pack, early_sum, 2)
    dn1 = tp_sum(dn1.astype(F32)) if n_tp != 2 else dn1.astype(F32) + lax.ppermute(dn1, "tp", [(0, 1), (1, 0)]).astype(F32)
    grad_tokens = (dhidden + norm_back(tokens.astype(F32), attn_gain, dn1)).astype(BF)

    def unpack(mine, shapes):
        found = []
        at = 0
        for height, cols in shapes:
            count = -(-cols // LANES)
            piece = mine[at : at + count * height].reshape(count, height, LANES).transpose(1, 0, 2).reshape(height, count * LANES)
            found.append(piece[:, :cols])
            at += count * height
        return found

    first_shapes = [(share, ranks), (low_rows, q_width * n_tp), (share, ranks), (low_rows, kv_width * n_tp), (share, ranks), (low_rows, kv_width * n_tp)]
    final = unpack(late, first_shapes) + unpack(early_sum, early_shapes)
    return (output, grad_tokens, *final)


def solution(mesh):
    both = P(("fsdp", "ctx"), None)
    split = P("fsdp", None)
    placed = (
        both, both, split, split, both, P(), P(),
        P("fsdp", "tp"), P("fsdp", "tp"), P("fsdp", "tp"), P("tp", "fsdp"), split,
        P("fsdp", None, "tp"), P("fsdp", None, "tp"), P("fsdp", "tp", None),
    ) + (split,) * 16
    return jax.shard_map(
        on_device, mesh=mesh, in_specs=placed, out_specs=(both, both) + (split,) * 16, check_vma=False
    )
```

```python
import functools

import jax
import jax.numpy as jnp
from jax import lax
from jax.experimental import pallas as pl
from jax.experimental.pallas import tpu as pltpu
from jax.sharding import PartitionSpec as P

HEAD_SIZE = 64
ADAPTER_RANK = 16
LANES = 128
norm_eps = 1e-05
BF = jnp.bfloat16
F32 = jnp.float32


MESH = pl.DeviceIdType.MESH


def dot(left, right, dims=((1,), (0,)), precision=None):
    return lax.dot_general(left, right, (dims, ((), ())), preferred_element_type=F32, precision=precision)


def dot_t(left, right):
    return dot(left, right, ((1,), (1,)))


def t_dot(left, right):
    return dot(left, right, ((0,), (0,)))


def rms_norm(values, gain):
    return values * lax.rsqrt(jnp.mean(values * values, axis=-1, keepdims=True) + norm_eps) * gain


def norm_back(values, gain, grad):
    unused, pull = jax.vjp(lambda inner: rms_norm(inner, gain), values)
    return pull(grad)[0]


def levels(n):
    outer = 4 if n % 4 == 0 else n
    return outer, n // outer


def fill_bias(bias, start_ref, begin_ref, rows):
    step = rows // 3
    for at in range(0, 2 * rows, step):
        key = start_ref[0] - rows + at + lax.broadcasted_iota(jnp.int32, (step, rows), 0)
        query = start_ref[0] + lax.broadcasted_iota(jnp.int32, (step, rows), 1)
        ok = (key <= query) & (key >= begin_ref[...]) & (key >= 0)
        bias[pl.ds(at, step), :] = jnp.where(ok, 0.0, -1e30)


def split_heads(ref, out, count, rows, at=0):
    for h in range(count):
        out[h, pl.ds(at, rows), :] = ref[:, h * HEAD_SIZE : (h + 1) * HEAD_SIZE]


def attend_kernel(group, q_blocks, start_ref, begin_ref, q_ref, ko_ref, vo_ref, kf_ref, vf_ref, o_ref, lse_ref, bias, ks, vts, qs, ots):
    rows = q_ref.shape[0]
    width = rows // q_blocks
    heads = 2 * group
    @pl.when(pl.program_id(0) == 0)
    def _():
        fill_bias(bias, start_ref, begin_ref, rows)
    split_heads(kf_ref, ks, 2, rows, 0)
    split_heads(ko_ref, ks, 2, rows, rows)
    split_heads(q_ref, qs, heads, rows, 0)
    vts[:, pl.ds(0, rows)] = vf_ref[...].astype(F32).T.astype(BF)
    vts[:, pl.ds(rows, rows)] = vo_ref[...].astype(F32).T.astype(BF)
    for b in range(q_blocks):
        keys = rows + (b + 1) * width
        def one(h, _):
            g = h // group
            s = dot_t(ks[g, pl.ds(0, keys), :], qs[h, pl.ds(b * width, width), :]) + bias[pl.ds(0, keys), pl.ds(b * width, width)]
            top = jnp.max(s, axis=0, keepdims=True)
            p = jnp.exp(s - top)
            total = jnp.sum(p, axis=0, keepdims=True)
            lse_ref[0, pl.ds(h, 1), pl.ds(b * width, width)] = top + jnp.log(total)
            vt = vts[pl.ds(pl.multiple_of(g * HEAD_SIZE, HEAD_SIZE), HEAD_SIZE), pl.ds(0, keys)]
            o = dot(vt, p.astype(BF)) / total
            ots[pl.ds(pl.multiple_of(h * HEAD_SIZE, HEAD_SIZE), HEAD_SIZE), pl.ds(b * width, width)] = o
            return 0
        lax.fori_loop(0, heads, one, 0)
    for j in range(group):
        o_ref[:, j * LANES : (j + 1) * LANES] = ots[pl.ds(j * LANES, LANES), :].T.astype(BF)


def attend(q, kv, far, begin, start, q_blocks=3):
    rows, q_width = q.shape
    kv_width = kv.shape[1] // 2
    pairs = kv_width // LANES
    group = q_width // kv_width
    spec = lambda off: pl.BlockSpec((rows, LANES), lambda i: (0, i + off))
    return pl.pallas_call(
        functools.partial(attend_kernel, group, q_blocks),
        grid=(pairs,),
        in_specs=[pl.BlockSpec(memory_space=pltpu.SMEM), pl.BlockSpec((1, rows), lambda i: (0, 0)),
                  pl.BlockSpec((rows, group * LANES), lambda i: (0, i)), spec(0), spec(pairs), spec(0), spec(pairs)],
        out_specs=[pl.BlockSpec((rows, group * LANES), lambda i: (0, i)), pl.BlockSpec((1, 8, rows), lambda i: (i, 0, 0))],
        out_shape=[jax.ShapeDtypeStruct((rows, q_width), BF), jax.ShapeDtypeStruct((pairs, 8, rows), F32)],
        scratch_shapes=[pltpu.VMEM((2 * rows, rows), F32), pltpu.VMEM((2, 2 * rows, HEAD_SIZE), BF), pltpu.VMEM((LANES, 2 * rows), BF),
                        pltpu.VMEM((2 * group, rows, HEAD_SIZE), BF), pltpu.VMEM((2 * group * HEAD_SIZE, rows), F32)],
        compiler_params=pltpu.CompilerParams(vmem_limit_bytes=50 << 20),
        cost_estimate=pl.CostEstimate(flops=8 * rows * rows * q_width, bytes_accessed=8 << 20, transcendentals=2 * rows * rows * 12),
    )(start, begin, q, kv, kv, far, far)


def attend_back_kernel(group, q_blocks, far, *refs):
    if far:
        start_ref, begin_ref, q_ref, k_ref, v_ref, o_ref, do_ref, lse_ref = refs[:8]
        dq_far = None
    else:
        start_ref, begin_ref, q_ref, k_ref, v_ref, o_ref, do_ref, lse_ref, dq_far = refs[:9]
    dq_ref, dk_ref, dv_ref, bias, ks, vs, kts, qs, dos, dqts, dks, dvs, deltas = refs[-13:]
    rows = q_ref.shape[0]
    width = rows // q_blocks
    heads = 2 * group

    @pl.when(pl.program_id(0) == 0)
    def _():
        first = start_ref[0] - rows if far else start_ref[0]
        for at in range(0, rows, width):
            key = first + at + lax.broadcasted_iota(jnp.int32, (width, rows), 0)
            query = start_ref[0] + lax.broadcasted_iota(jnp.int32, (width, rows), 1)
            ok = (key <= query) & (key >= begin_ref[...]) & (key >= 0)
            bias[pl.ds(at, width), :] = jnp.where(ok, 0.0, -1e30)

    split_heads(k_ref, ks, 2, rows, 0)
    split_heads(v_ref, vs, 2, rows, 0)
    split_heads(q_ref, qs, heads, rows, 0)
    split_heads(do_ref, dos, heads, rows, 0)
    kts[...] = k_ref[...].astype(F32).T.astype(BF)
    cols = heads * HEAD_SIZE
    pick = (
        lax.broadcasted_iota(jnp.int32, (8, cols), 1) // HEAD_SIZE == lax.broadcasted_iota(jnp.int32, (8, cols), 0)
    ).astype(F32)
    prod = o_ref[...].astype(F32) * do_ref[...].astype(F32)
    deltas[...] = dot(pick, prod, ((1,), (1,)), lax.Precision.HIGHEST)
    dks[...] = jnp.zeros_like(dks)
    dvs[...] = jnp.zeros_like(dvs)
    for b in range(q_blocks):
        keys = rows if far else (b + 1) * width

        def one(h, _):
            g = h // group
            at = pl.ds(b * width, width)
            qb = qs[h, at, :]
            dob = dos[h, at, :]
            s = dot_t(ks[g, pl.ds(0, keys), :], qb) + bias[pl.ds(0, keys), at]
            p = jnp.exp(s - lse_ref[0, pl.ds(h, 1), at])
            dp = dot_t(vs[g, pl.ds(0, keys), :], dob)
            ds = (p * (dp - deltas[pl.ds(h, 1), at])).astype(BF)
            dvs[g, pl.ds(0, keys), :] += dot(p.astype(BF), dob)
            dks[g, pl.ds(0, keys), :] += dot(ds, qb)
            kt = kts[pl.ds(pl.multiple_of(g * HEAD_SIZE, HEAD_SIZE), HEAD_SIZE), pl.ds(0, keys)]
            dqts[pl.ds(pl.multiple_of(h * HEAD_SIZE, HEAD_SIZE), HEAD_SIZE), at] = dot(kt, ds) * 0.125
            return 0

        lax.fori_loop(0, heads, one, 0)
    for j in range(group):
        at = slice(j * LANES, (j + 1) * LANES)
        part = dqts[pl.ds(j * LANES, LANES), :].T
        dq_ref[:, at] = part if far else part + dq_far[:, at]
    for g in range(2):
        at = slice(g * HEAD_SIZE, (g + 1) * HEAD_SIZE)
        dk_ref[:, at] = dks[g].astype(dk_ref.dtype)
        dv_ref[:, at] = dvs[g].astype(dv_ref.dtype)


def attend_back(q, keys, begin, start, o, do, lse, dq_far=None, q_blocks=3):
    far = dq_far is None
    rows, q_width = q.shape
    kv_width = keys.shape[1] // 2
    pairs = kv_width // LANES
    group = q_width // kv_width
    spec = lambda off: pl.BlockSpec((rows, LANES), lambda i: (0, i + off))
    wide = pl.BlockSpec((rows, group * LANES), lambda i: (0, i))
    sd = jax.ShapeDtypeStruct
    kind = BF if far else F32
    vm = pltpu.VMEM
    return pl.pallas_call(
        functools.partial(attend_back_kernel, group, q_blocks, far),
        grid=(pairs,),
        in_specs=[pl.BlockSpec(memory_space=pltpu.SMEM), pl.BlockSpec((1, rows), lambda i: (0, 0)), wide, spec(0), spec(pairs), wide, wide]
        + [pl.BlockSpec((1, 8, rows), lambda i: (i, 0, 0))] + ([] if far else [wide]),
        out_specs=[wide, spec(0), spec(0)],
        out_shape=[sd((rows, q_width), F32), sd((rows, kv_width), kind), sd((rows, kv_width), kind)],
        scratch_shapes=[
            vm((rows, rows), F32), vm((2, rows, HEAD_SIZE), BF), vm((2, rows, HEAD_SIZE), BF), vm((LANES, rows), BF),
            vm((2 * group, rows, HEAD_SIZE), BF), vm((2 * group, rows, HEAD_SIZE), BF), vm((2 * group * HEAD_SIZE, rows), F32),
            vm((2, rows, HEAD_SIZE), F32), vm((2, rows, HEAD_SIZE), F32), vm((8, rows), F32),
        ],
        compiler_params=pltpu.CompilerParams(vmem_limit_bytes=56 << 20),
        cost_estimate=pl.CostEstimate(flops=12 * rows * rows * q_width, bytes_accessed=16 << 20, transcendentals=rows * rows * 12),
    )(start, begin, q, keys, keys, o, do, lse, *(() if far else (dq_far,)))


def slab_of(rows, ctx):
    edge = 3 * rows // 8 // 16 * 16
    take = rows - edge
    return pl.ds(pl.multiple_of(ctx * edge, 16), take), pl.ds(pl.multiple_of(ctx * take, 16), edge)


def gather_kernel(n, count, extra, *refs):
    total = count + extra
    ins, outs = refs[:total], refs[total : 2 * total]
    own_sem, z_send, z_recv, y_send, y_recv, x_send, x_recv, extra_sem = refs[2 * total :]
    outer, inner = levels(n)
    me = lax.axis_index("fsdp")
    ctx = lax.axis_index("ctx")
    z, y = me // inner, me % inner
    right = (z + 1) % outer * inner + y
    left = (z + outer - 1) % outer * inner + y

    def shard(do, dj):
        return (z + outer - do) % outer * inner + (y + inner - dj) % inner

    own = [pltpu.make_async_copy(ins[a], outs[a].at[me], own_sem.at[a]) for a in range(count)]
    barrier = pltpu.get_barrier_semaphore()
    peers = [right, left] + [z * inner + (y + dj) % inner for dj in range(1, inner)]
    for peer in peers:
        pl.semaphore_signal(barrier, inc=1, device_id={"fsdp": peer}, device_id_type=MESH)
    pl.semaphore_signal(barrier, inc=1, device_id={"ctx": 1 - ctx}, device_id_type=MESH)
    pl.semaphore_wait(barrier, len(peers) + 1)

    def cut(a):
        return 3 * outs[a].shape[1] // 8 >= 16

    def taken(a, k):
        if not cut(a):
            return outs[a].at[k]
        return outs[a].at[k, slab_of(outs[a].shape[1], ctx)[0]]

    def remote(part, send, recv, to, src=None):
        src = part if src is None else src
        return pltpu.make_async_remote_copy(src_ref=src, dst_ref=part, send_sem=send, recv_sem=recv, device_id=to, device_id_type=MESH)

    def from_own(a):
        return ins[a].at[slab_of(ins[a].shape[0], ctx)[0]] if cut(a) else ins[a]

    def z_copy(a, k):
        src = from_own(a) if k == 1 else None
        return remote(taken(a, shard(k - 1, 0)), z_send.at[a, k - 1], z_recv.at[a, k - 1], {"fsdp": right}, src)

    def y_copy(a, do, dj):
        to = {"fsdp": z * inner + (y + dj) % inner}
        src = from_own(a) if do == 0 else None
        return remote(taken(a, shard(do, 0)), y_send.at[a, do, dj - 1], y_recv.at[a, do, dj - 1], to, src)

    def x_copy(a, do, dj):
        part = outs[a].at[shard(do, dj), slab_of(outs[a].shape[1], ctx)[1]]
        return remote(part, x_send.at[a, do, dj], x_recv.at[a, do, dj], {"ctx": 1 - ctx})

    started = []

    def go(copy):
        copy.start()
        started.append(copy)

    straight = [
        pltpu.make_async_remote_copy(
            src_ref=ins[count + i], dst_ref=outs[count + i], send_sem=extra_sem.at[0, i], recv_sem=extra_sem.at[1, i],
            device_id={"ctx": 1 - ctx}, device_id_type=MESH,
        )
        for i in range(extra)
    ]
    for c in straight:
        c.start()
    for a in range(count):
        go(z_copy(a, 1))
        for dj in range(1, inner):
            go(y_copy(a, 0, dj))
    for c in own:
        c.start()
    for do in range(1, outer + 1):
        for a in range(count):
            if do < outer:
                z_copy(a, do).wait_recv()
                if do + 1 < outer:
                    go(z_copy(a, do + 1))
                for dj in range(1, inner):
                    go(y_copy(a, do, dj))
                if cut(a):
                    go(x_copy(a, do, 0))
        for a in range(count):
            for dj in range(1, inner):
                y_copy(a, do - 1, dj).wait_recv()
                if cut(a):
                    go(x_copy(a, do - 1, dj))
    for a in range(count):
        if cut(a):
            for do in range(outer):
                for dj in range(inner):
                    if do or dj:
                        x_copy(a, do, dj).wait_recv()
    for c in started:
        c.wait_send()
    for c in straight:
        c.wait()
    for c in own:
        c.wait()


def gather_packs(packs, extra, collective_id):
    n = lax.axis_size("fsdp")
    outer, inner = levels(n)
    count = len(packs)
    tp_at = lax.axis_index("tp")
    arrays = []
    for parts in packs:
        cut = [a if cols == a.shape[1] else lax.dynamic_slice_in_dim(a, tp_at * cols, cols, 1) for a, cols in parts]
        arrays.append(jnp.concatenate(cut, axis=1) if len(cut) > 1 else cut[0])
    dma = pltpu.SemaphoreType.DMA
    anywhere = pl.BlockSpec(memory_space=pl.ANY)
    side = max(inner - 1, 1)
    return pl.pallas_call(
        functools.partial(gather_kernel, n, count, len(extra)),
        in_specs=[anywhere] * (count + len(extra)),
        out_specs=[anywhere] * (count + len(extra)),
        out_shape=[jax.ShapeDtypeStruct((n,) + a.shape, a.dtype) for a in arrays]
        + [jax.ShapeDtypeStruct(a.shape, a.dtype) for a in extra],
        scratch_shapes=[
            dma((count,)), dma((count, outer - 1)), dma((count, outer - 1)),
            dma((count, outer, side)), dma((count, outer, side)), dma((count, outer, inner)), dma((count, outer, inner)),
            dma((2, max(len(extra), 1))),
        ],
        compiler_params=pltpu.CompilerParams(collective_id=collective_id, has_side_effects=True),
    )(*arrays, *extra)


def t_dot_k(left, right):
    return dot(left, right, ((0,), (0,)))


def expert_loop(experts, ids_ref, t_ref, c_ref, w_refs, lows, kept, moe_acc, dn2_acc, spare):
    rows, width = c_ref.shape
    count = len(w_refs)
    ff = lows[0].shape[1]
    gl, ul, al = lows
    n2 = t_ref[:, :width]
    cot = c_ref[...]
    extra = t_ref[:, width:].astype(F32)
    lane = lax.broadcasted_iota(jnp.int32, extra.shape, 1)
    back_lane = lax.broadcasted_iota(jnp.int32, (rows, spare), 1)
    dgate = jnp.zeros((rows, spare), F32)
    act_sum, dg_sum, du_sum = kept
    for k in range(count):
        e = ids_ref[k]
        w = w_refs[k]
        gate = jnp.sum(jnp.where((lane == e) | (lane == experts + e), extra, 0.0), axis=1, keepdims=True)
        gv = dot(n2, w[:, :ff]) + gl
        uv = dot(n2, w[:, ff : 2 * ff]) + ul
        back = dot(cot, w[:, 2 * ff :]) + al
        sig = 1.0 / (1.0 + jnp.exp(-gv))
        silu = gv * sig
        act = silu * uv
        col = jnp.sum(act * back, axis=1, keepdims=True)
        high = col.astype(BF).astype(F32)
        at = e + ids_ref[count]
        dgate = dgate + jnp.where(back_lane == at, high, 0.0) + jnp.where(back_lane == at + experts, col - high, 0.0)
        back = back * gate
        act = act * gate
        du = back * silu
        dg = back * uv * (sig + silu * (1.0 - sig))
        act_sum = act if act_sum is None else act_sum + act
        dg_sum = dg if dg_sum is None else dg_sum + dg
        du_sum = du if du_sum is None else du_sum + du
        moe = dot_t(act.astype(BF), w[:, 2 * ff :])
        dn2 = dot_t(jnp.concatenate([dg.astype(BF), du.astype(BF)], axis=1), w[:, : 2 * ff])
        if k == 0:
            moe_acc[...] = moe
            dn2_acc[...] = dn2
        else:
            moe_acc[...] += moe
            dn2_acc[...] += dn2
    return dgate, act_sum, dg_sum, du_sum


def row_mask(experts, t_ref, width):
    extra = t_ref[:, width:].astype(F32)
    lane = lax.broadcasted_iota(jnp.int32, extra.shape, 1)
    chosen = jnp.sum(jnp.where(lane == 2 * experts, extra, 0.0), axis=1, keepdims=True)
    low_lane = lax.broadcasted_iota(jnp.int32, (extra.shape[0], LANES), 1)
    return ((low_lane // ADAPTER_RANK).astype(F32) == chosen).astype(F32)


def first_experts_kernel(experts, count, ids_ref, t_ref, c_ref, *refs):
    w_refs = refs[:count]
    ga_ref, ua_ref, gb_ref, ub_ref, db_ref, da_ref, r_ref, m_ref, wide_ref, thin_ref, moe_acc, dn2_acc = refs[count:]
    width = c_ref.shape[1]
    mask = row_mask(experts, t_ref, width)
    n2 = t_ref[:, :width]
    zg = (dot(n2, ga_ref[...]) * mask).astype(BF)
    zu = (dot(n2, ua_ref[...]) * mask).astype(BF)
    down_back = (dot_t(c_ref[...], db_ref[...]) * mask).astype(BF)
    lows = (dot(zg, gb_ref[...]), dot(zu, ub_ref[...]), dot_t(down_back, da_ref[...]))
    dgate, *sums = expert_loop(experts, ids_ref, t_ref, c_ref, w_refs, lows, (None, None, None), moe_acc, dn2_acc, r_ref.shape[1] - width)
    thin_ref[...] = jnp.concatenate([zg, zu, down_back], axis=1)
    wide_ref[...] = jnp.concatenate([*lows, *sums], axis=1)
    m_ref[...] = moe_acc[...].astype(BF)
    r_ref[:, :width] = dn2_acc[...].astype(BF)
    r_ref[:, width:] = dgate.astype(BF)


def last_experts_kernel(experts, count, before, ids_ref, t_ref, c_ref, *refs):
    w_refs = refs[:count]
    ga_ref, ua_ref, gb_ref, ub_ref, db_ref, da_ref = refs[count : count + 6]
    prior = refs[count + 6 : count + 6 + before]
    r1_ref, m1_ref, wide_ref, thin_ref, r_ref, m_ref = refs[-13:-7]
    sums = refs[-7:-2]
    moe_acc, dn2_acc = refs[-2:]
    width = c_ref.shape[1]
    ff = gb_ref.shape[1]

    @pl.when(pl.program_id(0) == 0)
    def _():
        for i, new in enumerate(sums):
            new[...] = prior[i][...] if before else jnp.zeros_like(new)

    mask = row_mask(experts, t_ref, width)
    parts = [wide_ref[:, i * ff : (i + 1) * ff] for i in range(6)]
    dgate, act_sum, dg_sum, du_sum = expert_loop(
        experts, ids_ref, t_ref, c_ref, w_refs, parts[:3], parts[3:], moe_acc, dn2_acc, r_ref.shape[1] - width
    )
    zg, zu, down_back = thin_ref[:, :LANES], thin_ref[:, LANES : 2 * LANES], thin_ref[:, 2 * LANES :]
    act_sum, dg_sum, du_sum = act_sum.astype(BF), dg_sum.astype(BF), du_sum.astype(BF)
    low = (dot(act_sum, da_ref[...]) * mask).astype(BF)
    gdu = (dot_t(dg_sum, gb_ref[...]) * mask).astype(BF)
    udu = (dot_t(du_sum, ub_ref[...]) * mask).astype(BF)
    m_ref[...] = (moe_acc[...] + dot(low, db_ref[...]) + m1_ref[...].astype(F32)).astype(BF)
    dn2 = dn2_acc[...] + dot_t(gdu, ga_ref[...]) + dot_t(udu, ua_ref[...])
    r_ref[:, :width] = (dn2 + r1_ref[:, :width].astype(F32)).astype(BF)
    r_ref[:, width:] = (dgate + r1_ref[:, width:].astype(F32)).astype(BF)
    bd_ref, ad_ref, bg_ref, bu_ref, a_ref = sums
    cot = c_ref[...]
    bd_ref[...] += t_dot_k(low, cot)
    ad_ref[...] += t_dot_k(act_sum, down_back)
    bg_ref[...] += t_dot_k(zg, dg_sum)
    bu_ref[...] += t_dot_k(zu, du_sum)
    a_ref[...] += t_dot_k(t_ref[:, :width], jnp.concatenate([gdu, udu], axis=1))


def experts_on(ids, experts, spare, t, cot, weights, w_two, first, low_two, down_b, down_at, prior=(), early=()):
    rows, width = cot.shape
    ff = down_at.shape[0]
    step = 256
    sd = jax.ShapeDtypeStruct
    whole = lambda a: pl.BlockSpec(a.shape, lambda i: (0, 0))
    once = lambda a: pl.BlockSpec(a.shape, lambda i: (0, 0), pipeline_mode=pl.Buffered(1))
    by_row = lambda cols: pl.BlockSpec((step, cols), lambda i: (i, 0))
    column = lambda height, cols, at: pl.BlockSpec((height, cols), lambda i: (0, at))
    low_rows = low_two.shape[0]
    count = len(weights)
    flops = 2 * rows * width * ff * 7 * count
    out_specs = [by_row(width + spare), by_row(width)]
    out_shape = [sd((rows, width + spare), BF), sd((rows, width), BF)]
    if early:
        shapes = [(LANES, width), (ff, LANES), (LANES, ff), (LANES, ff), (width, 2 * LANES)]
        out_specs += [pl.BlockSpec(shape, lambda i: (0, 0)) for shape in shapes]
        out_shape += [sd(shape, F32) for shape in shapes]
    else:
        out_specs += [by_row(6 * ff), by_row(3 * LANES)]
        out_shape += [sd((rows, 6 * ff), F32), sd((rows, 3 * LANES), BF)]
    outs = pl.pallas_call(
        functools.partial(last_experts_kernel, experts, count, len(prior)) if early else functools.partial(first_experts_kernel, experts, count),
        grid=(rows // step,),
        in_specs=[pl.BlockSpec(memory_space=pltpu.SMEM), by_row(t.shape[1]), by_row(width)]
        + [once(w) for w in weights]
        + [column(width, LANES, first), column(width, LANES, first + 1), column(low_rows, ff, 0), column(low_rows, ff, 1), whole(down_b), whole(down_at)]
        + [once(p) for p in prior] + [by_row(e.shape[1]) for e in early],
        out_specs=out_specs,
        out_shape=out_shape,
        scratch_shapes=[pltpu.VMEM((step, width), F32), pltpu.VMEM((step, width), F32)],
        input_output_aliases={3 + count + 6 + i: 2 + i for i in range(len(prior))},
        compiler_params=pltpu.CompilerParams(vmem_limit_bytes=58 << 20),
        cost_estimate=pl.CostEstimate(flops=flops, bytes_accessed=24 << 20, transcendentals=rows * ff * count),
    )(ids, t, cot, *weights, w_two, w_two, low_two, low_two, down_b, down_at, *prior, *early)
    return outs


class Crossing:
    def __init__(self):
        self.n_ctx, self.n_tp = lax.axis_size("ctx"), lax.axis_size("tp")
        self.tp_at = lax.axis_index("tp")

    def pairs(self, by):
        return [(c, (c + by) % self.n_ctx) for c in range(self.n_ctx)]

    def half(self, block):
        if self.n_tp != 2:
            return block
        size = block.shape[0] // 2
        return lax.dynamic_slice_in_dim(block, self.tp_at * size, size, 0)

    def other_half(self, block):
        size = block.shape[0] // 2
        return lax.dynamic_slice_in_dim(block, (1 - self.tp_at) * size, size, 0)

    def joined(self, half):
        if self.n_tp != 2:
            return half
        other = lax.ppermute(half, "tp", [(0, 1), (1, 0)])
        size = half.shape[0]
        whole = lax.dynamic_update_slice_in_dim(jnp.zeros((2 * size,) + half.shape[1:], half.dtype), half, self.tp_at * size, 0)
        return lax.dynamic_update_slice_in_dim(whole, other, (1 - self.tp_at) * size, 0)

    def fetch(self, block):
        half = self.half(block)
        return [lax.ppermute(half, "ctx", self.pairs(by)) for by in range(1, self.n_ctx)]

    def summed_half(self, block):
        if self.n_tp != 2:
            return block.astype(F32)
        return self.half(block).astype(F32) + lax.ppermute(self.other_half(block), "tp", [(0, 1), (1, 0)]).astype(F32)

    def swapped(self, blocks):
        if self.n_tp != 2:
            return [jnp.zeros_like(b) for b in blocks]
        return [lax.ppermute(self.other_half(b), "tp", [(0, 1), (1, 0)]) for b in blocks]

    def halves_of_total(self, own, parts):
        found = self.summed_half(own)
        for part in parts:
            found = found + part.astype(F32)
        if self.n_tp != 2:
            found = lax.psum(found, "tp").astype(BF)
            size = found.shape[0] // 2
            return found[:size], found[size:], 0
        found = found.astype(BF)
        return found, lax.ppermute(found, "tp", [(0, 1), (1, 0)]), self.tp_at


def put_rows(pack, value, at, height):
    for f in range(pack.shape[0]):
        pack[f, pl.ds(at, height), :] = value[f * height : (f + 1) * height, :].astype(pack.dtype)


def put_cols(pack, value, at, height, first):
    for i in range(value.shape[1] // LANES):
        for f in range(pack.shape[0]):
            spot = pl.ds(pl.multiple_of(at + (first + i) * height, 8 if height % 16 else 16), height)
            pack[f, spot, :] = value[f * height : (f + 1) * height, i * LANES : (i + 1) * LANES].astype(pack.dtype)


def adapter_mask(chosen_ref):
    rows = chosen_ref.shape[0]
    return (lax.broadcasted_iota(jnp.int32, (rows, LANES), 1) // ADAPTER_RANK == chosen_ref[...]).astype(F32)


def qkv_back_kernel(n_tp, low_rows, share, tp_ref, dq_ref, dko_ref, dvo_ref, fb_ref, cos_ref, sin_ref, n1_ref, u_ref, chosen_ref, w_ref, lb_ref, dn1_ref, pack_ref, a_acc, b_acc):
    q_width, kv_width = dq_ref.shape[1], dko_ref.shape[1]
    ranks = LANES
    rows = dq_ref.shape[0]
    step = pl.program_id(0)
    mask = adapter_mask(chosen_ref)
    head = lax.broadcasted_iota(jnp.int32, (rows, LANES), 1) % HEAD_SIZE < HEAD_SIZE // 2

    def turned_back(v):
        swapped = jnp.where(head, pltpu.roll(v, LANES - HEAD_SIZE // 2, 1), pltpu.roll(v, HEAD_SIZE // 2, 1))
        return (v * cos_ref[...] - swapped * sin_ref[...]).astype(BF)

    dq = [turned_back(dq_ref[:, i : i + LANES]) for i in range(0, q_width, LANES)]
    dk = [turned_back(dko_ref[:, i : i + LANES] + fb_ref[:, i : i + LANES].astype(F32)) for i in range(0, kv_width, LANES)]
    dv = (dvo_ref[...] + fb_ref[:, kv_width:].astype(F32)).astype(BF)
    dq = jnp.concatenate(dq, axis=1)
    dk = jnp.concatenate(dk, axis=1) if len(dk) > 1 else dk[0]
    lows = []
    at = 0
    for d in (dq, dk, dv):
        lows.append((dot_t(d, lb_ref[:, at : at + d.shape[1]]) * mask).astype(BF))
        at += d.shape[1]
    lows = jnp.concatenate(lows, axis=1)
    dn1_ref[...] = dot_t(jnp.concatenate([dq, dk, dv, lows], axis=1), w_ref[...]).astype(BF)
    n1 = n1_ref[...]
    parts = [
        (a_acc, slice(0, 3 * ranks), t_dot_k(n1, lows)),
        (b_acc, slice(0, q_width), t_dot_k(u_ref[:, :ranks], dq)),
        (b_acc, slice(q_width, q_width + kv_width), t_dot_k(u_ref[:, ranks : 2 * ranks], dk)),
        (b_acc, slice(q_width + kv_width, q_width + 2 * kv_width), t_dot_k(u_ref[:, 2 * ranks :], dv)),
    ]

    @pl.when(step == 0)
    def _():
        for acc, cols, value in parts:
            acc[:, cols] = value

    @pl.when(step > 0)
    def _():
        for acc, cols, value in parts:
            acc[:, cols] += value

    @pl.when(step == pl.num_programs(0) - 1)
    def _():
        pack_ref[...] = jnp.zeros_like(pack_ref)
        at, col = 0, 0
        for i, cols in enumerate((q_width, kv_width, kv_width)):
            put_rows(pack_ref, a_acc[:, i * ranks : (i + 1) * ranks], at, share)
            at += share
            put_cols(pack_ref, b_acc[:, col : col + cols], at, low_rows, tp_ref[0] * (cols // LANES))
            at += cols * n_tp // LANES * low_rows
            col += cols


def qkv_back(n, n_tp, low_rows, share, tp_at, dq, dko, dvo, fb, cos, sin, n1, u3, chosen, w_one, low_one, height):
    rows, q_width = dq.shape
    width = n1.shape[1]
    step = 256
    by_row = lambda a: pl.BlockSpec((step, a.shape[1]), lambda i: (i, 0))
    whole = lambda a: pl.BlockSpec(a.shape, lambda i: (0, 0), pipeline_mode=pl.Buffered(1))
    sd = jax.ShapeDtypeStruct
    return pl.pallas_call(
        functools.partial(qkv_back_kernel, n_tp, low_rows, share),
        grid=(rows // step,),
        in_specs=[pl.BlockSpec(memory_space=pltpu.SMEM)] + [by_row(a) for a in (dq, dko, dvo, fb, cos, sin, n1, u3, chosen)] + [whole(w_one), whole(low_one)],
        out_specs=[pl.BlockSpec((step, width), lambda i: (i, 0)), pl.BlockSpec((n, height, LANES), lambda i: (0, 0, 0))],
        out_shape=[sd((rows, width), BF), sd((n, height, LANES), F32)],
        scratch_shapes=[pltpu.VMEM((width, 3 * LANES), F32), pltpu.VMEM((LANES, low_one.shape[1]), F32)],
        compiler_params=pltpu.CompilerParams(vmem_limit_bytes=50 << 20),
        cost_estimate=pl.CostEstimate(flops=4 * rows * width * w_one.shape[1], bytes_accessed=24 << 20, transcendentals=0),
    )(tp_at, dq, dko, dvo, fb, cos, sin, n1, u3, chosen, w_one, low_one)


def normed_rows(v, gain):
    return v * lax.rsqrt(jnp.mean(v * v, axis=1, keepdims=True) + norm_eps) * gain


def turned(v, cos, sin):
    head = lax.broadcasted_iota(jnp.int32, v.shape, 1) % HEAD_SIZE < HEAD_SIZE // 2
    swapped = jnp.where(head, pltpu.roll(v, LANES - HEAD_SIZE // 2, 1), pltpu.roll(v, HEAD_SIZE // 2, 1))
    return v * cos + swapped * sin


def kv_kernel(q_width, x_ref, chosen_ref, cos_ref, sin_ref, gain_ref, w_ref, low_ref, n1_ref, u_ref, kv_ref):
    kv_width = kv_ref.shape[1] // 2
    mask = adapter_mask(chosen_ref)
    n1 = normed_rows(x_ref[...].astype(F32), gain_ref[...]).astype(BF)
    n1_ref[...] = n1
    raw = dot(n1, w_ref[:, q_width:])
    lows = (raw[:, 2 * kv_width :] * jnp.concatenate([mask] * 3, axis=1)).astype(BF)
    u_ref[...] = lows
    key = raw[:, :kv_width] + dot(lows[:, LANES : 2 * LANES], low_ref[:, q_width : q_width + kv_width])
    for i in range(0, kv_width, LANES):
        kv_ref[:, i : i + LANES] = turned(key[:, i : i + LANES], cos_ref[...], sin_ref[...]).astype(BF)
    value = raw[:, kv_width : 2 * kv_width] + dot(lows[:, 2 * LANES :], low_ref[:, q_width + kv_width :])
    kv_ref[:, kv_width:] = value.astype(BF)


def q_kernel(n1_ref, u_ref, cos_ref, sin_ref, w_ref, low_ref, q_ref):
    q_width = q_ref.shape[1]
    q = dot(n1_ref[...], w_ref[:, :q_width]) + dot(u_ref[:, :LANES], low_ref[:, :q_width])
    for i in range(0, q_width, LANES):
        q_ref[:, i : i + LANES] = (turned(q[:, i : i + LANES], cos_ref[...], sin_ref[...]) * 0.125).astype(BF)


def out_kernel(o_ref, chosen_ref, w_ref, oa_ref, low_ref, part_ref, u_ref):
    q_width, width = o_ref.shape[1], part_ref.shape[1]
    ff2 = low_ref.shape[1] - 2 * width - LANES
    o = o_ref[...]
    u = (dot(o, oa_ref[...]) * adapter_mask(chosen_ref)).astype(BF)
    u_ref[...] = u
    part_ref[...] = (dot_t(o, w_ref[:, :q_width]) + dot(u, low_ref[:, ff2 : ff2 + width])).astype(BF)


def route_kernel(experts, q_width, x_ref, one_ref, other_ref, chosen_ref, routes_ref, gain_ref, w_ref, low_ref, h_ref, t_ref, u_ref):
    width = h_ref.shape[1]
    rows = h_ref.shape[0]
    h = x_ref[...].astype(F32) + (one_ref[...].astype(F32) + other_ref[...].astype(F32))
    h_ref[...] = h
    n2 = normed_rows(h, gain_ref[...]).astype(BF)
    t_ref[:, :width] = n2
    u = (dot(n2, w_ref[:, q_width : q_width + LANES]) * adapter_mask(chosen_ref)).astype(BF)
    u_ref[...] = u
    logits = dot(n2, w_ref[:, q_width + 3 * LANES : q_width + 4 * LANES]) + dot(u, low_ref[:, low_ref.shape[1] - LANES :])
    lane = lax.broadcasted_iota(jnp.int32, (rows, LANES), 1)
    selected = lane == routes_ref[:, 0:1]
    for k in range(1, routes_ref.shape[1]):
        selected = selected | (lane == routes_ref[:, k : k + 1])
    top = jnp.max(jnp.where(selected, logits, -jnp.inf), axis=1, keepdims=True)
    gates = jnp.where(selected, jnp.exp(jnp.where(selected, logits - top, 0.0)), 0.0)
    gates = gates / jnp.sum(gates, axis=1, keepdims=True)
    high = gates.astype(BF).astype(F32)
    extra = high + pltpu.roll(gates - high, experts, 1) + jnp.where(lane == 2 * experts, chosen_ref[...].astype(F32), 0.0)
    t_ref[:, width:] = extra.astype(BF)


def by_rows(kernel, step, rowed, whole, outs, flops):
    rows = rowed[0].shape[0]
    block = lambda cols: pl.BlockSpec((step, cols), lambda i: (i, 0))
    return pl.pallas_call(
        kernel,
        grid=(rows // step,),
        in_specs=[block(a.shape[1]) for a in rowed] + [pl.BlockSpec(a.shape, lambda i: (0, 0), pipeline_mode=pl.Buffered(1)) for a in whole],
        out_specs=[block(cols) for cols, kind in outs],
        out_shape=[jax.ShapeDtypeStruct((rows, cols), kind) for cols, kind in outs],
        compiler_params=pltpu.CompilerParams(vmem_limit_bytes=48 << 20),
        cost_estimate=pl.CostEstimate(flops=flops, bytes_accessed=1 << 20, transcendentals=0),
    )(*rowed, *whole)


def mid_back_kernel(n, n_tp, experts, share, low_rows, sel_ref, mine_ref, other_ref, h_ref, c_ref, t_ref, o_ref, ou_ref, ru_ref, chosen_ref, gain_ref,
                    w_ref, low_ref, oa_ref, bd_ref, ad_ref, bg_ref, bu_ref, agu_ref, dh_ref, do_ref, pack_ref, ar_acc, ao_acc, bo_acc, br_acc):
    width = h_ref.shape[1]
    q_width = o_ref.shape[1]
    ff = bg_ref.shape[1]
    spare = mine_ref.shape[1] - width
    step = pl.program_id(0)
    mask = adapter_mask(chosen_ref)
    picked = step == sel_ref[0]

    def fold(height, top):
        lane = lax.broadcasted_iota(jnp.int32, (height, LANES), 0)
        return ((lane % experts == lax.broadcasted_iota(jnp.int32, (height, LANES), 1)) & (lane < top)).astype(BF)

    back = jnp.where(picked, mine_ref[:, :width].astype(F32), other_ref[:, :width].astype(F32))
    tail = jnp.where(picked, mine_ref[:, width:].astype(F32), other_ref[:, width:].astype(F32)).astype(BF)
    dgate = dot(tail, fold(spare, 2 * experts * n_tp))
    gates = dot(t_ref[:, width:], fold(LANES, 2 * experts))
    n2 = t_ref[:, :width]
    router_a, router_w = w_ref[:, q_width : q_width + LANES], w_ref[:, q_width + 3 * LANES : q_width + 4 * LANES]
    out_b, router_b = low_ref[:, 2 * ff : 2 * ff + width], low_ref[:, 2 * ff + 2 * width :]
    dlog = (gates * (dgate - jnp.sum(gates * dgate, axis=1, keepdims=True))).astype(BF)
    rdu = (dot_t(dlog, router_b) * mask).astype(BF)
    dn2 = back + dot_t(dlog, router_w) + dot_t(rdu, router_a)
    h = h_ref[...]
    r = lax.rsqrt(jnp.mean(h * h, axis=1, keepdims=True) + norm_eps)
    gd = dn2 * gain_ref[...]
    dh = c_ref[...].astype(F32) + r * gd - h * (r * r * r * jnp.mean(gd * h, axis=1, keepdims=True))
    dh_ref[...] = dh
    dattn = dh.astype(BF)
    odu = (dot_t(dattn, out_b) * mask).astype(BF)
    do_ref[...] = (dot(dattn, w_ref[:, :q_width]) + dot_t(odu, oa_ref[...])).astype(BF)
    parts = [
        (ar_acc, t_dot_k(n2, rdu)),
        (ao_acc, t_dot_k(o_ref[...], odu)),
        (bo_acc, t_dot_k(ou_ref[...], dattn)),
        (br_acc, t_dot_k(ru_ref[...], dlog)),
    ]

    @pl.when(step == 0)
    def _():
        for acc, value in parts:
            acc[...] = value

    @pl.when(step > 0)
    def _():
        for acc, value in parts:
            acc[...] += value

    @pl.when(step == pl.num_programs(0) - 1)
    def _():
        pack_ref[...] = jnp.zeros_like(pack_ref)
        tp = sel_ref[1]
        first = (tp == 0).astype(F32)
        own = n // n_tp
        at = 0
        for k in range(own):
            pack_ref[tp * own + k, pl.ds(at, share), :] = ao_acc[k * share : (k + 1) * share, :].astype(pack_ref.dtype)
        at += share
        put_cols(pack_ref, bo_acc, at, low_rows, 0)
        at += width // LANES * low_rows
        ar_acc[...] = ar_acc[...] * first
        put_rows(pack_ref, ar_acc, at, share)
        at += share
        br_acc[...] = br_acc[...] * first
        put_cols(pack_ref, br_acc, at, low_rows, 0)
        at += low_rows
        for i, ref in enumerate((bg_ref, bu_ref)):
            put_rows(pack_ref, agu_ref[:, i * LANES : (i + 1) * LANES], at, share)
            at += share
            put_cols(pack_ref, ref, at, low_rows, tp * (ff // LANES))
            at += ff * n_tp // LANES * low_rows
        size = ad_ref.shape[0] // own
        for k in range(own):
            pack_ref[tp * own + k, pl.ds(at, size), :] = ad_ref[k * size : (k + 1) * size, :].astype(pack_ref.dtype)
        at += size
        put_cols(pack_ref, bd_ref, at, low_rows, 0)


def mid_back(n, n_tp, experts, share, low_rows, sel, mine, other, hidden, cot, carried, mixed, out_u, router_u, chosen, gain, w_two, low_two, out_a, sums, height):
    rows, width = hidden.shape
    q_width = mixed.shape[1]
    step = rows // 2
    sd = jax.ShapeDtypeStruct
    by_row = lambda a: pl.BlockSpec((step, a.shape[1]), lambda i: (i, 0))
    whole = lambda a: pl.BlockSpec(a.shape, lambda i: (0, 0), pipeline_mode=pl.Buffered(1))
    return pl.pallas_call(
        functools.partial(mid_back_kernel, n, n_tp, experts, share, low_rows),
        grid=(2,),
        in_specs=[pl.BlockSpec(memory_space=pltpu.SMEM), whole(mine), whole(other)]
        + [by_row(a) for a in (hidden, cot, carried, mixed, out_u, router_u, chosen)]
        + [whole(a) for a in (gain, w_two, low_two, out_a, *sums)],
        out_specs=[by_row(hidden), by_row(mixed), pl.BlockSpec((n, height, LANES), lambda i: (0, 0, 0))],
        out_shape=[sd((rows, width), F32), sd((rows, q_width), BF), sd((n, height, LANES), F32 if low_rows % 16 else BF)],
        scratch_shapes=[pltpu.VMEM((width, LANES), F32), pltpu.VMEM((q_width, LANES), F32), pltpu.VMEM((LANES, width), F32), pltpu.VMEM((LANES, LANES), F32)],
        compiler_params=pltpu.CompilerParams(vmem_limit_bytes=58 << 20),
        cost_estimate=pl.CostEstimate(flops=8 * rows * width * q_width, bytes_accessed=32 << 20, transcendentals=0),
    )(sel, mine, other, hidden, cot, carried, mixed, out_u, router_u, chosen, gain, w_two, low_two, out_a, *sums)


def reduce_kernel(n, pack_ref, side_ref, out_ref, side_out, side_in, side_snd, snd1, rcv1, acc, snd2, rcv2, acc2, snd3, rcv3, fin, sems, send3, recv3):
    me = lax.axis_index("fsdp")
    ctx = lax.axis_index("ctx")
    tp = lax.axis_index("tp")
    half = pack_ref.shape[1] // 2
    part = half // 2
    barrier = pltpu.get_barrier_semaphore()
    pl.semaphore_signal(barrier, inc=1, device_id={"tp": 1 - tp}, device_id_type=MESH)
    pl.semaphore_signal(barrier, inc=1, device_id={"ctx": 1 - ctx}, device_id_type=MESH)
    for k in range(1, n):
        pl.semaphore_signal(barrier, inc=1, device_id={"fsdp": (me + k) % n}, device_id_type=MESH)
    snd1[...] = pack_ref[:, pl.ds(pl.multiple_of((1 - tp) * half, 16), half), :].astype(BF)
    pl.semaphore_wait(barrier, n + 1)

    def swap(src, dst, i, to):
        copy = pltpu.make_async_remote_copy(src_ref=src, dst_ref=dst, send_sem=sems.at[0, i], recv_sem=sems.at[1, i], device_id=to, device_id_type=MESH)
        copy.start()
        return copy

    copy = swap(snd1, rcv1, 0, {"tp": 1 - tp})
    side = swap(side_ref, side_in.at[0], 4, {"tp": 1 - tp})
    copy.wait()
    acc[...] = pack_ref[:, pl.ds(pl.multiple_of(tp * half, 16), half), :] + rcv1[...].astype(F32)
    snd2[...] = acc[:, pl.ds(pl.multiple_of((1 - ctx) * part, 16), part), :].astype(BF)
    copy = swap(snd2, rcv2, 1, {"ctx": 1 - ctx})
    side.wait()
    side_snd[...] = (side_ref[...].astype(F32) + side_in[0].astype(F32)).astype(BF)
    side = swap(side_snd, side_in.at[1], 5, {"ctx": 1 - ctx})
    copy.wait()
    acc2[...] = acc[:, pl.ds(pl.multiple_of(ctx * part, 16), part), :] + rcv2[...].astype(F32)
    snd3[...] = acc2[...].astype(BF)

    def ship(k):
        to = (me + k) % n
        return pltpu.make_async_remote_copy(
            src_ref=snd3.at[to], dst_ref=rcv3.at[me], send_sem=send3.at[k], recv_sem=recv3.at[k], device_id={"fsdp": to}, device_id_type=MESH
        )

    def came(k):
        return pltpu.make_async_remote_copy(
            src_ref=snd3.at[me], dst_ref=rcv3.at[(me + n - k) % n], send_sem=send3.at[k], recv_sem=recv3.at[k],
            device_id={"fsdp": (me + k) % n}, device_id_type=MESH,
        )

    for k in range(1, n):
        ship(k).start()
    total = acc2[me]
    for k in range(1, n):
        came(k).wait_recv()
        total = total + rcv3[(me + n - k) % n].astype(F32)
    for k in range(1, n):
        ship(k).wait_send()
    spot = tp * 2 + ctx
    fin[spot] = total.astype(BF)
    copy = swap(fin.at[spot], fin.at[spot], 2, {"ctx": 1 - ctx})
    copy.wait()
    both = fin.at[pl.ds(tp * 2, 2)]
    copy = swap(both, both, 3, {"tp": 1 - tp})
    copy.wait()
    for i in range(4):
        out_ref[pl.ds(i * part, part), :] = fin[i].astype(F32)
    side.wait()
    side_out[...] = side_snd[...].astype(F32) + side_in[1].astype(F32)


def reduce_pack(pack, side, collective_id):
    n, height = pack.shape[:2]
    if lax.axis_size("tp") != 2 or lax.axis_size("ctx") != 2 or height % 64 or side.shape[0] % 16:
        mine = lax.psum_scatter(pack.astype(BF), "fsdp", scatter_dimension=0, tiled=False)
        return lax.psum(mine, ("ctx", "tp")).astype(F32), lax.psum(side, ("ctx", "tp")).astype(F32)
    half, part = height // 2, height // 4
    vm = pltpu.VMEM
    dma = pltpu.SemaphoreType.DMA
    return pl.pallas_call(
        functools.partial(reduce_kernel, n),
        in_specs=[pl.BlockSpec(memory_space=vm)] * 2,
        out_specs=[pl.BlockSpec(memory_space=vm)] * 2,
        out_shape=[jax.ShapeDtypeStruct((height, LANES), F32), jax.ShapeDtypeStruct(side.shape, F32)],
        scratch_shapes=[
            vm((2,) + side.shape, BF), vm(side.shape, BF), vm((n, half, LANES), BF), vm((n, half, LANES), BF), vm((n, half, LANES), F32),
            vm((n, part, LANES), BF), vm((n, part, LANES), BF), vm((n, part, LANES), F32),
            vm((n, part, LANES), BF), vm((n, part, LANES), BF), vm((4, part, LANES), BF),
            dma((2, 6)), dma((n,)), dma((n,)),
        ],
        compiler_params=pltpu.CompilerParams(collective_id=collective_id, has_side_effects=True, vmem_limit_bytes=48 << 20),
    )(pack, side)


def tp_sum(value):
    if lax.axis_size("tp") != 2:
        return lax.psum(value, "tp")
    return value + lax.ppermute(value, "tp", [(0, 1), (1, 0)])


def on_device(
    tokens, out_cotangent, lengths, adapter_of_doc, routes, attn_gain, ffn_gain,
    w_query, key_matrix, value_matrix, w_out, w_router, w_gate, w_up, w_down,
    a_query, b_query, a_key, key_second_factor, a_value, value_second_factor,
    a_out, b_out, a_router, b_router, a_gate, b_gate, a_up, b_up, a_down, b_down,
):
    rows, width = tokens.shape
    n = lax.axis_size("fsdp")
    n_tp = lax.axis_size("tp")
    tp_at = lax.axis_index("tp")
    ctx_at = lax.axis_index("ctx")
    group = rows * lax.axis_size("ctx")
    q_width = w_query.shape[1]
    kv_width = key_matrix.shape[1]
    ff_width = w_gate.shape[2]
    local_experts = w_gate.shape[0]
    experts = w_router.shape[1]
    ranks = a_query.shape[1]
    share = w_query.shape[0]
    low_rows = b_query.shape[0]

    pad = ((0, 0), (0, LANES - experts))
    one, low_one = gather_packs(
        [
            [(a, a.shape[1]) for a in (w_query, key_matrix, value_matrix, a_query, a_key, a_value)],
            [(b_query, q_width), (key_second_factor, kv_width), (value_second_factor, kv_width)],
        ],
        (),
        0,
    )
    qkv = q_width + 2 * kv_width
    w_one = one.reshape(n * share, -1)
    low_one = low_one.reshape(n * low_rows, -1)

    ends = jnp.cumsum(lengths[0])
    starts = ends - lengths[0]
    place = jnp.arange(group, dtype=jnp.int32)
    doc = jnp.sum((place[:, None] >= ends[None, :]).astype(jnp.int32), axis=1)
    picked = (doc[:, None] == jnp.arange(lengths.shape[1], dtype=jnp.int32)[None, :]).astype(jnp.int32)
    begin = jnp.sum(picked * starts[None, :], axis=1)
    chosen = jnp.sum(picked * adapter_of_doc[0][None, :], axis=1)
    start = ctx_at * rows
    query_index = start + jnp.arange(rows, dtype=jnp.int32)
    begin_local = lax.dynamic_slice_in_dim(begin, start, rows)
    chosen_local = lax.dynamic_slice_in_dim(chosen, start, rows)
    freq = 10000.0 ** (-jnp.arange(HEAD_SIZE // 2, dtype=F32) / (HEAD_SIZE // 2))
    angles = (query_index - begin_local).astype(F32)[:, None] * freq[None, :]
    cosine, sine = jnp.cos(angles), jnp.sin(angles)
    cosine_wide = jnp.tile(cosine, (1, 2 * LANES // HEAD_SIZE))
    sine_wide = jnp.tile(jnp.concatenate([-sine, sine], axis=1), (1, LANES // HEAD_SIZE))
    chosen_col = chosen_local[:, None]
    gain_one, gain_two = attn_gain[None, :], ffn_gain[None, :]
    normed, low_u, kv = by_rows(
        functools.partial(kv_kernel, q_width), 256, (tokens, chosen_col, cosine_wide, sine_wide), (gain_one, w_one, low_one),
        ((width, BF), (3 * ranks, BF), (2 * kv_width, BF)), 2 * rows * width * (w_one.shape[1] - q_width),
    )
    cross = Crossing()
    outer, inner = levels(n)
    me = lax.axis_index("fsdp")
    ring = [(i, (i + inner) % n) for i in range(n)]
    turns = [[(i, i // inner * inner + (i % inner + dj) % inner) for i in range(n)] for dj in range(1, inner)]
    local = local_experts // cross.n_ctx
    mine = [lax.dynamic_slice_in_dim(a, ctx_at * local, local, 0) for a in (w_gate, w_up, w_down)]
    block = jnp.concatenate([mine[0], mine[1], jnp.swapaxes(mine[2], 1, 2)], axis=2)
    brought = {(0, 0): block}

    def bring(do, after):
        last = [brought[(do, 0)]] + [brought[(do - 1, dj)] for dj in range(1, inner) if do]
        last, after = lax.optimization_barrier((last, after))
        brought[(do, 0)] = last[0]
        for dj, value in zip(range(1, inner), last[1:]):
            brought[(do - 1, dj)] = value
        if do + 1 < outer:
            brought[(do + 1, 0)] = lax.ppermute(last[0], "fsdp", ring)
        for dj in range(1, inner):
            brought[(do, dj)] = lax.ppermute(last[0], "fsdp", turns[dj - 1])
        return after

    one = bring(0, one)
    (query_state,) = by_rows(
        q_kernel, 256, (normed, low_u, cosine_wide, sine_wide), (w_one, low_one), ((q_width, BF),), 2 * rows * width * q_width
    )
    w_out, w_router, b_router, query_state = lax.optimization_barrier((w_out, w_router, b_router, query_state))
    two, low_two, down_a, far = gather_packs(
        [
            [(a, a.shape[1]) for a in (w_out.T, a_router, a_gate, a_up, jnp.pad(w_router, pad), a_out)],
            [(b_gate, ff_width), (b_up, ff_width), (b_out, width), (b_down, width), (jnp.pad(b_router, pad), LANES)],
            [(a_down, ranks)],
        ],
        (kv,),
        1,
    )
    cot = lax.optimization_barrier((out_cotangent, two))[0]
    cot_halves = cross.fetch(cot)
    far = bring(1, far)
    w_two = two.reshape(n * share, -1)
    low_two = low_two.reshape(n * low_rows, -1)
    down_b = low_two[:, 2 * ff_width + width : 2 * ff_width + 2 * width]
    out_a = lax.dynamic_slice_in_dim(w_two[:, q_width + 4 * ranks : q_width + 5 * ranks], tp_at * q_width, q_width, 0)
    down_at = lax.dynamic_slice_in_dim(down_a.reshape(-1, ranks), tp_at * ff_width, ff_width, 0)
    begin_row = begin_local[None, :]
    start_at = jnp.reshape(start, (1,)).astype(jnp.int32)
    mixed_heads, log_total = attend(query_state, kv, far, begin_row, start_at)
    cot_halves, mixed_heads = lax.optimization_barrier((cot_halves, mixed_heads))
    attn_part, out_u = by_rows(
        out_kernel, 256, (mixed_heads, chosen_col), (w_two, out_a, low_two), ((width, BF), (ranks, BF)), 0
    )
    attn_part = bring(2, attn_part)
    if n_tp == 2:
        attn_other = lax.ppermute(attn_part, "tp", [(0, 1), (1, 0)])
    else:
        attn_part, attn_other = lax.psum(attn_part.astype(F32), "tp"), jnp.zeros_like(attn_part)
    spare = -(-2 * experts * n_tp // LANES) * LANES
    hidden, carried, router_u = by_rows(
        functools.partial(route_kernel, experts, q_width), 256, (tokens, attn_part, attn_other, chosen_col, routes), (gain_two, w_two, low_two),
        ((width, F32), (width + LANES, BF), (ranks, BF)), 0,
    )
    halves = cross.fetch(carried)
    early = [(0, 0), (1, 0)] + [(0, dj) for dj in range(1, inner)] + [(2, 0)] + [(1, dj) for dj in range(1, inner)]
    late = [(do, 0) for do in range(3, outer)] + [(do, dj) for do in range(2, outer) for dj in range(1, inner)]
    last = [k for k in late if k[0] == outer - 1 and k[1]]
    between = [k for k in late if k not in last]

    def weights_of(keys):
        ids = [((me // inner + outer - do) % outer * inner + (me % inner + inner - dj) % inner) * local_experts + ctx_at * local + j for do, dj in keys for j in range(local)]
        return jnp.stack(ids + [tp_at * 2 * experts]).astype(jnp.int32), [brought[k][j] for k in keys for j in range(local)]

    sums = ()
    at = q_width // LANES + 1
    work = [(carried, cot)] + [(None, None)] * (cross.n_ctx - 1)
    partial = []
    for by in range(cross.n_ctx):
        ids, weights = weights_of(early + between if by else early)
        if by:
            work[by] = (cross.joined(halves[by - 1]), cross.joined(cot_halves[by - 1]))
        r, m, wide, thin = experts_on(ids, experts, spare, *work[by], weights, w_two, at, low_two, down_b, down_at)
        if by == 0:
            for do in range(3, outer):
                r = bring(do, r)
            halves, cot_halves, r = lax.optimization_barrier((halves, cot_halves, r))
        partial.append((r, m, wide, thin))
    back_parts, moe_parts = [], []
    for by in list(range(1, cross.n_ctx)) + [0]:
        ids, weights = weights_of(last if by else late)
        r, m, *sums = experts_on(ids, experts, spare, *work[by], weights, w_two, at, low_two, down_b, down_at, sums, partial[by])
        moe_parts.append(m)
        if by:
            half = cross.summed_half(r).astype(BF)
            half, carried = lax.optimization_barrier((half, work[0][0]))
            work[0] = (carried, cot)
            back_parts.append(lax.ppermute(half, "ctx", cross.pairs(-by)))
    r, back_parts = lax.optimization_barrier((r, back_parts))
    mine_half, other, first = cross.halves_of_total(r, back_parts)
    swapped = cross.swapped(moe_parts)
    early_shapes = [
        (share, ranks), (low_rows, width), (share, ranks), (low_rows, experts), (share, ranks), (low_rows, ff_width * n_tp),
        (share, ranks), (low_rows, ff_width * n_tp), (a_down.shape[0], ranks), (low_rows, width),
    ]
    height = sum(-(-cols // LANES) * tall for tall, cols in early_shapes)
    sel = jnp.stack([jnp.asarray(first, jnp.int32), tp_at.astype(jnp.int32)])
    dhidden, dmixed, early_pack = mid_back(
        n, n_tp, experts, share, low_rows, sel, mine_half, other, hidden, cot, carried, mixed_heads, out_u, router_u,
        chosen_col, gain_two, w_two, low_two, out_a, sums, height,
    )
    early_pack, dmixed, swapped = lax.optimization_barrier((early_pack.astype(BF), dmixed, swapped))
    moe_halves = [cross.half(p).astype(F32) + q.astype(F32) for p, q in zip(moe_parts, swapped)]
    moe_got = [lax.ppermute(p.astype(BF), "ctx", cross.pairs(-by)) for by, p in zip(range(1, cross.n_ctx), moe_halves)]
    early_sum = lax.psum_scatter(early_pack, "fsdp", scatter_dimension=0, tiled=False)
    dq_far, dkey_far, dvalue_far = attend_back(query_state, far, begin_row, start_at, mixed_heads, dmixed, log_total)
    far_back = lax.ppermute(
        jnp.concatenate([dkey_far, dvalue_far], axis=1), "ctx", [(i + 1, i) for i in range(lax.axis_size("ctx") - 1)]
    )
    dquery, dkey_own, dvalue_own = attend_back(query_state, kv, begin_row, start_at, mixed_heads, dmixed, log_total, dq_far)
    far_back, moe_got, dquery = lax.optimization_barrier((far_back, moe_got, dquery))
    moe = moe_halves[-1]
    for part in moe_got:
        moe = moe + part.astype(F32)
    moe = cross.joined(moe.astype(BF)).astype(F32) if n_tp == 2 else lax.psum(moe, "tp")
    output = (hidden + moe).astype(BF)
    height = 3 * share + low_rows * n_tp * qkv // LANES
    dn1, pack = qkv_back(
        n, n_tp, low_rows, share, jnp.reshape(tp_at, (1,)).astype(jnp.int32), dquery, dkey_own, dvalue_own, far_back,
        cosine_wide, sine_wide, normed, low_u, chosen_col, w_one, low_one, height,
    )
    early_sum, dn1, pack = lax.optimization_barrier((early_sum, dn1, pack))
    late, early_sum = reduce_pack(pack, early_sum, 2)
    dn1 = tp_sum(dn1.astype(F32)) if n_tp != 2 else dn1.astype(F32) + lax.ppermute(dn1, "tp", [(0, 1), (1, 0)]).astype(F32)
    grad_tokens = (dhidden + norm_back(tokens.astype(F32), attn_gain, dn1)).astype(BF)

    def unpack(mine, shapes):
        found = []
        at = 0
        for height, cols in shapes:
            count = -(-cols // LANES)
            piece = mine[at : at + count * height].reshape(count, height, LANES).transpose(1, 0, 2).reshape(height, count * LANES)
            found.append(piece[:, :cols])
            at += count * height
        return found

    first_shapes = [(share, ranks), (low_rows, q_width * n_tp), (share, ranks), (low_rows, kv_width * n_tp), (share, ranks), (low_rows, kv_width * n_tp)]
    final = unpack(late, first_shapes) + unpack(early_sum, early_shapes)
    return (output, grad_tokens, *final)


def solution(mesh):
    both = P(("fsdp", "ctx"), None)
    split = P("fsdp", None)
    placed = (
        both, both, split, split, both, P(), P(),
        P("fsdp", "tp"), P("fsdp", "tp"), P("fsdp", "tp"), P("tp", "fsdp"), split,
        P("fsdp", None, "tp"), P("fsdp", None, "tp"), P("fsdp", "tp", None),
    ) + (split,) * 16
    return jax.shard_map(
        on_device, mesh=mesh, in_specs=placed, out_specs=(both, both) + (split,) * 16, check_vma=False
    )
```
